32 devices in a mesh: vis: 4 (over y, core), row: 4 (over z), col: 2 (over x).
Axes of the slice: x: 2, y: 2, z: 4, core: 2. Of those that a mesh axis runs over, the one named last changes fastest.
Arguments:
- partials: bfloat16 [4, 2, 512, 512], P('vis', None, 'row', 'col'), may hold values from -6 to 6
- coverage: int32 [4, 4, 4], P('vis', 'row', 'col'), may hold values from 0 to 1, as said below
- conv_one: float32 [32, 3, 3], replicated, may hold values from -2 to 2
- bias_one: float32 [32], replicated, may hold values from -3 to 3
- conv_two: bfloat16 [3, 3, 32, 32], replicated, may hold values from -0.375 to 0.375
- bias_two: float32 [32], replicated, may hold values from -3 to 3
Outputs:
- features: bfloat16 [32, 256, 256], P(None, ('vis', 'row', 'col'))
The draws below stay inside these ranges and needn't reach their ends.
Inputs may be any that keep to these rules, and one draw needn't show every extreme that they name: `coverage`: 0 or 1; blocks near the grid's centre are touched by more groups than those near its corners.
All inputs are finite; a program needn't handle non-finite values.
Results may differ from the reference program's by a relative error of at most 0.014.
Values may be sent and summed in bfloat16 or wider, within the bound.
No kernel may reach another device: no remote copies, remote signals or barrier semaphores. Data moves between devices by JAX's collectives and lax.ppermute only.
A program may use at most 64 MiB of HBM per device.

```python
import jax
import jax.numpy as jnp
from jax import lax

BLK = 128
CH = 32
N = 512
M = 256
GROUPS = 4
NB = 4


def draw_coverage(key, part):
    offset = jnp.arange(NB, dtype=jnp.int32) * 2 - (NB - 1)
    radius = offset[:, None] * offset[None, :] * 0 + offset[:, None] * offset[:, None] + offset[None, :] * offset[None, :]
    ceiling = 2 * (NB - 1) * (NB - 1) + 1
    picked = jax.random.randint(key, (GROUPS, NB, NB), 0, ceiling)
    return (picked < ceiling - radius * 4 // 5).astype(jnp.int32)


def shard_levels(rng, extent, pieces, smallest, high):
    def one(position, parts):
        draws = jax.random.uniform(jax.random.fold_in(jax.random.fold_in(rng, 6), position), (parts,), jnp.float32, smallest / len(pieces), high / len(pieces))
        return jnp.repeat(jnp.exp(draws), extent[position] // parts).reshape((-1,) + (1,) * (len(extent) - position - 1))

    level = one(*pieces[0])
    for cut in pieces[1:]:
        level = level * one(*cut)
    return level


def scatter_about(key, dims, scale, limit, shards=(), kind=jnp.bfloat16):
    drawn = scale * jax.random.normal(key, dims, jnp.float32)
    if shards:
        drawn = drawn * shard_levels(key, dims, shards, -0.22, 0.18)
    return jnp.clip(drawn, -limit, limit).astype(kind)


def setup_inputs(seed: int = 0) -> dict:
    streams_of = jax.random.split(jax.random.key(seed), 7)
    partials = scatter_about(streams_of[0], (GROUPS, 2, N, N), 1.0, 6.0, ((0, 4), (2, 4), (3, 2)))
    coverage = draw_coverage(jax.random.fold_in(streams_of[6], 71), 0)
    conv_one = scatter_about(streams_of[2], (CH, 3, 3), 9 ** -0.5, 2.0, (), jnp.float32)
    bias_one = scatter_about(streams_of[3], (CH,), 0.5, 3.0, (), jnp.float32)
    conv_two = scatter_about(streams_of[4], (3, 3, CH, CH), (9 * CH) ** -0.5, 0.375)
    bias_two = scatter_about(streams_of[5], (CH,), 0.5, 3.0, (), jnp.float32)
    return {"partials": partials, "coverage": coverage, "conv_one": conv_one, "bias_one": bias_one, "conv_two": conv_two, "bias_two": bias_two}


def reference(partials, coverage, conv_one, bias_one, conv_two, bias_two):
    grid_re = jnp.zeros((N, N), jnp.float32)
    grid_im = jnp.zeros((N, N), jnp.float32)
    for group in range(GROUPS):
        spread = jnp.repeat(jnp.repeat(coverage[group], BLK, axis=0), BLK, axis=1).astype(jnp.float32)
        grid_re = grid_re + spread * partials[group, 0].astype(jnp.float32)
        grid_im = grid_im + spread * partials[group, 1].astype(jnp.float32)
    quarter = jnp.array([1.0, -1.0j, -1.0, 1.0j])
    phase = quarter[jnp.arange(N, dtype=jnp.int32) % 4]
    shifted = (grid_re + 1j * grid_im) * phase[:, None] * phase[None, :]
    spectrum = jnp.fft.ifft2(shifted)[:M, :M] * (N * N)
    signs = (1 - 2 * (jnp.arange(M, dtype=jnp.int32) % 2)).astype(jnp.float32)
    image = jnp.real(spectrum).astype(jnp.float32) * signs[:, None] * signs[None, :] / N
    image = image.T
    first = lax.conv_general_dilated(image[None, None], conv_one[:, None], (1, 1), "SAME",
                                     precision=lax.Precision.HIGHEST)
    hidden = jnp.maximum(first[0] + bias_one[:, None, None], 0.0).astype(jnp.bfloat16)
    kernel = jnp.transpose(conv_two, (2, 3, 0, 1))
    second = lax.conv_general_dilated(hidden[None], kernel, (1, 1), "SAME",
                                      preferred_element_type=jnp.float32)
    return (second[0] + bias_two[:, None, None]).astype(jnp.bfloat16)
```

```python
import functools
import math

import jax
import jax.numpy as jnp
import numpy as np
from jax import lax
from jax.experimental import pallas as pl
from jax.experimental.pallas import tpu as pltpu
from jax.sharding import PartitionSpec as P

BLK = 128
ALL = ("vis", "row", "col")
DIRECT_BYTES = 4 * 2**20
HALO = 2
TILE = 8
LANES = 128


def with_halo(cells, sides, width):
    for axis, dim in sides:
        count = lax.axis_size(axis)
        ends = count - 1
        head = lax.slice_in_dim(cells, 0, width, axis=dim)
        tail = lax.slice_in_dim(cells, cells.shape[dim] - width, cells.shape[dim], axis=dim)
        cells = jnp.concatenate(
            [
                lax.ppermute(tail, axis, [(i, (i + 1) % count) for i in range(ends)]),
                cells,
                lax.ppermute(head, axis, [((i + 1) % count, i) for i in range(ends)]),
            ],
            axis=dim,
        )
    return cells


def phase_table(numer, denom):
    angle = numer.astype(jnp.float32) * (2.0 * math.pi / denom)
    return (jnp.cos(angle), jnp.sin(angle))


def partial_transform(real_part, imag_part, block_of, keep_imag):
    batch = real_part.shape[0]
    count_blocks = real_part.shape[1]
    block_len = real_part.shape[2]
    length = count_blocks * block_len
    highest = lax.Precision.HIGHEST
    outer = jnp.arange(count_blocks, dtype=jnp.int32)
    inner = jnp.arange(block_len, dtype=jnp.int32)
    cos_one, sin_one = phase_table(block_of[:, None] * outer[None, :] % count_blocks, count_blocks)
    mid_re = jnp.einsum("lpt,px->lxt", real_part, cos_one, precision=highest) - jnp.einsum(
        "lpt,px->lxt", imag_part, sin_one, precision=highest
    )
    mid_im = jnp.einsum("lpt,px->lxt", real_part, sin_one, precision=highest) + jnp.einsum(
        "lpt,px->lxt", imag_part, cos_one, precision=highest
    )
    cos_two, sin_two = phase_table(outer[:, None] * inner[None, :] % length, length)
    parity = (1 - 2 * (outer % 2)).astype(jnp.float32)[:, None]
    cos_two = cos_two * parity
    sin_two = sin_two * parity
    turn_re = mid_re * cos_two - mid_im * sin_two
    turn_im = mid_re * sin_two + mid_im * cos_two
    kept = jnp.arange(block_len // 2, dtype=jnp.int32)
    picked = (kept + 3 * block_len // 4) % block_len
    cos_three, sin_three = phase_table(inner[:, None] * picked[None, :] % block_len, block_len)
    out_re = jnp.einsum("lxt,tj->ljx", turn_re, cos_three, precision=highest) - jnp.einsum(
        "lxt,tj->ljx", turn_im, sin_three, precision=highest
    )
    out_re = out_re.reshape(batch, length // 2)
    if keep_imag:
        out_im = jnp.einsum("lxt,tj->ljx", turn_re, sin_three, precision=highest) + jnp.einsum(
            "lxt,tj->ljx", turn_im, cos_three, precision=highest
        )
        return (out_re, out_im.reshape(batch, length // 2))
    return (out_re, out_re)


def first_layer(extended, conv_one, bias_one, count_rows):
    width = extended.shape[1]
    padded = jnp.pad(extended, ((0, 0), (1, 1)))
    summed = (
        jnp.zeros((conv_one.shape[0], count_rows, width), jnp.float32) + bias_one[:, None, None]
    )
    for shift_b in range(3):
        for shift_a in range(3):
            summed = (
                summed
                + conv_one[:, shift_b, shift_a][:, None, None]
                * padded[None, shift_b : shift_b + count_rows, shift_a : shift_a + width]
            )
    return jnp.maximum(summed, 0.0)


def second_layer(hidden_ext, conv_two, bias_two, count_rows):
    width = hidden_ext.shape[2]
    padded = jnp.pad(hidden_ext, ((0, 0), (0, 0), (1, 1)))
    summed = jnp.zeros((conv_two.shape[2], count_rows, width), jnp.float32)
    for shift_b in range(3):
        for shift_a in range(3):
            summed = summed + jnp.einsum(
                "kj,jba->kba",
                conv_two[shift_b, shift_a],
                padded[:, shift_b : shift_b + count_rows, shift_a : shift_a + width],
                preferred_element_type=jnp.float32,
            )
    return (summed + bias_two[:, None, None]).astype(jnp.bfloat16)


def staged(partials, coverage, conv_one, bias_one, conv_two, bias_two):
    count_vis = lax.axis_size("vis")
    count_row = lax.axis_size("row")
    count_col = lax.axis_size("col")
    grid_len = partials.shape[3] * count_col
    cover = coverage[0]
    block_rows = cover.shape[0]
    block_cols = cover.shape[1]
    spread = jnp.broadcast_to(cover[:, None, :, None], (block_rows, BLK, block_cols, BLK))
    spread = spread.reshape(block_rows * BLK, block_cols * BLK)
    count_blocks = count_vis * count_row
    row_block = grid_len // count_blocks
    row_share = row_block // count_col
    masked = partials[0] * spread.astype(jnp.bfloat16)[None]
    reduced = lax.psum_scatter(
        masked.astype(jnp.float32).astype(jnp.bfloat16), "vis", scatter_dimension=1, tiled=True
    ).astype(jnp.float32)
    grid_rows = lax.all_to_all(
        reduced.astype(jnp.bfloat16), "col", split_axis=1, concat_axis=2, tiled=True
    ).astype(reduced.dtype)
    natural = jnp.arange(count_blocks, dtype=jnp.int32)
    shaped = grid_rows.reshape(2, row_share, count_blocks, row_block)
    first_re, first_im = partial_transform(shaped[0], shaped[1], natural, True)
    stacked = jnp.stack([first_re, first_im])
    moved = lax.all_to_all(
        lax.all_to_all(
            stacked.astype(jnp.bfloat16), ("vis", "row"), split_axis=2, concat_axis=1, tiled=True
        ),
        "col",
        split_axis=2,
        concat_axis=1,
        tiled=True,
    ).astype(stacked.dtype)
    img_rows = moved.shape[2]
    arranged = moved.reshape(2, count_col, count_blocks, row_share, img_rows)
    arranged = arranged.transpose(0, 4, 2, 1, 3).reshape(2, img_rows, count_blocks, row_block)
    owners = natural % count_row * count_vis + natural // count_row
    image, unused = partial_transform(arranged[0], arranged[1], owners, False)
    image = image * (1.0 / grid_len)
    extended = with_halo(image.astype(jnp.bfloat16), ((("vis", "row", "col"), 0),), 1).astype(
        image.dtype
    )
    hidden = first_layer(extended, conv_one, bias_one, img_rows).astype(jnp.bfloat16)
    hidden_ext = with_halo(hidden, ((("vis", "row", "col"), 1),), 1)
    return second_layer(hidden_ext, conv_two, bias_two, img_rows)


def grid_tables(length, count_row, count_col):
    image_len = length // 2
    place = np.arange(length)[:, None] - length // 2
    pixel = np.arange(image_len)[None, :] - image_len // 2
    angle = (place * pixel % length) * (2.0 * math.pi / length)
    cos, sin = np.cos(angle), np.sin(angle)
    cols = length // count_col
    first = np.concatenate([cos.T, sin.T], axis=0)
    first = first.reshape(2 * image_len, count_col, cols).transpose(1, 0, 2)
    rows = length // count_row
    second = np.stack([cos.reshape(count_row, rows, image_len), -sin.reshape(count_row, rows, image_len)], axis=1)
    second = second.reshape(count_row, 2 * rows, image_len) / length
    return first.astype(jnp.bfloat16), second.astype(jnp.bfloat16)


def share_kernel(cover, parts, first_all, second_all, out, first, second, padded, sems):
    col, row = lax.axis_index("col"), lax.axis_index("row")
    get_first = pltpu.make_async_copy(first_all.at[col], first, sems.at[0])
    get_second = pltpu.make_async_copy(second_all.at[row], second, sems.at[1])
    get_first.start()
    get_second.start()
    count_rows, count_cols = parts.shape[2], parts.shape[3]
    image_len = second.shape[1]
    halves = []
    for component in range(2):
        strips = []
        for i in range(cover.shape[1]):
            cells = []
            for j in range(cover.shape[2]):
                block = parts[0, component, i * BLK : (i + 1) * BLK, j * BLK : (j + 1) * BLK]
                cells.append(block.astype(jnp.float32) * cover[0, i, j].astype(jnp.float32))
            strips.append(jnp.concatenate(cells, axis=1))
        halves.append(jnp.concatenate(strips, axis=0))
    grid = jnp.concatenate(halves, axis=0).astype(jnp.bfloat16)
    get_first.wait()
    turned = lax.dot_general(first[...], grid, (((1,), (1,)), ((), ())), preferred_element_type=jnp.float32)
    mid_re = turned[:image_len, :count_rows] - turned[image_len:, count_rows:]
    mid_im = turned[image_len:, :count_rows] + turned[:image_len, count_rows:]
    mid = jnp.concatenate([mid_re, mid_im], axis=1).astype(jnp.bfloat16)
    get_second.wait()
    edge = jnp.zeros((TILE, image_len), jnp.float32)
    padded[:TILE] = edge
    padded[TILE + image_len :] = edge
    padded[TILE : TILE + image_len] = jnp.dot(mid, second[...], preferred_element_type=jnp.float32)
    upper = lax.broadcasted_iota(jnp.int32, (TILE, LANES), 0) < TILE // 2
    for device in range(out.shape[0]):
        top = TILE * (device + 1) - HALO
        left, right = slice(0, LANES), slice(LANES, 2 * LANES)
        shared = jnp.where(
            upper, padded[top + TILE : top + 2 * TILE, left], padded[top - TILE // 2 : top + TILE // 2, right]
        )
        window = [padded[top : top + TILE, left], shared, padded[top + TILE // 2 : top + 3 * TILE // 2, right]]
        out[device] = jnp.concatenate(window, axis=0).astype(out.dtype)


def split_bf16(values, count):
    pieces = []
    for _ in range(count):
        piece = lax.reduce_precision(values, 8, 7)
        pieces.append(piece.astype(jnp.bfloat16))
        values = values - piece
    return pieces


def first_weights(conv_one, bias_one):
    channels = conv_one.shape[0]
    taps = conv_one.transpose(0, 2, 1)
    rows = TILE + 2
    placed = jnp.stack([jnp.pad(taps, ((0, 0), (0, 0), (h, 13 - h))) for h in range(rows)])
    placed = placed.reshape(rows * channels, 48)
    high, low = split_bf16(placed, 2)
    bias = jnp.stack(split_bf16(bias_one, 3), axis=1)
    bias = jnp.pad(bias, ((0, 0), (12, 33)))
    bias = jnp.broadcast_to(bias[None], (rows, channels, 48)).reshape(rows * channels, 48)
    return jnp.concatenate([high + bias, high, low], axis=1)


def second_weights(conv_two, bias_two):
    _, _, outs, ins = conv_two.shape
    taps = conv_two.transpose(2, 1, 0, 3).reshape(outs, 3, 3 * ins)
    placed = jnp.stack(
        [jnp.pad(taps, ((0, 0), (0, 0), (b * ins, (TILE - 1 - b) * ins))) for b in range(TILE)], axis=1
    )
    placed = placed.reshape(outs * TILE, 3 * (TILE + 2) * ins)
    bias = jnp.pad(jnp.stack(split_bf16(bias_two, 3), axis=1), ((0, 0), (0, 13)))
    bias = jnp.broadcast_to(bias[:, None], (outs, TILE, 16)).reshape(outs * TILE, 16)
    return jnp.concatenate([placed, bias], axis=1)


def shifted(values, width):
    lane = lax.broadcasted_iota(jnp.int32, values.shape, 1)
    before = jnp.where(lane == 0, 0.0, pltpu.roll(values, 1, 1))
    after = jnp.where(lane == width - 1, 0.0, pltpu.roll(values, width - 1, 1))
    return before, values, after


def layers_kernel(shares, weights_one, weights_two, out):
    place = (lax.axis_index("vis") * lax.axis_size("row") + lax.axis_index("row")) * lax.axis_size(
        "col"
    ) + lax.axis_index("col")
    last = shares.shape[0] - 1
    total = shares[0].astype(jnp.float32)
    for device in range(1, shares.shape[0]):
        total = total + shares[device].astype(jnp.float32)
    width = out.shape[2]
    image = jnp.concatenate([total[:12], total[12:]], axis=1)
    image = jnp.concatenate([image, jnp.zeros((4, width), jnp.float32)], axis=0)
    columns = jnp.concatenate(shifted(image, width), axis=0)
    high = columns.astype(jnp.bfloat16).astype(jnp.float32)
    low = columns - high
    row = lax.broadcasted_iota(jnp.int32, (48, width), 0)
    with_ones = jnp.where((row >= 12) & (row < 15), 1.0, high)
    stacked = jnp.concatenate([with_ones, low, high], axis=0).astype(jnp.bfloat16)
    hidden = jnp.dot(weights_one[...], stacked, preferred_element_type=jnp.float32)
    hidden = jnp.maximum(hidden, 0.0)
    channels = hidden.shape[0] // (TILE + 2)
    row = lax.broadcasted_iota(jnp.int32, hidden.shape, 0)
    outside = ((row < channels) & (place == 0)) | ((row >= channels * (TILE + 1)) & (place == last))
    hidden = jnp.where(outside, 0.0, hidden)
    ones = jnp.where(lax.broadcasted_iota(jnp.int32, (16, width), 0) < 3, 1.0, 0.0)
    stacked = jnp.concatenate([*shifted(hidden, width), ones], axis=0).astype(jnp.bfloat16)
    features = jnp.dot(weights_two[...], stacked, preferred_element_type=jnp.float32)
    out[...] = features.reshape(out.shape).astype(out.dtype)


def direct(partials, coverage, conv_one, bias_one, conv_two, bias_two):
    count_row, count_col = lax.axis_size("row"), lax.axis_size("col")
    devices = lax.axis_size("vis") * count_row * count_col
    length = partials.shape[3] * count_col
    image_len = length // 2
    first, second = grid_tables(length, count_row, count_col)
    vmem, smem = pl.BlockSpec(memory_space=pltpu.VMEM), pl.BlockSpec(memory_space=pltpu.SMEM)
    anywhere = pl.BlockSpec(memory_space=pl.ANY)
    shares = pl.pallas_call(
        share_kernel,
        out_shape=jax.ShapeDtypeStruct((devices, 2 * (TILE + 2 * HALO), LANES), jnp.bfloat16),
        in_specs=[smem, vmem, anywhere, anywhere],
        out_specs=vmem,
        scratch_shapes=[
            pltpu.VMEM(first.shape[1:], jnp.bfloat16),
            pltpu.VMEM(second.shape[1:], jnp.bfloat16),
            pltpu.VMEM((image_len + 2 * TILE, image_len), jnp.float32),
            pltpu.SemaphoreType.DMA((2,)),
        ],
        compiler_params=pltpu.CompilerParams(vmem_limit_bytes=16 * 2**20),
        name="shares",
    )(coverage, partials, first, second)
    arrived = lax.all_to_all(shares, ALL, split_axis=0, concat_axis=0, tiled=True)
    return pl.pallas_call(
        layers_kernel,
        out_shape=jax.ShapeDtypeStruct((conv_two.shape[2], TILE, image_len), jnp.bfloat16),
        in_specs=[vmem] * 3,
        out_specs=vmem,
        compiler_params=pltpu.CompilerParams(vmem_limit_bytes=16 * 2**20),
        name="layers",
    )(arrived, first_weights(conv_one, bias_one), second_weights(conv_two, bias_two))


def local(partials, coverage, conv_one, bias_one, conv_two, bias_two):
    count_col = lax.axis_size("col")
    devices = lax.axis_size("vis") * lax.axis_size("row") * count_col
    image_len = partials.shape[3] * count_col // 2
    sent = devices * (TILE + 2 * HALO) * image_len * 2
    fits = image_len == devices * TILE and image_len == 2 * LANES and sent <= DIRECT_BYTES
    plan = direct if fits else staged
    return plan(partials, coverage, conv_one, bias_one, conv_two, bias_two)


def solution(mesh):
    placed = (P("vis", None, "row", "col"), P("vis", "row", "col"), P(), P(), P(), P())
    return jax.shard_map(
        local,
        mesh=mesh,
        in_specs=placed,
        out_specs=P(None, ALL, None),
        check_vma=False,
    )
```

```python
import functools
import math

import jax
import jax.numpy as jnp
import numpy as np
from jax import lax
from jax.experimental import pallas as pl
from jax.experimental.pallas import tpu as pltpu
from jax.sharding import PartitionSpec as P

BLK = 128
ALL = ("vis", "row", "col")
DIRECT_BYTES = 4 * 2**20
HALO = 2
TILE = 8
LANES = 128


def with_halo(cells, sides, width):
    for axis, dim in sides:
        count = lax.axis_size(axis)
        ends = count - 1
        head = lax.slice_in_dim(cells, 0, width, axis=dim)
        tail = lax.slice_in_dim(cells, cells.shape[dim] - width, cells.shape[dim], axis=dim)
        cells = jnp.concatenate(
            [
                lax.ppermute(tail, axis, [(i, (i + 1) % count) for i in range(ends)]),
                cells,
                lax.ppermute(head, axis, [((i + 1) % count, i) for i in range(ends)]),
            ],
            axis=dim,
        )
    return cells


def phase_table(numer, denom):
    angle = numer.astype(jnp.float32) * (2.0 * math.pi / denom)
    return (jnp.cos(angle), jnp.sin(angle))


def partial_transform(real_part, imag_part, block_of, keep_imag):
    batch = real_part.shape[0]
    count_blocks = real_part.shape[1]
    block_len = real_part.shape[2]
    length = count_blocks * block_len
    highest = lax.Precision.HIGHEST
    outer = jnp.arange(count_blocks, dtype=jnp.int32)
    inner = jnp.arange(block_len, dtype=jnp.int32)
    cos_one, sin_one = phase_table(block_of[:, None] * outer[None, :] % count_blocks, count_blocks)
    mid_re = jnp.einsum("lpt,px->lxt", real_part, cos_one, precision=highest) - jnp.einsum(
        "lpt,px->lxt", imag_part, sin_one, precision=highest
    )
    mid_im = jnp.einsum("lpt,px->lxt", real_part, sin_one, precision=highest) + jnp.einsum(
        "lpt,px->lxt", imag_part, cos_one, precision=highest
    )
    cos_two, sin_two = phase_table(outer[:, None] * inner[None, :] % length, length)
    parity = (1 - 2 * (outer % 2)).astype(jnp.float32)[:, None]
    cos_two = cos_two * parity
    sin_two = sin_two * parity
    turn_re = mid_re * cos_two - mid_im * sin_two
    turn_im = mid_re * sin_two + mid_im * cos_two
    kept = jnp.arange(block_len // 2, dtype=jnp.int32)
    picked = (kept + 3 * block_len // 4) % block_len
    cos_three, sin_three = phase_table(inner[:, None] * picked[None, :] % block_len, block_len)
    out_re = jnp.einsum("lxt,tj->ljx", turn_re, cos_three, precision=highest) - jnp.einsum(
        "lxt,tj->ljx", turn_im, sin_three, precision=highest
    )
    out_re = out_re.reshape(batch, length // 2)
    if keep_imag:
        out_im = jnp.einsum("lxt,tj->ljx", turn_re, sin_three, precision=highest) + jnp.einsum(
            "lxt,tj->ljx", turn_im, cos_three, precision=highest
        )
        return (out_re, out_im.reshape(batch, length // 2))
    return (out_re, out_re)


def first_layer(extended, conv_one, bias_one, count_rows):
    width = extended.shape[1]
    padded = jnp.pad(extended, ((0, 0), (1, 1)))
    summed = (
        jnp.zeros((conv_one.shape[0], count_rows, width), jnp.float32) + bias_one[:, None, None]
    )
    for shift_b in range(3):
        for shift_a in range(3):
            summed = (
                summed
                + conv_one[:, shift_b, shift_a][:, None, None]
                * padded[None, shift_b : shift_b + count_rows, shift_a : shift_a + width]
            )
    return jnp.maximum(summed, 0.0)


def second_layer(hidden_ext, conv_two, bias_two, count_rows):
    width = hidden_ext.shape[2]
    padded = jnp.pad(hidden_ext, ((0, 0), (0, 0), (1, 1)))
    summed = jnp.zeros((conv_two.shape[2], count_rows, width), jnp.float32)
    for shift_b in range(3):
        for shift_a in range(3):
            summed = summed + jnp.einsum(
                "kj,jba->kba",
                conv_two[shift_b, shift_a],
                padded[:, shift_b : shift_b + count_rows, shift_a : shift_a + width],
                preferred_element_type=jnp.float32,
            )
    return (summed + bias_two[:, None, None]).astype(jnp.bfloat16)


def staged(partials, coverage, conv_one, bias_one, conv_two, bias_two):
    count_vis = lax.axis_size("vis")
    count_row = lax.axis_size("row")
    count_col = lax.axis_size("col")
    grid_len = partials.shape[3] * count_col
    cover = coverage[0]
    block_rows = cover.shape[0]
    block_cols = cover.shape[1]
    spread = jnp.broadcast_to(cover[:, None, :, None], (block_rows, BLK, block_cols, BLK))
    spread = spread.reshape(block_rows * BLK, block_cols * BLK)
    count_blocks = count_vis * count_row
    row_block = grid_len // count_blocks
    row_share = row_block // count_col
    masked = partials[0] * spread.astype(jnp.bfloat16)[None]
    reduced = lax.psum_scatter(
        masked.astype(jnp.float32).astype(jnp.bfloat16), "vis", scatter_dimension=1, tiled=True
    ).astype(jnp.float32)
    grid_rows = lax.all_to_all(
        reduced.astype(jnp.bfloat16), "col", split_axis=1, concat_axis=2, tiled=True
    ).astype(reduced.dtype)
    natural = jnp.arange(count_blocks, dtype=jnp.int32)
    shaped = grid_rows.reshape(2, row_share, count_blocks, row_block)
    first_re, first_im = partial_transform(shaped[0], shaped[1], natural, True)
    stacked = jnp.stack([first_re, first_im])
    moved = lax.all_to_all(
        lax.all_to_all(
            stacked.astype(jnp.bfloat16), ("vis", "row"), split_axis=2, concat_axis=1, tiled=True
        ),
        "col",
        split_axis=2,
        concat_axis=1,
        tiled=True,
    ).astype(stacked.dtype)
    img_rows = moved.shape[2]
    arranged = moved.reshape(2, count_col, count_blocks, row_share, img_rows)
    arranged = arranged.transpose(0, 4, 2, 1, 3).reshape(2, img_rows, count_blocks, row_block)
    owners = natural % count_row * count_vis + natural // count_row
    image, unused = partial_transform(arranged[0], arranged[1], owners, False)
    image = image * (1.0 / grid_len)
    extended = with_halo(image.astype(jnp.bfloat16), ((("vis", "row", "col"), 0),), 1).astype(
        image.dtype
    )
    hidden = first_layer(extended, conv_one, bias_one, img_rows).astype(jnp.bfloat16)
    hidden_ext = with_halo(hidden, ((("vis", "row", "col"), 1),), 1)
    return second_layer(hidden_ext, conv_two, bias_two, img_rows)


def grid_tables(length, count_row, count_col):
    image_len = length // 2
    place = np.arange(length)[:, None] - length // 2
    pixel = np.arange(image_len)[None, :] - image_len // 2
    angle = (place * pixel % length) * (2.0 * math.pi / length)
    cos, sin = np.cos(angle), np.sin(angle)
    cols = length // count_col
    first = np.concatenate([cos.T, sin.T], axis=0)
    first = first.reshape(2 * image_len, count_col, cols).transpose(1, 0, 2)
    rows = length // count_row
    second = np.stack([cos.reshape(count_row, rows, image_len), -sin.reshape(count_row, rows, image_len)], axis=1)
    second = second.reshape(count_row, 2 * rows, image_len) / length
    return first.astype(jnp.bfloat16), second.astype(jnp.bfloat16)


def share_kernel(cover_in, parts_in, first_all, second_all, out, cover, parts, first, second, padded, cut, sems, sent):
    fetch = [
        pltpu.make_async_copy(parts_in, parts, sems.at[0]),
        pltpu.make_async_copy(first_all.at[lax.axis_index("col")], first, sems.at[1]),
        pltpu.make_async_copy(cover_in, cover, sems.at[2]),
        pltpu.make_async_copy(second_all.at[lax.axis_index("row")], second, sems.at[3]),
    ]
    for copy in fetch:
        copy.start()
    count_rows = parts.shape[2]
    image_len = second.shape[1]
    edge = jnp.zeros((TILE, image_len), jnp.float32)
    padded[:TILE] = edge
    padded[TILE + image_len :] = edge
    fetch[0].wait()
    fetch[2].wait()
    halves = []
    for component in range(2):
        strips = []
        for i in range(cover.shape[1]):
            cells = []
            for j in range(cover.shape[2]):
                block = parts[0, component, i * BLK : (i + 1) * BLK, j * BLK : (j + 1) * BLK]
                cells.append(block.astype(jnp.float32) * cover[0, i, j].astype(jnp.float32))
            strips.append(jnp.concatenate(cells, axis=1))
        halves.append(jnp.concatenate(strips, axis=0))
    grid = jnp.concatenate(halves, axis=0).astype(jnp.bfloat16)
    fetch[1].wait()
    turned = lax.dot_general(first[...], grid, (((1,), (1,)), ((), ())), preferred_element_type=jnp.float32)
    mid_re = turned[:image_len, :count_rows] - turned[image_len:, count_rows:]
    mid_im = turned[image_len:, :count_rows] + turned[:image_len, count_rows:]
    mid = jnp.concatenate([mid_re, mid_im], axis=1).astype(jnp.bfloat16)
    fetch[3].wait()
    padded[TILE : TILE + image_len] = jnp.dot(mid, second[...], preferred_element_type=jnp.float32)
    upper = lax.broadcasted_iota(jnp.int32, (TILE, LANES), 0) < TILE // 2
    left, right = slice(0, LANES), slice(LANES, 2 * LANES)
    devices = cut.shape[0]
    group = devices // sent.shape[0]
    copies = []
    for device in range(devices):
        top = TILE * (device + 1) - HALO
        middle = jnp.where(
            upper, padded[top + TILE : top + 2 * TILE, left], padded[top + TILE // 2 : top + 3 * TILE // 2, right]
        )
        window = [padded[top : top + TILE, left], middle, padded[top : top + TILE, right]]
        cut[device] = jnp.concatenate(window, axis=0).astype(cut.dtype)
        if (device + 1) % group == 0:
            part = pl.ds(device + 1 - group, group)
            copies.append(pltpu.make_async_copy(cut.at[part], out.at[part], sent.at[device // group]))
            copies[-1].start()
    for copy in copies:
        copy.wait()


def four_times(values):
    return jnp.concatenate([values] * 4, axis=1)


def weights_kernel(one_in, bias_in, two_in, bias_two_in, weights_one, weights_two, bias_rows, one, bias, two, bias_two, sems):
    fetch = [
        pltpu.make_async_copy(one_in, one, sems.at[0]),
        pltpu.make_async_copy(bias_in, bias, sems.at[1]),
        pltpu.make_async_copy(two_in, two, sems.at[2]),
        pltpu.make_async_copy(bias_two_in, bias_two, sems.at[3]),
    ]
    for copy in fetch:
        copy.start()
    for copy in fetch:
        copy.wait()
    channels = one.shape[2]
    rows = TILE + 2
    per_tile = LANES // channels
    lanes = -(-rows * channels // LANES) * LANES
    image_row = lax.broadcasted_iota(jnp.int32, (16, lanes), 0)
    hidden_row = lax.broadcasted_iota(jnp.int32, (16, lanes), 1) // channels
    held = hidden_row < rows
    high, low = [], []
    for tap in range(3):
        band = jnp.zeros((16, lanes), jnp.float32)
        for shift in range(3):
            line = jnp.concatenate([four_times(one[shift, tap : tap + 1])] * (lanes // LANES), axis=1)
            band = jnp.where(held & (image_row - hidden_row == shift), line, band)
        high.append(band.astype(jnp.bfloat16).astype(jnp.float32))
        low.append(band - high[-1])
    line = jnp.concatenate([four_times(bias[...])] * (lanes // LANES), axis=1)
    with_bias = high[0]
    for piece in range(3):
        rounded = line.astype(jnp.bfloat16).astype(jnp.float32)
        with_bias = jnp.where(held & (image_row == 12 + piece), rounded, with_bias)
        line = line - rounded
    stacked = jnp.concatenate([with_bias, *high[1:], *high, *low], axis=0)
    weights_one[...] = stacked.T[: weights_one.shape[0]].astype(jnp.bfloat16)
    row = lax.broadcasted_iota(jnp.int32, bias_rows.shape, 0) // TILE
    lane = lax.broadcasted_iota(jnp.int32, bias_rows.shape, 1)
    line = jnp.where(row == lane, four_times(bias_two[...]), 0.0)
    bias_rows[...] = jnp.broadcast_to(jnp.sum(line, axis=1, keepdims=True), bias_rows.shape)
    lines = [[four_times(two[shift, tap].astype(jnp.float32)) for shift in range(3)] for tap in range(3)]
    row = lax.broadcasted_iota(jnp.int32, (TILE, LANES), 0)
    lane = lax.broadcasted_iota(jnp.int32, (TILE, LANES), 1) // channels
    zero = jnp.zeros((TILE, LANES), jnp.float32)
    for tile in range(-(-3 * rows // per_tile)):
        taps = sorted({(tile * per_tile + g) // rows for g in range(per_tile)} & {0, 1, 2})
        masks = []
        for tap in taps:
            hidden_row = tile * per_tile + lane - tap * rows
            inside = (hidden_row >= 0) & (hidden_row < rows)
            masks += [(tap, shift, inside & (hidden_row - row == shift)) for shift in range(3)]
        width = min(LANES, weights_two.shape[1] - tile * LANES)
        for channel in range(0, channels, 2):
            pair = []
            for k in (channel, channel + 1):
                values = zero
                for tap, shift, mask in masks:
                    values = jnp.where(mask, lines[tap][shift][k : k + 1], values)
                pair.append(values)
            block = jnp.concatenate(pair, axis=0).astype(jnp.bfloat16)
            weights_two[TILE * channel : TILE * (channel + 2), tile * LANES : tile * LANES + width] = block[:, :width]


def shifted(values, width):
    lane = lax.broadcasted_iota(jnp.int32, values.shape, 1)
    before = jnp.where(lane == 0, 0.0, pltpu.roll(values, 1, 1))
    after = jnp.where(lane == width - 1, 0.0, pltpu.roll(values, width - 1, 1))
    return before, values, after


def layers_kernel(shares, weights_one, weights_two, bias_rows, out):
    place = (lax.axis_index("vis") * lax.axis_size("row") + lax.axis_index("row")) * lax.axis_size(
        "col"
    ) + lax.axis_index("col")
    last = shares.shape[0] - 1
    total = shares[0].astype(jnp.float32)
    for device in range(1, shares.shape[0]):
        total = total + shares[device].astype(jnp.float32)
    width = out.shape[2]
    middle = total[TILE : 2 * TILE]
    upper = lax.broadcasted_iota(jnp.int32, (TILE, width), 0) < TILE // 2
    lower_rows = jnp.concatenate([middle, pltpu.roll(middle, TILE // 2, 0)], axis=1)
    image = jnp.concatenate(
        [jnp.concatenate([total[:TILE], total[2 * TILE :]], axis=1), jnp.where(upper, lower_rows, 0.0)], axis=0
    )
    columns = jnp.concatenate(shifted(image, width), axis=0)
    high = columns.astype(jnp.bfloat16).astype(jnp.float32)
    low = columns - high
    row = lax.broadcasted_iota(jnp.int32, (48, width), 0)
    with_ones = jnp.where((row >= 12) & (row < 15), 1.0, high)
    stacked = jnp.concatenate([with_ones, low, high], axis=0).astype(jnp.bfloat16)
    hidden = jnp.dot(weights_one[...], stacked, preferred_element_type=jnp.float32)
    hidden = jnp.maximum(hidden, 0.0)
    channels = hidden.shape[0] // (TILE + 2)
    row = lax.broadcasted_iota(jnp.int32, hidden.shape, 0)
    outside = ((row < channels) & (place == 0)) | ((row >= channels * (TILE + 1)) & (place == last))
    hidden = jnp.where(outside, 0.0, hidden)
    stacked = jnp.concatenate(shifted(hidden, width), axis=0).astype(jnp.bfloat16)
    features = jnp.dot(weights_two[...], stacked, preferred_element_type=jnp.float32)
    features = features + jnp.concatenate([bias_rows[...]] * (width // LANES), axis=1)
    out[...] = features.reshape(out.shape).astype(out.dtype)


def in_hbm(*arrays):
    return [pltpu.with_memory_space_constraint(array, pltpu.HBM) for array in arrays]


def direct(partials, coverage, conv_one, bias_one, conv_two, bias_two):
    count_row, count_col = lax.axis_size("row"), lax.axis_size("col")
    devices = lax.axis_size("vis") * count_row * count_col
    length = partials.shape[3] * count_col
    image_len = length // 2
    channels = conv_two.shape[2]
    first, second = grid_tables(length, count_row, count_col)
    vmem, hbm = pl.BlockSpec(memory_space=pltpu.VMEM), pl.BlockSpec(memory_space=pltpu.HBM)
    limit = pltpu.CompilerParams(vmem_limit_bytes=16 * 2**20)
    share = (devices, 2 * (TILE + 2 * HALO), LANES)
    groups = math.gcd(devices, 4)
    shares = pl.pallas_call(
        share_kernel,
        out_shape=jax.ShapeDtypeStruct(share, jnp.bfloat16),
        in_specs=[hbm] * 4,
        out_specs=hbm,
        scratch_shapes=[
            pltpu.SMEM(coverage.shape, jnp.int32),
            pltpu.VMEM(partials.shape, jnp.bfloat16),
            pltpu.VMEM(first.shape[1:], jnp.bfloat16),
            pltpu.VMEM(second.shape[1:], jnp.bfloat16),
            pltpu.VMEM((image_len + 2 * TILE, image_len), jnp.float32),
            pltpu.VMEM(share, jnp.bfloat16),
            pltpu.SemaphoreType.DMA((4,)),
            pltpu.SemaphoreType.DMA((groups,)),
        ],
        compiler_params=limit,
        name="shares",
    )(*in_hbm(coverage, partials, jnp.asarray(first), jnp.asarray(second)))
    arrived = lax.all_to_all(shares, ALL, split_axis=0, concat_axis=0, tiled=True)
    rows = TILE + 2
    weights = pl.pallas_call(
        weights_kernel,
        out_shape=[
            jax.ShapeDtypeStruct((rows * channels, 3 * 48), jnp.bfloat16),
            jax.ShapeDtypeStruct((TILE * channels, 3 * rows * channels), jnp.bfloat16),
            jax.ShapeDtypeStruct((TILE * channels, LANES), jnp.float32),
        ],
        in_specs=[hbm] * 4,
        out_specs=[vmem] * 3,
        scratch_shapes=[
            pltpu.VMEM((3, 3, channels), jnp.float32),
            pltpu.VMEM((1, channels), jnp.float32),
            pltpu.VMEM(conv_two.shape, jnp.bfloat16),
            pltpu.VMEM((1, channels), jnp.float32),
            pltpu.SemaphoreType.DMA((4,)),
        ],
        compiler_params=limit,
        name="weights",
    )(*in_hbm(conv_one.transpose(1, 2, 0), bias_one[None], conv_two, bias_two[None]))
    return pl.pallas_call(
        layers_kernel,
        out_shape=jax.ShapeDtypeStruct((channels, TILE, image_len), jnp.bfloat16),
        in_specs=[vmem] * 4,
        out_specs=vmem,
        compiler_params=limit,
        name="layers",
    )(arrived, *weights)


def local(partials, coverage, conv_one, bias_one, conv_two, bias_two):
    count_col = lax.axis_size("col")
    devices = lax.axis_size("vis") * lax.axis_size("row") * count_col
    image_len = partials.shape[3] * count_col // 2
    sent = devices * (TILE + 2 * HALO) * image_len * 2
    fits = image_len == devices * TILE and conv_two.shape[2] * 4 == LANES and image_len == 2 * LANES and sent <= DIRECT_BYTES
    plan = direct if fits else staged
    return plan(partials, coverage, conv_one, bias_one, conv_two, bias_two)


def solution(mesh):
    placed = (P("vis", None, "row", "col"), P("vis", "row", "col"), P(), P(), P(), P())
    return jax.shard_map(
        local,
        mesh=mesh,
        in_specs=placed,
        out_specs=P(None, ALL, None),
        check_vma=False,
    )
```

```python
import functools
import math

import jax
import jax.numpy as jnp
import numpy as np
from jax import lax
from jax.experimental import pallas as pl
from jax.experimental.pallas import tpu as pltpu
from jax.sharding import PartitionSpec as P

BLK = 128
ALL = ("vis", "row", "col")
DIRECT_BYTES = 4 * 2**20
HALO = 2
TILE = 8
LANES = 128


def with_halo(cells, sides, width):
    for axis, dim in sides:
        count = lax.axis_size(axis)
        ends = count - 1
        head = lax.slice_in_dim(cells, 0, width, axis=dim)
        tail = lax.slice_in_dim(cells, cells.shape[dim] - width, cells.shape[dim], axis=dim)
        cells = jnp.concatenate(
            [
                lax.ppermute(tail, axis, [(i, (i + 1) % count) for i in range(ends)]),
                cells,
                lax.ppermute(head, axis, [((i + 1) % count, i) for i in range(ends)]),
            ],
            axis=dim,
        )
    return cells


def phase_table(numer, denom):
    angle = numer.astype(jnp.float32) * (2.0 * math.pi / denom)
    return (jnp.cos(angle), jnp.sin(angle))


def partial_transform(real_part, imag_part, block_of, keep_imag):
    batch = real_part.shape[0]
    count_blocks = real_part.shape[1]
    block_len = real_part.shape[2]
    length = count_blocks * block_len
    highest = lax.Precision.HIGHEST
    outer = jnp.arange(count_blocks, dtype=jnp.int32)
    inner = jnp.arange(block_len, dtype=jnp.int32)
    cos_one, sin_one = phase_table(block_of[:, None] * outer[None, :] % count_blocks, count_blocks)
    mid_re = jnp.einsum("lpt,px->lxt", real_part, cos_one, precision=highest) - jnp.einsum(
        "lpt,px->lxt", imag_part, sin_one, precision=highest
    )
    mid_im = jnp.einsum("lpt,px->lxt", real_part, sin_one, precision=highest) + jnp.einsum(
        "lpt,px->lxt", imag_part, cos_one, precision=highest
    )
    cos_two, sin_two = phase_table(outer[:, None] * inner[None, :] % length, length)
    parity = (1 - 2 * (outer % 2)).astype(jnp.float32)[:, None]
    cos_two = cos_two * parity
    sin_two = sin_two * parity
    turn_re = mid_re * cos_two - mid_im * sin_two
    turn_im = mid_re * sin_two + mid_im * cos_two
    kept = jnp.arange(block_len // 2, dtype=jnp.int32)
    picked = (kept + 3 * block_len // 4) % block_len
    cos_three, sin_three = phase_table(inner[:, None] * picked[None, :] % block_len, block_len)
    out_re = jnp.einsum("lxt,tj->ljx", turn_re, cos_three, precision=highest) - jnp.einsum(
        "lxt,tj->ljx", turn_im, sin_three, precision=highest
    )
    out_re = out_re.reshape(batch, length // 2)
    if keep_imag:
        out_im = jnp.einsum("lxt,tj->ljx", turn_re, sin_three, precision=highest) + jnp.einsum(
            "lxt,tj->ljx", turn_im, cos_three, precision=highest
        )
        return (out_re, out_im.reshape(batch, length // 2))
    return (out_re, out_re)


def first_layer(extended, conv_one, bias_one, count_rows):
    width = extended.shape[1]
    padded = jnp.pad(extended, ((0, 0), (1, 1)))
    summed = (
        jnp.zeros((conv_one.shape[0], count_rows, width), jnp.float32) + bias_one[:, None, None]
    )
    for shift_b in range(3):
        for shift_a in range(3):
            summed = (
                summed
                + conv_one[:, shift_b, shift_a][:, None, None]
                * padded[None, shift_b : shift_b + count_rows, shift_a : shift_a + width]
            )
    return jnp.maximum(summed, 0.0)


def second_layer(hidden_ext, conv_two, bias_two, count_rows):
    width = hidden_ext.shape[2]
    padded = jnp.pad(hidden_ext, ((0, 0), (0, 0), (1, 1)))
    summed = jnp.zeros((conv_two.shape[2], count_rows, width), jnp.float32)
    for shift_b in range(3):
        for shift_a in range(3):
            summed = summed + jnp.einsum(
                "kj,jba->kba",
                conv_two[shift_b, shift_a],
                padded[:, shift_b : shift_b + count_rows, shift_a : shift_a + width],
                preferred_element_type=jnp.float32,
            )
    return (summed + bias_two[:, None, None]).astype(jnp.bfloat16)


def staged(partials, coverage, conv_one, bias_one, conv_two, bias_two):
    count_vis = lax.axis_size("vis")
    count_row = lax.axis_size("row")
    count_col = lax.axis_size("col")
    grid_len = partials.shape[3] * count_col
    cover = coverage[0]
    block_rows = cover.shape[0]
    block_cols = cover.shape[1]
    spread = jnp.broadcast_to(cover[:, None, :, None], (block_rows, BLK, block_cols, BLK))
    spread = spread.reshape(block_rows * BLK, block_cols * BLK)
    count_blocks = count_vis * count_row
    row_block = grid_len // count_blocks
    row_share = row_block // count_col
    masked = partials[0] * spread.astype(jnp.bfloat16)[None]
    reduced = lax.psum_scatter(
        masked.astype(jnp.float32).astype(jnp.bfloat16), "vis", scatter_dimension=1, tiled=True
    ).astype(jnp.float32)
    grid_rows = lax.all_to_all(
        reduced.astype(jnp.bfloat16), "col", split_axis=1, concat_axis=2, tiled=True
    ).astype(reduced.dtype)
    natural = jnp.arange(count_blocks, dtype=jnp.int32)
    shaped = grid_rows.reshape(2, row_share, count_blocks, row_block)
    first_re, first_im = partial_transform(shaped[0], shaped[1], natural, True)
    stacked = jnp.stack([first_re, first_im])
    moved = lax.all_to_all(
        lax.all_to_all(
            stacked.astype(jnp.bfloat16), ("vis", "row"), split_axis=2, concat_axis=1, tiled=True
        ),
        "col",
        split_axis=2,
        concat_axis=1,
        tiled=True,
    ).astype(stacked.dtype)
    img_rows = moved.shape[2]
    arranged = moved.reshape(2, count_col, count_blocks, row_share, img_rows)
    arranged = arranged.transpose(0, 4, 2, 1, 3).reshape(2, img_rows, count_blocks, row_block)
    owners = natural % count_row * count_vis + natural // count_row
    image, unused = partial_transform(arranged[0], arranged[1], owners, False)
    image = image * (1.0 / grid_len)
    extended = with_halo(image.astype(jnp.bfloat16), ((("vis", "row", "col"), 0),), 1).astype(
        image.dtype
    )
    hidden = first_layer(extended, conv_one, bias_one, img_rows).astype(jnp.bfloat16)
    hidden_ext = with_halo(hidden, ((("vis", "row", "col"), 1),), 1)
    return second_layer(hidden_ext, conv_two, bias_two, img_rows)


def grid_tables(length, count_row, count_col):
    image_len = length // 2
    place = np.arange(length)[:, None] - length // 2
    pixel = np.arange(image_len)[None, :] - image_len // 2
    angle = (place * pixel % length) * (2.0 * math.pi / length)
    cos, sin = np.cos(angle), np.sin(angle)
    cols = length // count_col
    first = np.concatenate([cos.T, sin.T], axis=0)
    first = first.reshape(2 * image_len, count_col, cols).transpose(1, 0, 2)
    rows = length // count_row
    second = np.stack([cos.reshape(count_row, rows, image_len), -sin.reshape(count_row, rows, image_len)], axis=1)
    second = second.reshape(count_row, 2 * rows, image_len) / length
    return first.astype(jnp.bfloat16), second.astype(jnp.bfloat16)


def share_kernel(cover_in, parts_in, first_all, second_all, out, cover, parts, first, second, padded, sems):
    fetch = [
        pltpu.make_async_copy(parts_in, parts, sems.at[0]),
        pltpu.make_async_copy(first_all.at[lax.axis_index("col")], first, sems.at[1]),
        pltpu.make_async_copy(cover_in, cover, sems.at[2]),
        pltpu.make_async_copy(second_all.at[lax.axis_index("row")], second, sems.at[3]),
    ]
    for copy in fetch:
        copy.start()
    count_rows = parts.shape[2]
    image_len = second.shape[1]
    edge = jnp.zeros((TILE, image_len), jnp.float32)
    padded[:TILE] = edge
    padded[TILE + image_len :] = edge
    fetch[0].wait()
    fetch[2].wait()
    halves = []
    for component in range(2):
        strips = []
        for i in range(cover.shape[1]):
            cells = []
            for j in range(cover.shape[2]):
                block = parts[0, component, i * BLK : (i + 1) * BLK, j * BLK : (j + 1) * BLK]
                cells.append(block.astype(jnp.float32) * cover[0, i, j].astype(jnp.float32))
            strips.append(jnp.concatenate(cells, axis=1))
        halves.append(jnp.concatenate(strips, axis=0))
    grid = jnp.concatenate(halves, axis=0).astype(jnp.bfloat16)
    fetch[1].wait()
    turned = lax.dot_general(first[...], grid, (((1,), (1,)), ((), ())), preferred_element_type=jnp.float32)
    mid_re = turned[:image_len, :count_rows] - turned[image_len:, count_rows:]
    mid_im = turned[image_len:, :count_rows] + turned[:image_len, count_rows:]
    mid = jnp.concatenate([mid_re, mid_im], axis=1).astype(jnp.bfloat16)
    fetch[3].wait()
    padded[TILE : TILE + image_len] = jnp.dot(mid, second[...], preferred_element_type=jnp.float32)
    upper = lax.broadcasted_iota(jnp.int32, (TILE, LANES), 0) < TILE // 2
    left, right = slice(0, LANES), slice(LANES, 2 * LANES)
    for device in range(out.shape[0]):
        top = TILE * (device + 1) - HALO
        middle = jnp.where(
            upper, padded[top + TILE : top + 2 * TILE, left], padded[top + TILE // 2 : top + 3 * TILE // 2, right]
        )
        window = [padded[top : top + TILE, left], middle, padded[top : top + TILE, right]]
        out[device] = jnp.concatenate(window, axis=0).astype(out.dtype)


def four_times(values):
    return jnp.concatenate([values] * 4, axis=1)


def weights_kernel(one_in, bias_in, two_in, bias_two_in, weights_one, weights_two, bias_rows, one, bias, two, bias_two, sems):
    fetch = [
        pltpu.make_async_copy(one_in, one, sems.at[0]),
        pltpu.make_async_copy(bias_in, bias, sems.at[1]),
        pltpu.make_async_copy(two_in, two, sems.at[2]),
        pltpu.make_async_copy(bias_two_in, bias_two, sems.at[3]),
    ]
    for copy in fetch:
        copy.start()
    for copy in fetch:
        copy.wait()
    channels = one.shape[2]
    rows = TILE + 2
    per_tile = LANES // channels
    lanes = -(-rows * channels // LANES) * LANES
    image_row = lax.broadcasted_iota(jnp.int32, (16, lanes), 0)
    hidden_row = lax.broadcasted_iota(jnp.int32, (16, lanes), 1) // channels
    held = hidden_row < rows
    high, low = [], []
    for tap in range(3):
        band = jnp.zeros((16, lanes), jnp.float32)
        for shift in range(3):
            line = jnp.concatenate([four_times(one[shift, tap : tap + 1])] * (lanes // LANES), axis=1)
            band = jnp.where(held & (image_row - hidden_row == shift), line, band)
        high.append(band.astype(jnp.bfloat16).astype(jnp.float32))
        low.append(band - high[-1])
    line = jnp.concatenate([four_times(bias[...])] * (lanes // LANES), axis=1)
    with_bias = high[0]
    for piece in range(3):
        rounded = line.astype(jnp.bfloat16).astype(jnp.float32)
        with_bias = jnp.where(held & (image_row == 12 + piece), rounded, with_bias)
        line = line - rounded
    stacked = jnp.concatenate([with_bias, *high[1:], *high, *low], axis=0)
    weights_one[...] = stacked.T[: weights_one.shape[0]].astype(jnp.bfloat16)
    row = lax.broadcasted_iota(jnp.int32, bias_rows.shape, 0) // TILE
    lane = lax.broadcasted_iota(jnp.int32, bias_rows.shape, 1)
    line = jnp.where(row == lane, four_times(bias_two[...]), 0.0)
    bias_rows[...] = jnp.broadcast_to(jnp.sum(line, axis=1, keepdims=True), bias_rows.shape)
    lines = [[four_times(two[shift, tap].astype(jnp.float32)) for shift in range(3)] for tap in range(3)]
    row = lax.broadcasted_iota(jnp.int32, (TILE, LANES), 0)
    lane = lax.broadcasted_iota(jnp.int32, (TILE, LANES), 1) // channels
    zero = jnp.zeros((TILE, LANES), jnp.float32)
    for tile in range(-(-3 * rows // per_tile)):
        taps = sorted({(tile * per_tile + g) // rows for g in range(per_tile)} & {0, 1, 2})
        masks = []
        for tap in taps:
            hidden_row = tile * per_tile + lane - tap * rows
            inside = (hidden_row >= 0) & (hidden_row < rows)
            masks += [(tap, shift, inside & (hidden_row - row == shift)) for shift in range(3)]
        width = min(LANES, weights_two.shape[1] - tile * LANES)
        for channel in range(0, channels, 2):
            pair = []
            for k in (channel, channel + 1):
                values = zero
                for tap, shift, mask in masks:
                    values = jnp.where(mask, lines[tap][shift][k : k + 1], values)
                pair.append(values)
            block = jnp.concatenate(pair, axis=0).astype(jnp.bfloat16)
            weights_two[TILE * channel : TILE * (channel + 2), tile * LANES : tile * LANES + width] = block[:, :width]


def shifted(values, width):
    lane = lax.broadcasted_iota(jnp.int32, values.shape, 1)
    before = jnp.where(lane == 0, 0.0, pltpu.roll(values, 1, 1))
    after = jnp.where(lane == width - 1, 0.0, pltpu.roll(values, width - 1, 1))
    return before, values, after


def layers_kernel(shares, weights_one, weights_two, bias_rows, out, staged, sems):
    place = (lax.axis_index("vis") * lax.axis_size("row") + lax.axis_index("row")) * lax.axis_size(
        "col"
    ) + lax.axis_index("col")
    last = shares.shape[0] - 1
    total = shares[0].astype(jnp.float32)
    for device in range(1, shares.shape[0]):
        total = total + shares[device].astype(jnp.float32)
    width = out.shape[2]
    middle = total[TILE : 2 * TILE]
    upper = lax.broadcasted_iota(jnp.int32, (TILE, width), 0) < TILE // 2
    lower_rows = jnp.concatenate([middle, pltpu.roll(middle, TILE // 2, 0)], axis=1)
    image = jnp.concatenate(
        [jnp.concatenate([total[:TILE], total[2 * TILE :]], axis=1), jnp.where(upper, lower_rows, 0.0)], axis=0
    )
    columns = jnp.concatenate(shifted(image, width), axis=0)
    high = columns.astype(jnp.bfloat16).astype(jnp.float32)
    low = columns - high
    row = lax.broadcasted_iota(jnp.int32, (48, width), 0)
    with_ones = jnp.where((row >= 12) & (row < 15), 1.0, high)
    stacked = jnp.concatenate([with_ones, low, high], axis=0).astype(jnp.bfloat16)
    hidden = jnp.dot(weights_one[...], stacked, preferred_element_type=jnp.float32)
    hidden = jnp.maximum(hidden, 0.0)
    channels = hidden.shape[0] // (TILE + 2)
    row = lax.broadcasted_iota(jnp.int32, hidden.shape, 0)
    outside = ((row < channels) & (place == 0)) | ((row >= channels * (TILE + 1)) & (place == last))
    hidden = jnp.where(outside, 0.0, hidden)
    stacked = jnp.concatenate(shifted(hidden, width), axis=0).astype(jnp.bfloat16)
    half = out.shape[0] // 2
    copies = []
    for part in range(2):
        rows = pl.ds(part * half * TILE, half * TILE)
        features = jnp.dot(weights_two[rows], stacked, preferred_element_type=jnp.float32)
        features = features + jnp.concatenate([bias_rows[rows]] * (width // LANES), axis=1)
        channels_of = pl.ds(part * half, half)
        staged[channels_of] = features.reshape(half, TILE, width).astype(out.dtype)
        copies.append(pltpu.make_async_copy(staged.at[channels_of], out.at[channels_of], sems.at[part]))
        copies[-1].start()
    for copy in copies:
        copy.wait()


def in_hbm(*arrays):
    return [pltpu.with_memory_space_constraint(array, pltpu.HBM) for array in arrays]


def direct(partials, coverage, conv_one, bias_one, conv_two, bias_two):
    count_row, count_col = lax.axis_size("row"), lax.axis_size("col")
    devices = lax.axis_size("vis") * count_row * count_col
    length = partials.shape[3] * count_col
    image_len = length // 2
    channels = conv_two.shape[2]
    first, second = grid_tables(length, count_row, count_col)
    vmem, hbm = pl.BlockSpec(memory_space=pltpu.VMEM), pl.BlockSpec(memory_space=pltpu.HBM)
    limit = pltpu.CompilerParams(vmem_limit_bytes=16 * 2**20)
    share = (devices, 2 * (TILE + 2 * HALO), LANES)
    shares = pl.pallas_call(
        share_kernel,
        out_shape=pltpu.VMEM(share, jnp.bfloat16),
        in_specs=[hbm] * 4,
        out_specs=vmem,
        scratch_shapes=[
            pltpu.SMEM(coverage.shape, jnp.int32),
            pltpu.VMEM(partials.shape, jnp.bfloat16),
            pltpu.VMEM(first.shape[1:], jnp.bfloat16),
            pltpu.VMEM(second.shape[1:], jnp.bfloat16),
            pltpu.VMEM((image_len + 2 * TILE, image_len), jnp.float32),
            pltpu.SemaphoreType.DMA((4,)),
        ],
        compiler_params=limit,
        name="shares",
    )(*in_hbm(coverage, partials, jnp.asarray(first), jnp.asarray(second)))
    arrived = lax.all_to_all(shares, ALL, split_axis=0, concat_axis=0, tiled=True)
    rows = TILE + 2
    weights = pl.pallas_call(
        weights_kernel,
        out_shape=[
            jax.ShapeDtypeStruct((rows * channels, 3 * 48), jnp.bfloat16),
            jax.ShapeDtypeStruct((TILE * channels, 3 * rows * channels), jnp.bfloat16),
            jax.ShapeDtypeStruct((TILE * channels, LANES), jnp.float32),
        ],
        in_specs=[hbm] * 4,
        out_specs=[vmem] * 3,
        scratch_shapes=[
            pltpu.VMEM((3, 3, channels), jnp.float32),
            pltpu.VMEM((1, channels), jnp.float32),
            pltpu.VMEM(conv_two.shape, jnp.bfloat16),
            pltpu.VMEM((1, channels), jnp.float32),
            pltpu.SemaphoreType.DMA((4,)),
        ],
        compiler_params=limit,
        name="weights",
    )(*in_hbm(conv_one.transpose(1, 2, 0), bias_one[None], conv_two, bias_two[None]))
    return pl.pallas_call(
        layers_kernel,
        out_shape=jax.ShapeDtypeStruct((channels, TILE, image_len), jnp.bfloat16),
        in_specs=[vmem] * 4,
        out_specs=hbm,
        scratch_shapes=[
            pltpu.VMEM((channels, TILE, image_len), jnp.bfloat16),
            pltpu.SemaphoreType.DMA((2,)),
        ],
        compiler_params=limit,
        name="layers",
    )(arrived, *weights)


def local(partials, coverage, conv_one, bias_one, conv_two, bias_two):
    count_col = lax.axis_size("col")
    devices = lax.axis_size("vis") * lax.axis_size("row") * count_col
    image_len = partials.shape[3] * count_col // 2
    sent = devices * (TILE + 2 * HALO) * image_len * 2
    fits = image_len == devices * TILE and conv_two.shape[2] * 4 == LANES and image_len == 2 * LANES and sent <= DIRECT_BYTES
    plan = direct if fits else staged
    return plan(partials, coverage, conv_one, bias_one, conv_two, bias_two)


def solution(mesh):
    placed = (P("vis", None, "row", "col"), P("vis", "row", "col"), P(), P(), P(), P())
    return jax.shard_map(
        local,
        mesh=mesh,
        in_specs=placed,
        out_specs=P(None, ALL, None),
        check_vma=False,
    )
```

```python
import functools
import math

import jax
import jax.numpy as jnp
import numpy as np
from jax import lax
from jax.experimental import pallas as pl
from jax.experimental.pallas import tpu as pltpu
from jax.sharding import PartitionSpec as P

BLK = 128
ALL = ("vis", "row", "col")
SENT = ("col", "vis", "row")
DIRECT_BYTES = 4 * 2**20
HALO = 2
TILE = 8
LANES = 128


def with_halo(cells, sides, width):
    for axis, dim in sides:
        count = lax.axis_size(axis)
        ends = count - 1
        head = lax.slice_in_dim(cells, 0, width, axis=dim)
        tail = lax.slice_in_dim(cells, cells.shape[dim] - width, cells.shape[dim], axis=dim)
        cells = jnp.concatenate(
            [
                lax.ppermute(tail, axis, [(i, (i + 1) % count) for i in range(ends)]),
                cells,
                lax.ppermute(head, axis, [((i + 1) % count, i) for i in range(ends)]),
            ],
            axis=dim,
        )
    return cells


def phase_table(numer, denom):
    angle = numer.astype(jnp.float32) * (2.0 * math.pi / denom)
    return (jnp.cos(angle), jnp.sin(angle))


def partial_transform(real_part, imag_part, block_of, keep_imag):
    batch = real_part.shape[0]
    count_blocks = real_part.shape[1]
    block_len = real_part.shape[2]
    length = count_blocks * block_len
    highest = lax.Precision.HIGHEST
    outer = jnp.arange(count_blocks, dtype=jnp.int32)
    inner = jnp.arange(block_len, dtype=jnp.int32)
    cos_one, sin_one = phase_table(block_of[:, None] * outer[None, :] % count_blocks, count_blocks)
    mid_re = jnp.einsum("lpt,px->lxt", real_part, cos_one, precision=highest) - jnp.einsum(
        "lpt,px->lxt", imag_part, sin_one, precision=highest
    )
    mid_im = jnp.einsum("lpt,px->lxt", real_part, sin_one, precision=highest) + jnp.einsum(
        "lpt,px->lxt", imag_part, cos_one, precision=highest
    )
    cos_two, sin_two = phase_table(outer[:, None] * inner[None, :] % length, length)
    parity = (1 - 2 * (outer % 2)).astype(jnp.float32)[:, None]
    cos_two = cos_two * parity
    sin_two = sin_two * parity
    turn_re = mid_re * cos_two - mid_im * sin_two
    turn_im = mid_re * sin_two + mid_im * cos_two
    kept = jnp.arange(block_len // 2, dtype=jnp.int32)
    picked = (kept + 3 * block_len // 4) % block_len
    cos_three, sin_three = phase_table(inner[:, None] * picked[None, :] % block_len, block_len)
    out_re = jnp.einsum("lxt,tj->ljx", turn_re, cos_three, precision=highest) - jnp.einsum(
        "lxt,tj->ljx", turn_im, sin_three, precision=highest
    )
    out_re = out_re.reshape(batch, length // 2)
    if keep_imag:
        out_im = jnp.einsum("lxt,tj->ljx", turn_re, sin_three, precision=highest) + jnp.einsum(
            "lxt,tj->ljx", turn_im, cos_three, precision=highest
        )
        return (out_re, out_im.reshape(batch, length // 2))
    return (out_re, out_re)


def first_layer(extended, conv_one, bias_one, count_rows):
    width = extended.shape[1]
    padded = jnp.pad(extended, ((0, 0), (1, 1)))
    summed = (
        jnp.zeros((conv_one.shape[0], count_rows, width), jnp.float32) + bias_one[:, None, None]
    )
    for shift_b in range(3):
        for shift_a in range(3):
            summed = (
                summed
                + conv_one[:, shift_b, shift_a][:, None, None]
                * padded[None, shift_b : shift_b + count_rows, shift_a : shift_a + width]
            )
    return jnp.maximum(summed, 0.0)


def second_layer(hidden_ext, conv_two, bias_two, count_rows):
    width = hidden_ext.shape[2]
    padded = jnp.pad(hidden_ext, ((0, 0), (0, 0), (1, 1)))
    summed = jnp.zeros((conv_two.shape[2], count_rows, width), jnp.float32)
    for shift_b in range(3):
        for shift_a in range(3):
            summed = summed + jnp.einsum(
                "kj,jba->kba",
                conv_two[shift_b, shift_a],
                padded[:, shift_b : shift_b + count_rows, shift_a : shift_a + width],
                preferred_element_type=jnp.float32,
            )
    return (summed + bias_two[:, None, None]).astype(jnp.bfloat16)


def staged(partials, coverage, conv_one, bias_one, conv_two, bias_two):
    count_vis = lax.axis_size("vis")
    count_row = lax.axis_size("row")
    count_col = lax.axis_size("col")
    grid_len = partials.shape[3] * count_col
    cover = coverage[0]
    block_rows = cover.shape[0]
    block_cols = cover.shape[1]
    spread = jnp.broadcast_to(cover[:, None, :, None], (block_rows, BLK, block_cols, BLK))
    spread = spread.reshape(block_rows * BLK, block_cols * BLK)
    count_blocks = count_vis * count_row
    row_block = grid_len // count_blocks
    row_share = row_block // count_col
    masked = partials[0] * spread.astype(jnp.bfloat16)[None]
    reduced = lax.psum_scatter(
        masked.astype(jnp.float32).astype(jnp.bfloat16), "vis", scatter_dimension=1, tiled=True
    ).astype(jnp.float32)
    grid_rows = lax.all_to_all(
        reduced.astype(jnp.bfloat16), "col", split_axis=1, concat_axis=2, tiled=True
    ).astype(reduced.dtype)
    natural = jnp.arange(count_blocks, dtype=jnp.int32)
    shaped = grid_rows.reshape(2, row_share, count_blocks, row_block)
    first_re, first_im = partial_transform(shaped[0], shaped[1], natural, True)
    stacked = jnp.stack([first_re, first_im])
    moved = lax.all_to_all(
        lax.all_to_all(
            stacked.astype(jnp.bfloat16), ("vis", "row"), split_axis=2, concat_axis=1, tiled=True
        ),
        "col",
        split_axis=2,
        concat_axis=1,
        tiled=True,
    ).astype(stacked.dtype)
    img_rows = moved.shape[2]
    arranged = moved.reshape(2, count_col, count_blocks, row_share, img_rows)
    arranged = arranged.transpose(0, 4, 2, 1, 3).reshape(2, img_rows, count_blocks, row_block)
    owners = natural % count_row * count_vis + natural // count_row
    image, unused = partial_transform(arranged[0], arranged[1], owners, False)
    image = image * (1.0 / grid_len)
    extended = with_halo(image.astype(jnp.bfloat16), ((("vis", "row", "col"), 0),), 1).astype(
        image.dtype
    )
    hidden = first_layer(extended, conv_one, bias_one, img_rows).astype(jnp.bfloat16)
    hidden_ext = with_halo(hidden, ((("vis", "row", "col"), 1),), 1)
    return second_layer(hidden_ext, conv_two, bias_two, img_rows)


def grid_tables(length, count_row, count_col):
    image_len = length // 2
    place = np.arange(length)[:, None] - length // 2
    pixel = np.arange(image_len)[None, :] - image_len // 2
    angle = (place * pixel % length) * (2.0 * math.pi / length)
    cos, sin = np.cos(angle), np.sin(angle)
    cols = length // count_col
    first = np.concatenate([cos.T, sin.T], axis=0)
    first = first.reshape(2 * image_len, count_col, cols).transpose(1, 0, 2)
    rows = length // count_row
    second = np.stack([cos.reshape(count_row, rows, image_len), -sin.reshape(count_row, rows, image_len)], axis=1)
    second = second.reshape(count_row, 2 * rows, image_len) / length
    return first.astype(jnp.bfloat16), second.astype(jnp.bfloat16)


def send_order():
    sizes = [lax.axis_size(axis) for axis in ALL]
    places = np.arange(math.prod(sizes)).reshape(sizes)
    return places.transpose([ALL.index(axis) for axis in SENT]).reshape(-1).tolist()


def share_kernel(cover_in, parts_in, first_all, second_all, out, cover, parts, first, second, padded, sems):
    fetch = [
        pltpu.make_async_copy(parts_in, parts, sems.at[0]),
        pltpu.make_async_copy(first_all.at[lax.axis_index("col")], first, sems.at[1]),
        pltpu.make_async_copy(cover_in, cover, sems.at[2]),
        pltpu.make_async_copy(second_all.at[lax.axis_index("row")], second, sems.at[3]),
    ]
    for copy in fetch:
        copy.start()
    count_rows = parts.shape[2]
    image_len = second.shape[1]
    edge = jnp.zeros((TILE, image_len), jnp.float32)
    padded[:TILE] = edge
    padded[TILE + image_len :] = edge
    fetch[0].wait()
    fetch[2].wait()
    halves = []
    for component in range(2):
        strips = []
        for i in range(cover.shape[1]):
            cells = []
            for j in range(cover.shape[2]):
                block = parts[0, component, i * BLK : (i + 1) * BLK, j * BLK : (j + 1) * BLK]
                cells.append(block.astype(jnp.float32) * cover[0, i, j].astype(jnp.float32))
            strips.append(jnp.concatenate(cells, axis=1))
        halves.append(jnp.concatenate(strips, axis=0))
    grid = jnp.concatenate(halves, axis=0).astype(jnp.bfloat16)
    fetch[1].wait()
    turned = lax.dot_general(first[...], grid, (((1,), (1,)), ((), ())), preferred_element_type=jnp.float32)
    mid_re = turned[:image_len, :count_rows] - turned[image_len:, count_rows:]
    mid_im = turned[image_len:, :count_rows] + turned[:image_len, count_rows:]
    mid = jnp.concatenate([mid_re, mid_im], axis=1).astype(jnp.bfloat16)
    fetch[3].wait()
    padded[TILE : TILE + image_len] = jnp.dot(mid, second[...], preferred_element_type=jnp.float32)
    upper = lax.broadcasted_iota(jnp.int32, (TILE, LANES), 0) < TILE // 2
    left, right = slice(0, LANES), slice(LANES, 2 * LANES)
    for slot, device in enumerate(send_order()):
        top = TILE * (device + 1) - HALO
        middle = jnp.where(
            upper, padded[top + TILE : top + 2 * TILE, left], padded[top + TILE // 2 : top + 3 * TILE // 2, right]
        )
        window = [padded[top : top + TILE, left], middle, padded[top : top + TILE, right]]
        out[slot] = jnp.concatenate(window, axis=0).astype(out.dtype)


def four_times(values):
    return jnp.concatenate([values] * 4, axis=1)


def weights_kernel(one_in, bias_in, two_in, bias_two_in, weights_one, weights_two, bias_rows, one, bias, two, bias_two, sems):
    fetch = [
        pltpu.make_async_copy(one_in, one, sems.at[0]),
        pltpu.make_async_copy(bias_in, bias, sems.at[1]),
        pltpu.make_async_copy(two_in, two, sems.at[2]),
        pltpu.make_async_copy(bias_two_in, bias_two, sems.at[3]),
    ]
    for copy in fetch:
        copy.start()
    for copy in fetch:
        copy.wait()
    channels = one.shape[2]
    rows = TILE + 2
    per_tile = LANES // channels
    lanes = -(-rows * channels // LANES) * LANES
    image_row = lax.broadcasted_iota(jnp.int32, (16, lanes), 0)
    hidden_row = lax.broadcasted_iota(jnp.int32, (16, lanes), 1) // channels
    held = hidden_row < rows
    high, low = [], []
    for tap in range(3):
        band = jnp.zeros((16, lanes), jnp.float32)
        for shift in range(3):
            line = jnp.concatenate([four_times(one[shift, tap : tap + 1])] * (lanes // LANES), axis=1)
            band = jnp.where(held & (image_row - hidden_row == shift), line, band)
        high.append(band.astype(jnp.bfloat16).astype(jnp.float32))
        low.append(band - high[-1])
    line = jnp.concatenate([four_times(bias[...])] * (lanes // LANES), axis=1)
    with_bias = high[0]
    for piece in range(3):
        rounded = line.astype(jnp.bfloat16).astype(jnp.float32)
        with_bias = jnp.where(held & (image_row == 12 + piece), rounded, with_bias)
        line = line - rounded
    stacked = jnp.concatenate([with_bias, *high[1:], *high, *low], axis=0)
    weights_one[...] = stacked.T[: weights_one.shape[0]].astype(jnp.bfloat16)
    row = lax.broadcasted_iota(jnp.int32, bias_rows.shape, 0) // TILE
    lane = lax.broadcasted_iota(jnp.int32, bias_rows.shape, 1)
    line = jnp.where(row == lane, four_times(bias_two[...]), 0.0)
    bias_rows[...] = jnp.broadcast_to(jnp.sum(line, axis=1, keepdims=True), bias_rows.shape)
    lines = [[four_times(two[shift, tap].astype(jnp.float32)) for shift in range(3)] for tap in range(3)]
    row = lax.broadcasted_iota(jnp.int32, (TILE, LANES), 0)
    lane = lax.broadcasted_iota(jnp.int32, (TILE, LANES), 1) // channels
    zero = jnp.zeros((TILE, LANES), jnp.float32)
    for tile in range(-(-3 * rows // per_tile)):
        taps = sorted({(tile * per_tile + g) // rows for g in range(per_tile)} & {0, 1, 2})
        masks = []
        for tap in taps:
            hidden_row = tile * per_tile + lane - tap * rows
            inside = (hidden_row >= 0) & (hidden_row < rows)
            masks += [(tap, shift, inside & (hidden_row - row == shift)) for shift in range(3)]
        width = min(LANES, weights_two.shape[1] - tile * LANES)
        for channel in range(0, channels, 2):
            pair = []
            for k in (channel, channel + 1):
                values = zero
                for tap, shift, mask in masks:
                    values = jnp.where(mask, lines[tap][shift][k : k + 1], values)
                pair.append(values)
            block = jnp.concatenate(pair, axis=0).astype(jnp.bfloat16)
            weights_two[TILE * channel : TILE * (channel + 2), tile * LANES : tile * LANES + width] = block[:, :width]


def shifted(values, width):
    lane = lax.broadcasted_iota(jnp.int32, values.shape, 1)
    before = jnp.where(lane == 0, 0.0, pltpu.roll(values, 1, 1))
    after = jnp.where(lane == width - 1, 0.0, pltpu.roll(values, width - 1, 1))
    return before, values, after


def layers_kernel(shares, weights_one, weights_two, bias_rows, out, staged, sems):
    place = (lax.axis_index("vis") * lax.axis_size("row") + lax.axis_index("row")) * lax.axis_size(
        "col"
    ) + lax.axis_index("col")
    last = shares.shape[0] - 1
    total = shares[0].astype(jnp.float32)
    for device in range(1, shares.shape[0]):
        total = total + shares[device].astype(jnp.float32)
    width = out.shape[2]
    middle = total[TILE : 2 * TILE]
    upper = lax.broadcasted_iota(jnp.int32, (TILE, width), 0) < TILE // 2
    lower_rows = jnp.concatenate([middle, pltpu.roll(middle, TILE // 2, 0)], axis=1)
    image = jnp.concatenate(
        [jnp.concatenate([total[:TILE], total[2 * TILE :]], axis=1), jnp.where(upper, lower_rows, 0.0)], axis=0
    )
    columns = jnp.concatenate(shifted(image, width), axis=0)
    high = columns.astype(jnp.bfloat16).astype(jnp.float32)
    low = columns - high
    row = lax.broadcasted_iota(jnp.int32, (48, width), 0)
    with_ones = jnp.where((row >= 12) & (row < 15), 1.0, high)
    stacked = jnp.concatenate([with_ones, low, high], axis=0).astype(jnp.bfloat16)
    hidden = jnp.dot(weights_one[...], stacked, preferred_element_type=jnp.float32)
    hidden = jnp.maximum(hidden, 0.0)
    channels = hidden.shape[0] // (TILE + 2)
    row = lax.broadcasted_iota(jnp.int32, hidden.shape, 0)
    outside = ((row < channels) & (place == 0)) | ((row >= channels * (TILE + 1)) & (place == last))
    hidden = jnp.where(outside, 0.0, hidden)
    stacked = jnp.concatenate(shifted(hidden, width), axis=0).astype(jnp.bfloat16)
    half = out.shape[0] // 2
    copies = []
    for part in range(2):
        rows = pl.ds(part * half * TILE, half * TILE)
        features = jnp.dot(weights_two[rows], stacked, preferred_element_type=jnp.float32)
        features = features + jnp.concatenate([bias_rows[rows]] * (width // LANES), axis=1)
        channels_of = pl.ds(part * half, half)
        staged[channels_of] = features.reshape(half, TILE, width).astype(out.dtype)
        copies.append(pltpu.make_async_copy(staged.at[channels_of], out.at[channels_of], sems.at[part]))
        copies[-1].start()
    for copy in copies:
        copy.wait()


def in_hbm(*arrays):
    return [pltpu.with_memory_space_constraint(array, pltpu.HBM) for array in arrays]


def direct(partials, coverage, conv_one, bias_one, conv_two, bias_two):
    count_row, count_col = lax.axis_size("row"), lax.axis_size("col")
    devices = lax.axis_size("vis") * count_row * count_col
    length = partials.shape[3] * count_col
    image_len = length // 2
    channels = conv_two.shape[2]
    first, second = grid_tables(length, count_row, count_col)
    vmem, hbm = pl.BlockSpec(memory_space=pltpu.VMEM), pl.BlockSpec(memory_space=pltpu.HBM)
    limit = pltpu.CompilerParams(vmem_limit_bytes=16 * 2**20)
    share = (devices, 2 * (TILE + 2 * HALO), LANES)
    shares = pl.pallas_call(
        share_kernel,
        out_shape=pltpu.VMEM(share, jnp.bfloat16),
        in_specs=[hbm] * 4,
        out_specs=vmem,
        scratch_shapes=[
            pltpu.SMEM(coverage.shape, jnp.int32),
            pltpu.VMEM(partials.shape, jnp.bfloat16),
            pltpu.VMEM(first.shape[1:], jnp.bfloat16),
            pltpu.VMEM(second.shape[1:], jnp.bfloat16),
            pltpu.VMEM((image_len + 2 * TILE, image_len), jnp.float32),
            pltpu.SemaphoreType.DMA((4,)),
        ],
        compiler_params=limit,
        name="shares",
    )(*in_hbm(coverage, partials, jnp.asarray(first), jnp.asarray(second)))
    arrived = lax.all_to_all(shares, SENT, split_axis=0, concat_axis=0, tiled=True)
    rows = TILE + 2
    weights = pl.pallas_call(
        weights_kernel,
        out_shape=[
            jax.ShapeDtypeStruct((rows * channels, 3 * 48), jnp.bfloat16),
            jax.ShapeDtypeStruct((TILE * channels, 3 * rows * channels), jnp.bfloat16),
            jax.ShapeDtypeStruct((TILE * channels, LANES), jnp.float32),
        ],
        in_specs=[hbm] * 4,
        out_specs=[vmem] * 3,
        scratch_shapes=[
            pltpu.VMEM((3, 3, channels), jnp.float32),
            pltpu.VMEM((1, channels), jnp.float32),
            pltpu.VMEM(conv_two.shape, jnp.bfloat16),
            pltpu.VMEM((1, channels), jnp.float32),
            pltpu.SemaphoreType.DMA((4,)),
        ],
        compiler_params=limit,
        name="weights",
    )(*in_hbm(conv_one.transpose(1, 2, 0), bias_one[None], conv_two, bias_two[None]))
    return pl.pallas_call(
        layers_kernel,
        out_shape=jax.ShapeDtypeStruct((channels, TILE, image_len), jnp.bfloat16),
        in_specs=[vmem] * 4,
        out_specs=hbm,
        scratch_shapes=[
            pltpu.VMEM((channels, TILE, image_len), jnp.bfloat16),
            pltpu.SemaphoreType.DMA((2,)),
        ],
        compiler_params=limit,
        name="layers",
    )(arrived, *weights)


def local(partials, coverage, conv_one, bias_one, conv_two, bias_two):
    count_col = lax.axis_size("col")
    devices = lax.axis_size("vis") * lax.axis_size("row") * count_col
    image_len = partials.shape[3] * count_col // 2
    sent = devices * (TILE + 2 * HALO) * image_len * 2
    fits = image_len == devices * TILE and conv_two.shape[2] * 4 == LANES and image_len == 2 * LANES and sent <= DIRECT_BYTES
    plan = direct if fits else staged
    return plan(partials, coverage, conv_one, bias_one, conv_two, bias_two)


def solution(mesh):
    placed = (P("vis", None, "row", "col"), P("vis", "row", "col"), P(), P(), P(), P())
    return jax.shard_map(
        local,
        mesh=mesh,
        in_specs=placed,
        out_specs=P(None, ALL, None),
        check_vma=False,
    )
```

```python
import functools
import math

import jax
import jax.numpy as jnp
import numpy as np
from jax import lax
from jax.experimental import pallas as pl
from jax.experimental.pallas import tpu as pltpu
from jax.sharding import PartitionSpec as P

BLK = 128
ALL = ("vis", "row", "col")
SENT = ("row", "vis", "col")
DIRECT_BYTES = 4 * 2**20
HALO = 2
TILE = 8
LANES = 128


def with_halo(cells, sides, width):
    for axis, dim in sides:
        count = lax.axis_size(axis)
        ends = count - 1
        head = lax.slice_in_dim(cells, 0, width, axis=dim)
        tail = lax.slice_in_dim(cells, cells.shape[dim] - width, cells.shape[dim], axis=dim)
        cells = jnp.concatenate(
            [
                lax.ppermute(tail, axis, [(i, (i + 1) % count) for i in range(ends)]),
                cells,
                lax.ppermute(head, axis, [((i + 1) % count, i) for i in range(ends)]),
            ],
            axis=dim,
        )
    return cells


def phase_table(numer, denom):
    angle = numer.astype(jnp.float32) * (2.0 * math.pi / denom)
    return (jnp.cos(angle), jnp.sin(angle))


def partial_transform(real_part, imag_part, block_of, keep_imag):
    batch = real_part.shape[0]
    count_blocks = real_part.shape[1]
    block_len = real_part.shape[2]
    length = count_blocks * block_len
    highest = lax.Precision.HIGHEST
    outer = jnp.arange(count_blocks, dtype=jnp.int32)
    inner = jnp.arange(block_len, dtype=jnp.int32)
    cos_one, sin_one = phase_table(block_of[:, None] * outer[None, :] % count_blocks, count_blocks)
    mid_re = jnp.einsum("lpt,px->lxt", real_part, cos_one, precision=highest) - jnp.einsum(
        "lpt,px->lxt", imag_part, sin_one, precision=highest
    )
    mid_im = jnp.einsum("lpt,px->lxt", real_part, sin_one, precision=highest) + jnp.einsum(
        "lpt,px->lxt", imag_part, cos_one, precision=highest
    )
    cos_two, sin_two = phase_table(outer[:, None] * inner[None, :] % length, length)
    parity = (1 - 2 * (outer % 2)).astype(jnp.float32)[:, None]
    cos_two = cos_two * parity
    sin_two = sin_two * parity
    turn_re = mid_re * cos_two - mid_im * sin_two
    turn_im = mid_re * sin_two + mid_im * cos_two
    kept = jnp.arange(block_len // 2, dtype=jnp.int32)
    picked = (kept + 3 * block_len // 4) % block_len
    cos_three, sin_three = phase_table(inner[:, None] * picked[None, :] % block_len, block_len)
    out_re = jnp.einsum("lxt,tj->ljx", turn_re, cos_three, precision=highest) - jnp.einsum(
        "lxt,tj->ljx", turn_im, sin_three, precision=highest
    )
    out_re = out_re.reshape(batch, length // 2)
    if keep_imag:
        out_im = jnp.einsum("lxt,tj->ljx", turn_re, sin_three, precision=highest) + jnp.einsum(
            "lxt,tj->ljx", turn_im, cos_three, precision=highest
        )
        return (out_re, out_im.reshape(batch, length // 2))
    return (out_re, out_re)


def first_layer(extended, conv_one, bias_one, count_rows):
    width = extended.shape[1]
    padded = jnp.pad(extended, ((0, 0), (1, 1)))
    summed = (
        jnp.zeros((conv_one.shape[0], count_rows, width), jnp.float32) + bias_one[:, None, None]
    )
    for shift_b in range(3):
        for shift_a in range(3):
            summed = (
                summed
                + conv_one[:, shift_b, shift_a][:, None, None]
                * padded[None, shift_b : shift_b + count_rows, shift_a : shift_a + width]
            )
    return jnp.maximum(summed, 0.0)


def second_layer(hidden_ext, conv_two, bias_two, count_rows):
    width = hidden_ext.shape[2]
    padded = jnp.pad(hidden_ext, ((0, 0), (0, 0), (1, 1)))
    summed = jnp.zeros((conv_two.shape[2], count_rows, width), jnp.float32)
    for shift_b in range(3):
        for shift_a in range(3):
            summed = summed + jnp.einsum(
                "kj,jba->kba",
                conv_two[shift_b, shift_a],
                padded[:, shift_b : shift_b + count_rows, shift_a : shift_a + width],
                preferred_element_type=jnp.float32,
            )
    return (summed + bias_two[:, None, None]).astype(jnp.bfloat16)


def staged(partials, coverage, conv_one, bias_one, conv_two, bias_two):
    count_vis = lax.axis_size("vis")
    count_row = lax.axis_size("row")
    count_col = lax.axis_size("col")
    grid_len = partials.shape[3] * count_col
    cover = coverage[0]
    block_rows = cover.shape[0]
    block_cols = cover.shape[1]
    spread = jnp.broadcast_to(cover[:, None, :, None], (block_rows, BLK, block_cols, BLK))
    spread = spread.reshape(block_rows * BLK, block_cols * BLK)
    count_blocks = count_vis * count_row
    row_block = grid_len // count_blocks
    row_share = row_block // count_col
    masked = partials[0] * spread.astype(jnp.bfloat16)[None]
    reduced = lax.psum_scatter(
        masked.astype(jnp.float32).astype(jnp.bfloat16), "vis", scatter_dimension=1, tiled=True
    ).astype(jnp.float32)
    grid_rows = lax.all_to_all(
        reduced.astype(jnp.bfloat16), "col", split_axis=1, concat_axis=2, tiled=True
    ).astype(reduced.dtype)
    natural = jnp.arange(count_blocks, dtype=jnp.int32)
    shaped = grid_rows.reshape(2, row_share, count_blocks, row_block)
    first_re, first_im = partial_transform(shaped[0], shaped[1], natural, True)
    stacked = jnp.stack([first_re, first_im])
    moved = lax.all_to_all(
        lax.all_to_all(
            stacked.astype(jnp.bfloat16), ("vis", "row"), split_axis=2, concat_axis=1, tiled=True
        ),
        "col",
        split_axis=2,
        concat_axis=1,
        tiled=True,
    ).astype(stacked.dtype)
    img_rows = moved.shape[2]
    arranged = moved.reshape(2, count_col, count_blocks, row_share, img_rows)
    arranged = arranged.transpose(0, 4, 2, 1, 3).reshape(2, img_rows, count_blocks, row_block)
    owners = natural % count_row * count_vis + natural // count_row
    image, unused = partial_transform(arranged[0], arranged[1], owners, False)
    image = image * (1.0 / grid_len)
    extended = with_halo(image.astype(jnp.bfloat16), ((("vis", "row", "col"), 0),), 1).astype(
        image.dtype
    )
    hidden = first_layer(extended, conv_one, bias_one, img_rows).astype(jnp.bfloat16)
    hidden_ext = with_halo(hidden, ((("vis", "row", "col"), 1),), 1)
    return second_layer(hidden_ext, conv_two, bias_two, img_rows)


def grid_tables(length, count_row, count_col):
    image_len = length // 2
    place = np.arange(length)[:, None] - length // 2
    pixel = np.arange(image_len)[None, :] - image_len // 2
    angle = (place * pixel % length) * (2.0 * math.pi / length)
    cos, sin = np.cos(angle), np.sin(angle)
    cols = length // count_col
    first = np.concatenate([cos.T, sin.T], axis=0)
    first = first.reshape(2 * image_len, count_col, cols).transpose(1, 0, 2)
    rows = length // count_row
    second = np.stack([cos.reshape(count_row, rows, image_len), -sin.reshape(count_row, rows, image_len)], axis=1)
    second = second.reshape(count_row, 2 * rows, image_len) / length
    return first.astype(jnp.bfloat16), second.astype(jnp.bfloat16)


def send_order():
    sizes = [lax.axis_size(axis) for axis in ALL]
    places = np.arange(math.prod(sizes)).reshape(sizes)
    return places.transpose([ALL.index(axis) for axis in SENT]).reshape(-1).tolist()


def share_kernel(cover_in, parts_in, first_all, second_all, out, cover, parts, first, second, padded, sems):
    fetch = [
        pltpu.make_async_copy(parts_in, parts, sems.at[0]),
        pltpu.make_async_copy(first_all.at[lax.axis_index("col")], first, sems.at[1]),
        pltpu.make_async_copy(cover_in, cover, sems.at[2]),
        pltpu.make_async_copy(second_all.at[lax.axis_index("row")], second, sems.at[3]),
    ]
    for copy in fetch:
        copy.start()
    count_rows = parts.shape[2]
    image_len = second.shape[1]
    edge = jnp.zeros((TILE, image_len), jnp.float32)
    padded[:TILE] = edge
    padded[TILE + image_len :] = edge
    fetch[0].wait()
    fetch[2].wait()
    halves = []
    for component in range(2):
        strips = []
        for i in range(cover.shape[1]):
            cells = []
            for j in range(cover.shape[2]):
                block = parts[0, component, i * BLK : (i + 1) * BLK, j * BLK : (j + 1) * BLK]
                cells.append(block.astype(jnp.float32) * cover[0, i, j].astype(jnp.float32))
            strips.append(jnp.concatenate(cells, axis=1))
        halves.append(jnp.concatenate(strips, axis=0))
    grid = jnp.concatenate(halves, axis=0).astype(jnp.bfloat16)
    fetch[1].wait()
    turned = lax.dot_general(first[...], grid, (((1,), (1,)), ((), ())), preferred_element_type=jnp.float32)
    mid_re = turned[:image_len, :count_rows] - turned[image_len:, count_rows:]
    mid_im = turned[image_len:, :count_rows] + turned[:image_len, count_rows:]
    mid = jnp.concatenate([mid_re, mid_im], axis=1).astype(jnp.bfloat16)
    fetch[3].wait()
    padded[TILE : TILE + image_len] = jnp.dot(mid, second[...], preferred_element_type=jnp.float32)
    upper = lax.broadcasted_iota(jnp.int32, (TILE, LANES), 0) < TILE // 2
    left, right = slice(0, LANES), slice(LANES, 2 * LANES)
    for slot, device in enumerate(send_order()):
        top = TILE * (device + 1) - HALO
        middle = jnp.where(
            upper, padded[top + TILE : top + 2 * TILE, left], padded[top + TILE // 2 : top + 3 * TILE // 2, right]
        )
        window = [padded[top : top + TILE, left], middle, padded[top : top + TILE, right]]
        out[slot] = jnp.concatenate(window, axis=0).astype(out.dtype)


def four_times(values):
    return jnp.concatenate([values] * 4, axis=1)


def weights_kernel(one_in, bias_in, two_in, bias_two_in, weights_one, weights_two, bias_rows, one, bias, two, bias_two, sems):
    fetch = [
        pltpu.make_async_copy(one_in, one, sems.at[0]),
        pltpu.make_async_copy(bias_in, bias, sems.at[1]),
        pltpu.make_async_copy(two_in, two, sems.at[2]),
        pltpu.make_async_copy(bias_two_in, bias_two, sems.at[3]),
    ]
    for copy in fetch:
        copy.start()
    for copy in fetch:
        copy.wait()
    channels = one.shape[2]
    rows = TILE + 2
    per_tile = LANES // channels
    lanes = -(-rows * channels // LANES) * LANES
    image_row = lax.broadcasted_iota(jnp.int32, (16, lanes), 0)
    hidden_row = lax.broadcasted_iota(jnp.int32, (16, lanes), 1) // channels
    held = hidden_row < rows
    high, low = [], []
    for tap in range(3):
        band = jnp.zeros((16, lanes), jnp.float32)
        for shift in range(3):
            line = jnp.concatenate([four_times(one[shift, tap : tap + 1])] * (lanes // LANES), axis=1)
            band = jnp.where(held & (image_row - hidden_row == shift), line, band)
        high.append(band.astype(jnp.bfloat16).astype(jnp.float32))
        low.append(band - high[-1])
    line = jnp.concatenate([four_times(bias[...])] * (lanes // LANES), axis=1)
    with_bias = high[0]
    for piece in range(3):
        rounded = line.astype(jnp.bfloat16).astype(jnp.float32)
        with_bias = jnp.where(held & (image_row == 12 + piece), rounded, with_bias)
        line = line - rounded
    stacked = jnp.concatenate([with_bias, *high[1:], *high, *low], axis=0)
    weights_one[...] = stacked.T[: weights_one.shape[0]].astype(jnp.bfloat16)
    row = lax.broadcasted_iota(jnp.int32, bias_rows.shape, 0) // TILE
    lane = lax.broadcasted_iota(jnp.int32, bias_rows.shape, 1)
    line = jnp.where(row == lane, four_times(bias_two[...]), 0.0)
    bias_rows[...] = jnp.broadcast_to(jnp.sum(line, axis=1, keepdims=True), bias_rows.shape)
    lines = [[four_times(two[shift, tap].astype(jnp.float32)) for shift in range(3)] for tap in range(3)]
    row = lax.broadcasted_iota(jnp.int32, (TILE, LANES), 0)
    lane = lax.broadcasted_iota(jnp.int32, (TILE, LANES), 1) // channels
    zero = jnp.zeros((TILE, LANES), jnp.float32)
    for tile in range(-(-3 * rows // per_tile)):
        taps = sorted({(tile * per_tile + g) // rows for g in range(per_tile)} & {0, 1, 2})
        masks = []
        for tap in taps:
            hidden_row = tile * per_tile + lane - tap * rows
            inside = (hidden_row >= 0) & (hidden_row < rows)
            masks += [(tap, shift, inside & (hidden_row - row == shift)) for shift in range(3)]
        width = min(LANES, weights_two.shape[1] - tile * LANES)
        for channel in range(0, channels, 2):
            pair = []
            for k in (channel, channel + 1):
                values = zero
                for tap, shift, mask in masks:
                    values = jnp.where(mask, lines[tap][shift][k : k + 1], values)
                pair.append(values)
            block = jnp.concatenate(pair, axis=0).astype(jnp.bfloat16)
            weights_two[TILE * channel : TILE * (channel + 2), tile * LANES : tile * LANES + width] = block[:, :width]


def shifted(values, width):
    lane = lax.broadcasted_iota(jnp.int32, values.shape, 1)
    before = jnp.where(lane == 0, 0.0, pltpu.roll(values, 1, 1))
    after = jnp.where(lane == width - 1, 0.0, pltpu.roll(values, width - 1, 1))
    return before, values, after


def layers_kernel(shares, weights_one, weights_two, bias_rows, out, staged, sems):
    place = (lax.axis_index("vis") * lax.axis_size("row") + lax.axis_index("row")) * lax.axis_size(
        "col"
    ) + lax.axis_index("col")
    last = shares.shape[0] - 1
    total = shares[0].astype(jnp.float32)
    for device in range(1, shares.shape[0]):
        total = total + shares[device].astype(jnp.float32)
    width = out.shape[2]
    middle = total[TILE : 2 * TILE]
    upper = lax.broadcasted_iota(jnp.int32, (TILE, width), 0) < TILE // 2
    lower_rows = jnp.concatenate([middle, pltpu.roll(middle, TILE // 2, 0)], axis=1)
    image = jnp.concatenate(
        [jnp.concatenate([total[:TILE], total[2 * TILE :]], axis=1), jnp.where(upper, lower_rows, 0.0)], axis=0
    )
    columns = jnp.concatenate(shifted(image, width), axis=0)
    high = columns.astype(jnp.bfloat16).astype(jnp.float32)
    low = columns - high
    row = lax.broadcasted_iota(jnp.int32, (48, width), 0)
    with_ones = jnp.where((row >= 12) & (row < 15), 1.0, high)
    stacked = jnp.concatenate([with_ones, low, high], axis=0).astype(jnp.bfloat16)
    hidden = jnp.dot(weights_one[...], stacked, preferred_element_type=jnp.float32)
    hidden = jnp.maximum(hidden, 0.0)
    channels = hidden.shape[0] // (TILE + 2)
    row = lax.broadcasted_iota(jnp.int32, hidden.shape, 0)
    outside = ((row < channels) & (place == 0)) | ((row >= channels * (TILE + 1)) & (place == last))
    hidden = jnp.where(outside, 0.0, hidden)
    stacked = jnp.concatenate(shifted(hidden, width), axis=0).astype(jnp.bfloat16)
    half = out.shape[0] // 2
    copies = []
    for part in range(2):
        rows = pl.ds(part * half * TILE, half * TILE)
        features = jnp.dot(weights_two[rows], stacked, preferred_element_type=jnp.float32)
        features = features + jnp.concatenate([bias_rows[rows]] * (width // LANES), axis=1)
        channels_of = pl.ds(part * half, half)
        staged[channels_of] = features.reshape(half, TILE, width).astype(out.dtype)
        copies.append(pltpu.make_async_copy(staged.at[channels_of], out.at[channels_of], sems.at[part]))
        copies[-1].start()
    for copy in copies:
        copy.wait()


def in_hbm(*arrays):
    return [pltpu.with_memory_space_constraint(array, pltpu.HBM) for array in arrays]


def direct(partials, coverage, conv_one, bias_one, conv_two, bias_two):
    count_row, count_col = lax.axis_size("row"), lax.axis_size("col")
    devices = lax.axis_size("vis") * count_row * count_col
    length = partials.shape[3] * count_col
    image_len = length // 2
    channels = conv_two.shape[2]
    first, second = grid_tables(length, count_row, count_col)
    vmem, hbm = pl.BlockSpec(memory_space=pltpu.VMEM), pl.BlockSpec(memory_space=pltpu.HBM)
    limit = pltpu.CompilerParams(vmem_limit_bytes=16 * 2**20)
    share = (devices, 2 * (TILE + 2 * HALO), LANES)
    shares = pl.pallas_call(
        share_kernel,
        out_shape=pltpu.VMEM(share, jnp.bfloat16),
        in_specs=[hbm] * 4,
        out_specs=vmem,
        scratch_shapes=[
            pltpu.SMEM(coverage.shape, jnp.int32),
            pltpu.VMEM(partials.shape, jnp.bfloat16),
            pltpu.VMEM(first.shape[1:], jnp.bfloat16),
            pltpu.VMEM(second.shape[1:], jnp.bfloat16),
            pltpu.VMEM((image_len + 2 * TILE, image_len), jnp.float32),
            pltpu.SemaphoreType.DMA((4,)),
        ],
        compiler_params=limit,
        name="shares",
    )(*in_hbm(coverage, partials, jnp.asarray(first), jnp.asarray(second)))
    arrived = lax.all_to_all(shares, SENT, split_axis=0, concat_axis=0, tiled=True)
    rows = TILE + 2
    weights = pl.pallas_call(
        weights_kernel,
        out_shape=[
            jax.ShapeDtypeStruct((rows * channels, 3 * 48), jnp.bfloat16),
            jax.ShapeDtypeStruct((TILE * channels, 3 * rows * channels), jnp.bfloat16),
            jax.ShapeDtypeStruct((TILE * channels, LANES), jnp.float32),
        ],
        in_specs=[hbm] * 4,
        out_specs=[vmem] * 3,
        scratch_shapes=[
            pltpu.VMEM((3, 3, channels), jnp.float32),
            pltpu.VMEM((1, channels), jnp.float32),
            pltpu.VMEM(conv_two.shape, jnp.bfloat16),
            pltpu.VMEM((1, channels), jnp.float32),
            pltpu.SemaphoreType.DMA((4,)),
        ],
        compiler_params=limit,
        name="weights",
    )(*in_hbm(conv_one.transpose(1, 2, 0), bias_one[None], conv_two, bias_two[None]))
    return pl.pallas_call(
        layers_kernel,
        out_shape=jax.ShapeDtypeStruct((channels, TILE, image_len), jnp.bfloat16),
        in_specs=[vmem] * 4,
        out_specs=hbm,
        scratch_shapes=[
            pltpu.VMEM((channels, TILE, image_len), jnp.bfloat16),
            pltpu.SemaphoreType.DMA((2,)),
        ],
        compiler_params=limit,
        name="layers",
    )(arrived, *weights)


def local(partials, coverage, conv_one, bias_one, conv_two, bias_two):
    count_col = lax.axis_size("col")
    devices = lax.axis_size("vis") * lax.axis_size("row") * count_col
    image_len = partials.shape[3] * count_col // 2
    sent = devices * (TILE + 2 * HALO) * image_len * 2
    fits = image_len == devices * TILE and conv_two.shape[2] * 4 == LANES and image_len == 2 * LANES and sent <= DIRECT_BYTES
    plan = direct if fits else staged
    return plan(partials, coverage, conv_one, bias_one, conv_two, bias_two)


def solution(mesh):
    placed = (P("vis", None, "row", "col"), P("vis", "row", "col"), P(), P(), P(), P())
    return jax.shard_map(
        local,
        mesh=mesh,
        in_specs=placed,
        out_specs=P(None, ALL, None),
        check_vma=False,
    )
```

```python
import functools
import math

import jax
import jax.numpy as jnp
import numpy as np
from jax import lax
from jax.experimental import pallas as pl
from jax.experimental.pallas import tpu as pltpu
from jax.sharding import PartitionSpec as P

BLK = 128
ALL = ("vis", "row", "col")
DIRECT_BYTES = 4 * 2**20
HALO = 2
TILE = 8
LANES = 128


def with_halo(cells, sides, width):
    for axis, dim in sides:
        count = lax.axis_size(axis)
        ends = count - 1
        head = lax.slice_in_dim(cells, 0, width, axis=dim)
        tail = lax.slice_in_dim(cells, cells.shape[dim] - width, cells.shape[dim], axis=dim)
        cells = jnp.concatenate(
            [
                lax.ppermute(tail, axis, [(i, (i + 1) % count) for i in range(ends)]),
                cells,
                lax.ppermute(head, axis, [((i + 1) % count, i) for i in range(ends)]),
            ],
            axis=dim,
        )
    return cells


def phase_table(numer, denom):
    angle = numer.astype(jnp.float32) * (2.0 * math.pi / denom)
    return (jnp.cos(angle), jnp.sin(angle))


def partial_transform(real_part, imag_part, block_of, keep_imag):
    batch = real_part.shape[0]
    count_blocks = real_part.shape[1]
    block_len = real_part.shape[2]
    length = count_blocks * block_len
    highest = lax.Precision.HIGHEST
    outer = jnp.arange(count_blocks, dtype=jnp.int32)
    inner = jnp.arange(block_len, dtype=jnp.int32)
    cos_one, sin_one = phase_table(block_of[:, None] * outer[None, :] % count_blocks, count_blocks)
    mid_re = jnp.einsum("lpt,px->lxt", real_part, cos_one, precision=highest) - jnp.einsum(
        "lpt,px->lxt", imag_part, sin_one, precision=highest
    )
    mid_im = jnp.einsum("lpt,px->lxt", real_part, sin_one, precision=highest) + jnp.einsum(
        "lpt,px->lxt", imag_part, cos_one, precision=highest
    )
    cos_two, sin_two = phase_table(outer[:, None] * inner[None, :] % length, length)
    parity = (1 - 2 * (outer % 2)).astype(jnp.float32)[:, None]
    cos_two = cos_two * parity
    sin_two = sin_two * parity
    turn_re = mid_re * cos_two - mid_im * sin_two
    turn_im = mid_re * sin_two + mid_im * cos_two
    kept = jnp.arange(block_len // 2, dtype=jnp.int32)
    picked = (kept + 3 * block_len // 4) % block_len
    cos_three, sin_three = phase_table(inner[:, None] * picked[None, :] % block_len, block_len)
    out_re = jnp.einsum("lxt,tj->ljx", turn_re, cos_three, precision=highest) - jnp.einsum(
        "lxt,tj->ljx", turn_im, sin_three, precision=highest
    )
    out_re = out_re.reshape(batch, length // 2)
    if keep_imag:
        out_im = jnp.einsum("lxt,tj->ljx", turn_re, sin_three, precision=highest) + jnp.einsum(
            "lxt,tj->ljx", turn_im, cos_three, precision=highest
        )
        return (out_re, out_im.reshape(batch, length // 2))
    return (out_re, out_re)


def first_layer(extended, conv_one, bias_one, count_rows):
    width = extended.shape[1]
    padded = jnp.pad(extended, ((0, 0), (1, 1)))
    summed = (
        jnp.zeros((conv_one.shape[0], count_rows, width), jnp.float32) + bias_one[:, None, None]
    )
    for shift_b in range(3):
        for shift_a in range(3):
            summed = (
                summed
                + conv_one[:, shift_b, shift_a][:, None, None]
                * padded[None, shift_b : shift_b + count_rows, shift_a : shift_a + width]
            )
    return jnp.maximum(summed, 0.0)


def second_layer(hidden_ext, conv_two, bias_two, count_rows):
    width = hidden_ext.shape[2]
    padded = jnp.pad(hidden_ext, ((0, 0), (0, 0), (1, 1)))
    summed = jnp.zeros((conv_two.shape[2], count_rows, width), jnp.float32)
    for shift_b in range(3):
        for shift_a in range(3):
            summed = summed + jnp.einsum(
                "kj,jba->kba",
                conv_two[shift_b, shift_a],
                padded[:, shift_b : shift_b + count_rows, shift_a : shift_a + width],
                preferred_element_type=jnp.float32,
            )
    return (summed + bias_two[:, None, None]).astype(jnp.bfloat16)


def staged(partials, coverage, conv_one, bias_one, conv_two, bias_two):
    count_vis = lax.axis_size("vis")
    count_row = lax.axis_size("row")
    count_col = lax.axis_size("col")
    grid_len = partials.shape[3] * count_col
    cover = coverage[0]
    block_rows = cover.shape[0]
    block_cols = cover.shape[1]
    spread = jnp.broadcast_to(cover[:, None, :, None], (block_rows, BLK, block_cols, BLK))
    spread = spread.reshape(block_rows * BLK, block_cols * BLK)
    count_blocks = count_vis * count_row
    row_block = grid_len // count_blocks
    row_share = row_block // count_col
    masked = partials[0] * spread.astype(jnp.bfloat16)[None]
    reduced = lax.psum_scatter(
        masked.astype(jnp.float32).astype(jnp.bfloat16), "vis", scatter_dimension=1, tiled=True
    ).astype(jnp.float32)
    grid_rows = lax.all_to_all(
        reduced.astype(jnp.bfloat16), "col", split_axis=1, concat_axis=2, tiled=True
    ).astype(reduced.dtype)
    natural = jnp.arange(count_blocks, dtype=jnp.int32)
    shaped = grid_rows.reshape(2, row_share, count_blocks, row_block)
    first_re, first_im = partial_transform(shaped[0], shaped[1], natural, True)
    stacked = jnp.stack([first_re, first_im])
    moved = lax.all_to_all(
        lax.all_to_all(
            stacked.astype(jnp.bfloat16), ("vis", "row"), split_axis=2, concat_axis=1, tiled=True
        ),
        "col",
        split_axis=2,
        concat_axis=1,
        tiled=True,
    ).astype(stacked.dtype)
    img_rows = moved.shape[2]
    arranged = moved.reshape(2, count_col, count_blocks, row_share, img_rows)
    arranged = arranged.transpose(0, 4, 2, 1, 3).reshape(2, img_rows, count_blocks, row_block)
    owners = natural % count_row * count_vis + natural // count_row
    image, unused = partial_transform(arranged[0], arranged[1], owners, False)
    image = image * (1.0 / grid_len)
    extended = with_halo(image.astype(jnp.bfloat16), ((("vis", "row", "col"), 0),), 1).astype(
        image.dtype
    )
    hidden = first_layer(extended, conv_one, bias_one, img_rows).astype(jnp.bfloat16)
    hidden_ext = with_halo(hidden, ((("vis", "row", "col"), 1),), 1)
    return second_layer(hidden_ext, conv_two, bias_two, img_rows)


def grid_tables(length, count_row, count_col):
    image_len = length // 2
    place = np.arange(length)[:, None] - length // 2
    pixel = np.arange(image_len)[None, :] - image_len // 2
    angle = (place * pixel % length) * (2.0 * math.pi / length)
    cos, sin = np.cos(angle), np.sin(angle)
    cols = length // count_col
    first = np.concatenate([cos.T, sin.T], axis=0)
    first = first.reshape(2 * image_len, count_col, cols).transpose(1, 0, 2)
    rows = length // count_row
    second = np.stack([cos.reshape(count_row, rows, image_len), -sin.reshape(count_row, rows, image_len)], axis=1)
    second = second.reshape(count_row, 2 * rows, image_len) / length
    return first.astype(jnp.bfloat16), second.astype(jnp.bfloat16)


def share_kernel(cover_in, parts_in, first_all, second_all, out, cover, parts, first, second, padded, sems):
    fetch = [
        pltpu.make_async_copy(parts_in, parts, sems.at[0]),
        pltpu.make_async_copy(first_all.at[lax.axis_index("col")], first, sems.at[1]),
        pltpu.make_async_copy(cover_in, cover, sems.at[2]),
        pltpu.make_async_copy(second_all.at[lax.axis_index("row")], second, sems.at[3]),
    ]
    for copy in fetch:
        copy.start()
    count_rows = parts.shape[2]
    image_len = second.shape[1]
    edge = jnp.zeros((TILE, image_len), jnp.float32)
    padded[:TILE] = edge
    padded[TILE + image_len :] = edge
    fetch[0].wait()
    fetch[2].wait()
    halves = []
    for component in range(2):
        strips = []
        for i in range(cover.shape[1]):
            cells = []
            for j in range(cover.shape[2]):
                block = parts[0, component, i * BLK : (i + 1) * BLK, j * BLK : (j + 1) * BLK]
                cells.append(block.astype(jnp.float32) * cover[0, i, j].astype(jnp.float32))
            strips.append(jnp.concatenate(cells, axis=1))
        halves.append(jnp.concatenate(strips, axis=0))
    grid = jnp.concatenate(halves, axis=0).astype(jnp.bfloat16)
    fetch[1].wait()
    turned = lax.dot_general(first[...], grid, (((1,), (1,)), ((), ())), preferred_element_type=jnp.float32)
    mid_re = turned[:image_len, :count_rows] - turned[image_len:, count_rows:]
    mid_im = turned[image_len:, :count_rows] + turned[:image_len, count_rows:]
    mid = jnp.concatenate([mid_re, mid_im], axis=1).astype(jnp.bfloat16)
    fetch[3].wait()
    padded[TILE : TILE + image_len] = jnp.dot(mid, second[...], preferred_element_type=jnp.float32)
    upper = lax.broadcasted_iota(jnp.int32, (TILE, LANES), 0) < TILE // 2
    left, right = slice(0, LANES), slice(LANES, 2 * LANES)
    for slot, device in enumerate(reversed(range(out.shape[0]))):
        top = TILE * (device + 1) - HALO
        middle = jnp.where(
            upper, padded[top + TILE : top + 2 * TILE, left], padded[top + TILE // 2 : top + 3 * TILE // 2, right]
        )
        window = [padded[top : top + TILE, left], middle, padded[top : top + TILE, right]]
        out[slot] = jnp.concatenate(window, axis=0).astype(out.dtype)


def four_times(values):
    return jnp.concatenate([values] * 4, axis=1)


def weights_kernel(one_in, bias_in, two_in, bias_two_in, weights_one, weights_two, bias_rows, one, bias, two, bias_two, sems):
    fetch = [
        pltpu.make_async_copy(one_in, one, sems.at[0]),
        pltpu.make_async_copy(bias_in, bias, sems.at[1]),
        pltpu.make_async_copy(two_in, two, sems.at[2]),
        pltpu.make_async_copy(bias_two_in, bias_two, sems.at[3]),
    ]
    for copy in fetch:
        copy.start()
    for copy in fetch:
        copy.wait()
    channels = one.shape[2]
    rows = TILE + 2
    per_tile = LANES // channels
    lanes = -(-rows * channels // LANES) * LANES
    image_row = lax.broadcasted_iota(jnp.int32, (16, lanes), 0)
    hidden_row = lax.broadcasted_iota(jnp.int32, (16, lanes), 1) // channels
    held = hidden_row < rows
    high, low = [], []
    for tap in range(3):
        band = jnp.zeros((16, lanes), jnp.float32)
        for shift in range(3):
            line = jnp.concatenate([four_times(one[shift, tap : tap + 1])] * (lanes // LANES), axis=1)
            band = jnp.where(held & (image_row - hidden_row == shift), line, band)
        high.append(band.astype(jnp.bfloat16).astype(jnp.float32))
        low.append(band - high[-1])
    line = jnp.concatenate([four_times(bias[...])] * (lanes // LANES), axis=1)
    with_bias = high[0]
    for piece in range(3):
        rounded = line.astype(jnp.bfloat16).astype(jnp.float32)
        with_bias = jnp.where(held & (image_row == 12 + piece), rounded, with_bias)
        line = line - rounded
    stacked = jnp.concatenate([with_bias, *high[1:], *high, *low], axis=0)
    weights_one[...] = stacked.T[: weights_one.shape[0]].astype(jnp.bfloat16)
    row = lax.broadcasted_iota(jnp.int32, bias_rows.shape, 0) // TILE
    lane = lax.broadcasted_iota(jnp.int32, bias_rows.shape, 1)
    line = jnp.where(row == lane, four_times(bias_two[...]), 0.0)
    bias_rows[...] = jnp.broadcast_to(jnp.sum(line, axis=1, keepdims=True), bias_rows.shape)
    lines = [[four_times(two[shift, tap].astype(jnp.float32)) for shift in range(3)] for tap in range(3)]
    row = lax.broadcasted_iota(jnp.int32, (TILE, LANES), 0)
    lane = lax.broadcasted_iota(jnp.int32, (TILE, LANES), 1) // channels
    zero = jnp.zeros((TILE, LANES), jnp.float32)
    for tile in range(-(-3 * rows // per_tile)):
        taps = sorted({(tile * per_tile + g) // rows for g in range(per_tile)} & {0, 1, 2})
        masks = []
        for tap in taps:
            hidden_row = tile * per_tile + lane - tap * rows
            inside = (hidden_row >= 0) & (hidden_row < rows)
            masks += [(tap, shift, inside & (hidden_row - row == shift)) for shift in range(3)]
        width = min(LANES, weights_two.shape[1] - tile * LANES)
        for channel in range(0, channels, 2):
            pair = []
            for k in (channel, channel + 1):
                values = zero
                for tap, shift, mask in masks:
                    values = jnp.where(mask, lines[tap][shift][k : k + 1], values)
                pair.append(values)
            block = jnp.concatenate(pair, axis=0).astype(jnp.bfloat16)
            weights_two[TILE * channel : TILE * (channel + 2), tile * LANES : tile * LANES + width] = block[:, :width]


def shifted(values, width):
    lane = lax.broadcasted_iota(jnp.int32, values.shape, 1)
    before = jnp.where(lane == 0, 0.0, pltpu.roll(values, 1, 1))
    after = jnp.where(lane == width - 1, 0.0, pltpu.roll(values, width - 1, 1))
    return before, values, after


def layers_kernel(shares, weights_one, weights_two, bias_rows, out, staged, sems):
    place = (lax.axis_index("vis") * lax.axis_size("row") + lax.axis_index("row")) * lax.axis_size(
        "col"
    ) + lax.axis_index("col")
    last = shares.shape[0] - 1
    total = shares[0].astype(jnp.float32)
    for device in range(1, shares.shape[0]):
        total = total + shares[device].astype(jnp.float32)
    width = out.shape[2]
    middle = total[TILE : 2 * TILE]
    upper = lax.broadcasted_iota(jnp.int32, (TILE, width), 0) < TILE // 2
    lower_rows = jnp.concatenate([middle, pltpu.roll(middle, TILE // 2, 0)], axis=1)
    image = jnp.concatenate(
        [jnp.concatenate([total[:TILE], total[2 * TILE :]], axis=1), jnp.where(upper, lower_rows, 0.0)], axis=0
    )
    columns = jnp.concatenate(shifted(image, width), axis=0)
    high = columns.astype(jnp.bfloat16).astype(jnp.float32)
    low = columns - high
    row = lax.broadcasted_iota(jnp.int32, (48, width), 0)
    with_ones = jnp.where((row >= 12) & (row < 15), 1.0, high)
    stacked = jnp.concatenate([with_ones, low, high], axis=0).astype(jnp.bfloat16)
    hidden = jnp.dot(weights_one[...], stacked, preferred_element_type=jnp.float32)
    hidden = jnp.maximum(hidden, 0.0)
    channels = hidden.shape[0] // (TILE + 2)
    row = lax.broadcasted_iota(jnp.int32, hidden.shape, 0)
    outside = ((row < channels) & (place == 0)) | ((row >= channels * (TILE + 1)) & (place == last))
    hidden = jnp.where(outside, 0.0, hidden)
    stacked = jnp.concatenate(shifted(hidden, width), axis=0).astype(jnp.bfloat16)
    half = out.shape[0] // 2
    copies = []
    for part in range(2):
        rows = pl.ds(part * half * TILE, half * TILE)
        features = jnp.dot(weights_two[rows], stacked, preferred_element_type=jnp.float32)
        features = features + jnp.concatenate([bias_rows[rows]] * (width // LANES), axis=1)
        channels_of = pl.ds(part * half, half)
        staged[channels_of] = features.reshape(half, TILE, width).astype(out.dtype)
        copies.append(pltpu.make_async_copy(staged.at[channels_of], out.at[channels_of], sems.at[part]))
        copies[-1].start()
    for copy in copies:
        copy.wait()


def in_hbm(*arrays):
    return [pltpu.with_memory_space_constraint(array, pltpu.HBM) for array in arrays]


def direct(partials, coverage, conv_one, bias_one, conv_two, bias_two):
    count_row, count_col = lax.axis_size("row"), lax.axis_size("col")
    devices = lax.axis_size("vis") * count_row * count_col
    length = partials.shape[3] * count_col
    image_len = length // 2
    channels = conv_two.shape[2]
    first, second = grid_tables(length, count_row, count_col)
    vmem, hbm = pl.BlockSpec(memory_space=pltpu.VMEM), pl.BlockSpec(memory_space=pltpu.HBM)
    limit = pltpu.CompilerParams(vmem_limit_bytes=16 * 2**20)
    share = (devices, 2 * (TILE + 2 * HALO), LANES)
    shares = pl.pallas_call(
        share_kernel,
        out_shape=pltpu.VMEM(share, jnp.bfloat16),
        in_specs=[hbm] * 4,
        out_specs=vmem,
        scratch_shapes=[
            pltpu.SMEM(coverage.shape, jnp.int32),
            pltpu.VMEM(partials.shape, jnp.bfloat16),
            pltpu.VMEM(first.shape[1:], jnp.bfloat16),
            pltpu.VMEM(second.shape[1:], jnp.bfloat16),
            pltpu.VMEM((image_len + 2 * TILE, image_len), jnp.float32),
            pltpu.SemaphoreType.DMA((4,)),
        ],
        compiler_params=limit,
        name="shares",
    )(*in_hbm(coverage, partials, jnp.asarray(first), jnp.asarray(second)))
    arrived = lax.all_to_all(
        shares, ALL, split_axis=0, concat_axis=0, tiled=True, axis_index_groups=[list(reversed(range(devices)))]
    )
    rows = TILE + 2
    weights = pl.pallas_call(
        weights_kernel,
        out_shape=[
            jax.ShapeDtypeStruct((rows * channels, 3 * 48), jnp.bfloat16),
            jax.ShapeDtypeStruct((TILE * channels, 3 * rows * channels), jnp.bfloat16),
            jax.ShapeDtypeStruct((TILE * channels, LANES), jnp.float32),
        ],
        in_specs=[hbm] * 4,
        out_specs=[vmem] * 3,
        scratch_shapes=[
            pltpu.VMEM((3, 3, channels), jnp.float32),
            pltpu.VMEM((1, channels), jnp.float32),
            pltpu.VMEM(conv_two.shape, jnp.bfloat16),
            pltpu.VMEM((1, channels), jnp.float32),
            pltpu.SemaphoreType.DMA((4,)),
        ],
        compiler_params=limit,
        name="weights",
    )(*in_hbm(conv_one.transpose(1, 2, 0), bias_one[None], conv_two, bias_two[None]))
    return pl.pallas_call(
        layers_kernel,
        out_shape=jax.ShapeDtypeStruct((channels, TILE, image_len), jnp.bfloat16),
        in_specs=[vmem] * 4,
        out_specs=hbm,
        scratch_shapes=[
            pltpu.VMEM((channels, TILE, image_len), jnp.bfloat16),
            pltpu.SemaphoreType.DMA((2,)),
        ],
        compiler_params=limit,
        name="layers",
    )(arrived, *weights)


def local(partials, coverage, conv_one, bias_one, conv_two, bias_two):
    count_col = lax.axis_size("col")
    devices = lax.axis_size("vis") * lax.axis_size("row") * count_col
    image_len = partials.shape[3] * count_col // 2
    sent = devices * (TILE + 2 * HALO) * image_len * 2
    fits = image_len == devices * TILE and conv_two.shape[2] * 4 == LANES and image_len == 2 * LANES and sent <= DIRECT_BYTES
    plan = direct if fits else staged
    return plan(partials, coverage, conv_one, bias_one, conv_two, bias_two)


def solution(mesh):
    placed = (P("vis", None, "row", "col"), P("vis", "row", "col"), P(), P(), P(), P())
    return jax.shard_map(
        local,
        mesh=mesh,
        in_specs=placed,
        out_specs=P(None, ALL, None),
        check_vma=False,
    )
```

```python
import math

import jax
import jax.numpy as jnp
import numpy as np
from jax import lax
from jax.experimental import pallas as pl
from jax.experimental.pallas import tpu as pltpu
from jax.sharding import PartitionSpec as P

BLK = 128
ALL = ("vis", "row", "col")
DIRECT_BYTES = 4 * 2**20
HALO = 2
TILE = 8
LANES = 128
HALVES = 2


def with_halo(cells, sides, width):
    for axis, dim in sides:
        count = lax.axis_size(axis)
        ends = count - 1
        head = lax.slice_in_dim(cells, 0, width, axis=dim)
        tail = lax.slice_in_dim(cells, cells.shape[dim] - width, cells.shape[dim], axis=dim)
        cells = jnp.concatenate(
            [
                lax.ppermute(tail, axis, [(i, (i + 1) % count) for i in range(ends)]),
                cells,
                lax.ppermute(head, axis, [((i + 1) % count, i) for i in range(ends)]),
            ],
            axis=dim,
        )
    return cells


def phase_table(numer, denom):
    angle = numer.astype(jnp.float32) * (2.0 * math.pi / denom)
    return (jnp.cos(angle), jnp.sin(angle))


def partial_transform(real_part, imag_part, block_of, keep_imag):
    batch = real_part.shape[0]
    count_blocks = real_part.shape[1]
    block_len = real_part.shape[2]
    length = count_blocks * block_len
    highest = lax.Precision.HIGHEST
    outer = jnp.arange(count_blocks, dtype=jnp.int32)
    inner = jnp.arange(block_len, dtype=jnp.int32)
    cos_one, sin_one = phase_table(block_of[:, None] * outer[None, :] % count_blocks, count_blocks)
    mid_re = jnp.einsum("lpt,px->lxt", real_part, cos_one, precision=highest) - jnp.einsum(
        "lpt,px->lxt", imag_part, sin_one, precision=highest
    )
    mid_im = jnp.einsum("lpt,px->lxt", real_part, sin_one, precision=highest) + jnp.einsum(
        "lpt,px->lxt", imag_part, cos_one, precision=highest
    )
    cos_two, sin_two = phase_table(outer[:, None] * inner[None, :] % length, length)
    parity = (1 - 2 * (outer % 2)).astype(jnp.float32)[:, None]
    cos_two = cos_two * parity
    sin_two = sin_two * parity
    turn_re = mid_re * cos_two - mid_im * sin_two
    turn_im = mid_re * sin_two + mid_im * cos_two
    kept = jnp.arange(block_len // 2, dtype=jnp.int32)
    picked = (kept + 3 * block_len // 4) % block_len
    cos_three, sin_three = phase_table(inner[:, None] * picked[None, :] % block_len, block_len)
    out_re = jnp.einsum("lxt,tj->ljx", turn_re, cos_three, precision=highest) - jnp.einsum(
        "lxt,tj->ljx", turn_im, sin_three, precision=highest
    )
    out_re = out_re.reshape(batch, length // 2)
    if keep_imag:
        out_im = jnp.einsum("lxt,tj->ljx", turn_re, sin_three, precision=highest) + jnp.einsum(
            "lxt,tj->ljx", turn_im, cos_three, precision=highest
        )
        return (out_re, out_im.reshape(batch, length // 2))
    return (out_re, out_re)


def first_layer(extended, conv_one, bias_one, count_rows):
    width = extended.shape[1]
    padded = jnp.pad(extended, ((0, 0), (1, 1)))
    summed = (
        jnp.zeros((conv_one.shape[0], count_rows, width), jnp.float32) + bias_one[:, None, None]
    )
    for shift_b in range(3):
        for shift_a in range(3):
            summed = (
                summed
                + conv_one[:, shift_b, shift_a][:, None, None]
                * padded[None, shift_b : shift_b + count_rows, shift_a : shift_a + width]
            )
    return jnp.maximum(summed, 0.0)


def second_layer(hidden_ext, conv_two, bias_two, count_rows):
    width = hidden_ext.shape[2]
    padded = jnp.pad(hidden_ext, ((0, 0), (0, 0), (1, 1)))
    summed = jnp.zeros((conv_two.shape[2], count_rows, width), jnp.float32)
    for shift_b in range(3):
        for shift_a in range(3):
            summed = summed + jnp.einsum(
                "kj,jba->kba",
                conv_two[shift_b, shift_a],
                padded[:, shift_b : shift_b + count_rows, shift_a : shift_a + width],
                preferred_element_type=jnp.float32,
            )
    return (summed + bias_two[:, None, None]).astype(jnp.bfloat16)


def staged(partials, coverage, conv_one, bias_one, conv_two, bias_two):
    count_vis = lax.axis_size("vis")
    count_row = lax.axis_size("row")
    count_col = lax.axis_size("col")
    grid_len = partials.shape[3] * count_col
    cover = coverage[0]
    block_rows = cover.shape[0]
    block_cols = cover.shape[1]
    spread = jnp.broadcast_to(cover[:, None, :, None], (block_rows, BLK, block_cols, BLK))
    spread = spread.reshape(block_rows * BLK, block_cols * BLK)
    count_blocks = count_vis * count_row
    row_block = grid_len // count_blocks
    row_share = row_block // count_col
    masked = partials[0] * spread.astype(jnp.bfloat16)[None]
    reduced = lax.psum_scatter(
        masked.astype(jnp.float32).astype(jnp.bfloat16), "vis", scatter_dimension=1, tiled=True
    ).astype(jnp.float32)
    grid_rows = lax.all_to_all(
        reduced.astype(jnp.bfloat16), "col", split_axis=1, concat_axis=2, tiled=True
    ).astype(reduced.dtype)
    natural = jnp.arange(count_blocks, dtype=jnp.int32)
    shaped = grid_rows.reshape(2, row_share, count_blocks, row_block)
    first_re, first_im = partial_transform(shaped[0], shaped[1], natural, True)
    stacked = jnp.stack([first_re, first_im])
    moved = lax.all_to_all(
        lax.all_to_all(
            stacked.astype(jnp.bfloat16), ("vis", "row"), split_axis=2, concat_axis=1, tiled=True
        ),
        "col",
        split_axis=2,
        concat_axis=1,
        tiled=True,
    ).astype(stacked.dtype)
    img_rows = moved.shape[2]
    arranged = moved.reshape(2, count_col, count_blocks, row_share, img_rows)
    arranged = arranged.transpose(0, 4, 2, 1, 3).reshape(2, img_rows, count_blocks, row_block)
    owners = natural % count_row * count_vis + natural // count_row
    image, unused = partial_transform(arranged[0], arranged[1], owners, False)
    image = image * (1.0 / grid_len)
    extended = with_halo(image.astype(jnp.bfloat16), ((("vis", "row", "col"), 0),), 1).astype(
        image.dtype
    )
    hidden = first_layer(extended, conv_one, bias_one, img_rows).astype(jnp.bfloat16)
    hidden_ext = with_halo(hidden, ((("vis", "row", "col"), 1),), 1)
    return second_layer(hidden_ext, conv_two, bias_two, img_rows)


def grid_tables(length, count_row, count_col):
    image_len = length // 2
    place = np.arange(length)[:, None] - length // 2
    pixel = np.arange(image_len)[None, :] - image_len // 2
    angle = (place * pixel % length) * (2.0 * math.pi / length)
    cos, sin = np.cos(angle), np.sin(angle)
    half = image_len // HALVES
    padded = np.pad(np.stack([cos.T, sin.T]), ((0, 0), (HALO, TILE - HALO), (0, 0)))
    halves = np.stack([padded[:, i * half : (i + 1) * half + TILE] for i in range(HALVES)])
    first = halves.reshape(HALVES, 2 * (half + TILE), count_col, length // count_col).transpose(2, 0, 1, 3)
    rows = length // count_row
    second = np.stack([cos.reshape(count_row, rows, image_len), -sin.reshape(count_row, rows, image_len)], axis=1)
    second = second.reshape(count_row, 2 * rows, image_len) / length
    return first.astype(jnp.bfloat16), second.astype(jnp.bfloat16)


def share_kernel(cover_in, parts_in, first_all, second_all, out, cover, parts, first, second, cut, sems, sent):
    col, row = lax.axis_index("col"), lax.axis_index("row")
    get_cover = pltpu.make_async_copy(cover_in, cover, sems.at[0])
    get_parts = pltpu.make_async_copy(parts_in, parts, sems.at[1])
    get_second = pltpu.make_async_copy(second_all.at[row], second, sems.at[2])
    get_first = [
        pltpu.make_async_copy(first_all.at[col, i], first.at[i], sems.at[3 + i]) for i in range(HALVES)
    ]
    for copy in (get_cover, get_parts, get_first[0], get_second, *get_first[1:]):
        copy.start()
    count_rows = parts.shape[2]
    get_cover.wait()
    get_parts.wait()
    components = []
    for component in range(2):
        strips = []
        for i in range(cover.shape[1]):
            cells = []
            for j in range(cover.shape[2]):
                block = parts[0, component, i * BLK : (i + 1) * BLK, j * BLK : (j + 1) * BLK]
                level = jnp.full(block.shape, cover[0, i, j].astype(jnp.float32)).astype(jnp.bfloat16)
                cells.append(block * level)
            strips.append(jnp.concatenate(cells, axis=1))
        components.append(jnp.concatenate(strips, axis=0))
    grid = jnp.concatenate(components, axis=0)
    upper = lax.broadcasted_iota(jnp.int32, (TILE, LANES), 0) < TILE // 2
    group = cut.shape[0] // HALVES
    tall = first.shape[1] // 2
    copies = []
    for i in range(HALVES):
        get_first[i].wait()
        turned = lax.dot_general(first[i], grid, (((1,), (1,)), ((), ())), preferred_element_type=jnp.float32)
        mid_re = turned[:tall, :count_rows] - turned[tall:, count_rows:]
        mid_im = turned[tall:, :count_rows] + turned[:tall, count_rows:]
        mid = jnp.concatenate([mid_re, mid_im], axis=1).astype(jnp.bfloat16)
        if i == 0:
            get_second.wait()
        image = jnp.dot(mid, second[...], preferred_element_type=jnp.float32)
        for k in range(group):
            here, below = image[TILE * k : TILE * (k + 1)], image[TILE * (k + 1) : TILE * (k + 2)]
            middle = jnp.where(upper, below[:, :LANES], pltpu.roll(below[:, LANES:], TILE // 2, 0))
            window = jnp.concatenate([here[:, :LANES], middle, here[:, LANES:]], axis=0)
            cut[i * group + k] = window.astype(cut.dtype)
        part = pl.ds(i * group, group)
        copies.append(pltpu.make_async_copy(cut.at[part], out.at[part], sent.at[i]))
        copies[-1].start()
    for copy in copies:
        copy.wait()


def own_place():
    place, count = 0, 1
    for axis in ALL:
        place = place * lax.axis_size(axis) + lax.axis_index(axis)
        count = count * lax.axis_size(axis)
    return place, count - 1


def four_times(values):
    return jnp.concatenate([values] * 4, axis=1)


def weights_kernel(one_in, bias_in, two_in, bias_two_in, weights_one, weights_two, bias_rows, one, bias, two, bias_two, sems):
    fetch = [
        pltpu.make_async_copy(one_in, one, sems.at[0]),
        pltpu.make_async_copy(bias_in, bias, sems.at[1]),
        pltpu.make_async_copy(two_in, two, sems.at[2]),
        pltpu.make_async_copy(bias_two_in, bias_two, sems.at[3]),
    ]
    for copy in fetch:
        copy.start()
    for copy in fetch:
        copy.wait()
    channels = one.shape[2]
    rows = TILE + 2
    per_tile = LANES // channels
    lanes = -(-rows * channels // LANES) * LANES
    image_row = lax.broadcasted_iota(jnp.int32, (16, lanes), 0)
    hidden_row = lax.broadcasted_iota(jnp.int32, (16, lanes), 1) // channels
    place, last = own_place()
    held = (hidden_row >= jnp.where(place == 0, 1, 0)) & (hidden_row < jnp.where(place == last, rows - 1, rows))
    high, low = [], []
    for tap in range(3):
        band = jnp.zeros((16, lanes), jnp.float32)
        for shift in range(3):
            line = jnp.concatenate([four_times(one[shift, tap : tap + 1])] * (lanes // LANES), axis=1)
            band = jnp.where(held & (image_row - hidden_row == shift), line, band)
        high.append(band.astype(jnp.bfloat16).astype(jnp.float32))
        low.append(band - high[-1])
    line = jnp.concatenate([four_times(bias[...])] * (lanes // LANES), axis=1)
    with_bias = high[0]
    for piece in range(3):
        rounded = line.astype(jnp.bfloat16).astype(jnp.float32)
        with_bias = jnp.where(held & (image_row == 12 + piece), rounded, with_bias)
        line = line - rounded
    stacked = jnp.concatenate([with_bias, *high[1:], *high, *low], axis=0)
    weights_one[...] = stacked.T[: weights_one.shape[0]].astype(jnp.bfloat16)
    row = lax.broadcasted_iota(jnp.int32, bias_rows.shape, 0) // TILE
    lane = lax.broadcasted_iota(jnp.int32, bias_rows.shape, 1)
    line = jnp.where(row == lane, four_times(bias_two[...]), 0.0)
    bias_rows[...] = jnp.broadcast_to(jnp.sum(line, axis=1, keepdims=True), bias_rows.shape)
    lines = [[four_times(two[shift, tap].astype(jnp.float32)) for shift in range(3)] for tap in range(3)]
    row = lax.broadcasted_iota(jnp.int32, (TILE, LANES), 0)
    lane = lax.broadcasted_iota(jnp.int32, (TILE, LANES), 1) // channels
    zero = jnp.zeros((TILE, LANES), jnp.float32)
    for tile in range(-(-3 * rows // per_tile)):
        taps = sorted({(tile * per_tile + g) // rows for g in range(per_tile)} & {0, 1, 2})
        masks = []
        for tap in taps:
            hidden_row = tile * per_tile + lane - tap * rows
            inside = (hidden_row >= 0) & (hidden_row < rows)
            masks += [(tap, shift, inside & (hidden_row - row == shift)) for shift in range(3)]
        width = min(LANES, weights_two.shape[1] - tile * LANES)
        for channel in range(0, channels, 2):
            pair = []
            for k in (channel, channel + 1):
                values = zero
                for tap, shift, mask in masks:
                    values = jnp.where(mask, lines[tap][shift][k : k + 1], values)
                pair.append(values)
            block = jnp.concatenate(pair, axis=0).astype(jnp.bfloat16)
            weights_two[TILE * channel : TILE * (channel + 2), tile * LANES : tile * LANES + width] = block[:, :width]


def shifted(values, width):
    lane = lax.broadcasted_iota(jnp.int32, values.shape, 1)
    zero = jnp.zeros_like(values)
    before = jnp.where(lane == 0, zero, pltpu.roll(values, 1, 1))
    after = jnp.where(lane == width - 1, zero, pltpu.roll(values, width - 1, 1))
    return before, values, after


def layers_kernel(shares, weights_one, weights_two, bias_rows, out, staged, sems):
    total = shares[0].astype(jnp.float32)
    for device in range(1, shares.shape[0]):
        total = total + shares[device].astype(jnp.float32)
    width = out.shape[2]
    middle = total[TILE : 2 * TILE]
    upper = lax.broadcasted_iota(jnp.int32, (TILE, width), 0) < TILE // 2
    lower_rows = jnp.concatenate([middle, pltpu.roll(middle, TILE // 2, 0)], axis=1)
    image = jnp.concatenate(
        [jnp.concatenate([total[:TILE], total[2 * TILE :]], axis=1), jnp.where(upper, lower_rows, 0.0)], axis=0
    )
    columns = jnp.concatenate(shifted(image, width), axis=0)
    high = columns.astype(jnp.bfloat16).astype(jnp.float32)
    low = columns - high
    row = lax.broadcasted_iota(jnp.int32, (48, width), 0)
    with_ones = jnp.where((row >= 12) & (row < 15), 1.0, high)
    stacked = jnp.concatenate([with_ones, low, high], axis=0).astype(jnp.bfloat16)
    hidden = jnp.dot(weights_one[...], stacked, preferred_element_type=jnp.float32)
    hidden = jnp.maximum(hidden, 0.0).astype(jnp.bfloat16)
    stacked = jnp.concatenate(shifted(hidden, width), axis=0)
    half = out.shape[0] // 2
    copies = []
    for part in range(2):
        rows = pl.ds(part * half * TILE, half * TILE)
        features = jnp.dot(weights_two[rows], stacked, preferred_element_type=jnp.float32)
        features = features + jnp.concatenate([bias_rows[rows]] * (width // LANES), axis=1)
        channels_of = pl.ds(part * half, half)
        staged[channels_of] = features.reshape(half, TILE, width).astype(out.dtype)
        copies.append(pltpu.make_async_copy(staged.at[channels_of], out.at[channels_of], sems.at[part]))
        copies[-1].start()
    for copy in copies:
        copy.wait()


def in_hbm(*arrays):
    return [pltpu.with_memory_space_constraint(array, pltpu.HBM) for array in arrays]


def direct(partials, coverage, conv_one, bias_one, conv_two, bias_two):
    count_row, count_col = lax.axis_size("row"), lax.axis_size("col")
    devices = lax.axis_size("vis") * count_row * count_col
    length = partials.shape[3] * count_col
    image_len = length // 2
    channels = conv_two.shape[2]
    first, second = grid_tables(length, count_row, count_col)
    vmem, hbm = pl.BlockSpec(memory_space=pltpu.VMEM), pl.BlockSpec(memory_space=pltpu.HBM)
    limit = pltpu.CompilerParams(vmem_limit_bytes=16 * 2**20)
    share = (devices, 2 * (TILE + 2 * HALO), LANES)
    shares = pl.pallas_call(
        share_kernel,
        out_shape=jax.ShapeDtypeStruct(share, jnp.bfloat16),
        in_specs=[hbm] * 4,
        out_specs=hbm,
        scratch_shapes=[
            pltpu.SMEM(coverage.shape, jnp.int32),
            pltpu.VMEM(partials.shape, jnp.bfloat16),
            pltpu.VMEM(first.shape[1:], jnp.bfloat16),
            pltpu.VMEM(second.shape[1:], jnp.bfloat16),
            pltpu.VMEM(share, jnp.bfloat16),
            pltpu.SemaphoreType.DMA((3 + HALVES,)),
            pltpu.SemaphoreType.DMA((HALVES,)),
        ],
        compiler_params=limit,
        name="shares",
    )(*in_hbm(coverage, partials, jnp.asarray(first), jnp.asarray(second)))
    arrived = lax.all_to_all(shares, ALL, split_axis=0, concat_axis=0, tiled=True)
    rows = TILE + 2
    weights = pl.pallas_call(
        weights_kernel,
        out_shape=[
            jax.ShapeDtypeStruct((rows * channels, 3 * 48), jnp.bfloat16),
            jax.ShapeDtypeStruct((TILE * channels, 3 * rows * channels), jnp.bfloat16),
            jax.ShapeDtypeStruct((TILE * channels, LANES), jnp.float32),
        ],
        in_specs=[hbm] * 4,
        out_specs=[vmem] * 3,
        scratch_shapes=[
            pltpu.VMEM((3, 3, channels), jnp.float32),
            pltpu.VMEM((1, channels), jnp.float32),
            pltpu.VMEM(conv_two.shape, jnp.bfloat16),
            pltpu.VMEM((1, channels), jnp.float32),
            pltpu.SemaphoreType.DMA((4,)),
        ],
        compiler_params=limit,
        name="weights",
    )(*in_hbm(conv_one.transpose(1, 2, 0), bias_one[None], conv_two, bias_two[None]))
    return pl.pallas_call(
        layers_kernel,
        out_shape=jax.ShapeDtypeStruct((channels, TILE, image_len), jnp.bfloat16),
        in_specs=[vmem] * 4,
        out_specs=hbm,
        scratch_shapes=[
            pltpu.VMEM((channels, TILE, image_len), jnp.bfloat16),
            pltpu.SemaphoreType.DMA((2,)),
        ],
        compiler_params=limit,
        name="layers",
    )(arrived, *weights)


def local(partials, coverage, conv_one, bias_one, conv_two, bias_two):
    count_col = lax.axis_size("col")
    devices = lax.axis_size("vis") * lax.axis_size("row") * count_col
    image_len = partials.shape[3] * count_col // 2
    sent = devices * (TILE + 2 * HALO) * image_len * 2
    fits = image_len == devices * TILE and conv_two.shape[2] * 4 == LANES and image_len == 2 * LANES and sent <= DIRECT_BYTES
    plan = direct if fits else staged
    return plan(partials, coverage, conv_one, bias_one, conv_two, bias_two)


def solution(mesh):
    placed = (P("vis", None, "row", "col"), P("vis", "row", "col"), P(), P(), P(), P())
    return jax.shard_map(
        local,
        mesh=mesh,
        in_specs=placed,
        out_specs=P(None, ALL, None),
        check_vma=False,
    )
```

```python
import math

import jax
import jax.numpy as jnp
import numpy as np
from jax import lax
from jax.experimental import pallas as pl
from jax.experimental.pallas import tpu as pltpu
from jax.sharding import PartitionSpec as P

BLK = 128
ALL = ("vis", "row", "col")
SENT = ("vis", "col", "row")
DIRECT_BYTES = 4 * 2**20
HALO = 2
TILE = 8
LANES = 128
HALVES = 1


def with_halo(cells, sides, width):
    for axis, dim in sides:
        count = lax.axis_size(axis)
        ends = count - 1
        head = lax.slice_in_dim(cells, 0, width, axis=dim)
        tail = lax.slice_in_dim(cells, cells.shape[dim] - width, cells.shape[dim], axis=dim)
        cells = jnp.concatenate(
            [
                lax.ppermute(tail, axis, [(i, (i + 1) % count) for i in range(ends)]),
                cells,
                lax.ppermute(head, axis, [((i + 1) % count, i) for i in range(ends)]),
            ],
            axis=dim,
        )
    return cells


def phase_table(numer, denom):
    angle = numer.astype(jnp.float32) * (2.0 * math.pi / denom)
    return (jnp.cos(angle), jnp.sin(angle))


def partial_transform(real_part, imag_part, block_of, keep_imag):
    batch = real_part.shape[0]
    count_blocks = real_part.shape[1]
    block_len = real_part.shape[2]
    length = count_blocks * block_len
    highest = lax.Precision.HIGHEST
    outer = jnp.arange(count_blocks, dtype=jnp.int32)
    inner = jnp.arange(block_len, dtype=jnp.int32)
    cos_one, sin_one = phase_table(block_of[:, None] * outer[None, :] % count_blocks, count_blocks)
    mid_re = jnp.einsum("lpt,px->lxt", real_part, cos_one, precision=highest) - jnp.einsum(
        "lpt,px->lxt", imag_part, sin_one, precision=highest
    )
    mid_im = jnp.einsum("lpt,px->lxt", real_part, sin_one, precision=highest) + jnp.einsum(
        "lpt,px->lxt", imag_part, cos_one, precision=highest
    )
    cos_two, sin_two = phase_table(outer[:, None] * inner[None, :] % length, length)
    parity = (1 - 2 * (outer % 2)).astype(jnp.float32)[:, None]
    cos_two = cos_two * parity
    sin_two = sin_two * parity
    turn_re = mid_re * cos_two - mid_im * sin_two
    turn_im = mid_re * sin_two + mid_im * cos_two
    kept = jnp.arange(block_len // 2, dtype=jnp.int32)
    picked = (kept + 3 * block_len // 4) % block_len
    cos_three, sin_three = phase_table(inner[:, None] * picked[None, :] % block_len, block_len)
    out_re = jnp.einsum("lxt,tj->ljx", turn_re, cos_three, precision=highest) - jnp.einsum(
        "lxt,tj->ljx", turn_im, sin_three, precision=highest
    )
    out_re = out_re.reshape(batch, length // 2)
    if keep_imag:
        out_im = jnp.einsum("lxt,tj->ljx", turn_re, sin_three, precision=highest) + jnp.einsum(
            "lxt,tj->ljx", turn_im, cos_three, precision=highest
        )
        return (out_re, out_im.reshape(batch, length // 2))
    return (out_re, out_re)


def first_layer(extended, conv_one, bias_one, count_rows):
    width = extended.shape[1]
    padded = jnp.pad(extended, ((0, 0), (1, 1)))
    summed = (
        jnp.zeros((conv_one.shape[0], count_rows, width), jnp.float32) + bias_one[:, None, None]
    )
    for shift_b in range(3):
        for shift_a in range(3):
            summed = (
                summed
                + conv_one[:, shift_b, shift_a][:, None, None]
                * padded[None, shift_b : shift_b + count_rows, shift_a : shift_a + width]
            )
    return jnp.maximum(summed, 0.0)


def second_layer(hidden_ext, conv_two, bias_two, count_rows):
    width = hidden_ext.shape[2]
    padded = jnp.pad(hidden_ext, ((0, 0), (0, 0), (1, 1)))
    summed = jnp.zeros((conv_two.shape[2], count_rows, width), jnp.float32)
    for shift_b in range(3):
        for shift_a in range(3):
            summed = summed + jnp.einsum(
                "kj,jba->kba",
                conv_two[shift_b, shift_a],
                padded[:, shift_b : shift_b + count_rows, shift_a : shift_a + width],
                preferred_element_type=jnp.float32,
            )
    return (summed + bias_two[:, None, None]).astype(jnp.bfloat16)


def staged(partials, coverage, conv_one, bias_one, conv_two, bias_two):
    count_vis = lax.axis_size("vis")
    count_row = lax.axis_size("row")
    count_col = lax.axis_size("col")
    grid_len = partials.shape[3] * count_col
    cover = coverage[0]
    block_rows = cover.shape[0]
    block_cols = cover.shape[1]
    spread = jnp.broadcast_to(cover[:, None, :, None], (block_rows, BLK, block_cols, BLK))
    spread = spread.reshape(block_rows * BLK, block_cols * BLK)
    count_blocks = count_vis * count_row
    row_block = grid_len // count_blocks
    row_share = row_block // count_col
    masked = partials[0] * spread.astype(jnp.bfloat16)[None]
    reduced = lax.psum_scatter(
        masked.astype(jnp.float32).astype(jnp.bfloat16), "vis", scatter_dimension=1, tiled=True
    ).astype(jnp.float32)
    grid_rows = lax.all_to_all(
        reduced.astype(jnp.bfloat16), "col", split_axis=1, concat_axis=2, tiled=True
    ).astype(reduced.dtype)
    natural = jnp.arange(count_blocks, dtype=jnp.int32)
    shaped = grid_rows.reshape(2, row_share, count_blocks, row_block)
    first_re, first_im = partial_transform(shaped[0], shaped[1], natural, True)
    stacked = jnp.stack([first_re, first_im])
    moved = lax.all_to_all(
        lax.all_to_all(
            stacked.astype(jnp.bfloat16), ("vis", "row"), split_axis=2, concat_axis=1, tiled=True
        ),
        "col",
        split_axis=2,
        concat_axis=1,
        tiled=True,
    ).astype(stacked.dtype)
    img_rows = moved.shape[2]
    arranged = moved.reshape(2, count_col, count_blocks, row_share, img_rows)
    arranged = arranged.transpose(0, 4, 2, 1, 3).reshape(2, img_rows, count_blocks, row_block)
    owners = natural % count_row * count_vis + natural // count_row
    image, unused = partial_transform(arranged[0], arranged[1], owners, False)
    image = image * (1.0 / grid_len)
    extended = with_halo(image.astype(jnp.bfloat16), ((("vis", "row", "col"), 0),), 1).astype(
        image.dtype
    )
    hidden = first_layer(extended, conv_one, bias_one, img_rows).astype(jnp.bfloat16)
    hidden_ext = with_halo(hidden, ((("vis", "row", "col"), 1),), 1)
    return second_layer(hidden_ext, conv_two, bias_two, img_rows)


def grid_tables(length, count_row, count_col):
    image_len = length // 2
    place = np.arange(length)[:, None] - length // 2
    pixel = np.arange(image_len)[None, :] - image_len // 2
    angle = (place * pixel % length) * (2.0 * math.pi / length)
    cos, sin = np.cos(angle), np.sin(angle)
    half = image_len // HALVES
    padded = np.pad(np.stack([cos.T, sin.T]), ((0, 0), (HALO, TILE - HALO), (0, 0)))
    halves = np.stack([padded[:, i * half : (i + 1) * half + TILE] for i in range(HALVES)])
    first = halves.reshape(HALVES, 2 * (half + TILE), count_col, length // count_col).transpose(2, 0, 1, 3)
    rows = length // count_row
    second = np.stack([cos.reshape(count_row, rows, image_len), -sin.reshape(count_row, rows, image_len)], axis=1)
    second = second.reshape(count_row, 2 * rows, image_len) / length
    return first.astype(jnp.bfloat16), second.astype(jnp.bfloat16)


def send_order():
    sizes = [lax.axis_size(axis) for axis in ALL]
    places = np.arange(math.prod(sizes)).reshape(sizes)
    return places.transpose([ALL.index(axis) for axis in SENT]).reshape(-1).tolist()


def share_kernel(cover_in, parts_in, first_all, second_all, out, cover, parts, first, second, cut, sems, sent):
    col, row = lax.axis_index("col"), lax.axis_index("row")
    get_cover = pltpu.make_async_copy(cover_in, cover, sems.at[0])
    get_parts = pltpu.make_async_copy(parts_in, parts, sems.at[1])
    get_second = pltpu.make_async_copy(second_all.at[row], second, sems.at[2])
    get_first = [
        pltpu.make_async_copy(first_all.at[col, i], first.at[i], sems.at[3 + i]) for i in range(HALVES)
    ]
    for copy in (get_cover, get_parts, get_first[0], get_second, *get_first[1:]):
        copy.start()
    count_rows = parts.shape[2]
    get_cover.wait()
    get_parts.wait()
    components = []
    for component in range(2):
        strips = []
        for i in range(cover.shape[1]):
            cells = []
            for j in range(cover.shape[2]):
                block = parts[0, component, i * BLK : (i + 1) * BLK, j * BLK : (j + 1) * BLK]
                level = jnp.full(block.shape, cover[0, i, j].astype(jnp.float32)).astype(jnp.bfloat16)
                cells.append(block * level)
            strips.append(jnp.concatenate(cells, axis=1))
        components.append(jnp.concatenate(strips, axis=0))
    grid = jnp.concatenate(components, axis=0)
    upper = lax.broadcasted_iota(jnp.int32, (TILE, LANES), 0) < TILE // 2
    group = cut.shape[0] // HALVES
    tall = first.shape[1] // 2
    order = send_order()
    slots = [order.index(device) for device in range(len(order))]
    copies = []
    for i in range(HALVES):
        get_first[i].wait()
        turned = lax.dot_general(first[i], grid, (((1,), (1,)), ((), ())), preferred_element_type=jnp.float32)
        mid_re = turned[:tall, :count_rows] - turned[tall:, count_rows:]
        mid_im = turned[tall:, :count_rows] + turned[:tall, count_rows:]
        mid = jnp.concatenate([mid_re, mid_im], axis=1).astype(jnp.bfloat16)
        if i == 0:
            get_second.wait()
        image = jnp.dot(mid, second[...], preferred_element_type=jnp.float32)
        for k in range(group):
            here, below = image[TILE * k : TILE * (k + 1)], image[TILE * (k + 1) : TILE * (k + 2)]
            middle = jnp.where(upper, below[:, :LANES], pltpu.roll(below[:, LANES:], TILE // 2, 0))
            window = jnp.concatenate([here[:, :LANES], middle, here[:, LANES:]], axis=0)
            cut[slots[i * group + k]] = window.astype(cut.dtype)
        part = pl.ds(i * group, group)
        copies.append(pltpu.make_async_copy(cut.at[part], out.at[part], sent.at[i]))
        copies[-1].start()
    for copy in copies:
        copy.wait()


def own_place():
    place, count = 0, 1
    for axis in ALL:
        place = place * lax.axis_size(axis) + lax.axis_index(axis)
        count = count * lax.axis_size(axis)
    return place, count - 1


def four_times(values):
    return jnp.concatenate([values] * 4, axis=1)


def weights_kernel(one_in, bias_in, two_in, bias_two_in, weights_one, weights_two, bias_rows, one, bias, two, bias_two, sems):
    fetch = [
        pltpu.make_async_copy(one_in, one, sems.at[0]),
        pltpu.make_async_copy(bias_in, bias, sems.at[1]),
        pltpu.make_async_copy(two_in, two, sems.at[2]),
        pltpu.make_async_copy(bias_two_in, bias_two, sems.at[3]),
    ]
    for copy in fetch:
        copy.start()
    for copy in fetch:
        copy.wait()
    channels = one.shape[2]
    rows = TILE + 2
    per_tile = LANES // channels
    lanes = -(-rows * channels // LANES) * LANES
    image_row = lax.broadcasted_iota(jnp.int32, (16, lanes), 0)
    hidden_row = lax.broadcasted_iota(jnp.int32, (16, lanes), 1) // channels
    place, last = own_place()
    held = (hidden_row >= jnp.where(place == 0, 1, 0)) & (hidden_row < jnp.where(place == last, rows - 1, rows))
    high, low = [], []
    for tap in range(3):
        band = jnp.zeros((16, lanes), jnp.float32)
        for shift in range(3):
            line = jnp.concatenate([four_times(one[shift, tap : tap + 1])] * (lanes // LANES), axis=1)
            band = jnp.where(held & (image_row - hidden_row == shift), line, band)
        high.append(band.astype(jnp.bfloat16).astype(jnp.float32))
        low.append(band - high[-1])
    line = jnp.concatenate([four_times(bias[...])] * (lanes // LANES), axis=1)
    with_bias = high[0]
    for piece in range(3):
        rounded = line.astype(jnp.bfloat16).astype(jnp.float32)
        with_bias = jnp.where(held & (image_row == 12 + piece), rounded, with_bias)
        line = line - rounded
    stacked = jnp.concatenate([with_bias, *high[1:], *high, *low], axis=0)
    weights_one[...] = stacked.T[: weights_one.shape[0]].astype(jnp.bfloat16)
    row = lax.broadcasted_iota(jnp.int32, bias_rows.shape, 0) // TILE
    lane = lax.broadcasted_iota(jnp.int32, bias_rows.shape, 1)
    line = jnp.where(row == lane, four_times(bias_two[...]), 0.0)
    bias_rows[...] = jnp.broadcast_to(jnp.sum(line, axis=1, keepdims=True), bias_rows.shape)
    lines = [[four_times(two[shift, tap].astype(jnp.float32)) for shift in range(3)] for tap in range(3)]
    row = lax.broadcasted_iota(jnp.int32, (TILE, LANES), 0)
    lane = lax.broadcasted_iota(jnp.int32, (TILE, LANES), 1) // channels
    zero = jnp.zeros((TILE, LANES), jnp.float32)
    for tile in range(-(-3 * rows // per_tile)):
        taps = sorted({(tile * per_tile + g) // rows for g in range(per_tile)} & {0, 1, 2})
        masks = []
        for tap in taps:
            hidden_row = tile * per_tile + lane - tap * rows
            inside = (hidden_row >= 0) & (hidden_row < rows)
            masks += [(tap, shift, inside & (hidden_row - row == shift)) for shift in range(3)]
        width = min(LANES, weights_two.shape[1] - tile * LANES)
        for channel in range(0, channels, 2):
            pair = []
            for k in (channel, channel + 1):
                values = zero
                for tap, shift, mask in masks:
                    values = jnp.where(mask, lines[tap][shift][k : k + 1], values)
                pair.append(values)
            block = jnp.concatenate(pair, axis=0).astype(jnp.bfloat16)
            weights_two[TILE * channel : TILE * (channel + 2), tile * LANES : tile * LANES + width] = block[:, :width]


def shifted(values, width):
    lane = lax.broadcasted_iota(jnp.int32, values.shape, 1)
    zero = jnp.zeros_like(values)
    before = jnp.where(lane == 0, zero, pltpu.roll(values, 1, 1))
    after = jnp.where(lane == width - 1, zero, pltpu.roll(values, width - 1, 1))
    return before, values, after


def layers_kernel(shares, weights_one, weights_two, bias_rows, out, staged, sems):
    total = shares[0].astype(jnp.float32)
    for device in range(1, shares.shape[0]):
        total = total + shares[device].astype(jnp.float32)
    width = out.shape[2]
    middle = total[TILE : 2 * TILE]
    upper = lax.broadcasted_iota(jnp.int32, (TILE, width), 0) < TILE // 2
    lower_rows = jnp.concatenate([middle, pltpu.roll(middle, TILE // 2, 0)], axis=1)
    image = jnp.concatenate(
        [jnp.concatenate([total[:TILE], total[2 * TILE :]], axis=1), jnp.where(upper, lower_rows, 0.0)], axis=0
    )
    columns = jnp.concatenate(shifted(image, width), axis=0)
    high = columns.astype(jnp.bfloat16).astype(jnp.float32)
    low = columns - high
    row = lax.broadcasted_iota(jnp.int32, (48, width), 0)
    with_ones = jnp.where((row >= 12) & (row < 15), 1.0, high)
    stacked = jnp.concatenate([with_ones, low, high], axis=0).astype(jnp.bfloat16)
    hidden = jnp.dot(weights_one[...], stacked, preferred_element_type=jnp.float32)
    hidden = jnp.maximum(hidden, 0.0).astype(jnp.bfloat16)
    stacked = jnp.concatenate(shifted(hidden, width), axis=0)
    half = out.shape[0] // 2
    copies = []
    for part in range(2):
        rows = pl.ds(part * half * TILE, half * TILE)
        features = jnp.dot(weights_two[rows], stacked, preferred_element_type=jnp.float32)
        features = features + jnp.concatenate([bias_rows[rows]] * (width // LANES), axis=1)
        channels_of = pl.ds(part * half, half)
        staged[channels_of] = features.reshape(half, TILE, width).astype(out.dtype)
        copies.append(pltpu.make_async_copy(staged.at[channels_of], out.at[channels_of], sems.at[part]))
        copies[-1].start()
    for copy in copies:
        copy.wait()


def in_hbm(*arrays):
    return [pltpu.with_memory_space_constraint(array, pltpu.HBM) for array in arrays]


def direct(partials, coverage, conv_one, bias_one, conv_two, bias_two):
    count_row, count_col = lax.axis_size("row"), lax.axis_size("col")
    devices = lax.axis_size("vis") * count_row * count_col
    length = partials.shape[3] * count_col
    image_len = length // 2
    channels = conv_two.shape[2]
    first, second = grid_tables(length, count_row, count_col)
    vmem, hbm = pl.BlockSpec(memory_space=pltpu.VMEM), pl.BlockSpec(memory_space=pltpu.HBM)
    limit = pltpu.CompilerParams(vmem_limit_bytes=16 * 2**20)
    share = (devices, 2 * (TILE + 2 * HALO), LANES)
    shares = pl.pallas_call(
        share_kernel,
        out_shape=jax.ShapeDtypeStruct(share, jnp.bfloat16),
        in_specs=[hbm] * 4,
        out_specs=hbm,
        scratch_shapes=[
            pltpu.SMEM(coverage.shape, jnp.int32),
            pltpu.VMEM(partials.shape, jnp.bfloat16),
            pltpu.VMEM(first.shape[1:], jnp.bfloat16),
            pltpu.VMEM(second.shape[1:], jnp.bfloat16),
            pltpu.VMEM(share, jnp.bfloat16),
            pltpu.SemaphoreType.DMA((3 + HALVES,)),
            pltpu.SemaphoreType.DMA((HALVES,)),
        ],
        compiler_params=limit,
        name="shares",
    )(*in_hbm(coverage, partials, jnp.asarray(first), jnp.asarray(second)))
    arrived = lax.all_to_all(shares, SENT, split_axis=0, concat_axis=0, tiled=True)
    rows = TILE + 2
    weights = pl.pallas_call(
        weights_kernel,
        out_shape=[
            jax.ShapeDtypeStruct((rows * channels, 3 * 48), jnp.bfloat16),
            jax.ShapeDtypeStruct((TILE * channels, 3 * rows * channels), jnp.bfloat16),
            jax.ShapeDtypeStruct((TILE * channels, LANES), jnp.float32),
        ],
        in_specs=[hbm] * 4,
        out_specs=[vmem] * 3,
        scratch_shapes=[
            pltpu.VMEM((3, 3, channels), jnp.float32),
            pltpu.VMEM((1, channels), jnp.float32),
            pltpu.VMEM(conv_two.shape, jnp.bfloat16),
            pltpu.VMEM((1, channels), jnp.float32),
            pltpu.SemaphoreType.DMA((4,)),
        ],
        compiler_params=limit,
        name="weights",
    )(*in_hbm(conv_one.transpose(1, 2, 0), bias_one[None], conv_two, bias_two[None]))
    return pl.pallas_call(
        layers_kernel,
        out_shape=jax.ShapeDtypeStruct((channels, TILE, image_len), jnp.bfloat16),
        in_specs=[vmem] * 4,
        out_specs=hbm,
        scratch_shapes=[
            pltpu.VMEM((channels, TILE, image_len), jnp.bfloat16),
            pltpu.SemaphoreType.DMA((2,)),
        ],
        compiler_params=limit,
        name="layers",
    )(arrived, *weights)


def local(partials, coverage, conv_one, bias_one, conv_two, bias_two):
    count_col = lax.axis_size("col")
    devices = lax.axis_size("vis") * lax.axis_size("row") * count_col
    image_len = partials.shape[3] * count_col // 2
    sent = devices * (TILE + 2 * HALO) * image_len * 2
    fits = image_len == devices * TILE and conv_two.shape[2] * 4 == LANES and image_len == 2 * LANES and sent <= DIRECT_BYTES
    plan = direct if fits else staged
    return plan(partials, coverage, conv_one, bias_one, conv_two, bias_two)


def solution(mesh):
    placed = (P("vis", None, "row", "col"), P("vis", "row", "col"), P(), P(), P(), P())
    return jax.shard_map(
        local,
        mesh=mesh,
        in_specs=placed,
        out_specs=P(None, ALL, None),
        check_vma=False,
    )
```

```python
import math

import jax
import jax.numpy as jnp
import numpy as np
from jax import lax
from jax.experimental import pallas as pl
from jax.experimental.pallas import tpu as pltpu
from jax.sharding import PartitionSpec as P

BLK = 128
ALL = ("vis", "row", "col")
SENT = ("col", "row", "vis")
DIRECT_BYTES = 4 * 2**20
HALO = 2
TILE = 8
LANES = 128
HALVES = 1


def with_halo(cells, sides, width):
    for axis, dim in sides:
        count = lax.axis_size(axis)
        ends = count - 1
        head = lax.slice_in_dim(cells, 0, width, axis=dim)
        tail = lax.slice_in_dim(cells, cells.shape[dim] - width, cells.shape[dim], axis=dim)
        cells = jnp.concatenate(
            [
                lax.ppermute(tail, axis, [(i, (i + 1) % count) for i in range(ends)]),
                cells,
                lax.ppermute(head, axis, [((i + 1) % count, i) for i in range(ends)]),
            ],
            axis=dim,
        )
    return cells


def phase_table(numer, denom):
    angle = numer.astype(jnp.float32) * (2.0 * math.pi / denom)
    return (jnp.cos(angle), jnp.sin(angle))


def partial_transform(real_part, imag_part, block_of, keep_imag):
    batch = real_part.shape[0]
    count_blocks = real_part.shape[1]
    block_len = real_part.shape[2]
    length = count_blocks * block_len
    highest = lax.Precision.HIGHEST
    outer = jnp.arange(count_blocks, dtype=jnp.int32)
    inner = jnp.arange(block_len, dtype=jnp.int32)
    cos_one, sin_one = phase_table(block_of[:, None] * outer[None, :] % count_blocks, count_blocks)
    mid_re = jnp.einsum("lpt,px->lxt", real_part, cos_one, precision=highest) - jnp.einsum(
        "lpt,px->lxt", imag_part, sin_one, precision=highest
    )
    mid_im = jnp.einsum("lpt,px->lxt", real_part, sin_one, precision=highest) + jnp.einsum(
        "lpt,px->lxt", imag_part, cos_one, precision=highest
    )
    cos_two, sin_two = phase_table(outer[:, None] * inner[None, :] % length, length)
    parity = (1 - 2 * (outer % 2)).astype(jnp.float32)[:, None]
    cos_two = cos_two * parity
    sin_two = sin_two * parity
    turn_re = mid_re * cos_two - mid_im * sin_two
    turn_im = mid_re * sin_two + mid_im * cos_two
    kept = jnp.arange(block_len // 2, dtype=jnp.int32)
    picked = (kept + 3 * block_len // 4) % block_len
    cos_three, sin_three = phase_table(inner[:, None] * picked[None, :] % block_len, block_len)
    out_re = jnp.einsum("lxt,tj->ljx", turn_re, cos_three, precision=highest) - jnp.einsum(
        "lxt,tj->ljx", turn_im, sin_three, precision=highest
    )
    out_re = out_re.reshape(batch, length // 2)
    if keep_imag:
        out_im = jnp.einsum("lxt,tj->ljx", turn_re, sin_three, precision=highest) + jnp.einsum(
            "lxt,tj->ljx", turn_im, cos_three, precision=highest
        )
        return (out_re, out_im.reshape(batch, length // 2))
    return (out_re, out_re)


def first_layer(extended, conv_one, bias_one, count_rows):
    width = extended.shape[1]
    padded = jnp.pad(extended, ((0, 0), (1, 1)))
    summed = (
        jnp.zeros((conv_one.shape[0], count_rows, width), jnp.float32) + bias_one[:, None, None]
    )
    for shift_b in range(3):
        for shift_a in range(3):
            summed = (
                summed
                + conv_one[:, shift_b, shift_a][:, None, None]
                * padded[None, shift_b : shift_b + count_rows, shift_a : shift_a + width]
            )
    return jnp.maximum(summed, 0.0)


def second_layer(hidden_ext, conv_two, bias_two, count_rows):
    width = hidden_ext.shape[2]
    padded = jnp.pad(hidden_ext, ((0, 0), (0, 0), (1, 1)))
    summed = jnp.zeros((conv_two.shape[2], count_rows, width), jnp.float32)
    for shift_b in range(3):
        for shift_a in range(3):
            summed = summed + jnp.einsum(
                "kj,jba->kba",
                conv_two[shift_b, shift_a],
                padded[:, shift_b : shift_b + count_rows, shift_a : shift_a + width],
                preferred_element_type=jnp.float32,
            )
    return (summed + bias_two[:, None, None]).astype(jnp.bfloat16)


def staged(partials, coverage, conv_one, bias_one, conv_two, bias_two):
    count_vis = lax.axis_size("vis")
    count_row = lax.axis_size("row")
    count_col = lax.axis_size("col")
    grid_len = partials.shape[3] * count_col
    cover = coverage[0]
    block_rows = cover.shape[0]
    block_cols = cover.shape[1]
    spread = jnp.broadcast_to(cover[:, None, :, None], (block_rows, BLK, block_cols, BLK))
    spread = spread.reshape(block_rows * BLK, block_cols * BLK)
    count_blocks = count_vis * count_row
    row_block = grid_len // count_blocks
    row_share = row_block // count_col
    masked = partials[0] * spread.astype(jnp.bfloat16)[None]
    reduced = lax.psum_scatter(
        masked.astype(jnp.float32).astype(jnp.bfloat16), "vis", scatter_dimension=1, tiled=True
    ).astype(jnp.float32)
    grid_rows = lax.all_to_all(
        reduced.astype(jnp.bfloat16), "col", split_axis=1, concat_axis=2, tiled=True
    ).astype(reduced.dtype)
    natural = jnp.arange(count_blocks, dtype=jnp.int32)
    shaped = grid_rows.reshape(2, row_share, count_blocks, row_block)
    first_re, first_im = partial_transform(shaped[0], shaped[1], natural, True)
    stacked = jnp.stack([first_re, first_im])
    moved = lax.all_to_all(
        lax.all_to_all(
            stacked.astype(jnp.bfloat16), ("vis", "row"), split_axis=2, concat_axis=1, tiled=True
        ),
        "col",
        split_axis=2,
        concat_axis=1,
        tiled=True,
    ).astype(stacked.dtype)
    img_rows = moved.shape[2]
    arranged = moved.reshape(2, count_col, count_blocks, row_share, img_rows)
    arranged = arranged.transpose(0, 4, 2, 1, 3).reshape(2, img_rows, count_blocks, row_block)
    owners = natural % count_row * count_vis + natural // count_row
    image, unused = partial_transform(arranged[0], arranged[1], owners, False)
    image = image * (1.0 / grid_len)
    extended = with_halo(image.astype(jnp.bfloat16), ((("vis", "row", "col"), 0),), 1).astype(
        image.dtype
    )
    hidden = first_layer(extended, conv_one, bias_one, img_rows).astype(jnp.bfloat16)
    hidden_ext = with_halo(hidden, ((("vis", "row", "col"), 1),), 1)
    return second_layer(hidden_ext, conv_two, bias_two, img_rows)


def grid_tables(length, count_row, count_col):
    image_len = length // 2
    place = np.arange(length)[:, None] - length // 2
    pixel = np.arange(image_len)[None, :] - image_len // 2
    angle = (place * pixel % length) * (2.0 * math.pi / length)
    cos, sin = np.cos(angle), np.sin(angle)
    half = image_len // HALVES
    padded = np.pad(np.stack([cos.T, sin.T]), ((0, 0), (HALO, TILE - HALO), (0, 0)))
    halves = np.stack([padded[:, i * half : (i + 1) * half + TILE] for i in range(HALVES)])
    first = halves.reshape(HALVES, 2 * (half + TILE), count_col, length // count_col).transpose(2, 0, 1, 3)
    rows = length // count_row
    second = np.stack([cos.reshape(count_row, rows, image_len), -sin.reshape(count_row, rows, image_len)], axis=1)
    second = second.reshape(count_row, 2 * rows, image_len) / length
    return first.astype(jnp.bfloat16), second.astype(jnp.bfloat16)


def send_order():
    sizes = [lax.axis_size(axis) for axis in ALL]
    places = np.arange(math.prod(sizes)).reshape(sizes)
    return places.transpose([ALL.index(axis) for axis in SENT]).reshape(-1).tolist()


def share_kernel(cover_in, parts_in, first_all, second_all, out, cover, parts, first, second, cut, sems, sent):
    col, row = lax.axis_index("col"), lax.axis_index("row")
    get_cover = pltpu.make_async_copy(cover_in, cover, sems.at[0])
    get_parts = pltpu.make_async_copy(parts_in, parts, sems.at[1])
    get_second = pltpu.make_async_copy(second_all.at[row], second, sems.at[2])
    get_first = [
        pltpu.make_async_copy(first_all.at[col, i], first.at[i], sems.at[3 + i]) for i in range(HALVES)
    ]
    for copy in (get_cover, get_parts, get_first[0], get_second, *get_first[1:]):
        copy.start()
    count_rows = parts.shape[2]
    get_cover.wait()
    get_parts.wait()
    components = []
    for component in range(2):
        strips = []
        for i in range(cover.shape[1]):
            cells = []
            for j in range(cover.shape[2]):
                block = parts[0, component, i * BLK : (i + 1) * BLK, j * BLK : (j + 1) * BLK]
                level = jnp.broadcast_to(cover[0, i : i + 1, j : j + 1].astype(jnp.float32), block.shape)
                cells.append(block * level.astype(jnp.bfloat16))
            strips.append(jnp.concatenate(cells, axis=1))
        components.append(jnp.concatenate(strips, axis=0))
    grid = jnp.concatenate(components, axis=0)
    upper = lax.broadcasted_iota(jnp.int32, (TILE, LANES), 0) < TILE // 2
    group = cut.shape[0] // HALVES
    tall = first.shape[1] // 2
    order = send_order()
    slots = [order.index(device) for device in range(len(order))]
    copies = []
    for i in range(HALVES):
        get_first[i].wait()
        turned = lax.dot_general(first[i], grid, (((1,), (1,)), ((), ())), preferred_element_type=jnp.float32)
        mid_re = turned[:tall, :count_rows] - turned[tall:, count_rows:]
        mid_im = turned[tall:, :count_rows] + turned[:tall, count_rows:]
        mid = jnp.concatenate([mid_re, mid_im], axis=1).astype(jnp.bfloat16)
        if i == 0:
            get_second.wait()
        image = jnp.dot(mid, second[...], preferred_element_type=jnp.float32)
        for k in range(group):
            here, below = image[TILE * k : TILE * (k + 1)], image[TILE * (k + 1) : TILE * (k + 2)]
            middle = jnp.where(upper, below[:, :LANES], pltpu.roll(below[:, LANES:], TILE // 2, 0))
            window = jnp.concatenate([here[:, :LANES], middle, here[:, LANES:]], axis=0)
            cut[slots[i * group + k]] = window.astype(cut.dtype)
        part = pl.ds(i * group, group)
        copies.append(pltpu.make_async_copy(cut.at[part], out.at[part], sent.at[i]))
        copies[-1].start()
    for copy in copies:
        copy.wait()


def own_place():
    place, count = 0, 1
    for axis in ALL:
        place = place * lax.axis_size(axis) + lax.axis_index(axis)
        count = count * lax.axis_size(axis)
    return place, count - 1


def four_times(values):
    return jnp.concatenate([values] * 4, axis=1)


def weights_kernel(one_in, bias_in, two_in, bias_two_in, weights_one, weights_two, bias_rows, one, bias, two, bias_two, sems):
    fetch = [
        pltpu.make_async_copy(one_in, one, sems.at[0]),
        pltpu.make_async_copy(bias_in, bias, sems.at[1]),
        pltpu.make_async_copy(two_in, two, sems.at[2]),
        pltpu.make_async_copy(bias_two_in, bias_two, sems.at[3]),
    ]
    for copy in fetch:
        copy.start()
    for copy in fetch:
        copy.wait()
    channels = one.shape[2]
    rows = TILE + 2
    per_tile = LANES // channels
    lanes = -(-rows * channels // LANES) * LANES
    image_row = lax.broadcasted_iota(jnp.int32, (16, lanes), 0)
    hidden_row = lax.broadcasted_iota(jnp.int32, (16, lanes), 1) // channels
    place, last = own_place()
    held = (hidden_row >= jnp.where(place == 0, 1, 0)) & (hidden_row < jnp.where(place == last, rows - 1, rows))
    high, low = [], []
    for tap in range(3):
        band = jnp.zeros((16, lanes), jnp.float32)
        for shift in range(3):
            line = jnp.concatenate([four_times(one[shift, tap : tap + 1])] * (lanes // LANES), axis=1)
            band = jnp.where(held & (image_row - hidden_row == shift), line, band)
        high.append(band.astype(jnp.bfloat16).astype(jnp.float32))
        low.append(band - high[-1])
    line = jnp.concatenate([four_times(bias[...])] * (lanes // LANES), axis=1)
    with_bias = high[0]
    for piece in range(3):
        rounded = line.astype(jnp.bfloat16).astype(jnp.float32)
        with_bias = jnp.where(held & (image_row == 12 + piece), rounded, with_bias)
        line = line - rounded
    stacked = jnp.concatenate([with_bias, *high[1:], *high, *low], axis=0)
    weights_one[...] = stacked.T[: weights_one.shape[0]].astype(jnp.bfloat16)
    row = lax.broadcasted_iota(jnp.int32, bias_rows.shape, 0) // TILE
    lane = lax.broadcasted_iota(jnp.int32, bias_rows.shape, 1)
    line = jnp.where(row == lane, four_times(bias_two[...]), 0.0)
    bias_rows[...] = jnp.broadcast_to(jnp.sum(line, axis=1, keepdims=True), bias_rows.shape)
    lines = [[four_times(two[shift, tap].astype(jnp.float32)) for shift in range(3)] for tap in range(3)]
    row = lax.broadcasted_iota(jnp.int32, (TILE, LANES), 0)
    lane = lax.broadcasted_iota(jnp.int32, (TILE, LANES), 1) // channels
    zero = jnp.zeros((TILE, LANES), jnp.float32)
    for tile in range(-(-3 * rows // per_tile)):
        taps = sorted({(tile * per_tile + g) // rows for g in range(per_tile)} & {0, 1, 2})
        masks = []
        for tap in taps:
            hidden_row = tile * per_tile + lane - tap * rows
            inside = (hidden_row >= 0) & (hidden_row < rows)
            masks += [(tap, shift, inside & (hidden_row - row == shift)) for shift in range(3)]
        width = min(LANES, weights_two.shape[1] - tile * LANES)
        for channel in range(0, channels, 2):
            pair = []
            for k in (channel, channel + 1):
                values = zero
                for tap, shift, mask in masks:
                    values = jnp.where(mask, lines[tap][shift][k : k + 1], values)
                pair.append(values)
            block = jnp.concatenate(pair, axis=0).astype(jnp.bfloat16)
            weights_two[TILE * channel : TILE * (channel + 2), tile * LANES : tile * LANES + width] = block[:, :width]


def shifted(values, width):
    lane = lax.broadcasted_iota(jnp.int32, values.shape, 1)
    zero = jnp.zeros_like(values)
    before = jnp.where(lane == 0, zero, pltpu.roll(values, 1, 1))
    after = jnp.where(lane == width - 1, zero, pltpu.roll(values, width - 1, 1))
    return before, values, after


def layers_kernel(shares, weights_one, weights_two, bias_rows, out, staged, sems):
    total = shares[0].astype(jnp.float32)
    for device in range(1, shares.shape[0]):
        total = total + shares[device].astype(jnp.float32)
    width = out.shape[2]
    middle = total[TILE : 2 * TILE]
    upper = lax.broadcasted_iota(jnp.int32, (TILE, width), 0) < TILE // 2
    lower_rows = jnp.concatenate([middle, pltpu.roll(middle, TILE // 2, 0)], axis=1)
    image = jnp.concatenate(
        [jnp.concatenate([total[:TILE], total[2 * TILE :]], axis=1), jnp.where(upper, lower_rows, 0.0)], axis=0
    )
    columns = jnp.concatenate(shifted(image, width), axis=0)
    high = columns.astype(jnp.bfloat16).astype(jnp.float32)
    low = columns - high
    row = lax.broadcasted_iota(jnp.int32, (48, width), 0)
    with_ones = jnp.where((row >= 12) & (row < 15), 1.0, high)
    stacked = jnp.concatenate([with_ones, low, high], axis=0).astype(jnp.bfloat16)
    hidden = jnp.dot(weights_one[...], stacked, preferred_element_type=jnp.float32)
    hidden = jnp.maximum(hidden, 0.0)
    stacked = jnp.concatenate(shifted(hidden, width), axis=0).astype(jnp.bfloat16)
    half = out.shape[0] // 2
    copies = []
    for part in range(2):
        rows = pl.ds(part * half * TILE, half * TILE)
        features = jnp.dot(weights_two[rows], stacked, preferred_element_type=jnp.float32)
        features = features + jnp.concatenate([bias_rows[rows]] * (width // LANES), axis=1)
        channels_of = pl.ds(part * half, half)
        staged[channels_of] = features.reshape(half, TILE, width).astype(out.dtype)
        copies.append(pltpu.make_async_copy(staged.at[channels_of], out.at[channels_of], sems.at[part]))
        copies[-1].start()
    for copy in copies:
        copy.wait()


def in_hbm(*arrays):
    return [pltpu.with_memory_space_constraint(array, pltpu.HBM) for array in arrays]


def direct(partials, coverage, conv_one, bias_one, conv_two, bias_two):
    count_row, count_col = lax.axis_size("row"), lax.axis_size("col")
    devices = lax.axis_size("vis") * count_row * count_col
    length = partials.shape[3] * count_col
    image_len = length // 2
    channels = conv_two.shape[2]
    first, second = grid_tables(length, count_row, count_col)
    vmem, hbm = pl.BlockSpec(memory_space=pltpu.VMEM), pl.BlockSpec(memory_space=pltpu.HBM)
    limit = pltpu.CompilerParams(vmem_limit_bytes=16 * 2**20)
    share = (devices, 2 * (TILE + 2 * HALO), LANES)
    shares = pl.pallas_call(
        share_kernel,
        out_shape=jax.ShapeDtypeStruct(share, jnp.bfloat16),
        in_specs=[hbm] * 4,
        out_specs=hbm,
        scratch_shapes=[
            pltpu.VMEM(coverage.shape, jnp.int32),
            pltpu.VMEM(partials.shape, jnp.bfloat16),
            pltpu.VMEM(first.shape[1:], jnp.bfloat16),
            pltpu.VMEM(second.shape[1:], jnp.bfloat16),
            pltpu.VMEM(share, jnp.bfloat16),
            pltpu.SemaphoreType.DMA((3 + HALVES,)),
            pltpu.SemaphoreType.DMA((HALVES,)),
        ],
        compiler_params=limit,
        name="shares",
    )(*in_hbm(coverage, partials, jnp.asarray(first), jnp.asarray(second)))
    arrived = lax.all_to_all(shares, SENT, split_axis=0, concat_axis=0, tiled=True)
    rows = TILE + 2
    weights = pl.pallas_call(
        weights_kernel,
        out_shape=[
            jax.ShapeDtypeStruct((rows * channels, 3 * 48), jnp.bfloat16),
            jax.ShapeDtypeStruct((TILE * channels, 3 * rows * channels), jnp.bfloat16),
            jax.ShapeDtypeStruct((TILE * channels, LANES), jnp.float32),
        ],
        in_specs=[hbm] * 4,
        out_specs=[vmem] * 3,
        scratch_shapes=[
            pltpu.VMEM((3, 3, channels), jnp.float32),
            pltpu.VMEM((1, channels), jnp.float32),
            pltpu.VMEM(conv_two.shape, jnp.bfloat16),
            pltpu.VMEM((1, channels), jnp.float32),
            pltpu.SemaphoreType.DMA((4,)),
        ],
        compiler_params=limit,
        name="weights",
    )(*in_hbm(conv_one.transpose(1, 2, 0), bias_one[None], conv_two, bias_two[None]))
    return pl.pallas_call(
        layers_kernel,
        out_shape=jax.ShapeDtypeStruct((channels, TILE, image_len), jnp.bfloat16),
        in_specs=[vmem] * 4,
        out_specs=hbm,
        scratch_shapes=[
            pltpu.VMEM((channels, TILE, image_len), jnp.bfloat16),
            pltpu.SemaphoreType.DMA((2,)),
        ],
        compiler_params=limit,
        name="layers",
    )(arrived, *weights)


def local(partials, coverage, conv_one, bias_one, conv_two, bias_two):
    count_col = lax.axis_size("col")
    devices = lax.axis_size("vis") * lax.axis_size("row") * count_col
    image_len = partials.shape[3] * count_col // 2
    sent = devices * (TILE + 2 * HALO) * image_len * 2
    fits = image_len == devices * TILE and conv_two.shape[2] * 4 == LANES and image_len == 2 * LANES and sent <= DIRECT_BYTES
    plan = direct if fits else staged
    return plan(partials, coverage, conv_one, bias_one, conv_two, bias_two)


def solution(mesh):
    placed = (P("vis", None, "row", "col"), P("vis", "row", "col"), P(), P(), P(), P())
    return jax.shard_map(
        local,
        mesh=mesh,
        in_specs=placed,
        out_specs=P(None, ALL, None),
        check_vma=False,
    )
```

```python
import math

import jax
import jax.numpy as jnp
import numpy as np
from jax import lax
from jax.experimental import pallas as pl
from jax.experimental.pallas import tpu as pltpu
from jax.sharding import PartitionSpec as P

BLK = 128
ALL = ("vis", "row", "col")
DIRECT_BYTES = 4 * 2**20
HALO = 2
TILE = 8
LANES = 128


def with_halo(cells, sides, width):
    for axis, dim in sides:
        count = lax.axis_size(axis)
        ends = count - 1
        head = lax.slice_in_dim(cells, 0, width, axis=dim)
        tail = lax.slice_in_dim(cells, cells.shape[dim] - width, cells.shape[dim], axis=dim)
        cells = jnp.concatenate(
            [
                lax.ppermute(tail, axis, [(i, (i + 1) % count) for i in range(ends)]),
                cells,
                lax.ppermute(head, axis, [((i + 1) % count, i) for i in range(ends)]),
            ],
            axis=dim,
        )
    return cells


def phase_table(numer, denom):
    angle = numer.astype(jnp.float32) * (2.0 * math.pi / denom)
    return (jnp.cos(angle), jnp.sin(angle))


def partial_transform(real_part, imag_part, block_of, keep_imag):
    batch = real_part.shape[0]
    count_blocks = real_part.shape[1]
    block_len = real_part.shape[2]
    length = count_blocks * block_len
    highest = lax.Precision.HIGHEST
    outer = jnp.arange(count_blocks, dtype=jnp.int32)
    inner = jnp.arange(block_len, dtype=jnp.int32)
    cos_one, sin_one = phase_table(block_of[:, None] * outer[None, :] % count_blocks, count_blocks)
    mid_re = jnp.einsum("lpt,px->lxt", real_part, cos_one, precision=highest) - jnp.einsum(
        "lpt,px->lxt", imag_part, sin_one, precision=highest
    )
    mid_im = jnp.einsum("lpt,px->lxt", real_part, sin_one, precision=highest) + jnp.einsum(
        "lpt,px->lxt", imag_part, cos_one, precision=highest
    )
    cos_two, sin_two = phase_table(outer[:, None] * inner[None, :] % length, length)
    parity = (1 - 2 * (outer % 2)).astype(jnp.float32)[:, None]
    cos_two = cos_two * parity
    sin_two = sin_two * parity
    turn_re = mid_re * cos_two - mid_im * sin_two
    turn_im = mid_re * sin_two + mid_im * cos_two
    kept = jnp.arange(block_len // 2, dtype=jnp.int32)
    picked = (kept + 3 * block_len // 4) % block_len
    cos_three, sin_three = phase_table(inner[:, None] * picked[None, :] % block_len, block_len)
    out_re = jnp.einsum("lxt,tj->ljx", turn_re, cos_three, precision=highest) - jnp.einsum(
        "lxt,tj->ljx", turn_im, sin_three, precision=highest
    )
    out_re = out_re.reshape(batch, length // 2)
    if keep_imag:
        out_im = jnp.einsum("lxt,tj->ljx", turn_re, sin_three, precision=highest) + jnp.einsum(
            "lxt,tj->ljx", turn_im, cos_three, precision=highest
        )
        return (out_re, out_im.reshape(batch, length // 2))
    return (out_re, out_re)


def first_layer(extended, conv_one, bias_one, count_rows):
    width = extended.shape[1]
    padded = jnp.pad(extended, ((0, 0), (1, 1)))
    summed = (
        jnp.zeros((conv_one.shape[0], count_rows, width), jnp.float32) + bias_one[:, None, None]
    )
    for shift_b in range(3):
        for shift_a in range(3):
            summed = (
                summed
                + conv_one[:, shift_b, shift_a][:, None, None]
                * padded[None, shift_b : shift_b + count_rows, shift_a : shift_a + width]
            )
    return jnp.maximum(summed, 0.0)


def second_layer(hidden_ext, conv_two, bias_two, count_rows):
    width = hidden_ext.shape[2]
    padded = jnp.pad(hidden_ext, ((0, 0), (0, 0), (1, 1)))
    summed = jnp.zeros((conv_two.shape[2], count_rows, width), jnp.float32)
    for shift_b in range(3):
        for shift_a in range(3):
            summed = summed + jnp.einsum(
                "kj,jba->kba",
                conv_two[shift_b, shift_a],
                padded[:, shift_b : shift_b + count_rows, shift_a : shift_a + width],
                preferred_element_type=jnp.float32,
            )
    return (summed + bias_two[:, None, None]).astype(jnp.bfloat16)


def staged(partials, coverage, conv_one, bias_one, conv_two, bias_two):
    count_vis = lax.axis_size("vis")
    count_row = lax.axis_size("row")
    count_col = lax.axis_size("col")
    grid_len = partials.shape[3] * count_col
    cover = coverage[0]
    block_rows = cover.shape[0]
    block_cols = cover.shape[1]
    spread = jnp.broadcast_to(cover[:, None, :, None], (block_rows, BLK, block_cols, BLK))
    spread = spread.reshape(block_rows * BLK, block_cols * BLK)
    count_blocks = count_vis * count_row
    row_block = grid_len // count_blocks
    row_share = row_block // count_col
    masked = partials[0] * spread.astype(jnp.bfloat16)[None]
    reduced = lax.psum_scatter(
        masked.astype(jnp.float32).astype(jnp.bfloat16), "vis", scatter_dimension=1, tiled=True
    ).astype(jnp.float32)
    grid_rows = lax.all_to_all(
        reduced.astype(jnp.bfloat16), "col", split_axis=1, concat_axis=2, tiled=True
    ).astype(reduced.dtype)
    natural = jnp.arange(count_blocks, dtype=jnp.int32)
    shaped = grid_rows.reshape(2, row_share, count_blocks, row_block)
    first_re, first_im = partial_transform(shaped[0], shaped[1], natural, True)
    stacked = jnp.stack([first_re, first_im])
    moved = lax.all_to_all(
        lax.all_to_all(
            stacked.astype(jnp.bfloat16), ("vis", "row"), split_axis=2, concat_axis=1, tiled=True
        ),
        "col",
        split_axis=2,
        concat_axis=1,
        tiled=True,
    ).astype(stacked.dtype)
    img_rows = moved.shape[2]
    arranged = moved.reshape(2, count_col, count_blocks, row_share, img_rows)
    arranged = arranged.transpose(0, 4, 2, 1, 3).reshape(2, img_rows, count_blocks, row_block)
    owners = natural % count_row * count_vis + natural // count_row
    image, unused = partial_transform(arranged[0], arranged[1], owners, False)
    image = image * (1.0 / grid_len)
    extended = with_halo(image.astype(jnp.bfloat16), ((("vis", "row", "col"), 0),), 1).astype(
        image.dtype
    )
    hidden = first_layer(extended, conv_one, bias_one, img_rows).astype(jnp.bfloat16)
    hidden_ext = with_halo(hidden, ((("vis", "row", "col"), 1),), 1)
    return second_layer(hidden_ext, conv_two, bias_two, img_rows)


def grid_tables(length, count_row, count_col):
    image_len = length // 2
    place = np.arange(length)[:, None] - length // 2
    pixel = np.arange(image_len)[None, :] - image_len // 2
    angle = (place * pixel % length) * (2.0 * math.pi / length)
    cos, sin = np.cos(angle), np.sin(angle)
    padded = np.pad(np.stack([cos.T, sin.T]), ((0, 0), (HALO, TILE - HALO), (0, 0)))
    first = padded.reshape(2 * (image_len + TILE), count_col, length // count_col).transpose(1, 0, 2)
    rows = length // count_row
    second = np.stack([cos.reshape(count_row, rows, image_len), -sin.reshape(count_row, rows, image_len)], axis=1)
    second = second.reshape(count_row, 2 * rows, image_len) / length
    return first.astype(jnp.bfloat16), second.astype(jnp.bfloat16)


def pieces(source, target, sems):
    count = sems.shape[0]
    step = source.shape[0] // count
    parts = [pl.ds(i * step, step) for i in range(count)]
    return [pltpu.make_async_copy(source.at[part], target.at[part], sems.at[i]) for i, part in enumerate(parts)]


def share_kernel(cover_in, parts_in, first_all, second_all, out, cover, parts, first, second, cut, sems, sent):
    col, row = lax.axis_index("col"), lax.axis_index("row")
    get_cover = pltpu.make_async_copy(cover_in, cover, sems.at[0])
    get_parts = pieces(parts_in.at[0], parts.at[0], sems.at[pl.ds(1, 2)])
    get_first = pieces(first_all.at[col], first, sems.at[pl.ds(3, 3)])
    get_second = pieces(second_all.at[row], second, sems.at[pl.ds(6, 2)])
    for copy in (get_cover, *get_parts, *get_first, *get_second):
        copy.start()
    count_rows = parts.shape[2]
    get_cover.wait()
    for copy in get_parts:
        copy.wait()
    components = []
    for component in range(2):
        strips = []
        for i in range(cover.shape[1]):
            cells = []
            for j in range(cover.shape[2]):
                block = parts[0, component, i * BLK : (i + 1) * BLK, j * BLK : (j + 1) * BLK]
                level = jnp.full(block.shape, cover[0, i, j].astype(jnp.float32)).astype(jnp.bfloat16)
                cells.append(block * level)
            strips.append(jnp.concatenate(cells, axis=1))
        components.append(jnp.concatenate(strips, axis=0))
    grid = jnp.concatenate(components, axis=0)
    upper = lax.broadcasted_iota(jnp.int32, (TILE, LANES), 0) < TILE // 2
    devices = cut.shape[0]
    group = devices // sent.shape[0]
    tall = first.shape[0] // 2
    for copy in get_first:
        copy.wait()
    turned = lax.dot_general(first[...], grid, (((1,), (1,)), ((), ())), preferred_element_type=jnp.float32)
    mid_re = turned[:tall, :count_rows] - turned[tall:, count_rows:]
    mid_im = turned[tall:, :count_rows] + turned[:tall, count_rows:]
    mid = jnp.concatenate([mid_re, mid_im], axis=1).astype(jnp.bfloat16)
    for copy in get_second:
        copy.wait()
    image = jnp.dot(mid, second[...], preferred_element_type=jnp.float32)
    copies = []
    for device in range(devices):
        here, below = image[TILE * device : TILE * (device + 1)], image[TILE * (device + 1) : TILE * (device + 2)]
        middle = jnp.where(upper, below[:, :LANES], pltpu.roll(below[:, LANES:], TILE // 2, 0))
        window = jnp.concatenate([here[:, :LANES], middle, here[:, LANES:]], axis=0)
        cut[device] = window.astype(cut.dtype)
        if (device + 1) % group == 0:
            part = pl.ds(device + 1 - group, group)
            copies.append(pltpu.make_async_copy(cut.at[part], out.at[part], sent.at[device // group]))
            copies[-1].start()
    for copy in copies:
        copy.wait()


def own_place():
    place, count = 0, 1
    for axis in ALL:
        place = place * lax.axis_size(axis) + lax.axis_index(axis)
        count = count * lax.axis_size(axis)
    return place, count - 1


def four_times(values):
    return jnp.concatenate([values] * 4, axis=1)


def weights_kernel(one_in, bias_in, two_in, bias_two_in, weights_one, weights_two, bias_rows, one, bias, two, bias_two, sems):
    fetch = [
        pltpu.make_async_copy(one_in, one, sems.at[0]),
        pltpu.make_async_copy(bias_in, bias, sems.at[1]),
        pltpu.make_async_copy(two_in, two, sems.at[2]),
        pltpu.make_async_copy(bias_two_in, bias_two, sems.at[3]),
    ]
    for copy in fetch:
        copy.start()
    for copy in fetch:
        copy.wait()
    channels = one.shape[2]
    rows = TILE + 2
    per_tile = LANES // channels
    lanes = -(-rows * channels // LANES) * LANES
    image_row = lax.broadcasted_iota(jnp.int32, (16, lanes), 0)
    hidden_row = lax.broadcasted_iota(jnp.int32, (16, lanes), 1) // channels
    place, last = own_place()
    held = (hidden_row >= jnp.where(place == 0, 1, 0)) & (hidden_row < jnp.where(place == last, rows - 1, rows))
    high, low = [], []
    for tap in range(3):
        band = jnp.zeros((16, lanes), jnp.float32)
        for shift in range(3):
            line = jnp.concatenate([four_times(one[shift, tap : tap + 1])] * (lanes // LANES), axis=1)
            band = jnp.where(held & (image_row - hidden_row == shift), line, band)
        high.append(band.astype(jnp.bfloat16).astype(jnp.float32))
        low.append(band - high[-1])
    line = jnp.concatenate([four_times(bias[...])] * (lanes // LANES), axis=1)
    with_bias = high[0]
    for piece in range(3):
        rounded = line.astype(jnp.bfloat16).astype(jnp.float32)
        with_bias = jnp.where(held & (image_row == 12 + piece), rounded, with_bias)
        line = line - rounded
    stacked = jnp.concatenate([with_bias, *high[1:], *high, *low], axis=0)
    weights_one[...] = stacked.T[: weights_one.shape[0]].astype(jnp.bfloat16)
    row = lax.broadcasted_iota(jnp.int32, bias_rows.shape, 0) // TILE
    lane = lax.broadcasted_iota(jnp.int32, bias_rows.shape, 1)
    line = jnp.where(row == lane, four_times(bias_two[...]), 0.0)
    bias_rows[...] = jnp.broadcast_to(jnp.sum(line, axis=1, keepdims=True), bias_rows.shape)
    lines = [[four_times(two[shift, tap].astype(jnp.float32)) for shift in range(3)] for tap in range(3)]
    row = lax.broadcasted_iota(jnp.int32, (TILE, LANES), 0)
    lane = lax.broadcasted_iota(jnp.int32, (TILE, LANES), 1) // channels
    zero = jnp.zeros((TILE, LANES), jnp.float32)
    for tile in range(-(-3 * rows // per_tile)):
        taps = sorted({(tile * per_tile + g) // rows for g in range(per_tile)} & {0, 1, 2})
        masks = []
        for tap in taps:
            hidden_row = tile * per_tile + lane - tap * rows
            inside = (hidden_row >= 0) & (hidden_row < rows)
            masks += [(tap, shift, inside & (hidden_row - row == shift)) for shift in range(3)]
        width = min(LANES, weights_two.shape[1] - tile * LANES)
        for channel in range(0, channels, 2):
            pair = []
            for k in (channel, channel + 1):
                values = zero
                for tap, shift, mask in masks:
                    values = jnp.where(mask, lines[tap][shift][k : k + 1], values)
                pair.append(values)
            block = jnp.concatenate(pair, axis=0).astype(jnp.bfloat16)
            weights_two[TILE * channel : TILE * (channel + 2), tile * LANES : tile * LANES + width] = block[:, :width]


def shifted(values, width):
    lane = lax.broadcasted_iota(jnp.int32, values.shape, 1)
    zero = jnp.zeros_like(values)
    before = jnp.where(lane == 0, zero, pltpu.roll(values, 1, 1))
    after = jnp.where(lane == width - 1, zero, pltpu.roll(values, width - 1, 1))
    return before, values, after


def layers_kernel(shares, weights_one, weights_two, bias_rows, out, staged, sems):
    total = shares[0].astype(jnp.float32)
    for device in range(1, shares.shape[0]):
        total = total + shares[device].astype(jnp.float32)
    width = out.shape[2]
    middle = total[TILE : 2 * TILE]
    upper = lax.broadcasted_iota(jnp.int32, (TILE, width), 0) < TILE // 2
    lower_rows = jnp.concatenate([middle, pltpu.roll(middle, TILE // 2, 0)], axis=1)
    image = jnp.concatenate(
        [jnp.concatenate([total[:TILE], total[2 * TILE :]], axis=1), jnp.where(upper, lower_rows, 0.0)], axis=0
    )
    columns = jnp.concatenate(shifted(image, width), axis=0)
    high = columns.astype(jnp.bfloat16).astype(jnp.float32)
    low = columns - high
    row = lax.broadcasted_iota(jnp.int32, (48, width), 0)
    with_ones = jnp.where((row >= 12) & (row < 15), 1.0, high)
    stacked = jnp.concatenate([with_ones, low, high], axis=0).astype(jnp.bfloat16)
    hidden = jnp.dot(weights_one[...], stacked, preferred_element_type=jnp.float32)
    hidden = jnp.maximum(hidden, 0.0).astype(jnp.bfloat16)
    stacked = jnp.concatenate(shifted(hidden, width), axis=0)
    half = out.shape[0] // 2
    copies = []
    for part in range(2):
        rows = pl.ds(part * half * TILE, half * TILE)
        features = jnp.dot(weights_two[rows], stacked, preferred_element_type=jnp.float32)
        features = features + jnp.concatenate([bias_rows[rows]] * (width // LANES), axis=1)
        channels_of = pl.ds(part * half, half)
        staged[channels_of] = features.reshape(half, TILE, width).astype(out.dtype)
        copies.append(pltpu.make_async_copy(staged.at[channels_of], out.at[channels_of], sems.at[part]))
        copies[-1].start()
    for copy in copies:
        copy.wait()


def in_hbm(*arrays):
    return [pltpu.with_memory_space_constraint(array, pltpu.HBM) for array in arrays]


def direct(partials, coverage, conv_one, bias_one, conv_two, bias_two):
    count_row, count_col = lax.axis_size("row"), lax.axis_size("col")
    devices = lax.axis_size("vis") * count_row * count_col
    length = partials.shape[3] * count_col
    image_len = length // 2
    channels = conv_two.shape[2]
    first, second = grid_tables(length, count_row, count_col)
    vmem, hbm = pl.BlockSpec(memory_space=pltpu.VMEM), pl.BlockSpec(memory_space=pltpu.HBM)
    limit = pltpu.CompilerParams(vmem_limit_bytes=16 * 2**20)
    share = (devices, 2 * (TILE + 2 * HALO), LANES)
    shares = pl.pallas_call(
        share_kernel,
        out_shape=jax.ShapeDtypeStruct(share, jnp.bfloat16),
        in_specs=[hbm] * 4,
        out_specs=hbm,
        scratch_shapes=[
            pltpu.SMEM(coverage.shape, jnp.int32),
            pltpu.VMEM(partials.shape, jnp.bfloat16),
            pltpu.VMEM(first.shape[1:], jnp.bfloat16),
            pltpu.VMEM(second.shape[1:], jnp.bfloat16),
            pltpu.VMEM(share, jnp.bfloat16),
            pltpu.SemaphoreType.DMA((8,)),
            pltpu.SemaphoreType.DMA((math.gcd(devices, 4),)),
        ],
        compiler_params=limit,
        name="shares",
    )(*in_hbm(coverage, partials, jnp.asarray(first), jnp.asarray(second)))
    arrived = lax.all_to_all(shares, ALL, split_axis=0, concat_axis=0, tiled=True)
    rows = TILE + 2
    weights = pl.pallas_call(
        weights_kernel,
        out_shape=[
            jax.ShapeDtypeStruct((rows * channels, 3 * 48), jnp.bfloat16),
            jax.ShapeDtypeStruct((TILE * channels, 3 * rows * channels), jnp.bfloat16),
            jax.ShapeDtypeStruct((TILE * channels, LANES), jnp.float32),
        ],
        in_specs=[hbm] * 4,
        out_specs=[vmem] * 3,
        scratch_shapes=[
            pltpu.VMEM((3, 3, channels), jnp.float32),
            pltpu.VMEM((1, channels), jnp.float32),
            pltpu.VMEM(conv_two.shape, jnp.bfloat16),
            pltpu.VMEM((1, channels), jnp.float32),
            pltpu.SemaphoreType.DMA((4,)),
        ],
        compiler_params=limit,
        name="weights",
    )(*in_hbm(conv_one.transpose(1, 2, 0), bias_one[None], conv_two, bias_two[None]))
    return pl.pallas_call(
        layers_kernel,
        out_shape=jax.ShapeDtypeStruct((channels, TILE, image_len), jnp.bfloat16),
        in_specs=[vmem] * 4,
        out_specs=hbm,
        scratch_shapes=[
            pltpu.VMEM((channels, TILE, image_len), jnp.bfloat16),
            pltpu.SemaphoreType.DMA((2,)),
        ],
        compiler_params=limit,
        name="layers",
    )(arrived, *weights)


def local(partials, coverage, conv_one, bias_one, conv_two, bias_two):
    count_col = lax.axis_size("col")
    devices = lax.axis_size("vis") * lax.axis_size("row") * count_col
    image_len = partials.shape[3] * count_col // 2
    sent = devices * (TILE + 2 * HALO) * image_len * 2
    fits = image_len == devices * TILE and conv_two.shape[2] * 4 == LANES and image_len == 2 * LANES and sent <= DIRECT_BYTES
    plan = direct if fits else staged
    return plan(partials, coverage, conv_one, bias_one, conv_two, bias_two)


def solution(mesh):
    placed = (P("vis", None, "row", "col"), P("vis", "row", "col"), P(), P(), P(), P())
    return jax.shard_map(
        local,
        mesh=mesh,
        in_specs=placed,
        out_specs=P(None, ALL, None),
        check_vma=False,
    )
```

```python
import math

import jax
import jax.numpy as jnp
import numpy as np
from jax import lax
from jax.experimental import pallas as pl
from jax.experimental.pallas import tpu as pltpu
from jax.sharding import PartitionSpec as P

BLK = 128
ALL = ("vis", "row", "col")
DIRECT_BYTES = 4 * 2**20
HALO = 2
TILE = 8
LANES = 128


def with_halo(cells, sides, width):
    for axis, dim in sides:
        count = lax.axis_size(axis)
        ends = count - 1
        head = lax.slice_in_dim(cells, 0, width, axis=dim)
        tail = lax.slice_in_dim(cells, cells.shape[dim] - width, cells.shape[dim], axis=dim)
        cells = jnp.concatenate(
            [
                lax.ppermute(tail, axis, [(i, (i + 1) % count) for i in range(ends)]),
                cells,
                lax.ppermute(head, axis, [((i + 1) % count, i) for i in range(ends)]),
            ],
            axis=dim,
        )
    return cells


def phase_table(numer, denom):
    angle = numer.astype(jnp.float32) * (2.0 * math.pi / denom)
    return (jnp.cos(angle), jnp.sin(angle))


def partial_transform(real_part, imag_part, block_of, keep_imag):
    batch = real_part.shape[0]
    count_blocks = real_part.shape[1]
    block_len = real_part.shape[2]
    length = count_blocks * block_len
    highest = lax.Precision.HIGHEST
    outer = jnp.arange(count_blocks, dtype=jnp.int32)
    inner = jnp.arange(block_len, dtype=jnp.int32)
    cos_one, sin_one = phase_table(block_of[:, None] * outer[None, :] % count_blocks, count_blocks)
    mid_re = jnp.einsum("lpt,px->lxt", real_part, cos_one, precision=highest) - jnp.einsum(
        "lpt,px->lxt", imag_part, sin_one, precision=highest
    )
    mid_im = jnp.einsum("lpt,px->lxt", real_part, sin_one, precision=highest) + jnp.einsum(
        "lpt,px->lxt", imag_part, cos_one, precision=highest
    )
    cos_two, sin_two = phase_table(outer[:, None] * inner[None, :] % length, length)
    parity = (1 - 2 * (outer % 2)).astype(jnp.float32)[:, None]
    cos_two = cos_two * parity
    sin_two = sin_two * parity
    turn_re = mid_re * cos_two - mid_im * sin_two
    turn_im = mid_re * sin_two + mid_im * cos_two
    kept = jnp.arange(block_len // 2, dtype=jnp.int32)
    picked = (kept + 3 * block_len // 4) % block_len
    cos_three, sin_three = phase_table(inner[:, None] * picked[None, :] % block_len, block_len)
    out_re = jnp.einsum("lxt,tj->ljx", turn_re, cos_three, precision=highest) - jnp.einsum(
        "lxt,tj->ljx", turn_im, sin_three, precision=highest
    )
    out_re = out_re.reshape(batch, length // 2)
    if keep_imag:
        out_im = jnp.einsum("lxt,tj->ljx", turn_re, sin_three, precision=highest) + jnp.einsum(
            "lxt,tj->ljx", turn_im, cos_three, precision=highest
        )
        return (out_re, out_im.reshape(batch, length // 2))
    return (out_re, out_re)


def first_layer(extended, conv_one, bias_one, count_rows):
    width = extended.shape[1]
    padded = jnp.pad(extended, ((0, 0), (1, 1)))
    summed = (
        jnp.zeros((conv_one.shape[0], count_rows, width), jnp.float32) + bias_one[:, None, None]
    )
    for shift_b in range(3):
        for shift_a in range(3):
            summed = (
                summed
                + conv_one[:, shift_b, shift_a][:, None, None]
                * padded[None, shift_b : shift_b + count_rows, shift_a : shift_a + width]
            )
    return jnp.maximum(summed, 0.0)


def second_layer(hidden_ext, conv_two, bias_two, count_rows):
    width = hidden_ext.shape[2]
    padded = jnp.pad(hidden_ext, ((0, 0), (0, 0), (1, 1)))
    summed = jnp.zeros((conv_two.shape[2], count_rows, width), jnp.float32)
    for shift_b in range(3):
        for shift_a in range(3):
            summed = summed + jnp.einsum(
                "kj,jba->kba",
                conv_two[shift_b, shift_a],
                padded[:, shift_b : shift_b + count_rows, shift_a : shift_a + width],
                preferred_element_type=jnp.float32,
            )
    return (summed + bias_two[:, None, None]).astype(jnp.bfloat16)


def staged(partials, coverage, conv_one, bias_one, conv_two, bias_two):
    count_vis = lax.axis_size("vis")
    count_row = lax.axis_size("row")
    count_col = lax.axis_size("col")
    grid_len = partials.shape[3] * count_col
    cover = coverage[0]
    block_rows = cover.shape[0]
    block_cols = cover.shape[1]
    spread = jnp.broadcast_to(cover[:, None, :, None], (block_rows, BLK, block_cols, BLK))
    spread = spread.reshape(block_rows * BLK, block_cols * BLK)
    count_blocks = count_vis * count_row
    row_block = grid_len // count_blocks
    row_share = row_block // count_col
    masked = partials[0] * spread.astype(jnp.bfloat16)[None]
    reduced = lax.psum_scatter(
        masked.astype(jnp.float32).astype(jnp.bfloat16), "vis", scatter_dimension=1, tiled=True
    ).astype(jnp.float32)
    grid_rows = lax.all_to_all(
        reduced.astype(jnp.bfloat16), "col", split_axis=1, concat_axis=2, tiled=True
    ).astype(reduced.dtype)
    natural = jnp.arange(count_blocks, dtype=jnp.int32)
    shaped = grid_rows.reshape(2, row_share, count_blocks, row_block)
    first_re, first_im = partial_transform(shaped[0], shaped[1], natural, True)
    stacked = jnp.stack([first_re, first_im])
    moved = lax.all_to_all(
        lax.all_to_all(
            stacked.astype(jnp.bfloat16), ("vis", "row"), split_axis=2, concat_axis=1, tiled=True
        ),
        "col",
        split_axis=2,
        concat_axis=1,
        tiled=True,
    ).astype(stacked.dtype)
    img_rows = moved.shape[2]
    arranged = moved.reshape(2, count_col, count_blocks, row_share, img_rows)
    arranged = arranged.transpose(0, 4, 2, 1, 3).reshape(2, img_rows, count_blocks, row_block)
    owners = natural % count_row * count_vis + natural // count_row
    image, unused = partial_transform(arranged[0], arranged[1], owners, False)
    image = image * (1.0 / grid_len)
    extended = with_halo(image.astype(jnp.bfloat16), ((("vis", "row", "col"), 0),), 1).astype(
        image.dtype
    )
    hidden = first_layer(extended, conv_one, bias_one, img_rows).astype(jnp.bfloat16)
    hidden_ext = with_halo(hidden, ((("vis", "row", "col"), 1),), 1)
    return second_layer(hidden_ext, conv_two, bias_two, img_rows)


def grid_tables(length, count_row, count_col):
    image_len = length // 2
    place = np.arange(length)[:, None] - length // 2
    pixel = np.arange(image_len)[None, :] - image_len // 2
    angle = (place * pixel % length) * (2.0 * math.pi / length)
    cos, sin = np.cos(angle), np.sin(angle)
    padded = np.pad(np.stack([cos.T, sin.T]), ((0, 0), (HALO, TILE - HALO), (0, 0)))
    first = padded.reshape(2 * (image_len + TILE), count_col, length // count_col).transpose(1, 0, 2)
    rows = length // count_row
    second = np.stack([cos.reshape(count_row, rows, image_len), -sin.reshape(count_row, rows, image_len)], axis=1)
    second = second.reshape(count_row, 2 * rows, image_len) / length
    return first.astype(jnp.bfloat16), second.astype(jnp.bfloat16)


def send_order():
    vis, row, col = (lax.axis_size(axis) for axis in ALL)
    places = np.arange(vis * row * col).reshape(vis, row, col)
    return places[:, ::-1].reshape(-1).tolist()


def send_slots():
    order = send_order()
    return [order.index(device) for device in range(len(order))]


def share_kernel(cover_in, parts_in, first_all, second_all, out, cover, parts, first, second, sems):
    col, row = lax.axis_index("col"), lax.axis_index("row")
    get_cover = pltpu.make_async_copy(cover_in, cover, sems.at[0])
    get_parts = pltpu.make_async_copy(parts_in, parts, sems.at[1])
    get_first = pltpu.make_async_copy(first_all.at[col], first, sems.at[2])
    get_second = pltpu.make_async_copy(second_all.at[row], second, sems.at[3])
    for copy in (get_cover, get_parts, get_first, get_second):
        copy.start()
    count_rows = parts.shape[2]
    get_cover.wait()
    get_parts.wait()
    components = []
    for component in range(2):
        strips = []
        for i in range(cover.shape[1]):
            cells = []
            for j in range(cover.shape[2]):
                block = parts[0, component, i * BLK : (i + 1) * BLK, j * BLK : (j + 1) * BLK]
                level = jnp.full(block.shape, cover[0, i, j].astype(jnp.float32)).astype(jnp.bfloat16)
                cells.append(block * level)
            strips.append(jnp.concatenate(cells, axis=1))
        components.append(jnp.concatenate(strips, axis=0))
    grid = jnp.concatenate(components, axis=0)
    upper = lax.broadcasted_iota(jnp.int32, (TILE, LANES), 0) < TILE // 2
    devices = out.shape[0]
    tall = first.shape[0] // 2
    get_first.wait()
    turned = lax.dot_general(first[...], grid, (((1,), (1,)), ((), ())), preferred_element_type=jnp.float32)
    mid_re = turned[:tall, :count_rows] - turned[tall:, count_rows:]
    mid_im = turned[tall:, :count_rows] + turned[:tall, count_rows:]
    mid = jnp.concatenate([mid_re, mid_im], axis=1).astype(jnp.bfloat16)
    get_second.wait()
    image = jnp.dot(mid, second[...], preferred_element_type=jnp.float32)
    slots = send_slots()
    for device in range(devices):
        here, below = image[TILE * device : TILE * (device + 1)], image[TILE * (device + 1) : TILE * (device + 2)]
        middle = jnp.where(upper, below[:, :LANES], pltpu.roll(below[:, LANES:], TILE // 2, 0))
        window = jnp.concatenate([here[:, :LANES], middle, here[:, LANES:]], axis=0)
        out[slots[device]] = window.astype(out.dtype)


def own_place():
    place, count = 0, 1
    for axis in ALL:
        place = place * lax.axis_size(axis) + lax.axis_index(axis)
        count = count * lax.axis_size(axis)
    return place, count - 1


def four_times(values):
    return jnp.concatenate([values] * 4, axis=1)


def weights_kernel(one_in, bias_in, two_in, bias_two_in, weights_one, weights_two, bias_rows, one, bias, two, bias_two, sems):
    fetch = [
        pltpu.make_async_copy(one_in, one, sems.at[0]),
        pltpu.make_async_copy(bias_in, bias, sems.at[1]),
        pltpu.make_async_copy(two_in, two, sems.at[2]),
        pltpu.make_async_copy(bias_two_in, bias_two, sems.at[3]),
    ]
    for copy in fetch:
        copy.start()
    for copy in fetch:
        copy.wait()
    channels = one.shape[2]
    rows = TILE + 2
    per_tile = LANES // channels
    lanes = -(-rows * channels // LANES) * LANES
    image_row = lax.broadcasted_iota(jnp.int32, (16, lanes), 0)
    hidden_row = lax.broadcasted_iota(jnp.int32, (16, lanes), 1) // channels
    place, last = own_place()
    held = (hidden_row >= jnp.where(place == 0, 1, 0)) & (hidden_row < jnp.where(place == last, rows - 1, rows))
    high, low = [], []
    for tap in range(3):
        band = jnp.zeros((16, lanes), jnp.float32)
        for shift in range(3):
            line = jnp.concatenate([four_times(one[shift, tap : tap + 1])] * (lanes // LANES), axis=1)
            band = jnp.where(held & (image_row - hidden_row == shift), line, band)
        high.append(band.astype(jnp.bfloat16).astype(jnp.float32))
        low.append(band - high[-1])
    line = jnp.concatenate([four_times(bias[...])] * (lanes // LANES), axis=1)
    with_bias = high[0]
    for piece in range(3):
        rounded = line.astype(jnp.bfloat16).astype(jnp.float32)
        with_bias = jnp.where(held & (image_row == 12 + piece), rounded, with_bias)
        line = line - rounded
    stacked = jnp.concatenate([with_bias, *high[1:], *high, *low], axis=0)
    weights_one[...] = stacked.T[: weights_one.shape[0]].astype(jnp.bfloat16)
    row = lax.broadcasted_iota(jnp.int32, bias_rows.shape, 0) // TILE
    lane = lax.broadcasted_iota(jnp.int32, bias_rows.shape, 1)
    line = jnp.where(row == lane, four_times(bias_two[...]), 0.0)
    bias_rows[...] = jnp.broadcast_to(jnp.sum(line, axis=1, keepdims=True), bias_rows.shape)
    lines = [[four_times(two[shift, tap].astype(jnp.float32)) for shift in range(3)] for tap in range(3)]
    row = lax.broadcasted_iota(jnp.int32, (TILE, LANES), 0)
    lane = lax.broadcasted_iota(jnp.int32, (TILE, LANES), 1) // channels
    zero = jnp.zeros((TILE, LANES), jnp.float32)
    for tile in range(-(-3 * rows // per_tile)):
        taps = sorted({(tile * per_tile + g) // rows for g in range(per_tile)} & {0, 1, 2})
        masks = []
        for tap in taps:
            hidden_row = tile * per_tile + lane - tap * rows
            inside = (hidden_row >= 0) & (hidden_row < rows)
            masks += [(tap, shift, inside & (hidden_row - row == shift)) for shift in range(3)]
        width = min(LANES, weights_two.shape[1] - tile * LANES)
        for channel in range(0, channels, 2):
            pair = []
            for k in (channel, channel + 1):
                values = zero
                for tap, shift, mask in masks:
                    values = jnp.where(mask, lines[tap][shift][k : k + 1], values)
                pair.append(values)
            block = jnp.concatenate(pair, axis=0).astype(jnp.bfloat16)
            weights_two[TILE * channel : TILE * (channel + 2), tile * LANES : tile * LANES + width] = block[:, :width]


def shifted(values, width):
    lane = lax.broadcasted_iota(jnp.int32, values.shape, 1)
    zero = jnp.zeros_like(values)
    before = jnp.where(lane == 0, zero, pltpu.roll(values, 1, 1))
    after = jnp.where(lane == width - 1, zero, pltpu.roll(values, width - 1, 1))
    return before, values, after


def layers_kernel(shares, weights_one, weights_two, bias_rows, out, staged, sems):
    total = shares[0].astype(jnp.float32)
    for device in range(1, shares.shape[0]):
        total = total + shares[device].astype(jnp.float32)
    width = out.shape[2]
    middle = total[TILE : 2 * TILE]
    upper = lax.broadcasted_iota(jnp.int32, (TILE, width), 0) < TILE // 2
    lower_rows = jnp.concatenate([middle, pltpu.roll(middle, TILE // 2, 0)], axis=1)
    image = jnp.concatenate(
        [jnp.concatenate([total[:TILE], total[2 * TILE :]], axis=1), jnp.where(upper, lower_rows, 0.0)], axis=0
    )
    columns = jnp.concatenate(shifted(image, width), axis=0)
    high = columns.astype(jnp.bfloat16).astype(jnp.float32)
    low = columns - high
    row = lax.broadcasted_iota(jnp.int32, (48, width), 0)
    with_ones = jnp.where((row >= 12) & (row < 15), 1.0, high)
    stacked = jnp.concatenate([with_ones, low, high], axis=0).astype(jnp.bfloat16)
    hidden = jnp.dot(weights_one[...], stacked, preferred_element_type=jnp.float32)
    hidden = jnp.maximum(hidden, 0.0).astype(jnp.bfloat16)
    stacked = jnp.concatenate(shifted(hidden, width), axis=0)
    half = out.shape[0] // 2
    copies = []
    for part in range(2):
        rows = pl.ds(part * half * TILE, half * TILE)
        features = jnp.dot(weights_two[rows], stacked, preferred_element_type=jnp.float32)
        features = features + jnp.concatenate([bias_rows[rows]] * (width // LANES), axis=1)
        channels_of = pl.ds(part * half, half)
        staged[channels_of] = features.reshape(half, TILE, width).astype(out.dtype)
        copies.append(pltpu.make_async_copy(staged.at[channels_of], out.at[channels_of], sems.at[part]))
        copies[-1].start()
    for copy in copies:
        copy.wait()


def in_hbm(*arrays):
    return [pltpu.with_memory_space_constraint(array, pltpu.HBM) for array in arrays]


def direct(partials, coverage, conv_one, bias_one, conv_two, bias_two):
    count_row, count_col = lax.axis_size("row"), lax.axis_size("col")
    devices = lax.axis_size("vis") * count_row * count_col
    length = partials.shape[3] * count_col
    image_len = length // 2
    channels = conv_two.shape[2]
    first, second = grid_tables(length, count_row, count_col)
    vmem, hbm = pl.BlockSpec(memory_space=pltpu.VMEM), pl.BlockSpec(memory_space=pltpu.HBM)
    limit = pltpu.CompilerParams(vmem_limit_bytes=16 * 2**20)
    share = (devices, 2 * (TILE + 2 * HALO), LANES)
    shares = pl.pallas_call(
        share_kernel,
        out_shape=jax.ShapeDtypeStruct(share, jnp.bfloat16),
        in_specs=[hbm] * 4,
        out_specs=vmem,
        scratch_shapes=[
            pltpu.SMEM(coverage.shape, jnp.int32),
            pltpu.VMEM(partials.shape, jnp.bfloat16),
            pltpu.VMEM(first.shape[1:], jnp.bfloat16),
            pltpu.VMEM(second.shape[1:], jnp.bfloat16),
            pltpu.SemaphoreType.DMA((4,)),
        ],
        compiler_params=limit,
        name="shares",
    )(*in_hbm(coverage, partials, jnp.asarray(first), jnp.asarray(second)))
    arrived = lax.all_to_all(
        shares, ALL, split_axis=0, concat_axis=0, tiled=True, axis_index_groups=[send_order()]
    )
    rows = TILE + 2
    weights = pl.pallas_call(
        weights_kernel,
        out_shape=[
            jax.ShapeDtypeStruct((rows * channels, 3 * 48), jnp.bfloat16),
            jax.ShapeDtypeStruct((TILE * channels, 3 * rows * channels), jnp.bfloat16),
            jax.ShapeDtypeStruct((TILE * channels, LANES), jnp.float32),
        ],
        in_specs=[hbm] * 4,
        out_specs=[vmem] * 3,
        scratch_shapes=[
            pltpu.VMEM((3, 3, channels), jnp.float32),
            pltpu.VMEM((1, channels), jnp.float32),
            pltpu.VMEM(conv_two.shape, jnp.bfloat16),
            pltpu.VMEM((1, channels), jnp.float32),
            pltpu.SemaphoreType.DMA((4,)),
        ],
        compiler_params=limit,
        name="weights",
    )(*in_hbm(conv_one.transpose(1, 2, 0), bias_one[None], conv_two, bias_two[None]))
    return pl.pallas_call(
        layers_kernel,
        out_shape=jax.ShapeDtypeStruct((channels, TILE, image_len), jnp.bfloat16),
        in_specs=[vmem] * 4,
        out_specs=hbm,
        scratch_shapes=[
            pltpu.VMEM((channels, TILE, image_len), jnp.bfloat16),
            pltpu.SemaphoreType.DMA((2,)),
        ],
        compiler_params=limit,
        name="layers",
    )(arrived, *weights)


def local(partials, coverage, conv_one, bias_one, conv_two, bias_two):
    count_col = lax.axis_size("col")
    devices = lax.axis_size("vis") * lax.axis_size("row") * count_col
    image_len = partials.shape[3] * count_col // 2
    sent = devices * (TILE + 2 * HALO) * image_len * 2
    fits = image_len == devices * TILE and conv_two.shape[2] * 4 == LANES and image_len == 2 * LANES and sent <= DIRECT_BYTES
    plan = direct if fits else staged
    return plan(partials, coverage, conv_one, bias_one, conv_two, bias_two)


def solution(mesh):
    placed = (P("vis", None, "row", "col"), P("vis", "row", "col"), P(), P(), P(), P())
    return jax.shard_map(
        local,
        mesh=mesh,
        in_specs=placed,
        out_specs=P(None, ALL, None),
        check_vma=False,
    )
```

```python
import math

import jax
import jax.numpy as jnp
import numpy as np
from jax import lax
from jax.experimental import pallas as pl
from jax.experimental.pallas import tpu as pltpu
from jax.sharding import PartitionSpec as P

BLK = 128
ALL = ("vis", "row", "col")
DIRECT_BYTES = 4 * 2**20
HALO = 2
TILE = 8
LANES = 128


def with_halo(cells, sides, width):
    for axis, dim in sides:
        count = lax.axis_size(axis)
        ends = count - 1
        head = lax.slice_in_dim(cells, 0, width, axis=dim)
        tail = lax.slice_in_dim(cells, cells.shape[dim] - width, cells.shape[dim], axis=dim)
        cells = jnp.concatenate(
            [
                lax.ppermute(tail, axis, [(i, (i + 1) % count) for i in range(ends)]),
                cells,
                lax.ppermute(head, axis, [((i + 1) % count, i) for i in range(ends)]),
            ],
            axis=dim,
        )
    return cells


def phase_table(numer, denom):
    angle = numer.astype(jnp.float32) * (2.0 * math.pi / denom)
    return (jnp.cos(angle), jnp.sin(angle))


def partial_transform(real_part, imag_part, block_of, keep_imag):
    batch = real_part.shape[0]
    count_blocks = real_part.shape[1]
    block_len = real_part.shape[2]
    length = count_blocks * block_len
    highest = lax.Precision.HIGHEST
    outer = jnp.arange(count_blocks, dtype=jnp.int32)
    inner = jnp.arange(block_len, dtype=jnp.int32)
    cos_one, sin_one = phase_table(block_of[:, None] * outer[None, :] % count_blocks, count_blocks)
    mid_re = jnp.einsum("lpt,px->lxt", real_part, cos_one, precision=highest) - jnp.einsum(
        "lpt,px->lxt", imag_part, sin_one, precision=highest
    )
    mid_im = jnp.einsum("lpt,px->lxt", real_part, sin_one, precision=highest) + jnp.einsum(
        "lpt,px->lxt", imag_part, cos_one, precision=highest
    )
    cos_two, sin_two = phase_table(outer[:, None] * inner[None, :] % length, length)
    parity = (1 - 2 * (outer % 2)).astype(jnp.float32)[:, None]
    cos_two = cos_two * parity
    sin_two = sin_two * parity
    turn_re = mid_re * cos_two - mid_im * sin_two
    turn_im = mid_re * sin_two + mid_im * cos_two
    kept = jnp.arange(block_len // 2, dtype=jnp.int32)
    picked = (kept + 3 * block_len // 4) % block_len
    cos_three, sin_three = phase_table(inner[:, None] * picked[None, :] % block_len, block_len)
    out_re = jnp.einsum("lxt,tj->ljx", turn_re, cos_three, precision=highest) - jnp.einsum(
        "lxt,tj->ljx", turn_im, sin_three, precision=highest
    )
    out_re = out_re.reshape(batch, length // 2)
    if keep_imag:
        out_im = jnp.einsum("lxt,tj->ljx", turn_re, sin_three, precision=highest) + jnp.einsum(
            "lxt,tj->ljx", turn_im, cos_three, precision=highest
        )
        return (out_re, out_im.reshape(batch, length // 2))
    return (out_re, out_re)


def first_layer(extended, conv_one, bias_one, count_rows):
    width = extended.shape[1]
    padded = jnp.pad(extended, ((0, 0), (1, 1)))
    summed = (
        jnp.zeros((conv_one.shape[0], count_rows, width), jnp.float32) + bias_one[:, None, None]
    )
    for shift_b in range(3):
        for shift_a in range(3):
            summed = (
                summed
                + conv_one[:, shift_b, shift_a][:, None, None]
                * padded[None, shift_b : shift_b + count_rows, shift_a : shift_a + width]
            )
    return jnp.maximum(summed, 0.0)


def second_layer(hidden_ext, conv_two, bias_two, count_rows):
    width = hidden_ext.shape[2]
    padded = jnp.pad(hidden_ext, ((0, 0), (0, 0), (1, 1)))
    summed = jnp.zeros((conv_two.shape[2], count_rows, width), jnp.float32)
    for shift_b in range(3):
        for shift_a in range(3):
            summed = summed + jnp.einsum(
                "kj,jba->kba",
                conv_two[shift_b, shift_a],
                padded[:, shift_b : shift_b + count_rows, shift_a : shift_a + width],
                preferred_element_type=jnp.float32,
            )
    return (summed + bias_two[:, None, None]).astype(jnp.bfloat16)


def staged(partials, coverage, conv_one, bias_one, conv_two, bias_two):
    count_vis = lax.axis_size("vis")
    count_row = lax.axis_size("row")
    count_col = lax.axis_size("col")
    grid_len = partials.shape[3] * count_col
    cover = coverage[0]
    block_rows = cover.shape[0]
    block_cols = cover.shape[1]
    spread = jnp.broadcast_to(cover[:, None, :, None], (block_rows, BLK, block_cols, BLK))
    spread = spread.reshape(block_rows * BLK, block_cols * BLK)
    count_blocks = count_vis * count_row
    row_block = grid_len // count_blocks
    row_share = row_block // count_col
    masked = partials[0] * spread.astype(jnp.bfloat16)[None]
    reduced = lax.psum_scatter(
        masked.astype(jnp.float32).astype(jnp.bfloat16), "vis", scatter_dimension=1, tiled=True
    ).astype(jnp.float32)
    grid_rows = lax.all_to_all(
        reduced.astype(jnp.bfloat16), "col", split_axis=1, concat_axis=2, tiled=True
    ).astype(reduced.dtype)
    natural = jnp.arange(count_blocks, dtype=jnp.int32)
    shaped = grid_rows.reshape(2, row_share, count_blocks, row_block)
    first_re, first_im = partial_transform(shaped[0], shaped[1], natural, True)
    stacked = jnp.stack([first_re, first_im])
    moved = lax.all_to_all(
        lax.all_to_all(
            stacked.astype(jnp.bfloat16), ("vis", "row"), split_axis=2, concat_axis=1, tiled=True
        ),
        "col",
        split_axis=2,
        concat_axis=1,
        tiled=True,
    ).astype(stacked.dtype)
    img_rows = moved.shape[2]
    arranged = moved.reshape(2, count_col, count_blocks, row_share, img_rows)
    arranged = arranged.transpose(0, 4, 2, 1, 3).reshape(2, img_rows, count_blocks, row_block)
    owners = natural % count_row * count_vis + natural // count_row
    image, unused = partial_transform(arranged[0], arranged[1], owners, False)
    image = image * (1.0 / grid_len)
    extended = with_halo(image.astype(jnp.bfloat16), ((("vis", "row", "col"), 0),), 1).astype(
        image.dtype
    )
    hidden = first_layer(extended, conv_one, bias_one, img_rows).astype(jnp.bfloat16)
    hidden_ext = with_halo(hidden, ((("vis", "row", "col"), 1),), 1)
    return second_layer(hidden_ext, conv_two, bias_two, img_rows)


def grid_tables(length, count_row, count_col):
    image_len = length // 2
    place = np.arange(length)[:, None] - length // 2
    pixel = np.arange(image_len)[None, :] - image_len // 2
    angle = (place * pixel % length) * (2.0 * math.pi / length)
    cos, sin = np.cos(angle), np.sin(angle)
    padded = np.pad(np.stack([cos.T, sin.T]), ((0, 0), (HALO, TILE - HALO), (0, 0)))
    first = padded.reshape(2 * (image_len + TILE), count_col, length // count_col).transpose(1, 0, 2)
    rows = length // count_row
    second = np.stack([cos.reshape(count_row, rows, image_len), -sin.reshape(count_row, rows, image_len)], axis=1)
    second = second.reshape(2 * length, image_len) / length
    return first.astype(jnp.bfloat16), second.astype(jnp.bfloat16)


def share_kernel(cover_in, parts_in, first_all, out, cover, parts, first, sems):
    get_cover = pltpu.make_async_copy(cover_in, cover, sems.at[0])
    get_parts = pltpu.make_async_copy(parts_in, parts, sems.at[1])
    get_first = pltpu.make_async_copy(first_all.at[lax.axis_index("col")], first, sems.at[2])
    for copy in (get_cover, get_parts, get_first):
        copy.start()
    count_rows = parts.shape[2]
    get_cover.wait()
    get_parts.wait()
    components = []
    for component in range(2):
        strips = []
        for i in range(cover.shape[1]):
            cells = []
            for j in range(cover.shape[2]):
                block = parts[0, component, i * BLK : (i + 1) * BLK, j * BLK : (j + 1) * BLK]
                level = jnp.full(block.shape, cover[0, i, j].astype(jnp.float32)).astype(jnp.bfloat16)
                cells.append(block * level)
            strips.append(jnp.concatenate(cells, axis=1))
        components.append(jnp.concatenate(strips, axis=0))
    grid = jnp.concatenate(components, axis=0)
    upper = lax.broadcasted_iota(jnp.int32, (TILE, LANES), 0) < TILE // 2
    devices = out.shape[0]
    tall = first.shape[0] // 2
    get_first.wait()
    turned = lax.dot_general(first[...], grid, (((1,), (1,)), ((), ())), preferred_element_type=jnp.float32)
    mid_re = turned[:tall, :count_rows] - turned[tall:, count_rows:]
    mid_im = turned[tall:, :count_rows] + turned[:tall, count_rows:]
    for device in range(devices):
        here = slice(TILE * device, TILE * (device + 1))
        below = slice(TILE * (device + 1), TILE * (device + 2))
        middle = jnp.where(upper, mid_re[below], pltpu.roll(mid_im[below], TILE // 2, 0))
        out[device] = jnp.concatenate([mid_re[here], middle, mid_im[here]], axis=0).astype(out.dtype)


def own_place():
    place, count = 0, 1
    for axis in ALL:
        place = place * lax.axis_size(axis) + lax.axis_index(axis)
        count = count * lax.axis_size(axis)
    return place, count - 1


def four_times(values):
    return jnp.concatenate([values] * 4, axis=1)


def weights_kernel(
    one_in, bias_in, two_in, bias_two_in, table_in, weights_one, weights_two, bias_rows, table, one, bias, two, bias_two, sems
):
    fetch = [
        pltpu.make_async_copy(one_in, one, sems.at[0]),
        pltpu.make_async_copy(bias_in, bias, sems.at[1]),
        pltpu.make_async_copy(two_in, two, sems.at[2]),
        pltpu.make_async_copy(bias_two_in, bias_two, sems.at[3]),
    ]
    get_table = pltpu.make_async_copy(table_in, table, sems.at[4])
    for copy in (*fetch, get_table):
        copy.start()
    for copy in fetch:
        copy.wait()
    channels = one.shape[2]
    rows = TILE + 2
    per_tile = LANES // channels
    lanes = -(-rows * channels // LANES) * LANES
    image_row = lax.broadcasted_iota(jnp.int32, (16, lanes), 0)
    hidden_row = lax.broadcasted_iota(jnp.int32, (16, lanes), 1) // channels
    place, last = own_place()
    held = (hidden_row >= jnp.where(place == 0, 1, 0)) & (hidden_row < jnp.where(place == last, rows - 1, rows))
    high, low = [], []
    for tap in range(3):
        band = jnp.zeros((16, lanes), jnp.float32)
        for shift in range(3):
            line = jnp.concatenate([four_times(one[shift, tap : tap + 1])] * (lanes // LANES), axis=1)
            band = jnp.where(held & (image_row - hidden_row == shift), line, band)
        high.append(band.astype(jnp.bfloat16).astype(jnp.float32))
        low.append(band - high[-1])
    line = jnp.concatenate([four_times(bias[...])] * (lanes // LANES), axis=1)
    with_bias = high[0]
    for piece in range(3):
        rounded = line.astype(jnp.bfloat16).astype(jnp.float32)
        with_bias = jnp.where(held & (image_row == 12 + piece), rounded, with_bias)
        line = line - rounded
    stacked = jnp.concatenate([with_bias, *high[1:], *high, *low], axis=0)
    weights_one[...] = stacked.T[: weights_one.shape[0]].astype(jnp.bfloat16)
    row = lax.broadcasted_iota(jnp.int32, bias_rows.shape, 0) // TILE
    lane = lax.broadcasted_iota(jnp.int32, bias_rows.shape, 1)
    line = jnp.where(row == lane, four_times(bias_two[...]), 0.0)
    bias_rows[...] = jnp.broadcast_to(jnp.sum(line, axis=1, keepdims=True), bias_rows.shape)
    lines = [[four_times(two[shift, tap].astype(jnp.float32)) for shift in range(3)] for tap in range(3)]
    row = lax.broadcasted_iota(jnp.int32, (TILE, LANES), 0)
    lane = lax.broadcasted_iota(jnp.int32, (TILE, LANES), 1) // channels
    zero = jnp.zeros((TILE, LANES), jnp.float32)
    for tile in range(-(-3 * rows // per_tile)):
        taps = sorted({(tile * per_tile + g) // rows for g in range(per_tile)} & {0, 1, 2})
        masks = []
        for tap in taps:
            hidden_row = tile * per_tile + lane - tap * rows
            inside = (hidden_row >= 0) & (hidden_row < rows)
            masks += [(tap, shift, inside & (hidden_row - row == shift)) for shift in range(3)]
        width = min(LANES, weights_two.shape[1] - tile * LANES)
        for channel in range(0, channels, 2):
            pair = []
            for k in (channel, channel + 1):
                values = zero
                for tap, shift, mask in masks:
                    values = jnp.where(mask, lines[tap][shift][k : k + 1], values)
                pair.append(values)
            block = jnp.concatenate(pair, axis=0).astype(jnp.bfloat16)
            weights_two[TILE * channel : TILE * (channel + 2), tile * LANES : tile * LANES + width] = block[:, :width]
    get_table.wait()


def shifted(values, width):
    lane = lax.broadcasted_iota(jnp.int32, values.shape, 1)
    zero = jnp.zeros_like(values)
    before = jnp.where(lane == 0, zero, pltpu.roll(values, 1, 1))
    after = jnp.where(lane == width - 1, zero, pltpu.roll(values, width - 1, 1))
    return before, values, after


def layers_kernel(shares, weights_one, weights_two, bias_rows, table, out, staged, sems):
    width = out.shape[2]
    vis, row, col = (lax.axis_size(axis) for axis in ALL)
    upper = lax.broadcasted_iota(jnp.int32, (TILE, LANES), 0) < TILE // 2
    above, below = [], []
    for r in range(row):
        senders = [(v * row + r) * col + c for v in range(vis) for c in range(col)]
        total = shares[senders[0]].astype(jnp.float32)
        for sender in senders[1:]:
            total = total + shares[sender].astype(jnp.float32)
        middle = total[TILE : 2 * TILE]
        above += [total[:TILE], total[2 * TILE :]]
        below += [jnp.where(upper, middle, 0.0), jnp.where(upper, pltpu.roll(middle, TILE // 2, 0), 0.0)]
    turned = jnp.concatenate([jnp.concatenate(above, axis=1), jnp.concatenate(below, axis=1)], axis=0)
    high = turned.astype(jnp.bfloat16)
    low = (turned - high.astype(jnp.float32)).astype(jnp.bfloat16)
    image = jnp.dot(jnp.concatenate([high, low], axis=0), table[...], preferred_element_type=jnp.float32)
    image = image[: 2 * TILE] + image[2 * TILE :]
    columns = jnp.concatenate(shifted(image, width), axis=0)
    high = columns.astype(jnp.bfloat16).astype(jnp.float32)
    low = columns - high
    row = lax.broadcasted_iota(jnp.int32, (48, width), 0)
    with_ones = jnp.where((row >= 12) & (row < 15), 1.0, high)
    stacked = jnp.concatenate([with_ones, low, high], axis=0).astype(jnp.bfloat16)
    hidden = jnp.dot(weights_one[...], stacked, preferred_element_type=jnp.float32)
    hidden = jnp.maximum(hidden, 0.0).astype(jnp.bfloat16)
    stacked = jnp.concatenate(shifted(hidden, width), axis=0)
    half = out.shape[0] // 2
    copies = []
    for part in range(2):
        rows = pl.ds(part * half * TILE, half * TILE)
        features = jnp.dot(weights_two[rows], stacked, preferred_element_type=jnp.float32)
        features = features + jnp.concatenate([bias_rows[rows]] * (width // LANES), axis=1)
        channels_of = pl.ds(part * half, half)
        staged[channels_of] = features.reshape(half, TILE, width).astype(out.dtype)
        copies.append(pltpu.make_async_copy(staged.at[channels_of], out.at[channels_of], sems.at[part]))
        copies[-1].start()
    for copy in copies:
        copy.wait()


def in_hbm(*arrays):
    return [pltpu.with_memory_space_constraint(array, pltpu.HBM) for array in arrays]


def direct(partials, coverage, conv_one, bias_one, conv_two, bias_two):
    count_row, count_col = lax.axis_size("row"), lax.axis_size("col")
    devices = lax.axis_size("vis") * count_row * count_col
    length = partials.shape[3] * count_col
    image_len = length // 2
    channels = conv_two.shape[2]
    first, second = grid_tables(length, count_row, count_col)
    vmem, hbm = pl.BlockSpec(memory_space=pltpu.VMEM), pl.BlockSpec(memory_space=pltpu.HBM)
    limit = pltpu.CompilerParams(vmem_limit_bytes=16 * 2**20)
    share = (devices, 2 * (TILE + 2 * HALO), LANES)
    shares = pl.pallas_call(
        share_kernel,
        out_shape=jax.ShapeDtypeStruct(share, jnp.bfloat16),
        in_specs=[hbm] * 3,
        out_specs=vmem,
        scratch_shapes=[
            pltpu.SMEM(coverage.shape, jnp.int32),
            pltpu.VMEM(partials.shape, jnp.bfloat16),
            pltpu.VMEM(first.shape[1:], jnp.bfloat16),
            pltpu.SemaphoreType.DMA((3,)),
        ],
        compiler_params=limit,
        name="shares",
    )(*in_hbm(coverage, partials, jnp.asarray(first)))
    arrived = lax.all_to_all(shares, ALL, split_axis=0, concat_axis=0, tiled=True)
    rows = TILE + 2
    weights = pl.pallas_call(
        weights_kernel,
        out_shape=[
            jax.ShapeDtypeStruct((rows * channels, 3 * 48), jnp.bfloat16),
            jax.ShapeDtypeStruct((TILE * channels, 3 * rows * channels), jnp.bfloat16),
            jax.ShapeDtypeStruct((TILE * channels, LANES), jnp.float32),
            jax.ShapeDtypeStruct(second.shape, jnp.bfloat16),
        ],
        in_specs=[hbm] * 5,
        out_specs=[vmem] * 4,
        scratch_shapes=[
            pltpu.VMEM((3, 3, channels), jnp.float32),
            pltpu.VMEM((1, channels), jnp.float32),
            pltpu.VMEM(conv_two.shape, jnp.bfloat16),
            pltpu.VMEM((1, channels), jnp.float32),
            pltpu.SemaphoreType.DMA((5,)),
        ],
        compiler_params=limit,
        name="weights",
    )(*in_hbm(conv_one.transpose(1, 2, 0), bias_one[None], conv_two, bias_two[None], jnp.asarray(second)))
    return pl.pallas_call(
        layers_kernel,
        out_shape=jax.ShapeDtypeStruct((channels, TILE, image_len), jnp.bfloat16),
        in_specs=[vmem] * 5,
        out_specs=hbm,
        scratch_shapes=[
            pltpu.VMEM((channels, TILE, image_len), jnp.bfloat16),
            pltpu.SemaphoreType.DMA((2,)),
        ],
        compiler_params=limit,
        name="layers",
    )(arrived, *weights)


def local(partials, coverage, conv_one, bias_one, conv_two, bias_two):
    count_col = lax.axis_size("col")
    devices = lax.axis_size("vis") * lax.axis_size("row") * count_col
    image_len = partials.shape[3] * count_col // 2
    sent = devices * (TILE + 2 * HALO) * image_len * 2
    fits = partials.shape[2] == LANES and image_len == devices * TILE and conv_two.shape[2] * 4 == LANES and image_len == 2 * LANES and sent <= DIRECT_BYTES
    plan = direct if fits else staged
    return plan(partials, coverage, conv_one, bias_one, conv_two, bias_two)


def solution(mesh):
    placed = (P("vis", None, "row", "col"), P("vis", "row", "col"), P(), P(), P(), P())
    return jax.shard_map(
        local,
        mesh=mesh,
        in_specs=placed,
        out_specs=P(None, ALL, None),
        check_vma=False,
    )
```

```python
import math

import jax
import jax.numpy as jnp
import numpy as np
from jax import lax
from jax.experimental import pallas as pl
from jax.experimental.pallas import tpu as pltpu
from jax.sharding import PartitionSpec as P

BLK = 128
ALL = ("vis", "row", "col")
DIRECT_BYTES = 4 * 2**20
HALO = 2
TILE = 8
LANES = 128


def with_halo(cells, sides, width):
    for axis, dim in sides:
        count = lax.axis_size(axis)
        ends = count - 1
        head = lax.slice_in_dim(cells, 0, width, axis=dim)
        tail = lax.slice_in_dim(cells, cells.shape[dim] - width, cells.shape[dim], axis=dim)
        cells = jnp.concatenate(
            [
                lax.ppermute(tail, axis, [(i, (i + 1) % count) for i in range(ends)]),
                cells,
                lax.ppermute(head, axis, [((i + 1) % count, i) for i in range(ends)]),
            ],
            axis=dim,
        )
    return cells


def phase_table(numer, denom):
    angle = numer.astype(jnp.float32) * (2.0 * math.pi / denom)
    return (jnp.cos(angle), jnp.sin(angle))


def partial_transform(real_part, imag_part, block_of, keep_imag):
    batch = real_part.shape[0]
    count_blocks = real_part.shape[1]
    block_len = real_part.shape[2]
    length = count_blocks * block_len
    highest = lax.Precision.HIGHEST
    outer = jnp.arange(count_blocks, dtype=jnp.int32)
    inner = jnp.arange(block_len, dtype=jnp.int32)
    cos_one, sin_one = phase_table(block_of[:, None] * outer[None, :] % count_blocks, count_blocks)
    mid_re = jnp.einsum("lpt,px->lxt", real_part, cos_one, precision=highest) - jnp.einsum(
        "lpt,px->lxt", imag_part, sin_one, precision=highest
    )
    mid_im = jnp.einsum("lpt,px->lxt", real_part, sin_one, precision=highest) + jnp.einsum(
        "lpt,px->lxt", imag_part, cos_one, precision=highest
    )
    cos_two, sin_two = phase_table(outer[:, None] * inner[None, :] % length, length)
    parity = (1 - 2 * (outer % 2)).astype(jnp.float32)[:, None]
    cos_two = cos_two * parity
    sin_two = sin_two * parity
    turn_re = mid_re * cos_two - mid_im * sin_two
    turn_im = mid_re * sin_two + mid_im * cos_two
    kept = jnp.arange(block_len // 2, dtype=jnp.int32)
    picked = (kept + 3 * block_len // 4) % block_len
    cos_three, sin_three = phase_table(inner[:, None] * picked[None, :] % block_len, block_len)
    out_re = jnp.einsum("lxt,tj->ljx", turn_re, cos_three, precision=highest) - jnp.einsum(
        "lxt,tj->ljx", turn_im, sin_three, precision=highest
    )
    out_re = out_re.reshape(batch, length // 2)
    if keep_imag:
        out_im = jnp.einsum("lxt,tj->ljx", turn_re, sin_three, precision=highest) + jnp.einsum(
            "lxt,tj->ljx", turn_im, cos_three, precision=highest
        )
        return (out_re, out_im.reshape(batch, length // 2))
    return (out_re, out_re)


def first_layer(extended, conv_one, bias_one, count_rows):
    width = extended.shape[1]
    padded = jnp.pad(extended, ((0, 0), (1, 1)))
    summed = (
        jnp.zeros((conv_one.shape[0], count_rows, width), jnp.float32) + bias_one[:, None, None]
    )
    for shift_b in range(3):
        for shift_a in range(3):
            summed = (
                summed
                + conv_one[:, shift_b, shift_a][:, None, None]
                * padded[None, shift_b : shift_b + count_rows, shift_a : shift_a + width]
            )
    return jnp.maximum(summed, 0.0)


def second_layer(hidden_ext, conv_two, bias_two, count_rows):
    width = hidden_ext.shape[2]
    padded = jnp.pad(hidden_ext, ((0, 0), (0, 0), (1, 1)))
    summed = jnp.zeros((conv_two.shape[2], count_rows, width), jnp.float32)
    for shift_b in range(3):
        for shift_a in range(3):
            summed = summed + jnp.einsum(
                "kj,jba->kba",
                conv_two[shift_b, shift_a],
                padded[:, shift_b : shift_b + count_rows, shift_a : shift_a + width],
                preferred_element_type=jnp.float32,
            )
    return (summed + bias_two[:, None, None]).astype(jnp.bfloat16)


def staged(partials, coverage, conv_one, bias_one, conv_two, bias_two):
    count_vis = lax.axis_size("vis")
    count_row = lax.axis_size("row")
    count_col = lax.axis_size("col")
    grid_len = partials.shape[3] * count_col
    cover = coverage[0]
    block_rows = cover.shape[0]
    block_cols = cover.shape[1]
    spread = jnp.broadcast_to(cover[:, None, :, None], (block_rows, BLK, block_cols, BLK))
    spread = spread.reshape(block_rows * BLK, block_cols * BLK)
    count_blocks = count_vis * count_row
    row_block = grid_len // count_blocks
    row_share = row_block // count_col
    masked = partials[0] * spread.astype(jnp.bfloat16)[None]
    reduced = lax.psum_scatter(
        masked.astype(jnp.float32).astype(jnp.bfloat16), "vis", scatter_dimension=1, tiled=True
    ).astype(jnp.float32)
    grid_rows = lax.all_to_all(
        reduced.astype(jnp.bfloat16), "col", split_axis=1, concat_axis=2, tiled=True
    ).astype(reduced.dtype)
    natural = jnp.arange(count_blocks, dtype=jnp.int32)
    shaped = grid_rows.reshape(2, row_share, count_blocks, row_block)
    first_re, first_im = partial_transform(shaped[0], shaped[1], natural, True)
    stacked = jnp.stack([first_re, first_im])
    moved = lax.all_to_all(
        lax.all_to_all(
            stacked.astype(jnp.bfloat16), ("vis", "row"), split_axis=2, concat_axis=1, tiled=True
        ),
        "col",
        split_axis=2,
        concat_axis=1,
        tiled=True,
    ).astype(stacked.dtype)
    img_rows = moved.shape[2]
    arranged = moved.reshape(2, count_col, count_blocks, row_share, img_rows)
    arranged = arranged.transpose(0, 4, 2, 1, 3).reshape(2, img_rows, count_blocks, row_block)
    owners = natural % count_row * count_vis + natural // count_row
    image, unused = partial_transform(arranged[0], arranged[1], owners, False)
    image = image * (1.0 / grid_len)
    extended = with_halo(image.astype(jnp.bfloat16), ((("vis", "row", "col"), 0),), 1).astype(
        image.dtype
    )
    hidden = first_layer(extended, conv_one, bias_one, img_rows).astype(jnp.bfloat16)
    hidden_ext = with_halo(hidden, ((("vis", "row", "col"), 1),), 1)
    return second_layer(hidden_ext, conv_two, bias_two, img_rows)


def grid_tables(length, count_row, count_col):
    image_len = length // 2
    place = np.arange(length)[:, None] - length // 2
    pixel = np.arange(image_len)[None, :] - image_len // 2
    angle = (place * pixel % length) * (2.0 * math.pi / length)
    cos, sin = np.cos(angle), np.sin(angle)
    padded = np.pad(np.stack([cos.T, sin.T]), ((0, 0), (HALO, TILE - HALO), (0, 0)))
    first = padded.reshape(2 * (image_len + TILE), count_col, length // count_col).transpose(1, 0, 2)
    rows = length // count_row
    second = np.stack([cos.reshape(count_row, rows, image_len), -sin.reshape(count_row, rows, image_len)], axis=1)
    second = second.reshape(2 * length, image_len) / length
    return first.astype(jnp.bfloat16), second.astype(jnp.bfloat16)


def share_kernel(cover_in, parts_in, first_all, out, cover, parts, first, cut, sems, sent):
    get_cover = pltpu.make_async_copy(cover_in, cover, sems.at[0])
    get_parts = pltpu.make_async_copy(parts_in, parts, sems.at[1])
    get_first = pltpu.make_async_copy(first_all.at[lax.axis_index("col")], first, sems.at[2])
    for copy in (get_cover, get_parts, get_first):
        copy.start()
    count_rows = parts.shape[2]
    get_cover.wait()
    get_parts.wait()
    components = []
    for component in range(2):
        strips = []
        for i in range(cover.shape[1]):
            cells = []
            for j in range(cover.shape[2]):
                block = parts[0, component, i * BLK : (i + 1) * BLK, j * BLK : (j + 1) * BLK]
                level = jnp.full(block.shape, cover[0, i, j].astype(jnp.float32)).astype(jnp.bfloat16)
                cells.append(block * level)
            strips.append(jnp.concatenate(cells, axis=1))
        components.append(jnp.concatenate(strips, axis=0))
    grid = jnp.concatenate(components, axis=0)
    upper = lax.broadcasted_iota(jnp.int32, (TILE, LANES), 0) < TILE // 2
    devices = cut.shape[0]
    tall = first.shape[0] // 2
    group = devices // sent.shape[0]
    get_first.wait()
    copies = []
    for start in range(0, devices, group):
        rows = slice(TILE * start, TILE * (start + group + 1))
        table = jnp.concatenate([first[rows], first[tall + rows.start : tall + rows.stop]], axis=0)
        turned = lax.dot_general(table, grid, (((1,), (1,)), ((), ())), preferred_element_type=jnp.float32)
        half = turned.shape[0] // 2
        mid_re = turned[:half, :count_rows] - turned[half:, count_rows:]
        mid_im = turned[half:, :count_rows] + turned[:half, count_rows:]
        for k in range(group):
            here = slice(TILE * k, TILE * (k + 1))
            below = slice(TILE * (k + 1), TILE * (k + 2))
            middle = jnp.where(upper, mid_re[below], pltpu.roll(mid_im[below], TILE // 2, 0))
            cut[start + k] = jnp.concatenate([mid_re[here], middle, mid_im[here]], axis=0).astype(cut.dtype)
        part = pl.ds(start, group)
        copies.append(pltpu.make_async_copy(cut.at[part], out.at[part], sent.at[start // group]))
        copies[-1].start()
    for copy in copies:
        copy.wait()


def own_place():
    place, count = 0, 1
    for axis in ALL:
        place = place * lax.axis_size(axis) + lax.axis_index(axis)
        count = count * lax.axis_size(axis)
    return place, count - 1


def four_times(values):
    return jnp.concatenate([values] * 4, axis=1)


def weights_kernel(
    one_in, bias_in, two_in, bias_two_in, table_in, weights_one, weights_two, bias_rows, table, one, bias, two, bias_two, sems
):
    fetch = [
        pltpu.make_async_copy(one_in, one, sems.at[0]),
        pltpu.make_async_copy(bias_in, bias, sems.at[1]),
        pltpu.make_async_copy(two_in, two, sems.at[2]),
        pltpu.make_async_copy(bias_two_in, bias_two, sems.at[3]),
    ]
    get_table = pltpu.make_async_copy(table_in, table, sems.at[4])
    for copy in (*fetch, get_table):
        copy.start()
    for copy in fetch:
        copy.wait()
    channels = one.shape[2]
    rows = TILE + 2
    per_tile = LANES // channels
    lanes = -(-rows * channels // LANES) * LANES
    image_row = lax.broadcasted_iota(jnp.int32, (16, lanes), 0)
    hidden_row = lax.broadcasted_iota(jnp.int32, (16, lanes), 1) // channels
    place, last = own_place()
    held = (hidden_row >= jnp.where(place == 0, 1, 0)) & (hidden_row < jnp.where(place == last, rows - 1, rows))
    high, low = [], []
    for tap in range(3):
        band = jnp.zeros((16, lanes), jnp.float32)
        for shift in range(3):
            line = jnp.concatenate([four_times(one[shift, tap : tap + 1])] * (lanes // LANES), axis=1)
            band = jnp.where(held & (image_row - hidden_row == shift), line, band)
        high.append(band.astype(jnp.bfloat16).astype(jnp.float32))
        low.append(band - high[-1])
    line = jnp.concatenate([four_times(bias[...])] * (lanes // LANES), axis=1)
    with_bias = high[0]
    for piece in range(3):
        rounded = line.astype(jnp.bfloat16).astype(jnp.float32)
        with_bias = jnp.where(held & (image_row == 12 + piece), rounded, with_bias)
        line = line - rounded
    stacked = jnp.concatenate([with_bias, *high[1:], *high, *low], axis=0)
    weights_one[...] = stacked.T[: weights_one.shape[0]].astype(jnp.bfloat16)
    row = lax.broadcasted_iota(jnp.int32, bias_rows.shape, 0) // TILE
    lane = lax.broadcasted_iota(jnp.int32, bias_rows.shape, 1)
    line = jnp.where(row == lane, four_times(bias_two[...]), 0.0)
    bias_rows[...] = jnp.broadcast_to(jnp.sum(line, axis=1, keepdims=True), bias_rows.shape)
    lines = [[four_times(two[shift, tap].astype(jnp.float32)) for shift in range(3)] for tap in range(3)]
    row = lax.broadcasted_iota(jnp.int32, (TILE, LANES), 0)
    lane = lax.broadcasted_iota(jnp.int32, (TILE, LANES), 1) // channels
    zero = jnp.zeros((TILE, LANES), jnp.float32)
    for tile in range(-(-3 * rows // per_tile)):
        taps = sorted({(tile * per_tile + g) // rows for g in range(per_tile)} & {0, 1, 2})
        masks = []
        for tap in taps:
            hidden_row = tile * per_tile + lane - tap * rows
            inside = (hidden_row >= 0) & (hidden_row < rows)
            masks += [(tap, shift, inside & (hidden_row - row == shift)) for shift in range(3)]
        width = min(LANES, weights_two.shape[1] - tile * LANES)
        for channel in range(0, channels, 2):
            pair = []
            for k in (channel, channel + 1):
                values = zero
                for tap, shift, mask in masks:
                    values = jnp.where(mask, lines[tap][shift][k : k + 1], values)
                pair.append(values)
            block = jnp.concatenate(pair, axis=0).astype(jnp.bfloat16)
            weights_two[TILE * channel : TILE * (channel + 2), tile * LANES : tile * LANES + width] = block[:, :width]
    get_table.wait()


def shifted(values, by):
    if by == 0:
        return values
    width = values.shape[1]
    lane = lax.broadcasted_iota(jnp.int32, values.shape, 1) + by
    return jnp.where((lane >= 0) & (lane < width), pltpu.roll(values, -by % width, 1), 0.0)


def layers_kernel(shares, weights_one, weights_two, bias_rows, table, out, staged, sems):
    width = out.shape[2]
    vis, row, col = (lax.axis_size(axis) for axis in ALL)
    upper = lax.broadcasted_iota(jnp.int32, (TILE, LANES), 0) < TILE // 2
    above, below = [], []
    for r in range(row):
        senders = [(v * row + r) * col + c for v in range(vis) for c in range(col)]
        total = shares[senders[0]].astype(jnp.float32)
        for sender in senders[1:]:
            total = total + shares[sender].astype(jnp.float32)
        middle = total[TILE : 2 * TILE]
        above += [total[:TILE], total[2 * TILE :]]
        below += [jnp.where(upper, middle, 0.0), jnp.where(upper, pltpu.roll(middle, TILE // 2, 0), 0.0)]
    turned = jnp.concatenate([jnp.concatenate(above, axis=1), jnp.concatenate(below, axis=1)], axis=0)
    high = turned.astype(jnp.bfloat16)
    low = (turned - high.astype(jnp.float32)).astype(jnp.bfloat16)
    image = jnp.dot(jnp.concatenate([high, low], axis=0), table[...], preferred_element_type=jnp.float32)
    image = image[: 2 * TILE] + image[2 * TILE :]
    moved = [shifted(image, by) for by in range(-2, 3)]
    row = lax.broadcasted_iota(jnp.int32, (48, width), 0)
    lane = lax.broadcasted_iota(jnp.int32, (48, width), 1)
    stacked = []
    for by in (-1, 0, 1):
        columns = jnp.concatenate(moved[by + 1 : by + 4], axis=0)
        high = columns.astype(jnp.bfloat16).astype(jnp.float32)
        low = columns - high
        with_ones = jnp.where((row >= 12) & (row < 15), 1.0, high)
        inside = (lane + by >= 0) & (lane + by < width)
        pieces = [jnp.where(inside, piece, 0.0) for piece in (with_ones, low, high)]
        stacked.append(jnp.concatenate(pieces, axis=0).astype(jnp.bfloat16))
    hidden = jnp.dot(weights_one[...], jnp.concatenate(stacked, axis=1), preferred_element_type=jnp.float32)
    hidden = jnp.maximum(hidden, 0.0).astype(jnp.bfloat16)
    stacked = jnp.concatenate([hidden[:, i * width : (i + 1) * width] for i in range(3)], axis=0)
    half = out.shape[0] // 2
    copies = []
    for part in range(2):
        rows = pl.ds(part * half * TILE, half * TILE)
        features = jnp.dot(weights_two[rows], stacked, preferred_element_type=jnp.float32)
        features = features + jnp.concatenate([bias_rows[rows]] * (width // LANES), axis=1)
        channels_of = pl.ds(part * half, half)
        staged[channels_of] = features.reshape(half, TILE, width).astype(out.dtype)
        copies.append(pltpu.make_async_copy(staged.at[channels_of], out.at[channels_of], sems.at[part]))
        copies[-1].start()
    for copy in copies:
        copy.wait()


def in_hbm(*arrays):
    return [pltpu.with_memory_space_constraint(array, pltpu.HBM) for array in arrays]


def direct(partials, coverage, conv_one, bias_one, conv_two, bias_two):
    count_row, count_col = lax.axis_size("row"), lax.axis_size("col")
    devices = lax.axis_size("vis") * count_row * count_col
    length = partials.shape[3] * count_col
    image_len = length // 2
    channels = conv_two.shape[2]
    first, second = grid_tables(length, count_row, count_col)
    vmem, hbm = pl.BlockSpec(memory_space=pltpu.VMEM), pl.BlockSpec(memory_space=pltpu.HBM)
    limit = pltpu.CompilerParams(vmem_limit_bytes=16 * 2**20)
    share = (devices, 2 * (TILE + 2 * HALO), LANES)
    shares = pl.pallas_call(
        share_kernel,
        out_shape=jax.ShapeDtypeStruct(share, jnp.bfloat16),
        in_specs=[hbm] * 3,
        out_specs=hbm,
        scratch_shapes=[
            pltpu.SMEM(coverage.shape, jnp.int32),
            pltpu.VMEM(partials.shape, jnp.bfloat16),
            pltpu.VMEM(first.shape[1:], jnp.bfloat16),
            pltpu.VMEM(share, jnp.bfloat16),
            pltpu.SemaphoreType.DMA((3,)),
            pltpu.SemaphoreType.DMA((math.gcd(devices, 2),)),
        ],
        compiler_params=limit,
        name="shares",
    )(*in_hbm(coverage, partials, jnp.asarray(first)))
    arrived = lax.all_to_all(shares, ALL, split_axis=0, concat_axis=0, tiled=True)
    rows = TILE + 2
    weights = pl.pallas_call(
        weights_kernel,
        out_shape=[
            jax.ShapeDtypeStruct((rows * channels, 3 * 48), jnp.bfloat16),
            jax.ShapeDtypeStruct((TILE * channels, 3 * rows * channels), jnp.bfloat16),
            jax.ShapeDtypeStruct((TILE * channels, LANES), jnp.float32),
            jax.ShapeDtypeStruct(second.shape, jnp.bfloat16),
        ],
        in_specs=[hbm] * 5,
        out_specs=[vmem] * 4,
        scratch_shapes=[
            pltpu.VMEM((3, 3, channels), jnp.float32),
            pltpu.VMEM((1, channels), jnp.float32),
            pltpu.VMEM(conv_two.shape, jnp.bfloat16),
            pltpu.VMEM((1, channels), jnp.float32),
            pltpu.SemaphoreType.DMA((5,)),
        ],
        compiler_params=limit,
        name="weights",
    )(*in_hbm(conv_one.transpose(1, 2, 0), bias_one[None], conv_two, bias_two[None], jnp.asarray(second)))
    return pl.pallas_call(
        layers_kernel,
        out_shape=jax.ShapeDtypeStruct((channels, TILE, image_len), jnp.bfloat16),
        in_specs=[vmem] * 5,
        out_specs=hbm,
        scratch_shapes=[
            pltpu.VMEM((channels, TILE, image_len), jnp.bfloat16),
            pltpu.SemaphoreType.DMA((2,)),
        ],
        compiler_params=limit,
        name="layers",
    )(arrived, *weights)


def local(partials, coverage, conv_one, bias_one, conv_two, bias_two):
    count_col = lax.axis_size("col")
    devices = lax.axis_size("vis") * lax.axis_size("row") * count_col
    image_len = partials.shape[3] * count_col // 2
    sent = devices * (TILE + 2 * HALO) * image_len * 2
    fits = partials.shape[2] == LANES and image_len == devices * TILE and conv_two.shape[2] * 4 == LANES and image_len == 2 * LANES and sent <= DIRECT_BYTES
    plan = direct if fits else staged
    return plan(partials, coverage, conv_one, bias_one, conv_two, bias_two)


def solution(mesh):
    placed = (P("vis", None, "row", "col"), P("vis", "row", "col"), P(), P(), P(), P())
    return jax.shard_map(
        local,
        mesh=mesh,
        in_specs=placed,
        out_specs=P(None, ALL, None),
        check_vma=False,
    )
```

```python
import math

import jax
import jax.numpy as jnp
import numpy as np
from jax import lax
from jax.experimental import pallas as pl
from jax.experimental.pallas import tpu as pltpu
from jax.sharding import PartitionSpec as P

BLK = 128
ALL = ("vis", "row", "col")
DIRECT_BYTES = 4 * 2**20
HALO = 2
TILE = 8
LANES = 128


def with_halo(cells, sides, width):
    for axis, dim in sides:
        count = lax.axis_size(axis)
        ends = count - 1
        head = lax.slice_in_dim(cells, 0, width, axis=dim)
        tail = lax.slice_in_dim(cells, cells.shape[dim] - width, cells.shape[dim], axis=dim)
        cells = jnp.concatenate(
            [
                lax.ppermute(tail, axis, [(i, (i + 1) % count) for i in range(ends)]),
                cells,
                lax.ppermute(head, axis, [((i + 1) % count, i) for i in range(ends)]),
            ],
            axis=dim,
        )
    return cells


def phase_table(numer, denom):
    angle = numer.astype(jnp.float32) * (2.0 * math.pi / denom)
    return (jnp.cos(angle), jnp.sin(angle))


def partial_transform(real_part, imag_part, block_of, keep_imag):
    batch = real_part.shape[0]
    count_blocks = real_part.shape[1]
    block_len = real_part.shape[2]
    length = count_blocks * block_len
    highest = lax.Precision.HIGHEST
    outer = jnp.arange(count_blocks, dtype=jnp.int32)
    inner = jnp.arange(block_len, dtype=jnp.int32)
    cos_one, sin_one = phase_table(block_of[:, None] * outer[None, :] % count_blocks, count_blocks)
    mid_re = jnp.einsum("lpt,px->lxt", real_part, cos_one, precision=highest) - jnp.einsum(
        "lpt,px->lxt", imag_part, sin_one, precision=highest
    )
    mid_im = jnp.einsum("lpt,px->lxt", real_part, sin_one, precision=highest) + jnp.einsum(
        "lpt,px->lxt", imag_part, cos_one, precision=highest
    )
    cos_two, sin_two = phase_table(outer[:, None] * inner[None, :] % length, length)
    parity = (1 - 2 * (outer % 2)).astype(jnp.float32)[:, None]
    cos_two = cos_two * parity
    sin_two = sin_two * parity
    turn_re = mid_re * cos_two - mid_im * sin_two
    turn_im = mid_re * sin_two + mid_im * cos_two
    kept = jnp.arange(block_len // 2, dtype=jnp.int32)
    picked = (kept + 3 * block_len // 4) % block_len
    cos_three, sin_three = phase_table(inner[:, None] * picked[None, :] % block_len, block_len)
    out_re = jnp.einsum("lxt,tj->ljx", turn_re, cos_three, precision=highest) - jnp.einsum(
        "lxt,tj->ljx", turn_im, sin_three, precision=highest
    )
    out_re = out_re.reshape(batch, length // 2)
    if keep_imag:
        out_im = jnp.einsum("lxt,tj->ljx", turn_re, sin_three, precision=highest) + jnp.einsum(
            "lxt,tj->ljx", turn_im, cos_three, precision=highest
        )
        return (out_re, out_im.reshape(batch, length // 2))
    return (out_re, out_re)


def first_layer(extended, conv_one, bias_one, count_rows):
    width = extended.shape[1]
    padded = jnp.pad(extended, ((0, 0), (1, 1)))
    summed = (
        jnp.zeros((conv_one.shape[0], count_rows, width), jnp.float32) + bias_one[:, None, None]
    )
    for shift_b in range(3):
        for shift_a in range(3):
            summed = (
                summed
                + conv_one[:, shift_b, shift_a][:, None, None]
                * padded[None, shift_b : shift_b + count_rows, shift_a : shift_a + width]
            )
    return jnp.maximum(summed, 0.0)


def second_layer(hidden_ext, conv_two, bias_two, count_rows):
    width = hidden_ext.shape[2]
    padded = jnp.pad(hidden_ext, ((0, 0), (0, 0), (1, 1)))
    summed = jnp.zeros((conv_two.shape[2], count_rows, width), jnp.float32)
    for shift_b in range(3):
        for shift_a in range(3):
            summed = summed + jnp.einsum(
                "kj,jba->kba",
                conv_two[shift_b, shift_a],
                padded[:, shift_b : shift_b + count_rows, shift_a : shift_a + width],
                preferred_element_type=jnp.float32,
            )
    return (summed + bias_two[:, None, None]).astype(jnp.bfloat16)


def staged(partials, coverage, conv_one, bias_one, conv_two, bias_two):
    count_vis = lax.axis_size("vis")
    count_row = lax.axis_size("row")
    count_col = lax.axis_size("col")
    grid_len = partials.shape[3] * count_col
    cover = coverage[0]
    block_rows = cover.shape[0]
    block_cols = cover.shape[1]
    spread = jnp.broadcast_to(cover[:, None, :, None], (block_rows, BLK, block_cols, BLK))
    spread = spread.reshape(block_rows * BLK, block_cols * BLK)
    count_blocks = count_vis * count_row
    row_block = grid_len // count_blocks
    row_share = row_block // count_col
    masked = partials[0] * spread.astype(jnp.bfloat16)[None]
    reduced = lax.psum_scatter(
        masked.astype(jnp.float32).astype(jnp.bfloat16), "vis", scatter_dimension=1, tiled=True
    ).astype(jnp.float32)
    grid_rows = lax.all_to_all(
        reduced.astype(jnp.bfloat16), "col", split_axis=1, concat_axis=2, tiled=True
    ).astype(reduced.dtype)
    natural = jnp.arange(count_blocks, dtype=jnp.int32)
    shaped = grid_rows.reshape(2, row_share, count_blocks, row_block)
    first_re, first_im = partial_transform(shaped[0], shaped[1], natural, True)
    stacked = jnp.stack([first_re, first_im])
    moved = lax.all_to_all(
        lax.all_to_all(
            stacked.astype(jnp.bfloat16), ("vis", "row"), split_axis=2, concat_axis=1, tiled=True
        ),
        "col",
        split_axis=2,
        concat_axis=1,
        tiled=True,
    ).astype(stacked.dtype)
    img_rows = moved.shape[2]
    arranged = moved.reshape(2, count_col, count_blocks, row_share, img_rows)
    arranged = arranged.transpose(0, 4, 2, 1, 3).reshape(2, img_rows, count_blocks, row_block)
    owners = natural % count_row * count_vis + natural // count_row
    image, unused = partial_transform(arranged[0], arranged[1], owners, False)
    image = image * (1.0 / grid_len)
    extended = with_halo(image.astype(jnp.bfloat16), ((("vis", "row", "col"), 0),), 1).astype(
        image.dtype
    )
    hidden = first_layer(extended, conv_one, bias_one, img_rows).astype(jnp.bfloat16)
    hidden_ext = with_halo(hidden, ((("vis", "row", "col"), 1),), 1)
    return second_layer(hidden_ext, conv_two, bias_two, img_rows)


def grid_tables(length, count_row, count_col):
    image_len = length // 2
    place = np.arange(length)[:, None] - length // 2
    pixel = np.arange(image_len)[None, :] - image_len // 2
    angle = (place * pixel % length) * (2.0 * math.pi / length)
    cos, sin = np.cos(angle), np.sin(angle)
    padded = np.pad(np.stack([cos.T, sin.T]), ((0, 0), (HALO, TILE - HALO), (0, 0)))
    first = padded.reshape(2 * (image_len + TILE), count_col, length // count_col).transpose(1, 0, 2)
    rows = length // count_row
    second = np.stack([cos.reshape(count_row, rows, image_len), -sin.reshape(count_row, rows, image_len)], axis=1)
    second = second.reshape(2 * length, image_len) / length
    return first.astype(jnp.bfloat16), second.astype(jnp.bfloat16)


def send_order():
    vis, row, col = (lax.axis_size(axis) for axis in ALL)
    pairs = 2 if vis % 2 == 0 else 1
    places = np.arange(vis * row * col).reshape(vis // pairs, pairs, row, col)
    return places.transpose(1, 0, 2, 3).reshape(-1).tolist()


def share_kernel(cover_in, parts_in, first_all, out, cover, parts, first, sems):
    get_cover = pltpu.make_async_copy(cover_in, cover, sems.at[0])
    get_parts = pltpu.make_async_copy(parts_in, parts, sems.at[1])
    get_first = pltpu.make_async_copy(first_all.at[lax.axis_index("col")], first, sems.at[2])
    for copy in (get_cover, get_parts, get_first):
        copy.start()
    count_rows = parts.shape[2]
    get_cover.wait()
    get_parts.wait()
    components = []
    for component in range(2):
        strips = []
        for i in range(cover.shape[1]):
            cells = []
            for j in range(cover.shape[2]):
                block = parts[0, component, i * BLK : (i + 1) * BLK, j * BLK : (j + 1) * BLK]
                level = jnp.full(block.shape, cover[0, i, j].astype(jnp.float32)).astype(jnp.bfloat16)
                cells.append(block * level)
            strips.append(jnp.concatenate(cells, axis=1))
        components.append(jnp.concatenate(strips, axis=0))
    grid = jnp.concatenate(components, axis=0)
    upper = lax.broadcasted_iota(jnp.int32, (TILE, LANES), 0) < TILE // 2
    tall = first.shape[0] // 2
    get_first.wait()
    turned = lax.dot_general(first[...], grid, (((1,), (1,)), ((), ())), preferred_element_type=jnp.float32)
    mid_re = turned[:tall, :count_rows] - turned[tall:, count_rows:]
    mid_im = turned[tall:, :count_rows] + turned[:tall, count_rows:]
    for slot, device in enumerate(send_order()):
        here = slice(TILE * device, TILE * (device + 1))
        below = slice(TILE * (device + 1), TILE * (device + 2))
        middle = jnp.where(upper, mid_re[below], pltpu.roll(mid_im[below], TILE // 2, 0))
        out[slot] = jnp.concatenate([mid_re[here], middle, mid_im[here]], axis=0).astype(out.dtype)


def own_place():
    place, count = 0, 1
    for axis in ALL:
        place = place * lax.axis_size(axis) + lax.axis_index(axis)
        count = count * lax.axis_size(axis)
    return place, count - 1


def four_times(values):
    return jnp.concatenate([values] * 4, axis=1)


def weights_kernel(
    one_in, bias_in, two_in, bias_two_in, table_in, weights_one, weights_two, bias_rows, table, one, bias, two, bias_two, sems
):
    fetch = [
        pltpu.make_async_copy(one_in, one, sems.at[0]),
        pltpu.make_async_copy(bias_in, bias, sems.at[1]),
        pltpu.make_async_copy(two_in, two, sems.at[2]),
        pltpu.make_async_copy(bias_two_in, bias_two, sems.at[3]),
    ]
    get_table = pltpu.make_async_copy(table_in, table, sems.at[4])
    for copy in (*fetch, get_table):
        copy.start()
    for copy in fetch:
        copy.wait()
    channels = one.shape[2]
    rows = TILE + 2
    per_tile = LANES // channels
    lanes = -(-rows * channels // LANES) * LANES
    image_row = lax.broadcasted_iota(jnp.int32, (16, lanes), 0)
    hidden_row = lax.broadcasted_iota(jnp.int32, (16, lanes), 1) // channels
    place, last = own_place()
    held = (hidden_row >= jnp.where(place == 0, 1, 0)) & (hidden_row < jnp.where(place == last, rows - 1, rows))
    high, low = [], []
    for tap in range(3):
        band = jnp.zeros((16, lanes), jnp.float32)
        for shift in range(3):
            line = jnp.concatenate([four_times(one[shift, tap : tap + 1])] * (lanes // LANES), axis=1)
            band = jnp.where(held & (image_row - hidden_row == shift), line, band)
        high.append(band.astype(jnp.bfloat16).astype(jnp.float32))
        low.append(band - high[-1])
    line = jnp.concatenate([four_times(bias[...])] * (lanes // LANES), axis=1)
    with_bias = high[0]
    for piece in range(3):
        rounded = line.astype(jnp.bfloat16).astype(jnp.float32)
        with_bias = jnp.where(held & (image_row == 12 + piece), rounded, with_bias)
        line = line - rounded
    stacked = jnp.concatenate([with_bias, *high[1:], *high, *low], axis=0)
    weights_one[...] = stacked.T[: weights_one.shape[0]].astype(jnp.bfloat16)
    row = lax.broadcasted_iota(jnp.int32, bias_rows.shape, 0) // TILE
    lane = lax.broadcasted_iota(jnp.int32, bias_rows.shape, 1)
    line = jnp.where(row == lane, four_times(bias_two[...]), 0.0)
    bias_rows[...] = jnp.broadcast_to(jnp.sum(line, axis=1, keepdims=True), bias_rows.shape)
    lines = [[four_times(two[shift, tap].astype(jnp.float32)) for shift in range(3)] for tap in range(3)]
    row = lax.broadcasted_iota(jnp.int32, (TILE, LANES), 0)
    lane = lax.broadcasted_iota(jnp.int32, (TILE, LANES), 1) // channels
    zero = jnp.zeros((TILE, LANES), jnp.float32)
    for tile in range(-(-3 * rows // per_tile)):
        taps = sorted({(tile * per_tile + g) // rows for g in range(per_tile)} & {0, 1, 2})
        masks = []
        for tap in taps:
            hidden_row = tile * per_tile + lane - tap * rows
            inside = (hidden_row >= 0) & (hidden_row < rows)
            masks += [(tap, shift, inside & (hidden_row - row == shift)) for shift in range(3)]
        width = min(LANES, weights_two.shape[1] - tile * LANES)
        for channel in range(0, channels, 2):
            pair = []
            for k in (channel, channel + 1):
                values = zero
                for tap, shift, mask in masks:
                    values = jnp.where(mask, lines[tap][shift][k : k + 1], values)
                pair.append(values)
            block = jnp.concatenate(pair, axis=0).astype(jnp.bfloat16)
            weights_two[TILE * channel : TILE * (channel + 2), tile * LANES : tile * LANES + width] = block[:, :width]
    get_table.wait()


def shifted(values, width):
    lane = lax.broadcasted_iota(jnp.int32, values.shape, 1)
    zero = jnp.zeros_like(values)
    before = jnp.where(lane == 0, zero, pltpu.roll(values, 1, 1))
    after = jnp.where(lane == width - 1, zero, pltpu.roll(values, width - 1, 1))
    return before, values, after


def layers_kernel(shares, weights_one, weights_two, bias_rows, table, out, staged, sems):
    width = out.shape[2]
    row, col = lax.axis_size("row"), lax.axis_size("col")
    upper = lax.broadcasted_iota(jnp.int32, (TILE, LANES), 0) < TILE // 2
    above, below = [], []
    for r in range(row):
        senders = [slot for slot, place in enumerate(send_order()) if place // col % row == r]
        total = shares[senders[0]].astype(jnp.float32)
        for sender in senders[1:]:
            total = total + shares[sender].astype(jnp.float32)
        middle = total[TILE : 2 * TILE]
        above += [total[:TILE], total[2 * TILE :]]
        below += [jnp.where(upper, middle, 0.0), jnp.where(upper, pltpu.roll(middle, TILE // 2, 0), 0.0)]
    turned = jnp.concatenate([jnp.concatenate(above, axis=1), jnp.concatenate(below, axis=1)], axis=0)
    high = turned.astype(jnp.bfloat16)
    low = (turned - high.astype(jnp.float32)).astype(jnp.bfloat16)
    image = jnp.dot(jnp.concatenate([high, low], axis=0), table[...], preferred_element_type=jnp.float32)
    image = image[: 2 * TILE] + image[2 * TILE :]
    columns = jnp.concatenate(shifted(image, width), axis=0)
    high = columns.astype(jnp.bfloat16).astype(jnp.float32)
    low = columns - high
    row = lax.broadcasted_iota(jnp.int32, (48, width), 0)
    with_ones = jnp.where((row >= 12) & (row < 15), 1.0, high)
    stacked = jnp.concatenate([with_ones, low, high], axis=0).astype(jnp.bfloat16)
    hidden = jnp.dot(weights_one[...], stacked, preferred_element_type=jnp.float32)
    hidden = jnp.maximum(hidden, 0.0).astype(jnp.bfloat16)
    stacked = jnp.concatenate(shifted(hidden, width), axis=0)
    half = out.shape[0] // 2
    copies = []
    for part in range(2):
        rows = pl.ds(part * half * TILE, half * TILE)
        features = jnp.dot(weights_two[rows], stacked, preferred_element_type=jnp.float32)
        features = features + jnp.concatenate([bias_rows[rows]] * (width // LANES), axis=1)
        channels_of = pl.ds(part * half, half)
        staged[channels_of] = features.reshape(half, TILE, width).astype(out.dtype)
        copies.append(pltpu.make_async_copy(staged.at[channels_of], out.at[channels_of], sems.at[part]))
        copies[-1].start()
    for copy in copies:
        copy.wait()


def in_hbm(*arrays):
    return [pltpu.with_memory_space_constraint(array, pltpu.HBM) for array in arrays]


def direct(partials, coverage, conv_one, bias_one, conv_two, bias_two):
    count_row, count_col = lax.axis_size("row"), lax.axis_size("col")
    devices = lax.axis_size("vis") * count_row * count_col
    length = partials.shape[3] * count_col
    image_len = length // 2
    channels = conv_two.shape[2]
    first, second = grid_tables(length, count_row, count_col)
    vmem, hbm = pl.BlockSpec(memory_space=pltpu.VMEM), pl.BlockSpec(memory_space=pltpu.HBM)
    limit = pltpu.CompilerParams(vmem_limit_bytes=16 * 2**20)
    share = (devices, 2 * (TILE + 2 * HALO), LANES)
    shares = pl.pallas_call(
        share_kernel,
        out_shape=jax.ShapeDtypeStruct(share, jnp.bfloat16),
        in_specs=[hbm] * 3,
        out_specs=vmem,
        scratch_shapes=[
            pltpu.SMEM(coverage.shape, jnp.int32),
            pltpu.VMEM(partials.shape, jnp.bfloat16),
            pltpu.VMEM(first.shape[1:], jnp.bfloat16),
            pltpu.SemaphoreType.DMA((3,)),
        ],
        compiler_params=limit,
        name="shares",
    )(*in_hbm(coverage, partials, jnp.asarray(first)))
    arrived = lax.all_to_all(
        shares, ALL, split_axis=0, concat_axis=0, tiled=True, axis_index_groups=[send_order()]
    )
    rows = TILE + 2
    weights = pl.pallas_call(
        weights_kernel,
        out_shape=[
            jax.ShapeDtypeStruct((rows * channels, 3 * 48), jnp.bfloat16),
            jax.ShapeDtypeStruct((TILE * channels, 3 * rows * channels), jnp.bfloat16),
            jax.ShapeDtypeStruct((TILE * channels, LANES), jnp.float32),
            jax.ShapeDtypeStruct(second.shape, jnp.bfloat16),
        ],
        in_specs=[hbm] * 5,
        out_specs=[vmem] * 4,
        scratch_shapes=[
            pltpu.VMEM((3, 3, channels), jnp.float32),
            pltpu.VMEM((1, channels), jnp.float32),
            pltpu.VMEM(conv_two.shape, jnp.bfloat16),
            pltpu.VMEM((1, channels), jnp.float32),
            pltpu.SemaphoreType.DMA((5,)),
        ],
        compiler_params=limit,
        name="weights",
    )(*in_hbm(conv_one.transpose(1, 2, 0), bias_one[None], conv_two, bias_two[None], jnp.asarray(second)))
    return pl.pallas_call(
        layers_kernel,
        out_shape=jax.ShapeDtypeStruct((channels, TILE, image_len), jnp.bfloat16),
        in_specs=[vmem] * 5,
        out_specs=hbm,
        scratch_shapes=[
            pltpu.VMEM((channels, TILE, image_len), jnp.bfloat16),
            pltpu.SemaphoreType.DMA((2,)),
        ],
        compiler_params=limit,
        name="layers",
    )(arrived, *weights)


def local(partials, coverage, conv_one, bias_one, conv_two, bias_two):
    count_col = lax.axis_size("col")
    devices = lax.axis_size("vis") * lax.axis_size("row") * count_col
    image_len = partials.shape[3] * count_col // 2
    sent = devices * (TILE + 2 * HALO) * image_len * 2
    fits = partials.shape[2] == LANES and image_len == devices * TILE and conv_two.shape[2] * 4 == LANES and image_len == 2 * LANES and sent <= DIRECT_BYTES
    plan = direct if fits else staged
    return plan(partials, coverage, conv_one, bias_one, conv_two, bias_two)


def solution(mesh):
    placed = (P("vis", None, "row", "col"), P("vis", "row", "col"), P(), P(), P(), P())
    return jax.shard_map(
        local,
        mesh=mesh,
        in_specs=placed,
        out_specs=P(None, ALL, None),
        check_vma=False,
    )
```

```python
import math

import jax
import jax.numpy as jnp
import numpy as np
from jax import lax
from jax.experimental import pallas as pl
from jax.experimental.pallas import tpu as pltpu
from jax.sharding import PartitionSpec as P

BLK = 128
ALL = ("vis", "row", "col")
DIRECT_BYTES = 4 * 2**20
HALO = 2
TILE = 8
LANES = 128


def with_halo(cells, sides, width):
    for axis, dim in sides:
        count = lax.axis_size(axis)
        ends = count - 1
        head = lax.slice_in_dim(cells, 0, width, axis=dim)
        tail = lax.slice_in_dim(cells, cells.shape[dim] - width, cells.shape[dim], axis=dim)
        cells = jnp.concatenate(
            [
                lax.ppermute(tail, axis, [(i, (i + 1) % count) for i in range(ends)]),
                cells,
                lax.ppermute(head, axis, [((i + 1) % count, i) for i in range(ends)]),
            ],
            axis=dim,
        )
    return cells


def phase_table(numer, denom):
    angle = numer.astype(jnp.float32) * (2.0 * math.pi / denom)
    return (jnp.cos(angle), jnp.sin(angle))


def partial_transform(real_part, imag_part, block_of, keep_imag):
    batch = real_part.shape[0]
    count_blocks = real_part.shape[1]
    block_len = real_part.shape[2]
    length = count_blocks * block_len
    highest = lax.Precision.HIGHEST
    outer = jnp.arange(count_blocks, dtype=jnp.int32)
    inner = jnp.arange(block_len, dtype=jnp.int32)
    cos_one, sin_one = phase_table(block_of[:, None] * outer[None, :] % count_blocks, count_blocks)
    mid_re = jnp.einsum("lpt,px->lxt", real_part, cos_one, precision=highest) - jnp.einsum(
        "lpt,px->lxt", imag_part, sin_one, precision=highest
    )
    mid_im = jnp.einsum("lpt,px->lxt", real_part, sin_one, precision=highest) + jnp.einsum(
        "lpt,px->lxt", imag_part, cos_one, precision=highest
    )
    cos_two, sin_two = phase_table(outer[:, None] * inner[None, :] % length, length)
    parity = (1 - 2 * (outer % 2)).astype(jnp.float32)[:, None]
    cos_two = cos_two * parity
    sin_two = sin_two * parity
    turn_re = mid_re * cos_two - mid_im * sin_two
    turn_im = mid_re * sin_two + mid_im * cos_two
    kept = jnp.arange(block_len // 2, dtype=jnp.int32)
    picked = (kept + 3 * block_len // 4) % block_len
    cos_three, sin_three = phase_table(inner[:, None] * picked[None, :] % block_len, block_len)
    out_re = jnp.einsum("lxt,tj->ljx", turn_re, cos_three, precision=highest) - jnp.einsum(
        "lxt,tj->ljx", turn_im, sin_three, precision=highest
    )
    out_re = out_re.reshape(batch, length // 2)
    if keep_imag:
        out_im = jnp.einsum("lxt,tj->ljx", turn_re, sin_three, precision=highest) + jnp.einsum(
            "lxt,tj->ljx", turn_im, cos_three, precision=highest
        )
        return (out_re, out_im.reshape(batch, length // 2))
    return (out_re, out_re)


def first_layer(extended, conv_one, bias_one, count_rows):
    width = extended.shape[1]
    padded = jnp.pad(extended, ((0, 0), (1, 1)))
    summed = (
        jnp.zeros((conv_one.shape[0], count_rows, width), jnp.float32) + bias_one[:, None, None]
    )
    for shift_b in range(3):
        for shift_a in range(3):
            summed = (
                summed
                + conv_one[:, shift_b, shift_a][:, None, None]
                * padded[None, shift_b : shift_b + count_rows, shift_a : shift_a + width]
            )
    return jnp.maximum(summed, 0.0)


def second_layer(hidden_ext, conv_two, bias_two, count_rows):
    width = hidden_ext.shape[2]
    padded = jnp.pad(hidden_ext, ((0, 0), (0, 0), (1, 1)))
    summed = jnp.zeros((conv_two.shape[2], count_rows, width), jnp.float32)
    for shift_b in range(3):
        for shift_a in range(3):
            summed = summed + jnp.einsum(
                "kj,jba->kba",
                conv_two[shift_b, shift_a],
                padded[:, shift_b : shift_b + count_rows, shift_a : shift_a + width],
                preferred_element_type=jnp.float32,
            )
    return (summed + bias_two[:, None, None]).astype(jnp.bfloat16)


def staged(partials, coverage, conv_one, bias_one, conv_two, bias_two):
    count_vis = lax.axis_size("vis")
    count_row = lax.axis_size("row")
    count_col = lax.axis_size("col")
    grid_len = partials.shape[3] * count_col
    cover = coverage[0]
    block_rows = cover.shape[0]
    block_cols = cover.shape[1]
    spread = jnp.broadcast_to(cover[:, None, :, None], (block_rows, BLK, block_cols, BLK))
    spread = spread.reshape(block_rows * BLK, block_cols * BLK)
    count_blocks = count_vis * count_row
    row_block = grid_len // count_blocks
    row_share = row_block // count_col
    masked = partials[0] * spread.astype(jnp.bfloat16)[None]
    reduced = lax.psum_scatter(
        masked.astype(jnp.float32).astype(jnp.bfloat16), "vis", scatter_dimension=1, tiled=True
    ).astype(jnp.float32)
    grid_rows = lax.all_to_all(
        reduced.astype(jnp.bfloat16), "col", split_axis=1, concat_axis=2, tiled=True
    ).astype(reduced.dtype)
    natural = jnp.arange(count_blocks, dtype=jnp.int32)
    shaped = grid_rows.reshape(2, row_share, count_blocks, row_block)
    first_re, first_im = partial_transform(shaped[0], shaped[1], natural, True)
    stacked = jnp.stack([first_re, first_im])
    moved = lax.all_to_all(
        lax.all_to_all(
            stacked.astype(jnp.bfloat16), ("vis", "row"), split_axis=2, concat_axis=1, tiled=True
        ),
        "col",
        split_axis=2,
        concat_axis=1,
        tiled=True,
    ).astype(stacked.dtype)
    img_rows = moved.shape[2]
    arranged = moved.reshape(2, count_col, count_blocks, row_share, img_rows)
    arranged = arranged.transpose(0, 4, 2, 1, 3).reshape(2, img_rows, count_blocks, row_block)
    owners = natural % count_row * count_vis + natural // count_row
    image, unused = partial_transform(arranged[0], arranged[1], owners, False)
    image = image * (1.0 / grid_len)
    extended = with_halo(image.astype(jnp.bfloat16), ((("vis", "row", "col"), 0),), 1).astype(
        image.dtype
    )
    hidden = first_layer(extended, conv_one, bias_one, img_rows).astype(jnp.bfloat16)
    hidden_ext = with_halo(hidden, ((("vis", "row", "col"), 1),), 1)
    return second_layer(hidden_ext, conv_two, bias_two, img_rows)


def grid_tables(length, count_row, count_col):
    image_len = length // 2
    place = np.arange(length)[:, None] - length // 2
    pixel = np.arange(image_len)[None, :] - image_len // 2
    angle = (place * pixel % length) * (2.0 * math.pi / length)
    cos, sin = np.cos(angle), np.sin(angle)
    padded = np.pad(np.stack([cos.T, sin.T]), ((0, 0), (HALO, TILE - HALO), (0, 0)))
    first = padded.reshape(2 * (image_len + TILE), count_col, length // count_col).transpose(1, 0, 2)
    rows = length // count_row
    second = np.stack([cos.reshape(count_row, rows, image_len), -sin.reshape(count_row, rows, image_len)], axis=1)
    second = second.reshape(2 * length, image_len) / length
    return first.astype(jnp.bfloat16), second.astype(jnp.bfloat16)


def send_order():
    vis, row, col = (lax.axis_size(axis) for axis in ALL)
    pairs = 2 if vis % 2 == 0 else 1
    places = np.arange(vis * row * col).reshape(vis // pairs, pairs, row, col)
    return np.roll(places, -1, axis=2).reshape(-1).tolist()


def share_kernel(cover_in, parts_in, first_all, out, cover, parts, first, sems):
    get_cover = pltpu.make_async_copy(cover_in, cover, sems.at[0])
    get_parts = pltpu.make_async_copy(parts_in, parts, sems.at[1])
    get_first = pltpu.make_async_copy(first_all.at[lax.axis_index("col")], first, sems.at[2])
    for copy in (get_cover, get_parts, get_first):
        copy.start()
    count_rows = parts.shape[2]
    get_cover.wait()
    get_parts.wait()
    components = []
    for component in range(2):
        strips = []
        for i in range(cover.shape[1]):
            cells = []
            for j in range(cover.shape[2]):
                block = parts[0, component, i * BLK : (i + 1) * BLK, j * BLK : (j + 1) * BLK]
                level = jnp.full(block.shape, cover[0, i, j].astype(jnp.float32)).astype(jnp.bfloat16)
                cells.append(block * level)
            strips.append(jnp.concatenate(cells, axis=1))
        components.append(jnp.concatenate(strips, axis=0))
    grid = jnp.concatenate(components, axis=0)
    upper = lax.broadcasted_iota(jnp.int32, (TILE, LANES), 0) < TILE // 2
    tall = first.shape[0] // 2
    get_first.wait()
    turned = lax.dot_general(first[...], grid, (((1,), (1,)), ((), ())), preferred_element_type=jnp.float32)
    mid_re = turned[:tall, :count_rows] - turned[tall:, count_rows:]
    mid_im = turned[tall:, :count_rows] + turned[:tall, count_rows:]
    for slot, device in enumerate(send_order()):
        here = slice(TILE * device, TILE * (device + 1))
        below = slice(TILE * (device + 1), TILE * (device + 2))
        middle = jnp.where(upper, mid_re[below], pltpu.roll(mid_im[below], TILE // 2, 0))
        out[slot] = jnp.concatenate([mid_re[here], middle, mid_im[here]], axis=0).astype(out.dtype)


def own_place():
    place, count = 0, 1
    for axis in ALL:
        place = place * lax.axis_size(axis) + lax.axis_index(axis)
        count = count * lax.axis_size(axis)
    return place, count - 1


def four_times(values):
    return jnp.concatenate([values] * 4, axis=1)


def weights_kernel(
    one_in, bias_in, two_in, bias_two_in, table_in, weights_one, weights_two, bias_rows, table, one, bias, two, bias_two, sems
):
    fetch = [
        pltpu.make_async_copy(one_in, one, sems.at[0]),
        pltpu.make_async_copy(bias_in, bias, sems.at[1]),
        pltpu.make_async_copy(two_in, two, sems.at[2]),
        pltpu.make_async_copy(bias_two_in, bias_two, sems.at[3]),
    ]
    get_table = pltpu.make_async_copy(table_in, table, sems.at[4])
    for copy in (*fetch, get_table):
        copy.start()
    for copy in fetch:
        copy.wait()
    channels = one.shape[2]
    rows = TILE + 2
    per_tile = LANES // channels
    lanes = -(-rows * channels // LANES) * LANES
    image_row = lax.broadcasted_iota(jnp.int32, (16, lanes), 0)
    hidden_row = lax.broadcasted_iota(jnp.int32, (16, lanes), 1) // channels
    place, last = own_place()
    held = (hidden_row >= jnp.where(place == 0, 1, 0)) & (hidden_row < jnp.where(place == last, rows - 1, rows))
    high, low = [], []
    for tap in range(3):
        band = jnp.zeros((16, lanes), jnp.float32)
        for shift in range(3):
            line = jnp.concatenate([four_times(one[shift, tap : tap + 1])] * (lanes // LANES), axis=1)
            band = jnp.where(held & (image_row - hidden_row == shift), line, band)
        high.append(band.astype(jnp.bfloat16).astype(jnp.float32))
        low.append(band - high[-1])
    line = jnp.concatenate([four_times(bias[...])] * (lanes // LANES), axis=1)
    with_bias = high[0]
    for piece in range(3):
        rounded = line.astype(jnp.bfloat16).astype(jnp.float32)
        with_bias = jnp.where(held & (image_row == 12 + piece), rounded, with_bias)
        line = line - rounded
    stacked = jnp.concatenate([with_bias, *high[1:], *high, *low], axis=0)
    weights_one[...] = stacked.T[: weights_one.shape[0]].astype(jnp.bfloat16)
    row = lax.broadcasted_iota(jnp.int32, bias_rows.shape, 0) // TILE
    lane = lax.broadcasted_iota(jnp.int32, bias_rows.shape, 1)
    line = jnp.where(row == lane, four_times(bias_two[...]), 0.0)
    bias_rows[...] = jnp.broadcast_to(jnp.sum(line, axis=1, keepdims=True), bias_rows.shape)
    lines = [[four_times(two[shift, tap].astype(jnp.float32)) for shift in range(3)] for tap in range(3)]
    row = lax.broadcasted_iota(jnp.int32, (TILE, LANES), 0)
    lane = lax.broadcasted_iota(jnp.int32, (TILE, LANES), 1) // channels
    zero = jnp.zeros((TILE, LANES), jnp.float32)
    for tile in range(-(-3 * rows // per_tile)):
        taps = sorted({(tile * per_tile + g) // rows for g in range(per_tile)} & {0, 1, 2})
        masks = []
        for tap in taps:
            hidden_row = tile * per_tile + lane - tap * rows
            inside = (hidden_row >= 0) & (hidden_row < rows)
            masks += [(tap, shift, inside & (hidden_row - row == shift)) for shift in range(3)]
        width = min(LANES, weights_two.shape[1] - tile * LANES)
        for channel in range(0, channels, 2):
            pair = []
            for k in (channel, channel + 1):
                values = zero
                for tap, shift, mask in masks:
                    values = jnp.where(mask, lines[tap][shift][k : k + 1], values)
                pair.append(values)
            block = jnp.concatenate(pair, axis=0).astype(jnp.bfloat16)
            weights_two[TILE * channel : TILE * (channel + 2), tile * LANES : tile * LANES + width] = block[:, :width]
    get_table.wait()


def shifted(values, width):
    lane = lax.broadcasted_iota(jnp.int32, values.shape, 1)
    zero = jnp.zeros_like(values)
    before = jnp.where(lane == 0, zero, pltpu.roll(values, 1, 1))
    after = jnp.where(lane == width - 1, zero, pltpu.roll(values, width - 1, 1))
    return before, values, after


def layers_kernel(shares, weights_one, weights_two, bias_rows, table, out, staged, sems):
    width = out.shape[2]
    row, col = lax.axis_size("row"), lax.axis_size("col")
    upper = lax.broadcasted_iota(jnp.int32, (TILE, LANES), 0) < TILE // 2
    above, below = [], []
    for r in range(row):
        senders = [slot for slot, place in enumerate(send_order()) if place // col % row == r]
        total = shares[senders[0]].astype(jnp.float32)
        for sender in senders[1:]:
            total = total + shares[sender].astype(jnp.float32)
        middle = total[TILE : 2 * TILE]
        above += [total[:TILE], total[2 * TILE :]]
        below += [jnp.where(upper, middle, 0.0), jnp.where(upper, pltpu.roll(middle, TILE // 2, 0), 0.0)]
    turned = jnp.concatenate([jnp.concatenate(above, axis=1), jnp.concatenate(below, axis=1)], axis=0)
    high = turned.astype(jnp.bfloat16)
    low = (turned - high.astype(jnp.float32)).astype(jnp.bfloat16)
    image = jnp.dot(jnp.concatenate([high, low], axis=0), table[...], preferred_element_type=jnp.float32)
    image = image[: 2 * TILE] + image[2 * TILE :]
    columns = jnp.concatenate(shifted(image, width), axis=0)
    high = columns.astype(jnp.bfloat16).astype(jnp.float32)
    low = columns - high
    row = lax.broadcasted_iota(jnp.int32, (48, width), 0)
    with_ones = jnp.where((row >= 12) & (row < 15), 1.0, high)
    stacked = jnp.concatenate([with_ones, low, high], axis=0).astype(jnp.bfloat16)
    hidden = jnp.dot(weights_one[...], stacked, preferred_element_type=jnp.float32)
    hidden = jnp.maximum(hidden, 0.0).astype(jnp.bfloat16)
    stacked = jnp.concatenate(shifted(hidden, width), axis=0)
    half = out.shape[0] // 2
    copies = []
    for part in range(2):
        rows = pl.ds(part * half * TILE, half * TILE)
        features = jnp.dot(weights_two[rows], stacked, preferred_element_type=jnp.float32)
        features = features + jnp.concatenate([bias_rows[rows]] * (width // LANES), axis=1)
        channels_of = pl.ds(part * half, half)
        staged[channels_of] = features.reshape(half, TILE, width).astype(out.dtype)
        copies.append(pltpu.make_async_copy(staged.at[channels_of], out.at[channels_of], sems.at[part]))
        copies[-1].start()
    for copy in copies:
        copy.wait()


def in_hbm(*arrays):
    return [pltpu.with_memory_space_constraint(array, pltpu.HBM) for array in arrays]


def direct(partials, coverage, conv_one, bias_one, conv_two, bias_two):
    count_row, count_col = lax.axis_size("row"), lax.axis_size("col")
    devices = lax.axis_size("vis") * count_row * count_col
    length = partials.shape[3] * count_col
    image_len = length // 2
    channels = conv_two.shape[2]
    first, second = grid_tables(length, count_row, count_col)
    vmem, hbm = pl.BlockSpec(memory_space=pltpu.VMEM), pl.BlockSpec(memory_space=pltpu.HBM)
    limit = pltpu.CompilerParams(vmem_limit_bytes=16 * 2**20)
    share = (devices, 2 * (TILE + 2 * HALO), LANES)
    shares = pl.pallas_call(
        share_kernel,
        out_shape=jax.ShapeDtypeStruct(share, jnp.bfloat16),
        in_specs=[hbm] * 3,
        out_specs=vmem,
        scratch_shapes=[
            pltpu.SMEM(coverage.shape, jnp.int32),
            pltpu.VMEM(partials.shape, jnp.bfloat16),
            pltpu.VMEM(first.shape[1:], jnp.bfloat16),
            pltpu.SemaphoreType.DMA((3,)),
        ],
        compiler_params=limit,
        name="shares",
    )(*in_hbm(coverage, partials, jnp.asarray(first)))
    arrived = lax.all_to_all(
        shares, ALL, split_axis=0, concat_axis=0, tiled=True, axis_index_groups=[send_order()]
    )
    rows = TILE + 2
    weights = pl.pallas_call(
        weights_kernel,
        out_shape=[
            jax.ShapeDtypeStruct((rows * channels, 3 * 48), jnp.bfloat16),
            jax.ShapeDtypeStruct((TILE * channels, 3 * rows * channels), jnp.bfloat16),
            jax.ShapeDtypeStruct((TILE * channels, LANES), jnp.float32),
            jax.ShapeDtypeStruct(second.shape, jnp.bfloat16),
        ],
        in_specs=[hbm] * 5,
        out_specs=[vmem] * 4,
        scratch_shapes=[
            pltpu.VMEM((3, 3, channels), jnp.float32),
            pltpu.VMEM((1, channels), jnp.float32),
            pltpu.VMEM(conv_two.shape, jnp.bfloat16),
            pltpu.VMEM((1, channels), jnp.float32),
            pltpu.SemaphoreType.DMA((5,)),
        ],
        compiler_params=limit,
        name="weights",
    )(*in_hbm(conv_one.transpose(1, 2, 0), bias_one[None], conv_two, bias_two[None], jnp.asarray(second)))
    return pl.pallas_call(
        layers_kernel,
        out_shape=jax.ShapeDtypeStruct((channels, TILE, image_len), jnp.bfloat16),
        in_specs=[vmem] * 5,
        out_specs=hbm,
        scratch_shapes=[
            pltpu.VMEM((channels, TILE, image_len), jnp.bfloat16),
            pltpu.SemaphoreType.DMA((2,)),
        ],
        compiler_params=limit,
        name="layers",
    )(arrived, *weights)


def local(partials, coverage, conv_one, bias_one, conv_two, bias_two):
    count_col = lax.axis_size("col")
    devices = lax.axis_size("vis") * lax.axis_size("row") * count_col
    image_len = partials.shape[3] * count_col // 2
    sent = devices * (TILE + 2 * HALO) * image_len * 2
    fits = partials.shape[2] == LANES and image_len == devices * TILE and conv_two.shape[2] * 4 == LANES and image_len == 2 * LANES and sent <= DIRECT_BYTES
    plan = direct if fits else staged
    return plan(partials, coverage, conv_one, bias_one, conv_two, bias_two)


def solution(mesh):
    placed = (P("vis", None, "row", "col"), P("vis", "row", "col"), P(), P(), P(), P())
    return jax.shard_map(
        local,
        mesh=mesh,
        in_specs=placed,
        out_specs=P(None, ALL, None),
        check_vma=False,
    )
```

```python
import math

import jax
import jax.numpy as jnp
import numpy as np
from jax import lax
from jax.experimental import pallas as pl
from jax.experimental.pallas import tpu as pltpu
from jax.sharding import PartitionSpec as P

BLK = 128
ALL = ("vis", "row", "col")
DIRECT_BYTES = 4 * 2**20
HALO = 2
TILE = 8
LANES = 128


def with_halo(cells, sides, width):
    for axis, dim in sides:
        count = lax.axis_size(axis)
        ends = count - 1
        head = lax.slice_in_dim(cells, 0, width, axis=dim)
        tail = lax.slice_in_dim(cells, cells.shape[dim] - width, cells.shape[dim], axis=dim)
        cells = jnp.concatenate(
            [
                lax.ppermute(tail, axis, [(i, (i + 1) % count) for i in range(ends)]),
                cells,
                lax.ppermute(head, axis, [((i + 1) % count, i) for i in range(ends)]),
            ],
            axis=dim,
        )
    return cells


def phase_table(numer, denom):
    angle = numer.astype(jnp.float32) * (2.0 * math.pi / denom)
    return (jnp.cos(angle), jnp.sin(angle))


def partial_transform(real_part, imag_part, block_of, keep_imag):
    batch = real_part.shape[0]
    count_blocks = real_part.shape[1]
    block_len = real_part.shape[2]
    length = count_blocks * block_len
    highest = lax.Precision.HIGHEST
    outer = jnp.arange(count_blocks, dtype=jnp.int32)
    inner = jnp.arange(block_len, dtype=jnp.int32)
    cos_one, sin_one = phase_table(block_of[:, None] * outer[None, :] % count_blocks, count_blocks)
    mid_re = jnp.einsum("lpt,px->lxt", real_part, cos_one, precision=highest) - jnp.einsum(
        "lpt,px->lxt", imag_part, sin_one, precision=highest
    )
    mid_im = jnp.einsum("lpt,px->lxt", real_part, sin_one, precision=highest) + jnp.einsum(
        "lpt,px->lxt", imag_part, cos_one, precision=highest
    )
    cos_two, sin_two = phase_table(outer[:, None] * inner[None, :] % length, length)
    parity = (1 - 2 * (outer % 2)).astype(jnp.float32)[:, None]
    cos_two = cos_two * parity
    sin_two = sin_two * parity
    turn_re = mid_re * cos_two - mid_im * sin_two
    turn_im = mid_re * sin_two + mid_im * cos_two
    kept = jnp.arange(block_len // 2, dtype=jnp.int32)
    picked = (kept + 3 * block_len // 4) % block_len
    cos_three, sin_three = phase_table(inner[:, None] * picked[None, :] % block_len, block_len)
    out_re = jnp.einsum("lxt,tj->ljx", turn_re, cos_three, precision=highest) - jnp.einsum(
        "lxt,tj->ljx", turn_im, sin_three, precision=highest
    )
    out_re = out_re.reshape(batch, length // 2)
    if keep_imag:
        out_im = jnp.einsum("lxt,tj->ljx", turn_re, sin_three, precision=highest) + jnp.einsum(
            "lxt,tj->ljx", turn_im, cos_three, precision=highest
        )
        return (out_re, out_im.reshape(batch, length // 2))
    return (out_re, out_re)


def first_layer(extended, conv_one, bias_one, count_rows):
    width = extended.shape[1]
    padded = jnp.pad(extended, ((0, 0), (1, 1)))
    summed = (
        jnp.zeros((conv_one.shape[0], count_rows, width), jnp.float32) + bias_one[:, None, None]
    )
    for shift_b in range(3):
        for shift_a in range(3):
            summed = (
                summed
                + conv_one[:, shift_b, shift_a][:, None, None]
                * padded[None, shift_b : shift_b + count_rows, shift_a : shift_a + width]
            )
    return jnp.maximum(summed, 0.0)


def second_layer(hidden_ext, conv_two, bias_two, count_rows):
    width = hidden_ext.shape[2]
    padded = jnp.pad(hidden_ext, ((0, 0), (0, 0), (1, 1)))
    summed = jnp.zeros((conv_two.shape[2], count_rows, width), jnp.float32)
    for shift_b in range(3):
        for shift_a in range(3):
            summed = summed + jnp.einsum(
                "kj,jba->kba",
                conv_two[shift_b, shift_a],
                padded[:, shift_b : shift_b + count_rows, shift_a : shift_a + width],
                preferred_element_type=jnp.float32,
            )
    return (summed + bias_two[:, None, None]).astype(jnp.bfloat16)


def staged(partials, coverage, conv_one, bias_one, conv_two, bias_two):
    count_vis = lax.axis_size("vis")
    count_row = lax.axis_size("row")
    count_col = lax.axis_size("col")
    grid_len = partials.shape[3] * count_col
    cover = coverage[0]
    block_rows = cover.shape[0]
    block_cols = cover.shape[1]
    spread = jnp.broadcast_to(cover[:, None, :, None], (block_rows, BLK, block_cols, BLK))
    spread = spread.reshape(block_rows * BLK, block_cols * BLK)
    count_blocks = count_vis * count_row
    row_block = grid_len // count_blocks
    row_share = row_block // count_col
    masked = partials[0] * spread.astype(jnp.bfloat16)[None]
    reduced = lax.psum_scatter(
        masked.astype(jnp.float32).astype(jnp.bfloat16), "vis", scatter_dimension=1, tiled=True
    ).astype(jnp.float32)
    grid_rows = lax.all_to_all(
        reduced.astype(jnp.bfloat16), "col", split_axis=1, concat_axis=2, tiled=True
    ).astype(reduced.dtype)
    natural = jnp.arange(count_blocks, dtype=jnp.int32)
    shaped = grid_rows.reshape(2, row_share, count_blocks, row_block)
    first_re, first_im = partial_transform(shaped[0], shaped[1], natural, True)
    stacked = jnp.stack([first_re, first_im])
    moved = lax.all_to_all(
        lax.all_to_all(
            stacked.astype(jnp.bfloat16), ("vis", "row"), split_axis=2, concat_axis=1, tiled=True
        ),
        "col",
        split_axis=2,
        concat_axis=1,
        tiled=True,
    ).astype(stacked.dtype)
    img_rows = moved.shape[2]
    arranged = moved.reshape(2, count_col, count_blocks, row_share, img_rows)
    arranged = arranged.transpose(0, 4, 2, 1, 3).reshape(2, img_rows, count_blocks, row_block)
    owners = natural % count_row * count_vis + natural // count_row
    image, unused = partial_transform(arranged[0], arranged[1], owners, False)
    image = image * (1.0 / grid_len)
    extended = with_halo(image.astype(jnp.bfloat16), ((("vis", "row", "col"), 0),), 1).astype(
        image.dtype
    )
    hidden = first_layer(extended, conv_one, bias_one, img_rows).astype(jnp.bfloat16)
    hidden_ext = with_halo(hidden, ((("vis", "row", "col"), 1),), 1)
    return second_layer(hidden_ext, conv_two, bias_two, img_rows)


def grid_tables(length, count_row, count_col):
    image_len = length // 2
    place = np.arange(length)[:, None] - length // 2
    pixel = np.arange(image_len)[None, :] - image_len // 2
    angle = (place * pixel % length) * (2.0 * math.pi / length)
    cos, sin = np.cos(angle), np.sin(angle)
    padded = np.pad(np.stack([cos.T, sin.T]), ((0, 0), (HALO, TILE - HALO), (0, 0)))
    first = padded.reshape(2 * (image_len + TILE), count_col, length // count_col).transpose(1, 0, 2)
    rows = length // count_row
    second = np.stack([cos.reshape(count_row, rows, image_len), -sin.reshape(count_row, rows, image_len)], axis=1)
    second = second.reshape(2 * length, image_len) / length
    return first.astype(jnp.bfloat16), second.astype(jnp.bfloat16)


def share_kernel(cover_in, parts_in, first_all, out, cover, parts, first, sems):
    get_cover = pltpu.make_async_copy(cover_in, cover, sems.at[0])
    get_parts = pltpu.make_async_copy(parts_in, parts, sems.at[1])
    get_first = pltpu.make_async_copy(first_all.at[lax.axis_index("col")], first, sems.at[2])
    for copy in (get_cover, get_parts, get_first):
        copy.start()
    count_rows = parts.shape[2]
    get_cover.wait()
    get_parts.wait()
    components = []
    for component in range(2):
        strips = []
        for i in range(cover.shape[1]):
            cells = []
            for j in range(cover.shape[2]):
                block = parts[0, component, i * BLK : (i + 1) * BLK, j * BLK : (j + 1) * BLK]
                level = jnp.full(block.shape, cover[0, i, j].astype(jnp.float32)).astype(jnp.bfloat16)
                cells.append(block * level)
            strips.append(jnp.concatenate(cells, axis=1))
        components.append(jnp.concatenate(strips, axis=0))
    grid = jnp.concatenate(components, axis=0)
    upper = lax.broadcasted_iota(jnp.int32, (TILE, LANES), 0) < TILE // 2
    devices = out.shape[0]
    tall = first.shape[0] // 2
    get_first.wait()
    turned = lax.dot_general(first[...], grid, (((1,), (1,)), ((), ())), preferred_element_type=jnp.float32)
    mid_re = turned[:tall, :count_rows] - turned[tall:, count_rows:]
    mid_im = turned[tall:, :count_rows] + turned[:tall, count_rows:]
    for device in range(devices):
        here = slice(TILE * device, TILE * (device + 1))
        below = slice(TILE * (device + 1), TILE * (device + 2))
        middle = jnp.where(upper, mid_re[below], pltpu.roll(mid_im[below], TILE // 2, 0))
        out[device] = jnp.concatenate([mid_re[here], middle, mid_im[here]], axis=0).astype(out.dtype)


def own_place():
    place, count = 0, 1
    for axis in ALL:
        place = place * lax.axis_size(axis) + lax.axis_index(axis)
        count = count * lax.axis_size(axis)
    return place, count - 1


def four_times(values):
    return jnp.concatenate([values] * 4, axis=1)


def weights_kernel(
    one_in, bias_in, two_in, bias_two_in, table_in, weights_one, weights_two, bias_rows, table, one, bias, two, bias_two, sems
):
    fetch = [
        pltpu.make_async_copy(one_in, one, sems.at[0]),
        pltpu.make_async_copy(bias_in, bias, sems.at[1]),
        pltpu.make_async_copy(two_in, two, sems.at[2]),
        pltpu.make_async_copy(bias_two_in, bias_two, sems.at[3]),
    ]
    get_table = pltpu.make_async_copy(table_in, table, sems.at[4])
    for copy in (*fetch, get_table):
        copy.start()
    for copy in fetch:
        copy.wait()
    channels = one.shape[2]
    rows = TILE + 2
    per_tile = LANES // channels
    lanes = -(-rows * channels // LANES) * LANES
    image_row = lax.broadcasted_iota(jnp.int32, (16, lanes), 0)
    hidden_row = lax.broadcasted_iota(jnp.int32, (16, lanes), 1) // channels
    place, last = own_place()
    held = (hidden_row >= jnp.where(place == 0, 1, 0)) & (hidden_row < jnp.where(place == last, rows - 1, rows))
    high, low = [], []
    for tap in range(3):
        band = jnp.zeros((16, lanes), jnp.float32)
        for shift in range(3):
            line = jnp.concatenate([four_times(one[shift, tap : tap + 1])] * (lanes // LANES), axis=1)
            band = jnp.where(held & (image_row - hidden_row == shift), line, band)
        high.append(band.astype(jnp.bfloat16).astype(jnp.float32))
        low.append(band - high[-1])
    line = jnp.concatenate([four_times(bias[...])] * (lanes // LANES), axis=1)
    with_bias = high[0]
    for piece in range(3):
        rounded = line.astype(jnp.bfloat16).astype(jnp.float32)
        with_bias = jnp.where(held & (image_row == 12 + piece), rounded, with_bias)
        line = line - rounded
    stacked = jnp.concatenate([with_bias, *high[1:], *high, *low], axis=0)
    weights_one[...] = stacked.T[: weights_one.shape[0]].astype(jnp.bfloat16)
    row = lax.broadcasted_iota(jnp.int32, bias_rows.shape, 0) // TILE
    lane = lax.broadcasted_iota(jnp.int32, bias_rows.shape, 1)
    line = jnp.where(row == lane, four_times(bias_two[...]), 0.0)
    bias_rows[...] = jnp.broadcast_to(jnp.sum(line, axis=1, keepdims=True), bias_rows.shape)
    lines = [[four_times(two[shift, tap].astype(jnp.float32)) for shift in range(3)] for tap in range(3)]
    row = lax.broadcasted_iota(jnp.int32, (TILE, LANES), 0)
    lane = lax.broadcasted_iota(jnp.int32, (TILE, LANES), 1) // channels
    zero = jnp.zeros((TILE, LANES), jnp.float32)
    for tile in range(-(-3 * rows // per_tile)):
        taps = sorted({(tile * per_tile + g) // rows for g in range(per_tile)} & {0, 1, 2})
        masks = []
        for tap in taps:
            hidden_row = tile * per_tile + lane - tap * rows
            inside = (hidden_row >= 0) & (hidden_row < rows)
            masks += [(tap, shift, inside & (hidden_row - row == shift)) for shift in range(3)]
        width = min(LANES, weights_two.shape[1] - tile * LANES)
        for channel in range(0, channels, 2):
            pair = []
            for k in (channel, channel + 1):
                values = zero
                for tap, shift, mask in masks:
                    values = jnp.where(mask, lines[tap][shift][k : k + 1], values)
                pair.append(values)
            block = jnp.concatenate(pair, axis=0).astype(jnp.bfloat16)
            weights_two[TILE * channel : TILE * (channel + 2), tile * LANES : tile * LANES + width] = block[:, :width]
    get_table.wait()


def shifted(values, width):
    lane = lax.broadcasted_iota(jnp.int32, values.shape, 1)
    zero = jnp.zeros_like(values)
    before = jnp.where(lane == 0, zero, pltpu.roll(values, 1, 1))
    after = jnp.where(lane == width - 1, zero, pltpu.roll(values, width - 1, 1))
    return before, values, after


def layers_kernel(shares, weights_one, weights_two, bias_rows, table, out, staged, sems):
    width = out.shape[2]
    vis, row, col = (lax.axis_size(axis) for axis in ALL)
    upper = lax.broadcasted_iota(jnp.int32, (TILE, 2 * LANES), 0) < TILE // 2
    depth = 2 * LANES
    image = jnp.zeros((4 * TILE, width), jnp.float32)
    for r in range(row):
        senders = [(v * row + r) * col + c for v in range(vis) for c in range(col)]
        total = shares[senders[0]].astype(jnp.float32)
        for sender in senders[1:]:
            total = total + shares[sender].astype(jnp.float32)
        middle = total[TILE : 2 * TILE]
        above = jnp.concatenate([total[:TILE], total[2 * TILE :]], axis=1)
        below = jnp.concatenate([middle, pltpu.roll(middle, TILE // 2, 0)], axis=1)
        turned = jnp.concatenate([above, jnp.where(upper, below, 0.0)], axis=0)
        high = turned.astype(jnp.bfloat16)
        low = (turned - high.astype(jnp.float32)).astype(jnp.bfloat16)
        block = table[r * depth : (r + 1) * depth]
        image = image + jnp.dot(jnp.concatenate([high, low], axis=0), block, preferred_element_type=jnp.float32)
    image = image[: 2 * TILE] + image[2 * TILE :]
    columns = jnp.concatenate(shifted(image, width), axis=0)
    high = columns.astype(jnp.bfloat16).astype(jnp.float32)
    low = columns - high
    row = lax.broadcasted_iota(jnp.int32, (48, width), 0)
    with_ones = jnp.where((row >= 12) & (row < 15), 1.0, high)
    stacked = jnp.concatenate([with_ones, low, high], axis=0).astype(jnp.bfloat16)
    hidden = jnp.dot(weights_one[...], stacked, preferred_element_type=jnp.float32)
    hidden = jnp.maximum(hidden, 0.0).astype(jnp.bfloat16)
    stacked = jnp.concatenate(shifted(hidden, width), axis=0)
    half = out.shape[0] // 2
    copies = []
    for part in range(2):
        rows = pl.ds(part * half * TILE, half * TILE)
        features = jnp.dot(weights_two[rows], stacked, preferred_element_type=jnp.float32)
        features = features + jnp.concatenate([bias_rows[rows]] * (width // LANES), axis=1)
        channels_of = pl.ds(part * half, half)
        staged[channels_of] = features.reshape(half, TILE, width).astype(out.dtype)
        copies.append(pltpu.make_async_copy(staged.at[channels_of], out.at[channels_of], sems.at[part]))
        copies[-1].start()
    for copy in copies:
        copy.wait()


def in_hbm(*arrays):
    return [pltpu.with_memory_space_constraint(array, pltpu.HBM) for array in arrays]


def direct(partials, coverage, conv_one, bias_one, conv_two, bias_two):
    count_row, count_col = lax.axis_size("row"), lax.axis_size("col")
    devices = lax.axis_size("vis") * count_row * count_col
    length = partials.shape[3] * count_col
    image_len = length // 2
    channels = conv_two.shape[2]
    first, second = grid_tables(length, count_row, count_col)
    vmem, hbm = pl.BlockSpec(memory_space=pltpu.VMEM), pl.BlockSpec(memory_space=pltpu.HBM)
    limit = pltpu.CompilerParams(vmem_limit_bytes=16 * 2**20)
    share = (devices, 2 * (TILE + 2 * HALO), LANES)
    shares = pl.pallas_call(
        share_kernel,
        out_shape=jax.ShapeDtypeStruct(share, jnp.bfloat16),
        in_specs=[hbm] * 3,
        out_specs=vmem,
        scratch_shapes=[
            pltpu.SMEM(coverage.shape, jnp.int32),
            pltpu.VMEM(partials.shape, jnp.bfloat16),
            pltpu.VMEM(first.shape[1:], jnp.bfloat16),
            pltpu.SemaphoreType.DMA((3,)),
        ],
        compiler_params=limit,
        name="shares",
    )(*in_hbm(coverage, partials, jnp.asarray(first)))
    arrived = lax.all_to_all(shares, ALL, split_axis=0, concat_axis=0, tiled=True)
    rows = TILE + 2
    weights = pl.pallas_call(
        weights_kernel,
        out_shape=[
            jax.ShapeDtypeStruct((rows * channels, 3 * 48), jnp.bfloat16),
            jax.ShapeDtypeStruct((TILE * channels, 3 * rows * channels), jnp.bfloat16),
            jax.ShapeDtypeStruct((TILE * channels, LANES), jnp.float32),
            jax.ShapeDtypeStruct(second.shape, jnp.bfloat16),
        ],
        in_specs=[hbm] * 5,
        out_specs=[vmem] * 4,
        scratch_shapes=[
            pltpu.VMEM((3, 3, channels), jnp.float32),
            pltpu.VMEM((1, channels), jnp.float32),
            pltpu.VMEM(conv_two.shape, jnp.bfloat16),
            pltpu.VMEM((1, channels), jnp.float32),
            pltpu.SemaphoreType.DMA((5,)),
        ],
        compiler_params=limit,
        name="weights",
    )(*in_hbm(conv_one.transpose(1, 2, 0), bias_one[None], conv_two, bias_two[None], jnp.asarray(second)))
    return pl.pallas_call(
        layers_kernel,
        out_shape=jax.ShapeDtypeStruct((channels, TILE, image_len), jnp.bfloat16),
        in_specs=[vmem] * 5,
        out_specs=hbm,
        scratch_shapes=[
            pltpu.VMEM((channels, TILE, image_len), jnp.bfloat16),
            pltpu.SemaphoreType.DMA((2,)),
        ],
        compiler_params=limit,
        name="layers",
    )(arrived, *weights)


def local(partials, coverage, conv_one, bias_one, conv_two, bias_two):
    count_col = lax.axis_size("col")
    devices = lax.axis_size("vis") * lax.axis_size("row") * count_col
    image_len = partials.shape[3] * count_col // 2
    sent = devices * (TILE + 2 * HALO) * image_len * 2
    fits = partials.shape[2] == LANES and image_len == devices * TILE and conv_two.shape[2] * 4 == LANES and image_len == 2 * LANES and sent <= DIRECT_BYTES
    plan = direct if fits else staged
    return plan(partials, coverage, conv_one, bias_one, conv_two, bias_two)


def solution(mesh):
    placed = (P("vis", None, "row", "col"), P("vis", "row", "col"), P(), P(), P(), P())
    return jax.shard_map(
        local,
        mesh=mesh,
        in_specs=placed,
        out_specs=P(None, ALL, None),
        check_vma=False,
    )
```

```python
import math

import jax
import jax.numpy as jnp
import numpy as np
from jax import lax
from jax.experimental import pallas as pl
from jax.experimental.pallas import tpu as pltpu
from jax.sharding import PartitionSpec as P

BLK = 128
ALL = ("vis", "row", "col")
DIRECT_BYTES = 4 * 2**20
HALO = 2
TILE = 8
LANES = 128


def with_halo(cells, sides, width):
    for axis, dim in sides:
        count = lax.axis_size(axis)
        ends = count - 1
        head = lax.slice_in_dim(cells, 0, width, axis=dim)
        tail = lax.slice_in_dim(cells, cells.shape[dim] - width, cells.shape[dim], axis=dim)
        cells = jnp.concatenate(
            [
                lax.ppermute(tail, axis, [(i, (i + 1) % count) for i in range(ends)]),
                cells,
                lax.ppermute(head, axis, [((i + 1) % count, i) for i in range(ends)]),
            ],
            axis=dim,
        )
    return cells


def phase_table(numer, denom):
    angle = numer.astype(jnp.float32) * (2.0 * math.pi / denom)
    return (jnp.cos(angle), jnp.sin(angle))


def partial_transform(real_part, imag_part, block_of, keep_imag):
    batch = real_part.shape[0]
    count_blocks = real_part.shape[1]
    block_len = real_part.shape[2]
    length = count_blocks * block_len
    highest = lax.Precision.HIGHEST
    outer = jnp.arange(count_blocks, dtype=jnp.int32)
    inner = jnp.arange(block_len, dtype=jnp.int32)
    cos_one, sin_one = phase_table(block_of[:, None] * outer[None, :] % count_blocks, count_blocks)
    mid_re = jnp.einsum("lpt,px->lxt", real_part, cos_one, precision=highest) - jnp.einsum(
        "lpt,px->lxt", imag_part, sin_one, precision=highest
    )
    mid_im = jnp.einsum("lpt,px->lxt", real_part, sin_one, precision=highest) + jnp.einsum(
        "lpt,px->lxt", imag_part, cos_one, precision=highest
    )
    cos_two, sin_two = phase_table(outer[:, None] * inner[None, :] % length, length)
    parity = (1 - 2 * (outer % 2)).astype(jnp.float32)[:, None]
    cos_two = cos_two * parity
    sin_two = sin_two * parity
    turn_re = mid_re * cos_two - mid_im * sin_two
    turn_im = mid_re * sin_two + mid_im * cos_two
    kept = jnp.arange(block_len // 2, dtype=jnp.int32)
    picked = (kept + 3 * block_len // 4) % block_len
    cos_three, sin_three = phase_table(inner[:, None] * picked[None, :] % block_len, block_len)
    out_re = jnp.einsum("lxt,tj->ljx", turn_re, cos_three, precision=highest) - jnp.einsum(
        "lxt,tj->ljx", turn_im, sin_three, precision=highest
    )
    out_re = out_re.reshape(batch, length // 2)
    if keep_imag:
        out_im = jnp.einsum("lxt,tj->ljx", turn_re, sin_three, precision=highest) + jnp.einsum(
            "lxt,tj->ljx", turn_im, cos_three, precision=highest
        )
        return (out_re, out_im.reshape(batch, length // 2))
    return (out_re, out_re)


def first_layer(extended, conv_one, bias_one, count_rows):
    width = extended.shape[1]
    padded = jnp.pad(extended, ((0, 0), (1, 1)))
    summed = (
        jnp.zeros((conv_one.shape[0], count_rows, width), jnp.float32) + bias_one[:, None, None]
    )
    for shift_b in range(3):
        for shift_a in range(3):
            summed = (
                summed
                + conv_one[:, shift_b, shift_a][:, None, None]
                * padded[None, shift_b : shift_b + count_rows, shift_a : shift_a + width]
            )
    return jnp.maximum(summed, 0.0)


def second_layer(hidden_ext, conv_two, bias_two, count_rows):
    width = hidden_ext.shape[2]
    padded = jnp.pad(hidden_ext, ((0, 0), (0, 0), (1, 1)))
    summed = jnp.zeros((conv_two.shape[2], count_rows, width), jnp.float32)
    for shift_b in range(3):
        for shift_a in range(3):
            summed = summed + jnp.einsum(
                "kj,jba->kba",
                conv_two[shift_b, shift_a],
                padded[:, shift_b : shift_b + count_rows, shift_a : shift_a + width],
                preferred_element_type=jnp.float32,
            )
    return (summed + bias_two[:, None, None]).astype(jnp.bfloat16)


def staged(partials, coverage, conv_one, bias_one, conv_two, bias_two):
    count_vis = lax.axis_size("vis")
    count_row = lax.axis_size("row")
    count_col = lax.axis_size("col")
    grid_len = partials.shape[3] * count_col
    cover = coverage[0]
    block_rows = cover.shape[0]
    block_cols = cover.shape[1]
    spread = jnp.broadcast_to(cover[:, None, :, None], (block_rows, BLK, block_cols, BLK))
    spread = spread.reshape(block_rows * BLK, block_cols * BLK)
    count_blocks = count_vis * count_row
    row_block = grid_len // count_blocks
    row_share = row_block // count_col
    masked = partials[0] * spread.astype(jnp.bfloat16)[None]
    reduced = lax.psum_scatter(
        masked.astype(jnp.float32).astype(jnp.bfloat16), "vis", scatter_dimension=1, tiled=True
    ).astype(jnp.float32)
    grid_rows = lax.all_to_all(
        reduced.astype(jnp.bfloat16), "col", split_axis=1, concat_axis=2, tiled=True
    ).astype(reduced.dtype)
    natural = jnp.arange(count_blocks, dtype=jnp.int32)
    shaped = grid_rows.reshape(2, row_share, count_blocks, row_block)
    first_re, first_im = partial_transform(shaped[0], shaped[1], natural, True)
    stacked = jnp.stack([first_re, first_im])
    moved = lax.all_to_all(
        lax.all_to_all(
            stacked.astype(jnp.bfloat16), ("vis", "row"), split_axis=2, concat_axis=1, tiled=True
        ),
        "col",
        split_axis=2,
        concat_axis=1,
        tiled=True,
    ).astype(stacked.dtype)
    img_rows = moved.shape[2]
    arranged = moved.reshape(2, count_col, count_blocks, row_share, img_rows)
    arranged = arranged.transpose(0, 4, 2, 1, 3).reshape(2, img_rows, count_blocks, row_block)
    owners = natural % count_row * count_vis + natural // count_row
    image, unused = partial_transform(arranged[0], arranged[1], owners, False)
    image = image * (1.0 / grid_len)
    extended = with_halo(image.astype(jnp.bfloat16), ((("vis", "row", "col"), 0),), 1).astype(
        image.dtype
    )
    hidden = first_layer(extended, conv_one, bias_one, img_rows).astype(jnp.bfloat16)
    hidden_ext = with_halo(hidden, ((("vis", "row", "col"), 1),), 1)
    return second_layer(hidden_ext, conv_two, bias_two, img_rows)


def grid_tables(length, count_row, count_col):
    image_len = length // 2
    place = np.arange(length)[:, None] - length // 2
    pixel = np.arange(image_len)[None, :] - image_len // 2
    angle = (place * pixel % length) * (2.0 * math.pi / length)
    cos, sin = np.cos(angle), np.sin(angle)
    padded = np.pad(np.stack([cos.T, sin.T]), ((0, 0), (HALO, TILE - HALO), (0, 0)))
    first = padded.reshape(2 * (image_len + TILE), count_col, length // count_col).transpose(1, 0, 2)
    rows = length // count_row
    second = np.stack([cos.reshape(count_row, rows, image_len), -sin.reshape(count_row, rows, image_len)], axis=1)
    second = second.reshape(2 * length, image_len) / length
    return first.astype(jnp.bfloat16), second.astype(jnp.bfloat16)


def share_kernel(cover_in, parts_in, first_all, out, cover, parts, first, sems):
    get_cover = pltpu.make_async_copy(cover_in, cover, sems.at[0])
    get_parts = pltpu.make_async_copy(parts_in, parts, sems.at[1])
    get_first = pltpu.make_async_copy(first_all.at[lax.axis_index("col")], first, sems.at[2])
    for copy in (get_cover, get_parts, get_first):
        copy.start()
    count_rows = parts.shape[2]
    get_cover.wait()
    get_parts.wait()
    components = []
    for component in range(2):
        strips = []
        for i in range(cover.shape[1]):
            cells = []
            for j in range(cover.shape[2]):
                block = parts[0, component, i * BLK : (i + 1) * BLK, j * BLK : (j + 1) * BLK]
                level = jnp.full(block.shape, cover[0, i, j].astype(jnp.float32)).astype(jnp.bfloat16)
                cells.append(block * level)
            strips.append(jnp.concatenate(cells, axis=1))
        components.append(jnp.concatenate(strips, axis=0))
    grid = jnp.concatenate(components, axis=0)
    upper = lax.broadcasted_iota(jnp.int32, (TILE, LANES), 0) < TILE // 2
    devices = out.shape[0]
    tall = first.shape[0] // 2
    get_first.wait()
    turned = lax.dot_general(first[...], grid, (((1,), (1,)), ((), ())), preferred_element_type=jnp.float32)
    mid_re = turned[:tall, :count_rows] - turned[tall:, count_rows:]
    mid_im = turned[tall:, :count_rows] + turned[:tall, count_rows:]
    for device in range(devices):
        here = slice(TILE * device, TILE * (device + 1))
        below = slice(TILE * (device + 1), TILE * (device + 2))
        middle = jnp.where(upper, mid_re[below], pltpu.roll(mid_im[below], TILE // 2, 0))
        out[device] = jnp.concatenate([mid_re[here], middle, mid_im[here]], axis=0).astype(out.dtype)


def own_place():
    place, count = 0, 1
    for axis in ALL:
        place = place * lax.axis_size(axis) + lax.axis_index(axis)
        count = count * lax.axis_size(axis)
    return place, count - 1


def four_times(values):
    return jnp.concatenate([values] * 4, axis=1)


def weights_kernel(
    one_in, bias_in, two_in, bias_two_in, table_in, weights_one, weights_two, bias_rows, table, one, bias, two, bias_two, sems
):
    fetch = [
        pltpu.make_async_copy(one_in, one, sems.at[0]),
        pltpu.make_async_copy(bias_in, bias, sems.at[1]),
        pltpu.make_async_copy(two_in, two, sems.at[2]),
        pltpu.make_async_copy(bias_two_in, bias_two, sems.at[3]),
    ]
    get_table = pltpu.make_async_copy(table_in, table, sems.at[4])
    for copy in (*fetch, get_table):
        copy.start()
    for copy in fetch:
        copy.wait()
    channels = one.shape[2]
    rows = TILE + 2
    per_tile = LANES // channels
    lanes = -(-rows * channels // LANES) * LANES
    image_row = lax.broadcasted_iota(jnp.int32, (16, lanes), 0)
    hidden_row = lax.broadcasted_iota(jnp.int32, (16, lanes), 1) // channels
    place, last = own_place()
    held = (hidden_row >= jnp.where(place == 0, 1, 0)) & (hidden_row < jnp.where(place == last, rows - 1, rows))
    high, low = [], []
    for tap in range(3):
        band = jnp.zeros((16, lanes), jnp.float32)
        for shift in range(3):
            line = jnp.concatenate([four_times(one[shift, tap : tap + 1])] * (lanes // LANES), axis=1)
            band = jnp.where(held & (image_row - hidden_row == shift), line, band)
        high.append(band.astype(jnp.bfloat16).astype(jnp.float32))
        low.append(band - high[-1])
    line = jnp.concatenate([four_times(bias[...])] * (lanes // LANES), axis=1)
    with_bias = high[0]
    for piece in range(3):
        rounded = line.astype(jnp.bfloat16).astype(jnp.float32)
        with_bias = jnp.where(held & (image_row == 12 + piece), rounded, with_bias)
        line = line - rounded
    stacked = jnp.concatenate([with_bias, *high[1:], *high, *low], axis=0)
    weights_one[...] = stacked.T[: weights_one.shape[0]].astype(jnp.bfloat16)
    row = lax.broadcasted_iota(jnp.int32, bias_rows.shape, 0) // TILE
    lane = lax.broadcasted_iota(jnp.int32, bias_rows.shape, 1)
    line = jnp.where(row == lane, four_times(bias_two[...]), 0.0)
    bias_rows[...] = jnp.broadcast_to(jnp.sum(line, axis=1, keepdims=True), bias_rows.shape)
    lines = [[four_times(two[shift, tap].astype(jnp.float32)) for shift in range(3)] for tap in range(3)]
    row = lax.broadcasted_iota(jnp.int32, (TILE, LANES), 0)
    lane = lax.broadcasted_iota(jnp.int32, (TILE, LANES), 1) // channels
    zero = jnp.zeros((TILE, LANES), jnp.float32)
    for tile in range(lanes // LANES):
        hidden_row = tile * per_tile + lane
        masks = [(hidden_row < rows) & (hidden_row - row == shift) for shift in range(3)]
        for tap in range(3):
            at = tap * lanes + tile * LANES
            for channel in range(0, channels, 2):
                pair = []
                for k in (channel, channel + 1):
                    values = zero
                    for shift in range(3):
                        values = jnp.where(masks[shift], lines[tap][shift][k : k + 1], values)
                    pair.append(values)
                block = jnp.concatenate(pair, axis=0).astype(jnp.bfloat16)
                weights_two[TILE * channel : TILE * (channel + 2), at : at + LANES] = block
    get_table.wait()


def shifted(values, width):
    lane = lax.broadcasted_iota(jnp.int32, values.shape, 1)
    zero = jnp.zeros_like(values)
    before = jnp.where(lane == 0, zero, pltpu.roll(values, 1, 1))
    after = jnp.where(lane == width - 1, zero, pltpu.roll(values, width - 1, 1))
    return before, values, after


def layers_kernel(shares, weights_one, weights_two, bias_rows, table, out, staged, sems):
    width = out.shape[2]
    vis, row, col = (lax.axis_size(axis) for axis in ALL)
    upper = lax.broadcasted_iota(jnp.int32, (TILE, 2 * LANES), 0) < TILE // 2
    depth = 2 * LANES
    image = jnp.zeros((4 * TILE, width), jnp.float32)
    for r in range(row):
        senders = [(v * row + r) * col + c for v in range(vis) for c in range(col)]
        total = shares[senders[0]].astype(jnp.float32)
        for sender in senders[1:]:
            total = total + shares[sender].astype(jnp.float32)
        middle = total[TILE : 2 * TILE]
        above = jnp.concatenate([total[:TILE], total[2 * TILE :]], axis=1)
        below = jnp.concatenate([middle, pltpu.roll(middle, TILE // 2, 0)], axis=1)
        turned = jnp.concatenate([above, jnp.where(upper, below, 0.0)], axis=0)
        high = turned.astype(jnp.bfloat16)
        low = (turned - high.astype(jnp.float32)).astype(jnp.bfloat16)
        block = table[r * depth : (r + 1) * depth]
        image = image + jnp.dot(jnp.concatenate([high, low], axis=0), block, preferred_element_type=jnp.float32)
    image = image[: 2 * TILE] + image[2 * TILE :]
    columns = jnp.concatenate(shifted(image, width), axis=0)
    high = columns.astype(jnp.bfloat16).astype(jnp.float32)
    low = columns - high
    row = lax.broadcasted_iota(jnp.int32, (48, width), 0)
    with_ones = jnp.where((row >= 12) & (row < 15), 1.0, high)
    stacked = jnp.concatenate([with_ones, low, high], axis=0).astype(jnp.bfloat16)
    hidden = jnp.dot(weights_one[...], stacked, preferred_element_type=jnp.float32)
    hidden = jnp.maximum(hidden, 0.0).astype(jnp.bfloat16)
    depth = hidden.shape[0]
    step = weights_two.shape[1] // 3
    features = jnp.concatenate([bias_rows[...]] * (width // LANES), axis=1)
    before, middle, after = shifted(hidden, width)
    for tap, moved in ((1, middle), (0, before), (2, after)):
        taps = weights_two[:, tap * step : tap * step + depth]
        features = features + jnp.dot(taps, moved, preferred_element_type=jnp.float32)
    half = out.shape[0] // 2
    copies = []
    for part in range(2):
        channels_of = pl.ds(part * half, half)
        rows = features[part * half * TILE : (part + 1) * half * TILE]
        staged[channels_of] = rows.reshape(half, TILE, width).astype(out.dtype)
        copies.append(pltpu.make_async_copy(staged.at[channels_of], out.at[channels_of], sems.at[part]))
        copies[-1].start()
    for copy in copies:
        copy.wait()


def in_hbm(*arrays):
    return [pltpu.with_memory_space_constraint(array, pltpu.HBM) for array in arrays]


def direct(partials, coverage, conv_one, bias_one, conv_two, bias_two):
    count_row, count_col = lax.axis_size("row"), lax.axis_size("col")
    devices = lax.axis_size("vis") * count_row * count_col
    length = partials.shape[3] * count_col
    image_len = length // 2
    channels = conv_two.shape[2]
    first, second = grid_tables(length, count_row, count_col)
    vmem, hbm = pl.BlockSpec(memory_space=pltpu.VMEM), pl.BlockSpec(memory_space=pltpu.HBM)
    limit = pltpu.CompilerParams(vmem_limit_bytes=16 * 2**20)
    share = (devices, 2 * (TILE + 2 * HALO), LANES)
    shares = pl.pallas_call(
        share_kernel,
        out_shape=jax.ShapeDtypeStruct(share, jnp.bfloat16),
        in_specs=[hbm] * 3,
        out_specs=vmem,
        scratch_shapes=[
            pltpu.SMEM(coverage.shape, jnp.int32),
            pltpu.VMEM(partials.shape, jnp.bfloat16),
            pltpu.VMEM(first.shape[1:], jnp.bfloat16),
            pltpu.SemaphoreType.DMA((3,)),
        ],
        compiler_params=limit,
        name="shares",
    )(*in_hbm(coverage, partials, jnp.asarray(first)))
    arrived = lax.all_to_all(shares, ALL, split_axis=0, concat_axis=0, tiled=True)
    rows = TILE + 2
    banded = -(-rows * channels // LANES) * LANES
    weights = pl.pallas_call(
        weights_kernel,
        out_shape=[
            jax.ShapeDtypeStruct((rows * channels, 3 * 48), jnp.bfloat16),
            jax.ShapeDtypeStruct((TILE * channels, 3 * banded), jnp.bfloat16),
            jax.ShapeDtypeStruct((TILE * channels, LANES), jnp.float32),
            jax.ShapeDtypeStruct(second.shape, jnp.bfloat16),
        ],
        in_specs=[hbm] * 5,
        out_specs=[vmem] * 4,
        scratch_shapes=[
            pltpu.VMEM((3, 3, channels), jnp.float32),
            pltpu.VMEM((1, channels), jnp.float32),
            pltpu.VMEM(conv_two.shape, jnp.bfloat16),
            pltpu.VMEM((1, channels), jnp.float32),
            pltpu.SemaphoreType.DMA((5,)),
        ],
        compiler_params=limit,
        name="weights",
    )(*in_hbm(conv_one.transpose(1, 2, 0), bias_one[None], conv_two, bias_two[None], jnp.asarray(second)))
    return pl.pallas_call(
        layers_kernel,
        out_shape=jax.ShapeDtypeStruct((channels, TILE, image_len), jnp.bfloat16),
        in_specs=[vmem] * 5,
        out_specs=hbm,
        scratch_shapes=[
            pltpu.VMEM((channels, TILE, image_len), jnp.bfloat16),
            pltpu.SemaphoreType.DMA((2,)),
        ],
        compiler_params=limit,
        name="layers",
    )(arrived, *weights)


def local(partials, coverage, conv_one, bias_one, conv_two, bias_two):
    count_col = lax.axis_size("col")
    devices = lax.axis_size("vis") * lax.axis_size("row") * count_col
    image_len = partials.shape[3] * count_col // 2
    sent = devices * (TILE + 2 * HALO) * image_len * 2
    fits = partials.shape[2] == LANES and image_len == devices * TILE and conv_two.shape[2] * 4 == LANES and image_len == 2 * LANES and sent <= DIRECT_BYTES
    plan = direct if fits else staged
    return plan(partials, coverage, conv_one, bias_one, conv_two, bias_two)


def solution(mesh):
    placed = (P("vis", None, "row", "col"), P("vis", "row", "col"), P(), P(), P(), P())
    return jax.shard_map(
        local,
        mesh=mesh,
        in_specs=placed,
        out_specs=P(None, ALL, None),
        check_vma=False,
    )
```

```python
import math

import jax
import jax.numpy as jnp
import numpy as np
from jax import lax
from jax.experimental import pallas as pl
from jax.experimental.pallas import tpu as pltpu
from jax.sharding import PartitionSpec as P

BLK = 128
ALL = ("vis", "row", "col")
DIRECT_BYTES = 4 * 2**20
HALO = 2
TILE = 8
LANES = 128


def with_halo(cells, sides, width):
    for axis, dim in sides:
        count = lax.axis_size(axis)
        ends = count - 1
        head = lax.slice_in_dim(cells, 0, width, axis=dim)
        tail = lax.slice_in_dim(cells, cells.shape[dim] - width, cells.shape[dim], axis=dim)
        cells = jnp.concatenate(
            [
                lax.ppermute(tail, axis, [(i, (i + 1) % count) for i in range(ends)]),
                cells,
                lax.ppermute(head, axis, [((i + 1) % count, i) for i in range(ends)]),
            ],
            axis=dim,
        )
    return cells


def phase_table(numer, denom):
    angle = numer.astype(jnp.float32) * (2.0 * math.pi / denom)
    return (jnp.cos(angle), jnp.sin(angle))


def partial_transform(real_part, imag_part, block_of, keep_imag):
    batch = real_part.shape[0]
    count_blocks = real_part.shape[1]
    block_len = real_part.shape[2]
    length = count_blocks * block_len
    highest = lax.Precision.HIGHEST
    outer = jnp.arange(count_blocks, dtype=jnp.int32)
    inner = jnp.arange(block_len, dtype=jnp.int32)
    cos_one, sin_one = phase_table(block_of[:, None] * outer[None, :] % count_blocks, count_blocks)
    mid_re = jnp.einsum("lpt,px->lxt", real_part, cos_one, precision=highest) - jnp.einsum(
        "lpt,px->lxt", imag_part, sin_one, precision=highest
    )
    mid_im = jnp.einsum("lpt,px->lxt", real_part, sin_one, precision=highest) + jnp.einsum(
        "lpt,px->lxt", imag_part, cos_one, precision=highest
    )
    cos_two, sin_two = phase_table(outer[:, None] * inner[None, :] % length, length)
    parity = (1 - 2 * (outer % 2)).astype(jnp.float32)[:, None]
    cos_two = cos_two * parity
    sin_two = sin_two * parity
    turn_re = mid_re * cos_two - mid_im * sin_two
    turn_im = mid_re * sin_two + mid_im * cos_two
    kept = jnp.arange(block_len // 2, dtype=jnp.int32)
    picked = (kept + 3 * block_len // 4) % block_len
    cos_three, sin_three = phase_table(inner[:, None] * picked[None, :] % block_len, block_len)
    out_re = jnp.einsum("lxt,tj->ljx", turn_re, cos_three, precision=highest) - jnp.einsum(
        "lxt,tj->ljx", turn_im, sin_three, precision=highest
    )
    out_re = out_re.reshape(batch, length // 2)
    if keep_imag:
        out_im = jnp.einsum("lxt,tj->ljx", turn_re, sin_three, precision=highest) + jnp.einsum(
            "lxt,tj->ljx", turn_im, cos_three, precision=highest
        )
        return (out_re, out_im.reshape(batch, length // 2))
    return (out_re, out_re)


def first_layer(extended, conv_one, bias_one, count_rows):
    width = extended.shape[1]
    padded = jnp.pad(extended, ((0, 0), (1, 1)))
    summed = (
        jnp.zeros((conv_one.shape[0], count_rows, width), jnp.float32) + bias_one[:, None, None]
    )
    for shift_b in range(3):
        for shift_a in range(3):
            summed = (
                summed
                + conv_one[:, shift_b, shift_a][:, None, None]
                * padded[None, shift_b : shift_b + count_rows, shift_a : shift_a + width]
            )
    return jnp.maximum(summed, 0.0)


def second_layer(hidden_ext, conv_two, bias_two, count_rows):
    width = hidden_ext.shape[2]
    padded = jnp.pad(hidden_ext, ((0, 0), (0, 0), (1, 1)))
    summed = jnp.zeros((conv_two.shape[2], count_rows, width), jnp.float32)
    for shift_b in range(3):
        for shift_a in range(3):
            summed = summed + jnp.einsum(
                "kj,jba->kba",
                conv_two[shift_b, shift_a],
                padded[:, shift_b : shift_b + count_rows, shift_a : shift_a + width],
                preferred_element_type=jnp.float32,
            )
    return (summed + bias_two[:, None, None]).astype(jnp.bfloat16)


def staged(partials, coverage, conv_one, bias_one, conv_two, bias_two):
    count_vis = lax.axis_size("vis")
    count_row = lax.axis_size("row")
    count_col = lax.axis_size("col")
    grid_len = partials.shape[3] * count_col
    cover = coverage[0]
    block_rows = cover.shape[0]
    block_cols = cover.shape[1]
    spread = jnp.broadcast_to(cover[:, None, :, None], (block_rows, BLK, block_cols, BLK))
    spread = spread.reshape(block_rows * BLK, block_cols * BLK)
    count_blocks = count_vis * count_row
    row_block = grid_len // count_blocks
    row_share = row_block // count_col
    masked = partials[0] * spread.astype(jnp.bfloat16)[None]
    reduced = lax.psum_scatter(
        masked.astype(jnp.float32).astype(jnp.bfloat16), "vis", scatter_dimension=1, tiled=True
    ).astype(jnp.float32)
    grid_rows = lax.all_to_all(
        reduced.astype(jnp.bfloat16), "col", split_axis=1, concat_axis=2, tiled=True
    ).astype(reduced.dtype)
    natural = jnp.arange(count_blocks, dtype=jnp.int32)
    shaped = grid_rows.reshape(2, row_share, count_blocks, row_block)
    first_re, first_im = partial_transform(shaped[0], shaped[1], natural, True)
    stacked = jnp.stack([first_re, first_im])
    moved = lax.all_to_all(
        lax.all_to_all(
            stacked.astype(jnp.bfloat16), ("vis", "row"), split_axis=2, concat_axis=1, tiled=True
        ),
        "col",
        split_axis=2,
        concat_axis=1,
        tiled=True,
    ).astype(stacked.dtype)
    img_rows = moved.shape[2]
    arranged = moved.reshape(2, count_col, count_blocks, row_share, img_rows)
    arranged = arranged.transpose(0, 4, 2, 1, 3).reshape(2, img_rows, count_blocks, row_block)
    owners = natural % count_row * count_vis + natural // count_row
    image, unused = partial_transform(arranged[0], arranged[1], owners, False)
    image = image * (1.0 / grid_len)
    extended = with_halo(image.astype(jnp.bfloat16), ((("vis", "row", "col"), 0),), 1).astype(
        image.dtype
    )
    hidden = first_layer(extended, conv_one, bias_one, img_rows).astype(jnp.bfloat16)
    hidden_ext = with_halo(hidden, ((("vis", "row", "col"), 1),), 1)
    return second_layer(hidden_ext, conv_two, bias_two, img_rows)


def grid_tables(length, count_row, count_col):
    image_len = length // 2
    place = np.arange(length)[:, None] - length // 2
    pixel = np.arange(image_len)[None, :] - image_len // 2
    angle = (place * pixel % length) * (2.0 * math.pi / length)
    cos, sin = np.cos(angle), np.sin(angle)
    padded = np.pad(np.stack([cos.T, sin.T]), ((0, 0), (HALO, TILE - HALO), (0, 0)))
    first = padded.reshape(2 * (image_len + TILE), count_col, length // count_col).transpose(1, 0, 2)
    rows = length // count_row
    second = np.stack([cos.reshape(count_row, rows, image_len), -sin.reshape(count_row, rows, image_len)], axis=1)
    second = second.reshape(2 * length, image_len) / length
    return first.astype(jnp.bfloat16), second.astype(jnp.bfloat16)


def share_kernel(cover_in, parts_in, first_all, out, cover, parts, first, sems):
    get_cover = pltpu.make_async_copy(cover_in, cover, sems.at[0])
    get_parts = pltpu.make_async_copy(parts_in, parts, sems.at[1])
    get_first = pltpu.make_async_copy(first_all.at[lax.axis_index("col")], first, sems.at[2])
    for copy in (get_cover, get_parts, get_first):
        copy.start()
    count_rows = parts.shape[2]
    get_cover.wait()
    get_parts.wait()
    components = []
    for component in range(2):
        strips = []
        for i in range(cover.shape[1]):
            cells = []
            for j in range(cover.shape[2]):
                block = parts[0, component, i * BLK : (i + 1) * BLK, j * BLK : (j + 1) * BLK]
                level = jnp.full(block.shape, cover[0, i, j].astype(jnp.float32)).astype(jnp.bfloat16)
                cells.append(block * level)
            strips.append(jnp.concatenate(cells, axis=1))
        components.append(jnp.concatenate(strips, axis=0))
    grid = jnp.concatenate(components, axis=0)
    upper = lax.broadcasted_iota(jnp.int32, (TILE, LANES), 0) < TILE // 2
    devices = out.shape[0]
    tall = first.shape[0] // 2
    get_first.wait()
    turned = lax.dot_general(first[...], grid, (((1,), (1,)), ((), ())), preferred_element_type=jnp.float32)
    mid_re = turned[:tall, :count_rows] - turned[tall:, count_rows:]
    mid_im = turned[tall:, :count_rows] + turned[:tall, count_rows:]
    for device in range(devices):
        here = slice(TILE * device, TILE * (device + 1))
        below = slice(TILE * (device + 1), TILE * (device + 2))
        middle = jnp.where(upper, mid_re[below], pltpu.roll(mid_im[below], TILE // 2, 0))
        out[device] = jnp.concatenate([mid_re[here], middle, mid_im[here]], axis=0).astype(out.dtype)


def own_place():
    place, count = 0, 1
    for axis in ALL:
        place = place * lax.axis_size(axis) + lax.axis_index(axis)
        count = count * lax.axis_size(axis)
    return place, count - 1


def four_times(values):
    return jnp.concatenate([values] * 4, axis=1)


def weights_kernel(
    one_in, bias_in, two_in, bias_two_in, table_in, weights_one, weights_two, bias_rows, table, one, bias, two, bias_two, sems
):
    fetch = [
        pltpu.make_async_copy(one_in, one, sems.at[0]),
        pltpu.make_async_copy(bias_in, bias, sems.at[1]),
        pltpu.make_async_copy(two_in, two, sems.at[2]),
        pltpu.make_async_copy(bias_two_in, bias_two, sems.at[3]),
    ]
    get_table = pltpu.make_async_copy(table_in, table, sems.at[4])
    for copy in (*fetch, get_table):
        copy.start()
    for copy in fetch:
        copy.wait()
    channels = one.shape[2]
    rows = TILE + 2
    per_tile = LANES // channels
    lanes = -(-rows * channels // LANES) * LANES
    image_row = lax.broadcasted_iota(jnp.int32, (16, lanes), 0)
    hidden_row = lax.broadcasted_iota(jnp.int32, (16, lanes), 1) // channels
    place, last = own_place()
    held = (hidden_row >= jnp.where(place == 0, 1, 0)) & (hidden_row < jnp.where(place == last, rows - 1, rows))
    high, low = [], []
    for tap in range(3):
        band = jnp.zeros((16, lanes), jnp.float32)
        for shift in range(3):
            line = jnp.concatenate([four_times(one[shift, tap : tap + 1])] * (lanes // LANES), axis=1)
            band = jnp.where(held & (image_row - hidden_row == shift), line, band)
        high.append(band.astype(jnp.bfloat16).astype(jnp.float32))
        low.append(band - high[-1])
    line = jnp.concatenate([four_times(bias[...])] * (lanes // LANES), axis=1)
    with_bias = high[0]
    for piece in range(3):
        rounded = line.astype(jnp.bfloat16).astype(jnp.float32)
        with_bias = jnp.where(held & (image_row == 12 + piece), rounded, with_bias)
        line = line - rounded
    stacked = jnp.concatenate([with_bias, *high[1:], *high, *low], axis=0)
    weights_one[...] = stacked.T[: weights_one.shape[0]].astype(jnp.bfloat16)
    row = lax.broadcasted_iota(jnp.int32, bias_rows.shape, 0) // TILE
    lane = lax.broadcasted_iota(jnp.int32, bias_rows.shape, 1)
    line = jnp.where(row == lane, four_times(bias_two[...]), 0.0)
    bias_rows[...] = jnp.broadcast_to(jnp.sum(line, axis=1, keepdims=True), bias_rows.shape)
    lines = [[four_times(two[shift, tap].astype(jnp.float32)) for shift in range(3)] for tap in range(3)]
    row = lax.broadcasted_iota(jnp.int32, (TILE, LANES), 0)
    lane = lax.broadcasted_iota(jnp.int32, (TILE, LANES), 1) // channels
    zero = jnp.zeros((TILE, LANES), jnp.float32)
    for tile in range(-(-3 * rows // per_tile)):
        taps = sorted({(tile * per_tile + g) // rows for g in range(per_tile)} & {0, 1, 2})
        masks = []
        for tap in taps:
            hidden_row = tile * per_tile + lane - tap * rows
            inside = (hidden_row >= 0) & (hidden_row < rows)
            masks += [(tap, shift, inside & (hidden_row - row == shift)) for shift in range(3)]
        width = min(LANES, weights_two.shape[1] - tile * LANES)
        for channel in range(0, channels, 2):
            pair = []
            for k in (channel, channel + 1):
                values = zero
                for tap, shift, mask in masks:
                    values = jnp.where(mask, lines[tap][shift][k : k + 1], values)
                pair.append(values)
            block = jnp.concatenate(pair, axis=0).astype(jnp.bfloat16)
            weights_two[TILE * channel : TILE * (channel + 2), tile * LANES : tile * LANES + width] = block[:, :width]
    get_table.wait()


def shifted(values, width):
    lane = lax.broadcasted_iota(jnp.int32, values.shape, 1)
    zero = jnp.zeros_like(values)
    before = jnp.where(lane == 0, zero, pltpu.roll(values, 1, 1))
    after = jnp.where(lane == width - 1, zero, pltpu.roll(values, width - 1, 1))
    return before, values, after


def layers_kernel(shares, weights_one, weights_two, bias_rows, table, out, staged, sems):
    width = out.shape[2]
    vis, row, col = (lax.axis_size(axis) for axis in ALL)
    upper = lax.broadcasted_iota(jnp.int32, (TILE, 2 * LANES), 0) < TILE // 2
    depth = 2 * LANES
    image = jnp.zeros((4 * TILE, width), jnp.float32)
    for r in range(row):
        senders = [(v * row + r) * col + c for v in range(vis) for c in range(col)]
        total = shares[senders[0]].astype(jnp.float32)
        for sender in senders[1:]:
            total = total + shares[sender].astype(jnp.float32)
        middle = total[TILE : 2 * TILE]
        above = jnp.concatenate([total[:TILE], total[2 * TILE :]], axis=1)
        below = jnp.concatenate([middle, pltpu.roll(middle, TILE // 2, 0)], axis=1)
        turned = jnp.concatenate([above, jnp.where(upper, below, 0.0)], axis=0)
        high = turned.astype(jnp.bfloat16)
        low = (turned - high.astype(jnp.float32)).astype(jnp.bfloat16)
        block = table[r * depth : (r + 1) * depth]
        image = image + jnp.dot(jnp.concatenate([high, low], axis=0), block, preferred_element_type=jnp.float32)
    image = image[: 2 * TILE] + image[2 * TILE :]
    columns = jnp.concatenate(shifted(image, width), axis=0)
    high = columns.astype(jnp.bfloat16).astype(jnp.float32)
    low = columns - high
    row = lax.broadcasted_iota(jnp.int32, (48, width), 0)
    with_ones = jnp.where((row >= 12) & (row < 15), 1.0, high)
    stacked = jnp.concatenate([with_ones, low, high], axis=0).astype(jnp.bfloat16)
    hidden = jnp.dot(weights_one[...], stacked, preferred_element_type=jnp.float32)
    hidden = jnp.maximum(hidden, 0.0).astype(jnp.bfloat16)
    stacked = jnp.concatenate(shifted(hidden, width), axis=0)
    features = jnp.dot(weights_two[...], stacked, preferred_element_type=jnp.float32)
    half = out.shape[0] // 2
    copies = []
    for part in range(2):
        channels_of = pl.ds(part * half, half)
        rows = slice(part * half * TILE, (part + 1) * half * TILE)
        biased = features[rows] + jnp.concatenate([bias_rows[rows]] * (width // LANES), axis=1)
        staged[channels_of] = biased.reshape(half, TILE, width).astype(out.dtype)
        copies.append(pltpu.make_async_copy(staged.at[channels_of], out.at[channels_of], sems.at[part]))
        copies[-1].start()
    for copy in copies:
        copy.wait()


def in_hbm(*arrays):
    return [pltpu.with_memory_space_constraint(array, pltpu.HBM) for array in arrays]


def direct(partials, coverage, conv_one, bias_one, conv_two, bias_two):
    count_row, count_col = lax.axis_size("row"), lax.axis_size("col")
    devices = lax.axis_size("vis") * count_row * count_col
    length = partials.shape[3] * count_col
    image_len = length // 2
    channels = conv_two.shape[2]
    first, second = grid_tables(length, count_row, count_col)
    vmem, hbm = pl.BlockSpec(memory_space=pltpu.VMEM), pl.BlockSpec(memory_space=pltpu.HBM)
    limit = pltpu.CompilerParams(vmem_limit_bytes=16 * 2**20)
    share = (devices, 2 * (TILE + 2 * HALO), LANES)
    shares = pl.pallas_call(
        share_kernel,
        out_shape=jax.ShapeDtypeStruct(share, jnp.bfloat16),
        in_specs=[hbm] * 3,
        out_specs=vmem,
        scratch_shapes=[
            pltpu.SMEM(coverage.shape, jnp.int32),
            pltpu.VMEM(partials.shape, jnp.bfloat16),
            pltpu.VMEM(first.shape[1:], jnp.bfloat16),
            pltpu.SemaphoreType.DMA((3,)),
        ],
        compiler_params=limit,
        name="shares",
    )(*in_hbm(coverage, partials, jnp.asarray(first)))
    arrived = lax.all_to_all(shares, ALL, split_axis=0, concat_axis=0, tiled=True)
    rows = TILE + 2
    weights = pl.pallas_call(
        weights_kernel,
        out_shape=[
            jax.ShapeDtypeStruct((rows * channels, 3 * 48), jnp.bfloat16),
            jax.ShapeDtypeStruct((TILE * channels, 3 * rows * channels), jnp.bfloat16),
            jax.ShapeDtypeStruct((TILE * channels, LANES), jnp.float32),
            jax.ShapeDtypeStruct(second.shape, jnp.bfloat16),
        ],
        in_specs=[hbm] * 5,
        out_specs=[vmem] * 4,
        scratch_shapes=[
            pltpu.VMEM((3, 3, channels), jnp.float32),
            pltpu.VMEM((1, channels), jnp.float32),
            pltpu.VMEM(conv_two.shape, jnp.bfloat16),
            pltpu.VMEM((1, channels), jnp.float32),
            pltpu.SemaphoreType.DMA((5,)),
        ],
        compiler_params=limit,
        name="weights",
    )(*in_hbm(conv_one.transpose(1, 2, 0), bias_one[None], conv_two, bias_two[None], jnp.asarray(second)))
    return pl.pallas_call(
        layers_kernel,
        out_shape=jax.ShapeDtypeStruct((channels, TILE, image_len), jnp.bfloat16),
        in_specs=[vmem] * 5,
        out_specs=hbm,
        scratch_shapes=[
            pltpu.VMEM((channels, TILE, image_len), jnp.bfloat16),
            pltpu.SemaphoreType.DMA((2,)),
        ],
        compiler_params=limit,
        name="layers",
    )(arrived, *weights)


def local(partials, coverage, conv_one, bias_one, conv_two, bias_two):
    count_col = lax.axis_size("col")
    devices = lax.axis_size("vis") * lax.axis_size("row") * count_col
    image_len = partials.shape[3] * count_col // 2
    sent = devices * (TILE + 2 * HALO) * image_len * 2
    fits = partials.shape[2] == LANES and image_len == devices * TILE and conv_two.shape[2] * 4 == LANES and image_len == 2 * LANES and sent <= DIRECT_BYTES
    plan = direct if fits else staged
    return plan(partials, coverage, conv_one, bias_one, conv_two, bias_two)


def solution(mesh):
    placed = (P("vis", None, "row", "col"), P("vis", "row", "col"), P(), P(), P(), P())
    return jax.shard_map(
        local,
        mesh=mesh,
        in_specs=placed,
        out_specs=P(None, ALL, None),
        check_vma=False,
    )
```

```python
import math

import jax
import jax.numpy as jnp
import numpy as np
from jax import lax
from jax.experimental import pallas as pl
from jax.experimental.pallas import tpu as pltpu
from jax.sharding import PartitionSpec as P

BLK = 128
ALL = ("vis", "row", "col")
DIRECT_BYTES = 4 * 2**20
HALO = 2
TILE = 8
LANES = 128


def with_halo(cells, sides, width):
    for axis, dim in sides:
        count = lax.axis_size(axis)
        ends = count - 1
        head = lax.slice_in_dim(cells, 0, width, axis=dim)
        tail = lax.slice_in_dim(cells, cells.shape[dim] - width, cells.shape[dim], axis=dim)
        cells = jnp.concatenate(
            [
                lax.ppermute(tail, axis, [(i, (i + 1) % count) for i in range(ends)]),
                cells,
                lax.ppermute(head, axis, [((i + 1) % count, i) for i in range(ends)]),
            ],
            axis=dim,
        )
    return cells


def phase_table(numer, denom):
    angle = numer.astype(jnp.float32) * (2.0 * math.pi / denom)
    return (jnp.cos(angle), jnp.sin(angle))


def partial_transform(real_part, imag_part, block_of, keep_imag):
    batch = real_part.shape[0]
    count_blocks = real_part.shape[1]
    block_len = real_part.shape[2]
    length = count_blocks * block_len
    highest = lax.Precision.HIGHEST
    outer = jnp.arange(count_blocks, dtype=jnp.int32)
    inner = jnp.arange(block_len, dtype=jnp.int32)
    cos_one, sin_one = phase_table(block_of[:, None] * outer[None, :] % count_blocks, count_blocks)
    mid_re = jnp.einsum("lpt,px->lxt", real_part, cos_one, precision=highest) - jnp.einsum(
        "lpt,px->lxt", imag_part, sin_one, precision=highest
    )
    mid_im = jnp.einsum("lpt,px->lxt", real_part, sin_one, precision=highest) + jnp.einsum(
        "lpt,px->lxt", imag_part, cos_one, precision=highest
    )
    cos_two, sin_two = phase_table(outer[:, None] * inner[None, :] % length, length)
    parity = (1 - 2 * (outer % 2)).astype(jnp.float32)[:, None]
    cos_two = cos_two * parity
    sin_two = sin_two * parity
    turn_re = mid_re * cos_two - mid_im * sin_two
    turn_im = mid_re * sin_two + mid_im * cos_two
    kept = jnp.arange(block_len // 2, dtype=jnp.int32)
    picked = (kept + 3 * block_len // 4) % block_len
    cos_three, sin_three = phase_table(inner[:, None] * picked[None, :] % block_len, block_len)
    out_re = jnp.einsum("lxt,tj->ljx", turn_re, cos_three, precision=highest) - jnp.einsum(
        "lxt,tj->ljx", turn_im, sin_three, precision=highest
    )
    out_re = out_re.reshape(batch, length // 2)
    if keep_imag:
        out_im = jnp.einsum("lxt,tj->ljx", turn_re, sin_three, precision=highest) + jnp.einsum(
            "lxt,tj->ljx", turn_im, cos_three, precision=highest
        )
        return (out_re, out_im.reshape(batch, length // 2))
    return (out_re, out_re)


def first_layer(extended, conv_one, bias_one, count_rows):
    width = extended.shape[1]
    padded = jnp.pad(extended, ((0, 0), (1, 1)))
    summed = (
        jnp.zeros((conv_one.shape[0], count_rows, width), jnp.float32) + bias_one[:, None, None]
    )
    for shift_b in range(3):
        for shift_a in range(3):
            summed = (
                summed
                + conv_one[:, shift_b, shift_a][:, None, None]
                * padded[None, shift_b : shift_b + count_rows, shift_a : shift_a + width]
            )
    return jnp.maximum(summed, 0.0)


def second_layer(hidden_ext, conv_two, bias_two, count_rows):
    width = hidden_ext.shape[2]
    padded = jnp.pad(hidden_ext, ((0, 0), (0, 0), (1, 1)))
    summed = jnp.zeros((conv_two.shape[2], count_rows, width), jnp.float32)
    for shift_b in range(3):
        for shift_a in range(3):
            summed = summed + jnp.einsum(
                "kj,jba->kba",
                conv_two[shift_b, shift_a],
                padded[:, shift_b : shift_b + count_rows, shift_a : shift_a + width],
                preferred_element_type=jnp.float32,
            )
    return (summed + bias_two[:, None, None]).astype(jnp.bfloat16)


def staged(partials, coverage, conv_one, bias_one, conv_two, bias_two):
    count_vis = lax.axis_size("vis")
    count_row = lax.axis_size("row")
    count_col = lax.axis_size("col")
    grid_len = partials.shape[3] * count_col
    cover = coverage[0]
    block_rows = cover.shape[0]
    block_cols = cover.shape[1]
    spread = jnp.broadcast_to(cover[:, None, :, None], (block_rows, BLK, block_cols, BLK))
    spread = spread.reshape(block_rows * BLK, block_cols * BLK)
    count_blocks = count_vis * count_row
    row_block = grid_len // count_blocks
    row_share = row_block // count_col
    masked = partials[0] * spread.astype(jnp.bfloat16)[None]
    reduced = lax.psum_scatter(
        masked.astype(jnp.float32).astype(jnp.bfloat16), "vis", scatter_dimension=1, tiled=True
    ).astype(jnp.float32)
    grid_rows = lax.all_to_all(
        reduced.astype(jnp.bfloat16), "col", split_axis=1, concat_axis=2, tiled=True
    ).astype(reduced.dtype)
    natural = jnp.arange(count_blocks, dtype=jnp.int32)
    shaped = grid_rows.reshape(2, row_share, count_blocks, row_block)
    first_re, first_im = partial_transform(shaped[0], shaped[1], natural, True)
    stacked = jnp.stack([first_re, first_im])
    moved = lax.all_to_all(
        lax.all_to_all(
            stacked.astype(jnp.bfloat16), ("vis", "row"), split_axis=2, concat_axis=1, tiled=True
        ),
        "col",
        split_axis=2,
        concat_axis=1,
        tiled=True,
    ).astype(stacked.dtype)
    img_rows = moved.shape[2]
    arranged = moved.reshape(2, count_col, count_blocks, row_share, img_rows)
    arranged = arranged.transpose(0, 4, 2, 1, 3).reshape(2, img_rows, count_blocks, row_block)
    owners = natural % count_row * count_vis + natural // count_row
    image, unused = partial_transform(arranged[0], arranged[1], owners, False)
    image = image * (1.0 / grid_len)
    extended = with_halo(image.astype(jnp.bfloat16), ((("vis", "row", "col"), 0),), 1).astype(
        image.dtype
    )
    hidden = first_layer(extended, conv_one, bias_one, img_rows).astype(jnp.bfloat16)
    hidden_ext = with_halo(hidden, ((("vis", "row", "col"), 1),), 1)
    return second_layer(hidden_ext, conv_two, bias_two, img_rows)


def grid_tables(length, count_row, count_col):
    image_len = length // 2
    place = np.arange(length)[:, None] - length // 2
    pixel = np.arange(image_len)[None, :] - image_len // 2
    angle = (place * pixel % length) * (2.0 * math.pi / length)
    cos, sin = np.cos(angle), np.sin(angle)
    padded = np.pad(np.stack([cos.T, sin.T]), ((0, 0), (HALO, TILE - HALO), (0, 0)))
    first = padded.reshape(2 * (image_len + TILE), count_col, length // count_col).transpose(1, 0, 2)
    rows = length // count_row
    second = np.stack([cos.reshape(count_row, rows, image_len), -sin.reshape(count_row, rows, image_len)], axis=1)
    second = second.reshape(2 * length, image_len) / length
    return first.astype(jnp.bfloat16), second.astype(jnp.bfloat16)


def share_kernel(cover_in, parts_in, first_all, out, cover, parts, first, sems):
    get_cover = pltpu.make_async_copy(cover_in, cover, sems.at[0])
    get_parts = pltpu.make_async_copy(parts_in, parts, sems.at[1])
    get_first = pltpu.make_async_copy(first_all.at[lax.axis_index("col")], first, sems.at[2])
    for copy in (get_cover, get_parts, get_first):
        copy.start()
    count_rows = parts.shape[2]
    get_cover.wait()
    get_parts.wait()
    components = []
    for component in range(2):
        strips = []
        for i in range(cover.shape[1]):
            cells = []
            for j in range(cover.shape[2]):
                block = parts[0, component, i * BLK : (i + 1) * BLK, j * BLK : (j + 1) * BLK]
                level = jnp.full(block.shape, cover[0, i, j].astype(jnp.float32)).astype(jnp.bfloat16)
                cells.append(block * level)
            strips.append(jnp.concatenate(cells, axis=1))
        components.append(jnp.concatenate(strips, axis=0))
    grid = jnp.concatenate(components, axis=0)
    upper = lax.broadcasted_iota(jnp.int32, (TILE, LANES), 0) < TILE // 2
    devices = out.shape[0]
    tall = first.shape[0] // 2
    get_first.wait()
    turned = lax.dot_general(first[...], grid, (((1,), (1,)), ((), ())), preferred_element_type=jnp.float32)
    mid_re = turned[:tall, :count_rows] - turned[tall:, count_rows:]
    mid_im = turned[tall:, :count_rows] + turned[:tall, count_rows:]
    for device in range(devices):
        here = slice(TILE * device, TILE * (device + 1))
        below = slice(TILE * (device + 1), TILE * (device + 2))
        middle = jnp.where(upper, mid_re[below], pltpu.roll(mid_im[below], TILE // 2, 0))
        out[device] = jnp.concatenate([mid_re[here], middle, mid_im[here]], axis=0).astype(out.dtype)


def own_place():
    place, count = 0, 1
    for axis in ALL:
        place = place * lax.axis_size(axis) + lax.axis_index(axis)
        count = count * lax.axis_size(axis)
    return place, count - 1


def four_times(values):
    return jnp.concatenate([values] * 4, axis=1)


def weights_kernel(
    one_in, bias_in, two_in, bias_two_in, table_in, weights_one, weights_two, bias_rows, table, one, bias, two, bias_two, sems
):
    fetch = [
        pltpu.make_async_copy(one_in, one, sems.at[0]),
        pltpu.make_async_copy(bias_in, bias, sems.at[1]),
        pltpu.make_async_copy(two_in, two, sems.at[2]),
        pltpu.make_async_copy(bias_two_in, bias_two, sems.at[3]),
    ]
    get_table = pltpu.make_async_copy(table_in, table, sems.at[4])
    for copy in (*fetch, get_table):
        copy.start()
    for copy in fetch:
        copy.wait()
    channels = one.shape[2]
    rows = TILE + 2
    per_tile = LANES // channels
    lanes = -(-rows * channels // LANES) * LANES
    image_row = lax.broadcasted_iota(jnp.int32, (16, lanes), 0)
    hidden_row = lax.broadcasted_iota(jnp.int32, (16, lanes), 1) // channels
    place, last = own_place()
    held = (hidden_row >= jnp.where(place == 0, 1, 0)) & (hidden_row < jnp.where(place == last, rows - 1, rows))
    high, low = [], []
    for tap in range(3):
        band = jnp.zeros((16, lanes), jnp.float32)
        for shift in range(3):
            line = jnp.concatenate([four_times(one[shift, tap : tap + 1])] * (lanes // LANES), axis=1)
            band = jnp.where(held & (image_row - hidden_row == shift), line, band)
        high.append(band.astype(jnp.bfloat16).astype(jnp.float32))
        low.append(band - high[-1])
    line = jnp.concatenate([four_times(bias[...])] * (lanes // LANES), axis=1)
    with_bias = high[0]
    for piece in range(3):
        rounded = line.astype(jnp.bfloat16).astype(jnp.float32)
        with_bias = jnp.where(held & (image_row == 12 + piece), rounded, with_bias)
        line = line - rounded
    stacked = jnp.concatenate([with_bias, *high[1:], *high, *low], axis=0)
    weights_one[...] = stacked.T[: weights_one.shape[0]].astype(jnp.bfloat16)
    row = lax.broadcasted_iota(jnp.int32, bias_rows.shape, 0) // TILE
    lane = lax.broadcasted_iota(jnp.int32, bias_rows.shape, 1)
    line = jnp.where(row == lane, four_times(bias_two[...]), 0.0)
    bias_rows[...] = jnp.broadcast_to(jnp.sum(line, axis=1, keepdims=True), bias_rows.shape)
    lines = [[four_times(two[shift, tap].astype(jnp.float32)) for shift in range(3)] for tap in range(3)]
    row = lax.broadcasted_iota(jnp.int32, (TILE, LANES), 0)
    lane = lax.broadcasted_iota(jnp.int32, (TILE, LANES), 1) // channels
    zero = jnp.zeros((TILE, LANES), jnp.float32)
    for tile in range(-(-3 * rows // per_tile)):
        taps = sorted({(tile * per_tile + g) // rows for g in range(per_tile)} & {0, 1, 2})
        masks = []
        for tap in taps:
            hidden_row = tile * per_tile + lane - tap * rows
            inside = (hidden_row >= 0) & (hidden_row < rows)
            masks += [(tap, shift, inside & (hidden_row - row == shift)) for shift in range(3)]
        width = min(LANES, weights_two.shape[1] - tile * LANES)
        for channel in range(0, channels, 2):
            pair = []
            for k in (channel, channel + 1):
                values = zero
                for tap, shift, mask in masks:
                    values = jnp.where(mask, lines[tap][shift][k : k + 1], values)
                pair.append(values)
            block = jnp.concatenate(pair, axis=0).astype(jnp.bfloat16)
            weights_two[TILE * channel : TILE * (channel + 2), tile * LANES : tile * LANES + width] = block[:, :width]
    get_table.wait()


def shifted(values, width):
    lane = lax.broadcasted_iota(jnp.int32, values.shape, 1)
    zero = jnp.zeros_like(values)
    before = jnp.where(lane == 0, zero, pltpu.roll(values, 1, 1))
    after = jnp.where(lane == width - 1, zero, pltpu.roll(values, width - 1, 1))
    return before, values, after


def layers_kernel(shares, weights_one, weights_two, bias_rows, table, out, staged, sems):
    width = out.shape[2]
    vis, row, col = (lax.axis_size(axis) for axis in ALL)
    upper = lax.broadcasted_iota(jnp.int32, (TILE, 2 * LANES), 0) < TILE // 2
    depth = 2 * LANES
    image = jnp.zeros((4 * TILE, width), jnp.float32)
    for r in range(row):
        senders = [(v * row + r) * col + c for v in range(vis) for c in range(col)]
        total = shares[senders[0]].astype(jnp.float32)
        for sender in senders[1:]:
            total = total + shares[sender].astype(jnp.float32)
        middle = total[TILE : 2 * TILE]
        above = jnp.concatenate([total[:TILE], total[2 * TILE :]], axis=1)
        below = jnp.concatenate([middle, pltpu.roll(middle, TILE // 2, 0)], axis=1)
        turned = jnp.concatenate([above, jnp.where(upper, below, 0.0)], axis=0)
        high = turned.astype(jnp.bfloat16)
        low = (turned - high.astype(jnp.float32)).astype(jnp.bfloat16)
        block = table[r * depth : (r + 1) * depth]
        image = image + jnp.dot(jnp.concatenate([high, low], axis=0), block, preferred_element_type=jnp.float32)
    image = image[: 2 * TILE] + image[2 * TILE :]
    columns = jnp.concatenate(shifted(image, width), axis=0)
    high = columns.astype(jnp.bfloat16).astype(jnp.float32)
    low = columns - high
    row = lax.broadcasted_iota(jnp.int32, (48, width), 0)
    with_ones = jnp.where((row >= 12) & (row < 15), 1.0, high)
    stacked = jnp.concatenate([with_ones, low, high], axis=0).astype(jnp.bfloat16)
    hidden = jnp.dot(weights_one[...], stacked, preferred_element_type=jnp.float32)
    hidden = jnp.maximum(hidden, 0.0).astype(jnp.bfloat16)
    stacked = jnp.concatenate(shifted(hidden, width), axis=0)
    parts = sems.shape[0]
    group = out.shape[0] // parts
    copies = []
    for part in range(parts):
        rows = pl.ds(part * group * TILE, group * TILE)
        features = jnp.dot(weights_two[rows], stacked, preferred_element_type=jnp.float32)
        features = features + jnp.concatenate([bias_rows[rows]] * (width // LANES), axis=1)
        channels_of = pl.ds(part * group, group)
        staged[channels_of] = features.reshape(group, TILE, width).astype(out.dtype)
        copies.append(pltpu.make_async_copy(staged.at[channels_of], out.at[channels_of], sems.at[part]))
        copies[-1].start()
    for copy in copies:
        copy.wait()


def in_hbm(*arrays):
    return [pltpu.with_memory_space_constraint(array, pltpu.HBM) for array in arrays]


def direct(partials, coverage, conv_one, bias_one, conv_two, bias_two):
    count_row, count_col = lax.axis_size("row"), lax.axis_size("col")
    devices = lax.axis_size("vis") * count_row * count_col
    length = partials.shape[3] * count_col
    image_len = length // 2
    channels = conv_two.shape[2]
    first, second = grid_tables(length, count_row, count_col)
    vmem, hbm = pl.BlockSpec(memory_space=pltpu.VMEM), pl.BlockSpec(memory_space=pltpu.HBM)
    limit = pltpu.CompilerParams(vmem_limit_bytes=16 * 2**20)
    share = (devices, 2 * (TILE + 2 * HALO), LANES)
    shares = pl.pallas_call(
        share_kernel,
        out_shape=jax.ShapeDtypeStruct(share, jnp.bfloat16),
        in_specs=[hbm] * 3,
        out_specs=vmem,
        scratch_shapes=[
            pltpu.SMEM(coverage.shape, jnp.int32),
            pltpu.VMEM(partials.shape, jnp.bfloat16),
            pltpu.VMEM(first.shape[1:], jnp.bfloat16),
            pltpu.SemaphoreType.DMA((3,)),
        ],
        compiler_params=limit,
        name="shares",
    )(*in_hbm(coverage, partials, jnp.asarray(first)))
    arrived = lax.all_to_all(shares, ALL, split_axis=0, concat_axis=0, tiled=True)
    rows = TILE + 2
    weights = pl.pallas_call(
        weights_kernel,
        out_shape=[
            jax.ShapeDtypeStruct((rows * channels, 3 * 48), jnp.bfloat16),
            jax.ShapeDtypeStruct((TILE * channels, 3 * rows * channels), jnp.bfloat16),
            jax.ShapeDtypeStruct((TILE * channels, LANES), jnp.float32),
            jax.ShapeDtypeStruct(second.shape, jnp.bfloat16),
        ],
        in_specs=[hbm] * 5,
        out_specs=[vmem] * 4,
        scratch_shapes=[
            pltpu.VMEM((3, 3, channels), jnp.float32),
            pltpu.VMEM((1, channels), jnp.float32),
            pltpu.VMEM(conv_two.shape, jnp.bfloat16),
            pltpu.VMEM((1, channels), jnp.float32),
            pltpu.SemaphoreType.DMA((5,)),
        ],
        compiler_params=limit,
        name="weights",
    )(*in_hbm(conv_one.transpose(1, 2, 0), bias_one[None], conv_two, bias_two[None], jnp.asarray(second)))
    return pl.pallas_call(
        layers_kernel,
        out_shape=jax.ShapeDtypeStruct((channels, TILE, image_len), jnp.bfloat16),
        in_specs=[vmem] * 5,
        out_specs=hbm,
        scratch_shapes=[
            pltpu.VMEM((channels, TILE, image_len), jnp.bfloat16),
            pltpu.SemaphoreType.DMA((4,)),
        ],
        compiler_params=limit,
        name="layers",
    )(arrived, *weights)


def local(partials, coverage, conv_one, bias_one, conv_two, bias_two):
    count_col = lax.axis_size("col")
    devices = lax.axis_size("vis") * lax.axis_size("row") * count_col
    image_len = partials.shape[3] * count_col // 2
    sent = devices * (TILE + 2 * HALO) * image_len * 2
    fits = partials.shape[2] == LANES and image_len == devices * TILE and conv_two.shape[2] * 4 == LANES and image_len == 2 * LANES and sent <= DIRECT_BYTES
    plan = direct if fits else staged
    return plan(partials, coverage, conv_one, bias_one, conv_two, bias_two)


def solution(mesh):
    placed = (P("vis", None, "row", "col"), P("vis", "row", "col"), P(), P(), P(), P())
    return jax.shard_map(
        local,
        mesh=mesh,
        in_specs=placed,
        out_specs=P(None, ALL, None),
        check_vma=False,
    )
```

```python
import math

import jax
import jax.numpy as jnp
import numpy as np
from jax import lax
from jax.experimental import pallas as pl
from jax.experimental.pallas import tpu as pltpu
from jax.sharding import PartitionSpec as P

BLK = 128
ALL = ("vis", "row", "col")
DIRECT_BYTES = 4 * 2**20
HALO = 2
TILE = 8
LANES = 128


def with_halo(cells, sides, width):
    for axis, dim in sides:
        count = lax.axis_size(axis)
        ends = count - 1
        head = lax.slice_in_dim(cells, 0, width, axis=dim)
        tail = lax.slice_in_dim(cells, cells.shape[dim] - width, cells.shape[dim], axis=dim)
        cells = jnp.concatenate(
            [
                lax.ppermute(tail, axis, [(i, (i + 1) % count) for i in range(ends)]),
                cells,
                lax.ppermute(head, axis, [((i + 1) % count, i) for i in range(ends)]),
            ],
            axis=dim,
        )
    return cells


def phase_table(numer, denom):
    angle = numer.astype(jnp.float32) * (2.0 * math.pi / denom)
    return (jnp.cos(angle), jnp.sin(angle))


def partial_transform(real_part, imag_part, block_of, keep_imag):
    batch = real_part.shape[0]
    count_blocks = real_part.shape[1]
    block_len = real_part.shape[2]
    length = count_blocks * block_len
    highest = lax.Precision.HIGHEST
    outer = jnp.arange(count_blocks, dtype=jnp.int32)
    inner = jnp.arange(block_len, dtype=jnp.int32)
    cos_one, sin_one = phase_table(block_of[:, None] * outer[None, :] % count_blocks, count_blocks)
    mid_re = jnp.einsum("lpt,px->lxt", real_part, cos_one, precision=highest) - jnp.einsum(
        "lpt,px->lxt", imag_part, sin_one, precision=highest
    )
    mid_im = jnp.einsum("lpt,px->lxt", real_part, sin_one, precision=highest) + jnp.einsum(
        "lpt,px->lxt", imag_part, cos_one, precision=highest
    )
    cos_two, sin_two = phase_table(outer[:, None] * inner[None, :] % length, length)
    parity = (1 - 2 * (outer % 2)).astype(jnp.float32)[:, None]
    cos_two = cos_two * parity
    sin_two = sin_two * parity
    turn_re = mid_re * cos_two - mid_im * sin_two
    turn_im = mid_re * sin_two + mid_im * cos_two
    kept = jnp.arange(block_len // 2, dtype=jnp.int32)
    picked = (kept + 3 * block_len // 4) % block_len
    cos_three, sin_three = phase_table(inner[:, None] * picked[None, :] % block_len, block_len)
    out_re = jnp.einsum("lxt,tj->ljx", turn_re, cos_three, precision=highest) - jnp.einsum(
        "lxt,tj->ljx", turn_im, sin_three, precision=highest
    )
    out_re = out_re.reshape(batch, length // 2)
    if keep_imag:
        out_im = jnp.einsum("lxt,tj->ljx", turn_re, sin_three, precision=highest) + jnp.einsum(
            "lxt,tj->ljx", turn_im, cos_three, precision=highest
        )
        return (out_re, out_im.reshape(batch, length // 2))
    return (out_re, out_re)


def first_layer(extended, conv_one, bias_one, count_rows):
    width = extended.shape[1]
    padded = jnp.pad(extended, ((0, 0), (1, 1)))
    summed = (
        jnp.zeros((conv_one.shape[0], count_rows, width), jnp.float32) + bias_one[:, None, None]
    )
    for shift_b in range(3):
        for shift_a in range(3):
            summed = (
                summed
                + conv_one[:, shift_b, shift_a][:, None, None]
                * padded[None, shift_b : shift_b + count_rows, shift_a : shift_a + width]
            )
    return jnp.maximum(summed, 0.0)


def second_layer(hidden_ext, conv_two, bias_two, count_rows):
    width = hidden_ext.shape[2]
    padded = jnp.pad(hidden_ext, ((0, 0), (0, 0), (1, 1)))
    summed = jnp.zeros((conv_two.shape[2], count_rows, width), jnp.float32)
    for shift_b in range(3):
        for shift_a in range(3):
            summed = summed + jnp.einsum(
                "kj,jba->kba",
                conv_two[shift_b, shift_a],
                padded[:, shift_b : shift_b + count_rows, shift_a : shift_a + width],
                preferred_element_type=jnp.float32,
            )
    return (summed + bias_two[:, None, None]).astype(jnp.bfloat16)


def staged(partials, coverage, conv_one, bias_one, conv_two, bias_two):
    count_vis = lax.axis_size("vis")
    count_row = lax.axis_size("row")
    count_col = lax.axis_size("col")
    grid_len = partials.shape[3] * count_col
    cover = coverage[0]
    block_rows = cover.shape[0]
    block_cols = cover.shape[1]
    spread = jnp.broadcast_to(cover[:, None, :, None], (block_rows, BLK, block_cols, BLK))
    spread = spread.reshape(block_rows * BLK, block_cols * BLK)
    count_blocks = count_vis * count_row
    row_block = grid_len // count_blocks
    row_share = row_block // count_col
    masked = partials[0] * spread.astype(jnp.bfloat16)[None]
    reduced = lax.psum_scatter(
        masked.astype(jnp.float32).astype(jnp.bfloat16), "vis", scatter_dimension=1, tiled=True
    ).astype(jnp.float32)
    grid_rows = lax.all_to_all(
        reduced.astype(jnp.bfloat16), "col", split_axis=1, concat_axis=2, tiled=True
    ).astype(reduced.dtype)
    natural = jnp.arange(count_blocks, dtype=jnp.int32)
    shaped = grid_rows.reshape(2, row_share, count_blocks, row_block)
    first_re, first_im = partial_transform(shaped[0], shaped[1], natural, True)
    stacked = jnp.stack([first_re, first_im])
    moved = lax.all_to_all(
        lax.all_to_all(
            stacked.astype(jnp.bfloat16), ("vis", "row"), split_axis=2, concat_axis=1, tiled=True
        ),
        "col",
        split_axis=2,
        concat_axis=1,
        tiled=True,
    ).astype(stacked.dtype)
    img_rows = moved.shape[2]
    arranged = moved.reshape(2, count_col, count_blocks, row_share, img_rows)
    arranged = arranged.transpose(0, 4, 2, 1, 3).reshape(2, img_rows, count_blocks, row_block)
    owners = natural % count_row * count_vis + natural // count_row
    image, unused = partial_transform(arranged[0], arranged[1], owners, False)
    image = image * (1.0 / grid_len)
    extended = with_halo(image.astype(jnp.bfloat16), ((("vis", "row", "col"), 0),), 1).astype(
        image.dtype
    )
    hidden = first_layer(extended, conv_one, bias_one, img_rows).astype(jnp.bfloat16)
    hidden_ext = with_halo(hidden, ((("vis", "row", "col"), 1),), 1)
    return second_layer(hidden_ext, conv_two, bias_two, img_rows)


def grid_tables(length, count_row, count_col):
    image_len = length // 2
    place = np.arange(length)[:, None] - length // 2
    pixel = np.arange(image_len)[None, :] - image_len // 2
    angle = (place * pixel % length) * (2.0 * math.pi / length)
    cos, sin = np.cos(angle), np.sin(angle)
    padded = np.pad(np.stack([cos.T, sin.T]), ((0, 0), (HALO, TILE - HALO), (0, 0)))
    first = padded.reshape(2 * (image_len + TILE), count_col, length // count_col).transpose(1, 0, 2)
    rows = length // count_row
    second = np.stack([cos.reshape(count_row, rows, image_len), -sin.reshape(count_row, rows, image_len)], axis=1)
    second = second.reshape(2 * length, image_len) / length
    return first.astype(jnp.bfloat16), second.astype(jnp.bfloat16)


def share_kernel(cover_in, parts_in, first_all, out, cover, parts, first, sems):
    get_cover = pltpu.make_async_copy(cover_in, cover, sems.at[0])
    get_parts = pltpu.make_async_copy(parts_in, parts, sems.at[1])
    get_first = pltpu.make_async_copy(first_all.at[lax.axis_index("col")], first, sems.at[2])
    for copy in (get_cover, get_parts, get_first):
        copy.start()
    count_rows = parts.shape[2]
    get_cover.wait()
    get_parts.wait()
    components = []
    for component in range(2):
        strips = []
        for i in range(cover.shape[1]):
            cells = []
            for j in range(cover.shape[2]):
                block = parts[0, component, i * BLK : (i + 1) * BLK, j * BLK : (j + 1) * BLK]
                level = jnp.full(block.shape, cover[0, i, j].astype(jnp.float32)).astype(jnp.bfloat16)
                cells.append(block * level)
            strips.append(jnp.concatenate(cells, axis=1))
        components.append(jnp.concatenate(strips, axis=0))
    grid = jnp.concatenate(components, axis=0).T
    upper = lax.broadcasted_iota(jnp.int32, (TILE, LANES), 0) < TILE // 2
    devices = out.shape[0]
    tall = first.shape[0] // 2
    get_first.wait()
    turned = jnp.dot(first[...], grid, preferred_element_type=jnp.float32)
    mid_re = turned[:tall, :count_rows] - turned[tall:, count_rows:]
    mid_im = turned[tall:, :count_rows] + turned[:tall, count_rows:]
    for device in range(devices):
        here = slice(TILE * device, TILE * (device + 1))
        below = slice(TILE * (device + 1), TILE * (device + 2))
        middle = jnp.where(upper, mid_re[below], pltpu.roll(mid_im[below], TILE // 2, 0))
        out[device] = jnp.concatenate([mid_re[here], middle, mid_im[here]], axis=0).astype(out.dtype)


def own_place():
    place, count = 0, 1
    for axis in ALL:
        place = place * lax.axis_size(axis) + lax.axis_index(axis)
        count = count * lax.axis_size(axis)
    return place, count - 1


def four_times(values):
    return jnp.concatenate([values] * 4, axis=1)


def weights_kernel(
    one_in, bias_in, two_in, bias_two_in, table_in, weights_one, weights_two, bias_rows, table, one, bias, two, bias_two, sems
):
    fetch = [
        pltpu.make_async_copy(one_in, one, sems.at[0]),
        pltpu.make_async_copy(bias_in, bias, sems.at[1]),
        pltpu.make_async_copy(two_in, two, sems.at[2]),
        pltpu.make_async_copy(bias_two_in, bias_two, sems.at[3]),
    ]
    get_table = pltpu.make_async_copy(table_in, table, sems.at[4])
    for copy in (*fetch, get_table):
        copy.start()
    for copy in fetch:
        copy.wait()
    channels = one.shape[2]
    rows = TILE + 2
    per_tile = LANES // channels
    lanes = -(-rows * channels // LANES) * LANES
    image_row = lax.broadcasted_iota(jnp.int32, (16, lanes), 0)
    hidden_row = lax.broadcasted_iota(jnp.int32, (16, lanes), 1) // channels
    place, last = own_place()
    held = (hidden_row >= jnp.where(place == 0, 1, 0)) & (hidden_row < jnp.where(place == last, rows - 1, rows))
    high, low = [], []
    for tap in range(3):
        band = jnp.zeros((16, lanes), jnp.float32)
        for shift in range(3):
            line = jnp.concatenate([four_times(one[shift, tap : tap + 1])] * (lanes // LANES), axis=1)
            band = jnp.where(held & (image_row - hidden_row == shift), line, band)
        high.append(band.astype(jnp.bfloat16).astype(jnp.float32))
        low.append(band - high[-1])
    line = jnp.concatenate([four_times(bias[...])] * (lanes // LANES), axis=1)
    with_bias = high[0]
    for piece in range(3):
        rounded = line.astype(jnp.bfloat16).astype(jnp.float32)
        with_bias = jnp.where(held & (image_row == 12 + piece), rounded, with_bias)
        line = line - rounded
    stacked = jnp.concatenate([with_bias, *high[1:], *high, *low], axis=0)
    weights_one[...] = stacked.T[: weights_one.shape[0]].astype(jnp.bfloat16)
    row = lax.broadcasted_iota(jnp.int32, bias_rows.shape, 0) // TILE
    lane = lax.broadcasted_iota(jnp.int32, bias_rows.shape, 1)
    line = jnp.where(row == lane, four_times(bias_two[...]), 0.0)
    bias_rows[...] = jnp.broadcast_to(jnp.sum(line, axis=1, keepdims=True), bias_rows.shape)
    lines = [[four_times(two[shift, tap].astype(jnp.float32)) for shift in range(3)] for tap in range(3)]
    row = lax.broadcasted_iota(jnp.int32, (TILE, LANES), 0)
    lane = lax.broadcasted_iota(jnp.int32, (TILE, LANES), 1) // channels
    zero = jnp.zeros((TILE, LANES), jnp.float32)
    for tile in range(-(-3 * rows // per_tile)):
        taps = sorted({(tile * per_tile + g) // rows for g in range(per_tile)} & {0, 1, 2})
        masks = []
        for tap in taps:
            hidden_row = tile * per_tile + lane - tap * rows
            inside = (hidden_row >= 0) & (hidden_row < rows)
            masks += [(tap, shift, inside & (hidden_row - row == shift)) for shift in range(3)]
        width = min(LANES, weights_two.shape[1] - tile * LANES)
        for channel in range(0, channels, 2):
            pair = []
            for k in (channel, channel + 1):
                values = zero
                for tap, shift, mask in masks:
                    values = jnp.where(mask, lines[tap][shift][k : k + 1], values)
                pair.append(values)
            block = jnp.concatenate(pair, axis=0).astype(jnp.bfloat16)
            weights_two[TILE * channel : TILE * (channel + 2), tile * LANES : tile * LANES + width] = block[:, :width]
    get_table.wait()


def shifted(values, width):
    lane = lax.broadcasted_iota(jnp.int32, values.shape, 1)
    zero = jnp.zeros_like(values)
    before = jnp.where(lane == 0, zero, pltpu.roll(values, 1, 1))
    after = jnp.where(lane == width - 1, zero, pltpu.roll(values, width - 1, 1))
    return before, values, after


def layers_kernel(shares, weights_one, weights_two, bias_rows, table, out, staged, sems):
    width = out.shape[2]
    vis, row, col = (lax.axis_size(axis) for axis in ALL)
    upper = lax.broadcasted_iota(jnp.int32, (TILE, 2 * LANES), 0) < TILE // 2
    depth = 2 * LANES
    image = jnp.zeros((4 * TILE, width), jnp.float32)
    for r in range(row):
        senders = [(v * row + r) * col + c for v in range(vis) for c in range(col)]
        total = shares[senders[0]].astype(jnp.float32)
        for sender in senders[1:]:
            total = total + shares[sender].astype(jnp.float32)
        middle = total[TILE : 2 * TILE]
        above = jnp.concatenate([total[:TILE], total[2 * TILE :]], axis=1)
        below = jnp.concatenate([middle, pltpu.roll(middle, TILE // 2, 0)], axis=1)
        turned = jnp.concatenate([above, jnp.where(upper, below, 0.0)], axis=0)
        high = turned.astype(jnp.bfloat16)
        low = (turned - high.astype(jnp.float32)).astype(jnp.bfloat16)
        block = table[r * depth : (r + 1) * depth]
        image = image + jnp.dot(jnp.concatenate([high, low], axis=0), block, preferred_element_type=jnp.float32)
    image = image[: 2 * TILE] + image[2 * TILE :]
    columns = jnp.concatenate(shifted(image, width), axis=0)
    high = columns.astype(jnp.bfloat16).astype(jnp.float32)
    low = columns - high
    row = lax.broadcasted_iota(jnp.int32, (48, width), 0)
    with_ones = jnp.where((row >= 12) & (row < 15), 1.0, high)
    stacked = jnp.concatenate([with_ones, low, high], axis=0).astype(jnp.bfloat16)
    hidden = jnp.dot(weights_one[...], stacked, preferred_element_type=jnp.float32)
    hidden = jnp.maximum(hidden, 0.0).astype(jnp.bfloat16)
    stacked = jnp.concatenate(shifted(hidden, width), axis=0)
    half = out.shape[0] // 2
    copies = []
    for part in range(2):
        rows = pl.ds(part * half * TILE, half * TILE)
        features = jnp.dot(weights_two[rows], stacked, preferred_element_type=jnp.float32)
        features = features + jnp.concatenate([bias_rows[rows]] * (width // LANES), axis=1)
        channels_of = pl.ds(part * half, half)
        staged[channels_of] = features.reshape(half, TILE, width).astype(out.dtype)
        copies.append(pltpu.make_async_copy(staged.at[channels_of], out.at[channels_of], sems.at[part]))
        copies[-1].start()
    for copy in copies:
        copy.wait()


def in_hbm(*arrays):
    return [pltpu.with_memory_space_constraint(array, pltpu.HBM) for array in arrays]


def direct(partials, coverage, conv_one, bias_one, conv_two, bias_two):
    count_row, count_col = lax.axis_size("row"), lax.axis_size("col")
    devices = lax.axis_size("vis") * count_row * count_col
    length = partials.shape[3] * count_col
    image_len = length // 2
    channels = conv_two.shape[2]
    first, second = grid_tables(length, count_row, count_col)
    vmem, hbm = pl.BlockSpec(memory_space=pltpu.VMEM), pl.BlockSpec(memory_space=pltpu.HBM)
    limit = pltpu.CompilerParams(vmem_limit_bytes=16 * 2**20)
    share = (devices, 2 * (TILE + 2 * HALO), LANES)
    shares = pl.pallas_call(
        share_kernel,
        out_shape=jax.ShapeDtypeStruct(share, jnp.bfloat16),
        in_specs=[hbm] * 3,
        out_specs=vmem,
        scratch_shapes=[
            pltpu.SMEM(coverage.shape, jnp.int32),
            pltpu.VMEM(partials.shape, jnp.bfloat16),
            pltpu.VMEM(first.shape[1:], jnp.bfloat16),
            pltpu.SemaphoreType.DMA((3,)),
        ],
        compiler_params=limit,
        name="shares",
    )(*in_hbm(coverage, partials, jnp.asarray(first)))
    arrived = lax.all_to_all(shares, ALL, split_axis=0, concat_axis=0, tiled=True)
    rows = TILE + 2
    weights = pl.pallas_call(
        weights_kernel,
        out_shape=[
            jax.ShapeDtypeStruct((rows * channels, 3 * 48), jnp.bfloat16),
            jax.ShapeDtypeStruct((TILE * channels, 3 * rows * channels), jnp.bfloat16),
            jax.ShapeDtypeStruct((TILE * channels, LANES), jnp.float32),
            jax.ShapeDtypeStruct(second.shape, jnp.bfloat16),
        ],
        in_specs=[hbm] * 5,
        out_specs=[vmem] * 4,
        scratch_shapes=[
            pltpu.VMEM((3, 3, channels), jnp.float32),
            pltpu.VMEM((1, channels), jnp.float32),
            pltpu.VMEM(conv_two.shape, jnp.bfloat16),
            pltpu.VMEM((1, channels), jnp.float32),
            pltpu.SemaphoreType.DMA((5,)),
        ],
        compiler_params=limit,
        name="weights",
    )(*in_hbm(conv_one.transpose(1, 2, 0), bias_one[None], conv_two, bias_two[None], jnp.asarray(second)))
    return pl.pallas_call(
        layers_kernel,
        out_shape=jax.ShapeDtypeStruct((channels, TILE, image_len), jnp.bfloat16),
        in_specs=[vmem] * 5,
        out_specs=hbm,
        scratch_shapes=[
            pltpu.VMEM((channels, TILE, image_len), jnp.bfloat16),
            pltpu.SemaphoreType.DMA((2,)),
        ],
        compiler_params=limit,
        name="layers",
    )(arrived, *weights)


def local(partials, coverage, conv_one, bias_one, conv_two, bias_two):
    count_col = lax.axis_size("col")
    devices = lax.axis_size("vis") * lax.axis_size("row") * count_col
    image_len = partials.shape[3] * count_col // 2
    sent = devices * (TILE + 2 * HALO) * image_len * 2
    fits = partials.shape[2] == LANES and image_len == devices * TILE and conv_two.shape[2] * 4 == LANES and image_len == 2 * LANES and sent <= DIRECT_BYTES
    plan = direct if fits else staged
    return plan(partials, coverage, conv_one, bias_one, conv_two, bias_two)


def solution(mesh):
    placed = (P("vis", None, "row", "col"), P("vis", "row", "col"), P(), P(), P(), P())
    return jax.shard_map(
        local,
        mesh=mesh,
        in_specs=placed,
        out_specs=P(None, ALL, None),
        check_vma=False,
    )
```

```python
import math

import jax
import jax.numpy as jnp
import numpy as np
from jax import lax
from jax.experimental import pallas as pl
from jax.experimental.pallas import tpu as pltpu
from jax.sharding import PartitionSpec as P

BLK = 128
ALL = ("vis", "row", "col")
DIRECT_BYTES = 4 * 2**20
HALO = 2
TILE = 8
LANES = 128


def with_halo(cells, sides, width):
    for axis, dim in sides:
        count = lax.axis_size(axis)
        ends = count - 1
        head = lax.slice_in_dim(cells, 0, width, axis=dim)
        tail = lax.slice_in_dim(cells, cells.shape[dim] - width, cells.shape[dim], axis=dim)
        cells = jnp.concatenate(
            [
                lax.ppermute(tail, axis, [(i, (i + 1) % count) for i in range(ends)]),
                cells,
                lax.ppermute(head, axis, [((i + 1) % count, i) for i in range(ends)]),
            ],
            axis=dim,
        )
    return cells


def phase_table(numer, denom):
    angle = numer.astype(jnp.float32) * (2.0 * math.pi / denom)
    return (jnp.cos(angle), jnp.sin(angle))


def partial_transform(real_part, imag_part, block_of, keep_imag):
    batch = real_part.shape[0]
    count_blocks = real_part.shape[1]
    block_len = real_part.shape[2]
    length = count_blocks * block_len
    highest = lax.Precision.HIGHEST
    outer = jnp.arange(count_blocks, dtype=jnp.int32)
    inner = jnp.arange(block_len, dtype=jnp.int32)
    cos_one, sin_one = phase_table(block_of[:, None] * outer[None, :] % count_blocks, count_blocks)
    mid_re = jnp.einsum("lpt,px->lxt", real_part, cos_one, precision=highest) - jnp.einsum(
        "lpt,px->lxt", imag_part, sin_one, precision=highest
    )
    mid_im = jnp.einsum("lpt,px->lxt", real_part, sin_one, precision=highest) + jnp.einsum(
        "lpt,px->lxt", imag_part, cos_one, precision=highest
    )
    cos_two, sin_two = phase_table(outer[:, None] * inner[None, :] % length, length)
    parity = (1 - 2 * (outer % 2)).astype(jnp.float32)[:, None]
    cos_two = cos_two * parity
    sin_two = sin_two * parity
    turn_re = mid_re * cos_two - mid_im * sin_two
    turn_im = mid_re * sin_two + mid_im * cos_two
    kept = jnp.arange(block_len // 2, dtype=jnp.int32)
    picked = (kept + 3 * block_len // 4) % block_len
    cos_three, sin_three = phase_table(inner[:, None] * picked[None, :] % block_len, block_len)
    out_re = jnp.einsum("lxt,tj->ljx", turn_re, cos_three, precision=highest) - jnp.einsum(
        "lxt,tj->ljx", turn_im, sin_three, precision=highest
    )
    out_re = out_re.reshape(batch, length // 2)
    if keep_imag:
        out_im = jnp.einsum("lxt,tj->ljx", turn_re, sin_three, precision=highest) + jnp.einsum(
            "lxt,tj->ljx", turn_im, cos_three, precision=highest
        )
        return (out_re, out_im.reshape(batch, length // 2))
    return (out_re, out_re)


def first_layer(extended, conv_one, bias_one, count_rows):
    width = extended.shape[1]
    padded = jnp.pad(extended, ((0, 0), (1, 1)))
    summed = (
        jnp.zeros((conv_one.shape[0], count_rows, width), jnp.float32) + bias_one[:, None, None]
    )
    for shift_b in range(3):
        for shift_a in range(3):
            summed = (
                summed
                + conv_one[:, shift_b, shift_a][:, None, None]
                * padded[None, shift_b : shift_b + count_rows, shift_a : shift_a + width]
            )
    return jnp.maximum(summed, 0.0)


def second_layer(hidden_ext, conv_two, bias_two, count_rows):
    width = hidden_ext.shape[2]
    padded = jnp.pad(hidden_ext, ((0, 0), (0, 0), (1, 1)))
    summed = jnp.zeros((conv_two.shape[2], count_rows, width), jnp.float32)
    for shift_b in range(3):
        for shift_a in range(3):
            summed = summed + jnp.einsum(
                "kj,jba->kba",
                conv_two[shift_b, shift_a],
                padded[:, shift_b : shift_b + count_rows, shift_a : shift_a + width],
                preferred_element_type=jnp.float32,
            )
    return (summed + bias_two[:, None, None]).astype(jnp.bfloat16)


def staged(partials, coverage, conv_one, bias_one, conv_two, bias_two):
    count_vis = lax.axis_size("vis")
    count_row = lax.axis_size("row")
    count_col = lax.axis_size("col")
    grid_len = partials.shape[3] * count_col
    cover = coverage[0]
    block_rows = cover.shape[0]
    block_cols = cover.shape[1]
    spread = jnp.broadcast_to(cover[:, None, :, None], (block_rows, BLK, block_cols, BLK))
    spread = spread.reshape(block_rows * BLK, block_cols * BLK)
    count_blocks = count_vis * count_row
    row_block = grid_len // count_blocks
    row_share = row_block // count_col
    masked = partials[0] * spread.astype(jnp.bfloat16)[None]
    reduced = lax.psum_scatter(
        masked.astype(jnp.float32).astype(jnp.bfloat16), "vis", scatter_dimension=1, tiled=True
    ).astype(jnp.float32)
    grid_rows = lax.all_to_all(
        reduced.astype(jnp.bfloat16), "col", split_axis=1, concat_axis=2, tiled=True
    ).astype(reduced.dtype)
    natural = jnp.arange(count_blocks, dtype=jnp.int32)
    shaped = grid_rows.reshape(2, row_share, count_blocks, row_block)
    first_re, first_im = partial_transform(shaped[0], shaped[1], natural, True)
    stacked = jnp.stack([first_re, first_im])
    moved = lax.all_to_all(
        lax.all_to_all(
            stacked.astype(jnp.bfloat16), ("vis", "row"), split_axis=2, concat_axis=1, tiled=True
        ),
        "col",
        split_axis=2,
        concat_axis=1,
        tiled=True,
    ).astype(stacked.dtype)
    img_rows = moved.shape[2]
    arranged = moved.reshape(2, count_col, count_blocks, row_share, img_rows)
    arranged = arranged.transpose(0, 4, 2, 1, 3).reshape(2, img_rows, count_blocks, row_block)
    owners = natural % count_row * count_vis + natural // count_row
    image, unused = partial_transform(arranged[0], arranged[1], owners, False)
    image = image * (1.0 / grid_len)
    extended = with_halo(image.astype(jnp.bfloat16), ((("vis", "row", "col"), 0),), 1).astype(
        image.dtype
    )
    hidden = first_layer(extended, conv_one, bias_one, img_rows).astype(jnp.bfloat16)
    hidden_ext = with_halo(hidden, ((("vis", "row", "col"), 1),), 1)
    return second_layer(hidden_ext, conv_two, bias_two, img_rows)


def grid_tables(length, count_row, count_col):
    image_len = length // 2
    place = np.arange(length)[:, None] - length // 2
    pixel = np.arange(image_len)[None, :] - image_len // 2
    angle = (place * pixel % length) * (2.0 * math.pi / length)
    cos, sin = np.cos(angle), np.sin(angle)
    padded = np.pad(np.stack([cos.T, sin.T]), ((0, 0), (HALO, TILE - HALO), (0, 0)))
    first = padded.reshape(2 * (image_len + TILE), count_col, length // count_col).transpose(1, 0, 2)
    rows = length // count_row
    second = np.stack([cos.reshape(count_row, rows, image_len), -sin.reshape(count_row, rows, image_len)], axis=1)
    second = second.reshape(2 * length, image_len) / length
    return first.astype(jnp.bfloat16), second.astype(jnp.bfloat16)


def send_order():
    vis, row, col = (lax.axis_size(axis) for axis in ALL)
    pairs = 2 if vis % 2 == 0 else 1
    places = np.arange(vis * row * col).reshape(vis // pairs, pairs, row, col)
    return places[..., ::-1].reshape(-1).tolist()


def share_kernel(cover_in, parts_in, first_all, out, cover, parts, first, sems):
    get_cover = pltpu.make_async_copy(cover_in, cover, sems.at[0])
    get_parts = pltpu.make_async_copy(parts_in, parts, sems.at[1])
    get_first = pltpu.make_async_copy(first_all.at[lax.axis_index("col")], first, sems.at[2])
    for copy in (get_cover, get_parts, get_first):
        copy.start()
    count_rows = parts.shape[2]
    get_cover.wait()
    get_parts.wait()
    components = []
    for component in range(2):
        strips = []
        for i in range(cover.shape[1]):
            cells = []
            for j in range(cover.shape[2]):
                block = parts[0, component, i * BLK : (i + 1) * BLK, j * BLK : (j + 1) * BLK]
                level = jnp.full(block.shape, cover[0, i, j].astype(jnp.float32)).astype(jnp.bfloat16)
                cells.append(block * level)
            strips.append(jnp.concatenate(cells, axis=1))
        components.append(jnp.concatenate(strips, axis=0))
    grid = jnp.concatenate(components, axis=0)
    upper = lax.broadcasted_iota(jnp.int32, (TILE, LANES), 0) < TILE // 2
    tall = first.shape[0] // 2
    get_first.wait()
    turned = lax.dot_general(first[...], grid, (((1,), (1,)), ((), ())), preferred_element_type=jnp.float32)
    mid_re = turned[:tall, :count_rows] - turned[tall:, count_rows:]
    mid_im = turned[tall:, :count_rows] + turned[:tall, count_rows:]
    for slot, device in enumerate(send_order()):
        here = slice(TILE * device, TILE * (device + 1))
        below = slice(TILE * (device + 1), TILE * (device + 2))
        middle = jnp.where(upper, mid_re[below], pltpu.roll(mid_im[below], TILE // 2, 0))
        out[slot] = jnp.concatenate([mid_re[here], middle, mid_im[here]], axis=0).astype(out.dtype)


def own_place():
    place, count = 0, 1
    for axis in ALL:
        place = place * lax.axis_size(axis) + lax.axis_index(axis)
        count = count * lax.axis_size(axis)
    return place, count - 1


def four_times(values):
    return jnp.concatenate([values] * 4, axis=1)


def weights_kernel(
    one_in, bias_in, two_in, bias_two_in, table_in, weights_one, weights_two, bias_rows, table, one, bias, two, bias_two, sems
):
    fetch = [
        pltpu.make_async_copy(one_in, one, sems.at[0]),
        pltpu.make_async_copy(bias_in, bias, sems.at[1]),
        pltpu.make_async_copy(two_in, two, sems.at[2]),
        pltpu.make_async_copy(bias_two_in, bias_two, sems.at[3]),
    ]
    get_table = pltpu.make_async_copy(table_in, table, sems.at[4])
    for copy in (*fetch, get_table):
        copy.start()
    for copy in fetch:
        copy.wait()
    channels = one.shape[2]
    rows = TILE + 2
    per_tile = LANES // channels
    lanes = -(-rows * channels // LANES) * LANES
    image_row = lax.broadcasted_iota(jnp.int32, (16, lanes), 0)
    hidden_row = lax.broadcasted_iota(jnp.int32, (16, lanes), 1) // channels
    place, last = own_place()
    held = (hidden_row >= jnp.where(place == 0, 1, 0)) & (hidden_row < jnp.where(place == last, rows - 1, rows))
    high, low = [], []
    for tap in range(3):
        band = jnp.zeros((16, lanes), jnp.float32)
        for shift in range(3):
            line = jnp.concatenate([four_times(one[shift, tap : tap + 1])] * (lanes // LANES), axis=1)
            band = jnp.where(held & (image_row - hidden_row == shift), line, band)
        high.append(band.astype(jnp.bfloat16).astype(jnp.float32))
        low.append(band - high[-1])
    line = jnp.concatenate([four_times(bias[...])] * (lanes // LANES), axis=1)
    with_bias = high[0]
    for piece in range(3):
        rounded = line.astype(jnp.bfloat16).astype(jnp.float32)
        with_bias = jnp.where(held & (image_row == 12 + piece), rounded, with_bias)
        line = line - rounded
    stacked = jnp.concatenate([with_bias, *high[1:], *high, *low], axis=0)
    weights_one[...] = stacked.T[: weights_one.shape[0]].astype(jnp.bfloat16)
    row = lax.broadcasted_iota(jnp.int32, bias_rows.shape, 0) // TILE
    lane = lax.broadcasted_iota(jnp.int32, bias_rows.shape, 1)
    line = jnp.where(row == lane, four_times(bias_two[...]), 0.0)
    bias_rows[...] = jnp.broadcast_to(jnp.sum(line, axis=1, keepdims=True), bias_rows.shape)
    lines = [[four_times(two[shift, tap].astype(jnp.float32)) for shift in range(3)] for tap in range(3)]
    row = lax.broadcasted_iota(jnp.int32, (TILE, LANES), 0)
    lane = lax.broadcasted_iota(jnp.int32, (TILE, LANES), 1) // channels
    zero = jnp.zeros((TILE, LANES), jnp.float32)
    for tile in range(-(-3 * rows // per_tile)):
        taps = sorted({(tile * per_tile + g) // rows for g in range(per_tile)} & {0, 1, 2})
        masks = []
        for tap in taps:
            hidden_row = tile * per_tile + lane - tap * rows
            inside = (hidden_row >= 0) & (hidden_row < rows)
            masks += [(tap, shift, inside & (hidden_row - row == shift)) for shift in range(3)]
        width = min(LANES, weights_two.shape[1] - tile * LANES)
        for channel in range(0, channels, 2):
            pair = []
            for k in (channel, channel + 1):
                values = zero
                for tap, shift, mask in masks:
                    values = jnp.where(mask, lines[tap][shift][k : k + 1], values)
                pair.append(values)
            block = jnp.concatenate(pair, axis=0).astype(jnp.bfloat16)
            weights_two[TILE * channel : TILE * (channel + 2), tile * LANES : tile * LANES + width] = block[:, :width]
    get_table.wait()


def shifted(values, width):
    lane = lax.broadcasted_iota(jnp.int32, values.shape, 1)
    zero = jnp.zeros_like(values)
    before = jnp.where(lane == 0, zero, pltpu.roll(values, 1, 1))
    after = jnp.where(lane == width - 1, zero, pltpu.roll(values, width - 1, 1))
    return before, values, after


def layers_kernel(shares, weights_one, weights_two, bias_rows, table, out, staged, sems):
    width = out.shape[2]
    row, col = lax.axis_size("row"), lax.axis_size("col")
    upper = lax.broadcasted_iota(jnp.int32, (TILE, 2 * LANES), 0) < TILE // 2
    depth = 2 * LANES
    image = jnp.zeros((4 * TILE, width), jnp.float32)
    for r in range(row):
        senders = [slot for slot, place in enumerate(send_order()) if place // col % row == r]
        total = shares[senders[0]].astype(jnp.float32)
        for sender in senders[1:]:
            total = total + shares[sender].astype(jnp.float32)
        middle = total[TILE : 2 * TILE]
        above = jnp.concatenate([total[:TILE], total[2 * TILE :]], axis=1)
        below = jnp.concatenate([middle, pltpu.roll(middle, TILE // 2, 0)], axis=1)
        turned = jnp.concatenate([above, jnp.where(upper, below, 0.0)], axis=0)
        high = turned.astype(jnp.bfloat16)
        low = (turned - high.astype(jnp.float32)).astype(jnp.bfloat16)
        block = table[r * depth : (r + 1) * depth]
        image = image + jnp.dot(jnp.concatenate([high, low], axis=0), block, preferred_element_type=jnp.float32)
    image = image[: 2 * TILE] + image[2 * TILE :]
    columns = jnp.concatenate(shifted(image, width), axis=0)
    high = columns.astype(jnp.bfloat16).astype(jnp.float32)
    low = columns - high
    row = lax.broadcasted_iota(jnp.int32, (48, width), 0)
    with_ones = jnp.where((row >= 12) & (row < 15), 1.0, high)
    stacked = jnp.concatenate([with_ones, low, high], axis=0).astype(jnp.bfloat16)
    hidden = jnp.dot(weights_one[...], stacked, preferred_element_type=jnp.float32)
    hidden = jnp.maximum(hidden, 0.0).astype(jnp.bfloat16)
    stacked = jnp.concatenate(shifted(hidden, width), axis=0)
    half = out.shape[0] // 2
    copies = []
    for part in range(2):
        rows = pl.ds(part * half * TILE, half * TILE)
        features = jnp.dot(weights_two[rows], stacked, preferred_element_type=jnp.float32)
        features = features + jnp.concatenate([bias_rows[rows]] * (width // LANES), axis=1)
        channels_of = pl.ds(part * half, half)
        staged[channels_of] = features.reshape(half, TILE, width).astype(out.dtype)
        copies.append(pltpu.make_async_copy(staged.at[channels_of], out.at[channels_of], sems.at[part]))
        copies[-1].start()
    for copy in copies:
        copy.wait()


def in_hbm(*arrays):
    return [pltpu.with_memory_space_constraint(array, pltpu.HBM) for array in arrays]


def direct(partials, coverage, conv_one, bias_one, conv_two, bias_two):
    count_row, count_col = lax.axis_size("row"), lax.axis_size("col")
    devices = lax.axis_size("vis") * count_row * count_col
    length = partials.shape[3] * count_col
    image_len = length // 2
    channels = conv_two.shape[2]
    first, second = grid_tables(length, count_row, count_col)
    vmem, hbm = pl.BlockSpec(memory_space=pltpu.VMEM), pl.BlockSpec(memory_space=pltpu.HBM)
    limit = pltpu.CompilerParams(vmem_limit_bytes=16 * 2**20)
    share = (devices, 2 * (TILE + 2 * HALO), LANES)
    shares = pl.pallas_call(
        share_kernel,
        out_shape=jax.ShapeDtypeStruct(share, jnp.bfloat16),
        in_specs=[hbm] * 3,
        out_specs=vmem,
        scratch_shapes=[
            pltpu.SMEM(coverage.shape, jnp.int32),
            pltpu.VMEM(partials.shape, jnp.bfloat16),
            pltpu.VMEM(first.shape[1:], jnp.bfloat16),
            pltpu.SemaphoreType.DMA((3,)),
        ],
        compiler_params=limit,
        name="shares",
    )(*in_hbm(coverage, partials, jnp.asarray(first)))
    arrived = lax.all_to_all(
        shares, ALL, split_axis=0, concat_axis=0, tiled=True, axis_index_groups=[send_order()]
    )
    rows = TILE + 2
    weights = pl.pallas_call(
        weights_kernel,
        out_shape=[
            jax.ShapeDtypeStruct((rows * channels, 3 * 48), jnp.bfloat16),
            jax.ShapeDtypeStruct((TILE * channels, 3 * rows * channels), jnp.bfloat16),
            jax.ShapeDtypeStruct((TILE * channels, LANES), jnp.float32),
            jax.ShapeDtypeStruct(second.shape, jnp.bfloat16),
        ],
        in_specs=[hbm] * 5,
        out_specs=[vmem] * 4,
        scratch_shapes=[
            pltpu.VMEM((3, 3, channels), jnp.float32),
            pltpu.VMEM((1, channels), jnp.float32),
            pltpu.VMEM(conv_two.shape, jnp.bfloat16),
            pltpu.VMEM((1, channels), jnp.float32),
            pltpu.SemaphoreType.DMA((5,)),
        ],
        compiler_params=limit,
        name="weights",
    )(*in_hbm(conv_one.transpose(1, 2, 0), bias_one[None], conv_two, bias_two[None], jnp.asarray(second)))
    return pl.pallas_call(
        layers_kernel,
        out_shape=jax.ShapeDtypeStruct((channels, TILE, image_len), jnp.bfloat16),
        in_specs=[vmem] * 5,
        out_specs=hbm,
        scratch_shapes=[
            pltpu.VMEM((channels, TILE, image_len), jnp.bfloat16),
            pltpu.SemaphoreType.DMA((2,)),
        ],
        compiler_params=limit,
        name="layers",
    )(arrived, *weights)


def local(partials, coverage, conv_one, bias_one, conv_two, bias_two):
    count_col = lax.axis_size("col")
    devices = lax.axis_size("vis") * lax.axis_size("row") * count_col
    image_len = partials.shape[3] * count_col // 2
    sent = devices * (TILE + 2 * HALO) * image_len * 2
    fits = partials.shape[2] == LANES and image_len == devices * TILE and conv_two.shape[2] * 4 == LANES and image_len == 2 * LANES and sent <= DIRECT_BYTES
    plan = direct if fits else staged
    return plan(partials, coverage, conv_one, bias_one, conv_two, bias_two)


def solution(mesh):
    placed = (P("vis", None, "row", "col"), P("vis", "row", "col"), P(), P(), P(), P())
    return jax.shard_map(
        local,
        mesh=mesh,
        in_specs=placed,
        out_specs=P(None, ALL, None),
        check_vma=False,
    )
```

```python
import math

import jax
import jax.numpy as jnp
import numpy as np
from jax import lax
from jax.experimental import pallas as pl
from jax.experimental.pallas import tpu as pltpu
from jax.sharding import PartitionSpec as P

BLK = 128
ALL = ("vis", "row", "col")
DIRECT_BYTES = 4 * 2**20
HALO = 2
TILE = 8
LANES = 128


def with_halo(cells, sides, width):
    for axis, dim in sides:
        count = lax.axis_size(axis)
        ends = count - 1
        head = lax.slice_in_dim(cells, 0, width, axis=dim)
        tail = lax.slice_in_dim(cells, cells.shape[dim] - width, cells.shape[dim], axis=dim)
        cells = jnp.concatenate(
            [
                lax.ppermute(tail, axis, [(i, (i + 1) % count) for i in range(ends)]),
                cells,
                lax.ppermute(head, axis, [((i + 1) % count, i) for i in range(ends)]),
            ],
            axis=dim,
        )
    return cells


def phase_table(numer, denom):
    angle = numer.astype(jnp.float32) * (2.0 * math.pi / denom)
    return (jnp.cos(angle), jnp.sin(angle))


def partial_transform(real_part, imag_part, block_of, keep_imag):
    batch = real_part.shape[0]
    count_blocks = real_part.shape[1]
    block_len = real_part.shape[2]
    length = count_blocks * block_len
    highest = lax.Precision.HIGHEST
    outer = jnp.arange(count_blocks, dtype=jnp.int32)
    inner = jnp.arange(block_len, dtype=jnp.int32)
    cos_one, sin_one = phase_table(block_of[:, None] * outer[None, :] % count_blocks, count_blocks)
    mid_re = jnp.einsum("lpt,px->lxt", real_part, cos_one, precision=highest) - jnp.einsum(
        "lpt,px->lxt", imag_part, sin_one, precision=highest
    )
    mid_im = jnp.einsum("lpt,px->lxt", real_part, sin_one, precision=highest) + jnp.einsum(
        "lpt,px->lxt", imag_part, cos_one, precision=highest
    )
    cos_two, sin_two = phase_table(outer[:, None] * inner[None, :] % length, length)
    parity = (1 - 2 * (outer % 2)).astype(jnp.float32)[:, None]
    cos_two = cos_two * parity
    sin_two = sin_two * parity
    turn_re = mid_re * cos_two - mid_im * sin_two
    turn_im = mid_re * sin_two + mid_im * cos_two
    kept = jnp.arange(block_len // 2, dtype=jnp.int32)
    picked = (kept + 3 * block_len // 4) % block_len
    cos_three, sin_three = phase_table(inner[:, None] * picked[None, :] % block_len, block_len)
    out_re = jnp.einsum("lxt,tj->ljx", turn_re, cos_three, precision=highest) - jnp.einsum(
        "lxt,tj->ljx", turn_im, sin_three, precision=highest
    )
    out_re = out_re.reshape(batch, length // 2)
    if keep_imag:
        out_im = jnp.einsum("lxt,tj->ljx", turn_re, sin_three, precision=highest) + jnp.einsum(
            "lxt,tj->ljx", turn_im, cos_three, precision=highest
        )
        return (out_re, out_im.reshape(batch, length // 2))
    return (out_re, out_re)


def first_layer(extended, conv_one, bias_one, count_rows):
    width = extended.shape[1]
    padded = jnp.pad(extended, ((0, 0), (1, 1)))
    summed = (
        jnp.zeros((conv_one.shape[0], count_rows, width), jnp.float32) + bias_one[:, None, None]
    )
    for shift_b in range(3):
        for shift_a in range(3):
            summed = (
                summed
                + conv_one[:, shift_b, shift_a][:, None, None]
                * padded[None, shift_b : shift_b + count_rows, shift_a : shift_a + width]
            )
    return jnp.maximum(summed, 0.0)


def second_layer(hidden_ext, conv_two, bias_two, count_rows):
    width = hidden_ext.shape[2]
    padded = jnp.pad(hidden_ext, ((0, 0), (0, 0), (1, 1)))
    summed = jnp.zeros((conv_two.shape[2], count_rows, width), jnp.float32)
    for shift_b in range(3):
        for shift_a in range(3):
            summed = summed + jnp.einsum(
                "kj,jba->kba",
                conv_two[shift_b, shift_a],
                padded[:, shift_b : shift_b + count_rows, shift_a : shift_a + width],
                preferred_element_type=jnp.float32,
            )
    return (summed + bias_two[:, None, None]).astype(jnp.bfloat16)


def staged(partials, coverage, conv_one, bias_one, conv_two, bias_two):
    count_vis = lax.axis_size("vis")
    count_row = lax.axis_size("row")
    count_col = lax.axis_size("col")
    grid_len = partials.shape[3] * count_col
    cover = coverage[0]
    block_rows = cover.shape[0]
    block_cols = cover.shape[1]
    spread = jnp.broadcast_to(cover[:, None, :, None], (block_rows, BLK, block_cols, BLK))
    spread = spread.reshape(block_rows * BLK, block_cols * BLK)
    count_blocks = count_vis * count_row
    row_block = grid_len // count_blocks
    row_share = row_block // count_col
    masked = partials[0] * spread.astype(jnp.bfloat16)[None]
    reduced = lax.psum_scatter(
        masked.astype(jnp.float32).astype(jnp.bfloat16), "vis", scatter_dimension=1, tiled=True
    ).astype(jnp.float32)
    grid_rows = lax.all_to_all(
        reduced.astype(jnp.bfloat16), "col", split_axis=1, concat_axis=2, tiled=True
    ).astype(reduced.dtype)
    natural = jnp.arange(count_blocks, dtype=jnp.int32)
    shaped = grid_rows.reshape(2, row_share, count_blocks, row_block)
    first_re, first_im = partial_transform(shaped[0], shaped[1], natural, True)
    stacked = jnp.stack([first_re, first_im])
    moved = lax.all_to_all(
        lax.all_to_all(
            stacked.astype(jnp.bfloat16), ("vis", "row"), split_axis=2, concat_axis=1, tiled=True
        ),
        "col",
        split_axis=2,
        concat_axis=1,
        tiled=True,
    ).astype(stacked.dtype)
    img_rows = moved.shape[2]
    arranged = moved.reshape(2, count_col, count_blocks, row_share, img_rows)
    arranged = arranged.transpose(0, 4, 2, 1, 3).reshape(2, img_rows, count_blocks, row_block)
    owners = natural % count_row * count_vis + natural // count_row
    image, unused = partial_transform(arranged[0], arranged[1], owners, False)
    image = image * (1.0 / grid_len)
    extended = with_halo(image.astype(jnp.bfloat16), ((("vis", "row", "col"), 0),), 1).astype(
        image.dtype
    )
    hidden = first_layer(extended, conv_one, bias_one, img_rows).astype(jnp.bfloat16)
    hidden_ext = with_halo(hidden, ((("vis", "row", "col"), 1),), 1)
    return second_layer(hidden_ext, conv_two, bias_two, img_rows)


def grid_tables(length, count_row, count_col):
    image_len = length // 2
    place = np.arange(length)[:, None] - length // 2
    pixel = np.arange(image_len)[None, :] - image_len // 2
    angle = (place * pixel % length) * (2.0 * math.pi / length)
    cos, sin = np.cos(angle), np.sin(angle)
    padded = np.pad(np.stack([cos.T, sin.T]), ((0, 0), (HALO, TILE - HALO), (0, 0)))
    first = padded.reshape(2 * (image_len + TILE), count_col, length // count_col).transpose(1, 0, 2)
    rows = length // count_row
    second = np.stack([cos.reshape(count_row, rows, image_len), -sin.reshape(count_row, rows, image_len)], axis=1)
    second = second.reshape(2 * length, image_len) / length
    return first.astype(jnp.bfloat16), second.astype(jnp.bfloat16)


def send_order():
    vis, row, col = (lax.axis_size(axis) for axis in ALL)
    pairs = 2 if vis % 2 == 0 else 1
    places = np.arange(vis * row * col).reshape(vis // pairs, pairs, row, col)
    return places[::-1].reshape(-1).tolist()


def share_kernel(cover_in, parts_in, first_all, out, cover, parts, first, sems):
    get_cover = pltpu.make_async_copy(cover_in, cover, sems.at[0])
    get_parts = pltpu.make_async_copy(parts_in, parts, sems.at[1])
    get_first = pltpu.make_async_copy(first_all.at[lax.axis_index("col")], first, sems.at[2])
    for copy in (get_cover, get_parts, get_first):
        copy.start()
    count_rows = parts.shape[2]
    get_cover.wait()
    get_parts.wait()
    components = []
    for component in range(2):
        strips = []
        for i in range(cover.shape[1]):
            cells = []
            for j in range(cover.shape[2]):
                block = parts[0, component, i * BLK : (i + 1) * BLK, j * BLK : (j + 1) * BLK]
                level = jnp.full(block.shape, cover[0, i, j].astype(jnp.float32)).astype(jnp.bfloat16)
                cells.append(block * level)
            strips.append(jnp.concatenate(cells, axis=1))
        components.append(jnp.concatenate(strips, axis=0))
    grid = jnp.concatenate(components, axis=0)
    upper = lax.broadcasted_iota(jnp.int32, (TILE, LANES), 0) < TILE // 2
    tall = first.shape[0] // 2
    get_first.wait()
    turned = lax.dot_general(first[...], grid, (((1,), (1,)), ((), ())), preferred_element_type=jnp.float32)
    mid_re = turned[:tall, :count_rows] - turned[tall:, count_rows:]
    mid_im = turned[tall:, :count_rows] + turned[:tall, count_rows:]
    for slot, device in enumerate(send_order()):
        here = slice(TILE * device, TILE * (device + 1))
        below = slice(TILE * (device + 1), TILE * (device + 2))
        middle = jnp.where(upper, mid_re[below], pltpu.roll(mid_im[below], TILE // 2, 0))
        out[slot] = jnp.concatenate([mid_re[here], middle, mid_im[here]], axis=0).astype(out.dtype)


def own_place():
    place, count = 0, 1
    for axis in ALL:
        place = place * lax.axis_size(axis) + lax.axis_index(axis)
        count = count * lax.axis_size(axis)
    return place, count - 1


def four_times(values):
    return jnp.concatenate([values] * 4, axis=1)


def weights_kernel(
    one_in, bias_in, two_in, bias_two_in, table_in, weights_one, weights_two, bias_rows, table, one, bias, two, bias_two, sems
):
    fetch = [
        pltpu.make_async_copy(one_in, one, sems.at[0]),
        pltpu.make_async_copy(bias_in, bias, sems.at[1]),
        pltpu.make_async_copy(two_in, two, sems.at[2]),
        pltpu.make_async_copy(bias_two_in, bias_two, sems.at[3]),
    ]
    get_table = pltpu.make_async_copy(table_in, table, sems.at[4])
    for copy in (*fetch, get_table):
        copy.start()
    for copy in fetch:
        copy.wait()
    channels = one.shape[2]
    rows = TILE + 2
    per_tile = LANES // channels
    lanes = -(-rows * channels // LANES) * LANES
    image_row = lax.broadcasted_iota(jnp.int32, (16, lanes), 0)
    hidden_row = lax.broadcasted_iota(jnp.int32, (16, lanes), 1) // channels
    place, last = own_place()
    held = (hidden_row >= jnp.where(place == 0, 1, 0)) & (hidden_row < jnp.where(place == last, rows - 1, rows))
    high, low = [], []
    for tap in range(3):
        band = jnp.zeros((16, lanes), jnp.float32)
        for shift in range(3):
            line = jnp.concatenate([four_times(one[shift, tap : tap + 1])] * (lanes // LANES), axis=1)
            band = jnp.where(held & (image_row - hidden_row == shift), line, band)
        high.append(band.astype(jnp.bfloat16).astype(jnp.float32))
        low.append(band - high[-1])
    line = jnp.concatenate([four_times(bias[...])] * (lanes // LANES), axis=1)
    with_bias = high[0]
    for piece in range(3):
        rounded = line.astype(jnp.bfloat16).astype(jnp.float32)
        with_bias = jnp.where(held & (image_row == 12 + piece), rounded, with_bias)
        line = line - rounded
    stacked = jnp.concatenate([with_bias, *high[1:], *high, *low], axis=0)
    weights_one[...] = stacked.T[: weights_one.shape[0]].astype(jnp.bfloat16)
    row = lax.broadcasted_iota(jnp.int32, bias_rows.shape, 0) // TILE
    lane = lax.broadcasted_iota(jnp.int32, bias_rows.shape, 1)
    line = jnp.where(row == lane, four_times(bias_two[...]), 0.0)
    bias_rows[...] = jnp.broadcast_to(jnp.sum(line, axis=1, keepdims=True), bias_rows.shape)
    lines = [[four_times(two[shift, tap].astype(jnp.float32)) for shift in range(3)] for tap in range(3)]
    row = lax.broadcasted_iota(jnp.int32, (TILE, LANES), 0)
    lane = lax.broadcasted_iota(jnp.int32, (TILE, LANES), 1) // channels
    zero = jnp.zeros((TILE, LANES), jnp.float32)
    for tile in range(-(-3 * rows // per_tile)):
        taps = sorted({(tile * per_tile + g) // rows for g in range(per_tile)} & {0, 1, 2})
        masks = []
        for tap in taps:
            hidden_row = tile * per_tile + lane - tap * rows
            inside = (hidden_row >= 0) & (hidden_row < rows)
            masks += [(tap, shift, inside & (hidden_row - row == shift)) for shift in range(3)]
        width = min(LANES, weights_two.shape[1] - tile * LANES)
        for channel in range(0, channels, 2):
            pair = []
            for k in (channel, channel + 1):
                values = zero
                for tap, shift, mask in masks:
                    values = jnp.where(mask, lines[tap][shift][k : k + 1], values)
                pair.append(values)
            block = jnp.concatenate(pair, axis=0).astype(jnp.bfloat16)
            weights_two[TILE * channel : TILE * (channel + 2), tile * LANES : tile * LANES + width] = block[:, :width]
    get_table.wait()


def shifted(values, width):
    lane = lax.broadcasted_iota(jnp.int32, values.shape, 1)
    zero = jnp.zeros_like(values)
    before = jnp.where(lane == 0, zero, pltpu.roll(values, 1, 1))
    after = jnp.where(lane == width - 1, zero, pltpu.roll(values, width - 1, 1))
    return before, values, after


def layers_kernel(shares, weights_one, weights_two, bias_rows, table, out, staged, sems):
    width = out.shape[2]
    row, col = lax.axis_size("row"), lax.axis_size("col")
    upper = lax.broadcasted_iota(jnp.int32, (TILE, 2 * LANES), 0) < TILE // 2
    depth = 2 * LANES
    image = jnp.zeros((4 * TILE, width), jnp.float32)
    for r in range(row):
        senders = [slot for slot, place in enumerate(send_order()) if place // col % row == r]
        total = shares[senders[0]].astype(jnp.float32)
        for sender in senders[1:]:
            total = total + shares[sender].astype(jnp.float32)
        middle = total[TILE : 2 * TILE]
        above = jnp.concatenate([total[:TILE], total[2 * TILE :]], axis=1)
        below = jnp.concatenate([middle, pltpu.roll(middle, TILE // 2, 0)], axis=1)
        turned = jnp.concatenate([above, jnp.where(upper, below, 0.0)], axis=0)
        high = turned.astype(jnp.bfloat16)
        low = (turned - high.astype(jnp.float32)).astype(jnp.bfloat16)
        block = table[r * depth : (r + 1) * depth]
        image = image + jnp.dot(jnp.concatenate([high, low], axis=0), block, preferred_element_type=jnp.float32)
    image = image[: 2 * TILE] + image[2 * TILE :]
    columns = jnp.concatenate(shifted(image, width), axis=0)
    high = columns.astype(jnp.bfloat16).astype(jnp.float32)
    low = columns - high
    row = lax.broadcasted_iota(jnp.int32, (48, width), 0)
    with_ones = jnp.where((row >= 12) & (row < 15), 1.0, high)
    stacked = jnp.concatenate([with_ones, low, high], axis=0).astype(jnp.bfloat16)
    hidden = jnp.dot(weights_one[...], stacked, preferred_element_type=jnp.float32)
    hidden = jnp.maximum(hidden, 0.0).astype(jnp.bfloat16)
    stacked = jnp.concatenate(shifted(hidden, width), axis=0)
    half = out.shape[0] // 2
    copies = []
    for part in range(2):
        rows = pl.ds(part * half * TILE, half * TILE)
        features = jnp.dot(weights_two[rows], stacked, preferred_element_type=jnp.float32)
        features = features + jnp.concatenate([bias_rows[rows]] * (width // LANES), axis=1)
        channels_of = pl.ds(part * half, half)
        staged[channels_of] = features.reshape(half, TILE, width).astype(out.dtype)
        copies.append(pltpu.make_async_copy(staged.at[channels_of], out.at[channels_of], sems.at[part]))
        copies[-1].start()
    for copy in copies:
        copy.wait()


def in_hbm(*arrays):
    return [pltpu.with_memory_space_constraint(array, pltpu.HBM) for array in arrays]


def direct(partials, coverage, conv_one, bias_one, conv_two, bias_two):
    count_row, count_col = lax.axis_size("row"), lax.axis_size("col")
    devices = lax.axis_size("vis") * count_row * count_col
    length = partials.shape[3] * count_col
    image_len = length // 2
    channels = conv_two.shape[2]
    first, second = grid_tables(length, count_row, count_col)
    vmem, hbm = pl.BlockSpec(memory_space=pltpu.VMEM), pl.BlockSpec(memory_space=pltpu.HBM)
    limit = pltpu.CompilerParams(vmem_limit_bytes=16 * 2**20)
    share = (devices, 2 * (TILE + 2 * HALO), LANES)
    shares = pl.pallas_call(
        share_kernel,
        out_shape=jax.ShapeDtypeStruct(share, jnp.bfloat16),
        in_specs=[hbm] * 3,
        out_specs=vmem,
        scratch_shapes=[
            pltpu.SMEM(coverage.shape, jnp.int32),
            pltpu.VMEM(partials.shape, jnp.bfloat16),
            pltpu.VMEM(first.shape[1:], jnp.bfloat16),
            pltpu.SemaphoreType.DMA((3,)),
        ],
        compiler_params=limit,
        name="shares",
    )(*in_hbm(coverage, partials, jnp.asarray(first)))
    arrived = lax.all_to_all(
        shares, ALL, split_axis=0, concat_axis=0, tiled=True, axis_index_groups=[send_order()]
    )
    rows = TILE + 2
    weights = pl.pallas_call(
        weights_kernel,
        out_shape=[
            jax.ShapeDtypeStruct((rows * channels, 3 * 48), jnp.bfloat16),
            jax.ShapeDtypeStruct((TILE * channels, 3 * rows * channels), jnp.bfloat16),
            jax.ShapeDtypeStruct((TILE * channels, LANES), jnp.float32),
            jax.ShapeDtypeStruct(second.shape, jnp.bfloat16),
        ],
        in_specs=[hbm] * 5,
        out_specs=[vmem] * 4,
        scratch_shapes=[
            pltpu.VMEM((3, 3, channels), jnp.float32),
            pltpu.VMEM((1, channels), jnp.float32),
            pltpu.VMEM(conv_two.shape, jnp.bfloat16),
            pltpu.VMEM((1, channels), jnp.float32),
            pltpu.SemaphoreType.DMA((5,)),
        ],
        compiler_params=limit,
        name="weights",
    )(*in_hbm(conv_one.transpose(1, 2, 0), bias_one[None], conv_two, bias_two[None], jnp.asarray(second)))
    return pl.pallas_call(
        layers_kernel,
        out_shape=jax.ShapeDtypeStruct((channels, TILE, image_len), jnp.bfloat16),
        in_specs=[vmem] * 5,
        out_specs=hbm,
        scratch_shapes=[
            pltpu.VMEM((channels, TILE, image_len), jnp.bfloat16),
            pltpu.SemaphoreType.DMA((2,)),
        ],
        compiler_params=limit,
        name="layers",
    )(arrived, *weights)


def local(partials, coverage, conv_one, bias_one, conv_two, bias_two):
    count_col = lax.axis_size("col")
    devices = lax.axis_size("vis") * lax.axis_size("row") * count_col
    image_len = partials.shape[3] * count_col // 2
    sent = devices * (TILE + 2 * HALO) * image_len * 2
    fits = partials.shape[2] == LANES and image_len == devices * TILE and conv_two.shape[2] * 4 == LANES and image_len == 2 * LANES and sent <= DIRECT_BYTES
    plan = direct if fits else staged
    return plan(partials, coverage, conv_one, bias_one, conv_two, bias_two)


def solution(mesh):
    placed = (P("vis", None, "row", "col"), P("vis", "row", "col"), P(), P(), P(), P())
    return jax.shard_map(
        local,
        mesh=mesh,
        in_specs=placed,
        out_specs=P(None, ALL, None),
        check_vma=False,
    )
```

```python
import math

import jax
import jax.numpy as jnp
import numpy as np
from jax import lax
from jax.experimental import pallas as pl
from jax.experimental.pallas import tpu as pltpu
from jax.sharding import PartitionSpec as P

BLK = 128
ALL = ("vis", "row", "col")
DIRECT_BYTES = 4 * 2**20
HALO = 2
TILE = 8
LANES = 128


def with_halo(cells, sides, width):
    for axis, dim in sides:
        count = lax.axis_size(axis)
        ends = count - 1
        head = lax.slice_in_dim(cells, 0, width, axis=dim)
        tail = lax.slice_in_dim(cells, cells.shape[dim] - width, cells.shape[dim], axis=dim)
        cells = jnp.concatenate(
            [
                lax.ppermute(tail, axis, [(i, (i + 1) % count) for i in range(ends)]),
                cells,
                lax.ppermute(head, axis, [((i + 1) % count, i) for i in range(ends)]),
            ],
            axis=dim,
        )
    return cells


def phase_table(numer, denom):
    angle = numer.astype(jnp.float32) * (2.0 * math.pi / denom)
    return (jnp.cos(angle), jnp.sin(angle))


def partial_transform(real_part, imag_part, block_of, keep_imag):
    batch = real_part.shape[0]
    count_blocks = real_part.shape[1]
    block_len = real_part.shape[2]
    length = count_blocks * block_len
    highest = lax.Precision.HIGHEST
    outer = jnp.arange(count_blocks, dtype=jnp.int32)
    inner = jnp.arange(block_len, dtype=jnp.int32)
    cos_one, sin_one = phase_table(block_of[:, None] * outer[None, :] % count_blocks, count_blocks)
    mid_re = jnp.einsum("lpt,px->lxt", real_part, cos_one, precision=highest) - jnp.einsum(
        "lpt,px->lxt", imag_part, sin_one, precision=highest
    )
    mid_im = jnp.einsum("lpt,px->lxt", real_part, sin_one, precision=highest) + jnp.einsum(
        "lpt,px->lxt", imag_part, cos_one, precision=highest
    )
    cos_two, sin_two = phase_table(outer[:, None] * inner[None, :] % length, length)
    parity = (1 - 2 * (outer % 2)).astype(jnp.float32)[:, None]
    cos_two = cos_two * parity
    sin_two = sin_two * parity
    turn_re = mid_re * cos_two - mid_im * sin_two
    turn_im = mid_re * sin_two + mid_im * cos_two
    kept = jnp.arange(block_len // 2, dtype=jnp.int32)
    picked = (kept + 3 * block_len // 4) % block_len
    cos_three, sin_three = phase_table(inner[:, None] * picked[None, :] % block_len, block_len)
    out_re = jnp.einsum("lxt,tj->ljx", turn_re, cos_three, precision=highest) - jnp.einsum(
        "lxt,tj->ljx", turn_im, sin_three, precision=highest
    )
    out_re = out_re.reshape(batch, length // 2)
    if keep_imag:
        out_im = jnp.einsum("lxt,tj->ljx", turn_re, sin_three, precision=highest) + jnp.einsum(
            "lxt,tj->ljx", turn_im, cos_three, precision=highest
        )
        return (out_re, out_im.reshape(batch, length // 2))
    return (out_re, out_re)


def first_layer(extended, conv_one, bias_one, count_rows):
    width = extended.shape[1]
    padded = jnp.pad(extended, ((0, 0), (1, 1)))
    summed = (
        jnp.zeros((conv_one.shape[0], count_rows, width), jnp.float32) + bias_one[:, None, None]
    )
    for shift_b in range(3):
        for shift_a in range(3):
            summed = (
                summed
                + conv_one[:, shift_b, shift_a][:, None, None]
                * padded[None, shift_b : shift_b + count_rows, shift_a : shift_a + width]
            )
    return jnp.maximum(summed, 0.0)


def second_layer(hidden_ext, conv_two, bias_two, count_rows):
    width = hidden_ext.shape[2]
    padded = jnp.pad(hidden_ext, ((0, 0), (0, 0), (1, 1)))
    summed = jnp.zeros((conv_two.shape[2], count_rows, width), jnp.float32)
    for shift_b in range(3):
        for shift_a in range(3):
            summed = summed + jnp.einsum(
                "kj,jba->kba",
                conv_two[shift_b, shift_a],
                padded[:, shift_b : shift_b + count_rows, shift_a : shift_a + width],
                preferred_element_type=jnp.float32,
            )
    return (summed + bias_two[:, None, None]).astype(jnp.bfloat16)


def staged(partials, coverage, conv_one, bias_one, conv_two, bias_two):
    count_vis = lax.axis_size("vis")
    count_row = lax.axis_size("row")
    count_col = lax.axis_size("col")
    grid_len = partials.shape[3] * count_col
    cover = coverage[0]
    block_rows = cover.shape[0]
    block_cols = cover.shape[1]
    spread = jnp.broadcast_to(cover[:, None, :, None], (block_rows, BLK, block_cols, BLK))
    spread = spread.reshape(block_rows * BLK, block_cols * BLK)
    count_blocks = count_vis * count_row
    row_block = grid_len // count_blocks
    row_share = row_block // count_col
    masked = partials[0] * spread.astype(jnp.bfloat16)[None]
    reduced = lax.psum_scatter(
        masked.astype(jnp.float32).astype(jnp.bfloat16), "vis", scatter_dimension=1, tiled=True
    ).astype(jnp.float32)
    grid_rows = lax.all_to_all(
        reduced.astype(jnp.bfloat16), "col", split_axis=1, concat_axis=2, tiled=True
    ).astype(reduced.dtype)
    natural = jnp.arange(count_blocks, dtype=jnp.int32)
    shaped = grid_rows.reshape(2, row_share, count_blocks, row_block)
    first_re, first_im = partial_transform(shaped[0], shaped[1], natural, True)
    stacked = jnp.stack([first_re, first_im])
    moved = lax.all_to_all(
        lax.all_to_all(
            stacked.astype(jnp.bfloat16), ("vis", "row"), split_axis=2, concat_axis=1, tiled=True
        ),
        "col",
        split_axis=2,
        concat_axis=1,
        tiled=True,
    ).astype(stacked.dtype)
    img_rows = moved.shape[2]
    arranged = moved.reshape(2, count_col, count_blocks, row_share, img_rows)
    arranged = arranged.transpose(0, 4, 2, 1, 3).reshape(2, img_rows, count_blocks, row_block)
    owners = natural % count_row * count_vis + natural // count_row
    image, unused = partial_transform(arranged[0], arranged[1], owners, False)
    image = image * (1.0 / grid_len)
    extended = with_halo(image.astype(jnp.bfloat16), ((("vis", "row", "col"), 0),), 1).astype(
        image.dtype
    )
    hidden = first_layer(extended, conv_one, bias_one, img_rows).astype(jnp.bfloat16)
    hidden_ext = with_halo(hidden, ((("vis", "row", "col"), 1),), 1)
    return second_layer(hidden_ext, conv_two, bias_two, img_rows)


def grid_tables(length, count_row, count_col):
    image_len = length // 2
    place = np.arange(length)[:, None] - length // 2
    pixel = np.arange(image_len)[None, :] - image_len // 2
    angle = (place * pixel % length) * (2.0 * math.pi / length)
    cos, sin = np.cos(angle), np.sin(angle)
    padded = np.pad(np.stack([cos.T, sin.T]), ((0, 0), (HALO, TILE - HALO), (0, 0)))
    first = padded.reshape(2 * (image_len + TILE), count_col, length // count_col).transpose(1, 0, 2)
    rows = length // count_row
    second = np.stack([cos.reshape(count_row, rows, image_len), -sin.reshape(count_row, rows, image_len)], axis=1)
    second = second.reshape(2 * length, image_len) / length
    return first.astype(jnp.bfloat16), second.astype(jnp.bfloat16)


def send_order():
    vis, row, col = (lax.axis_size(axis) for axis in ALL)
    pairs = 2 if vis % 2 == 0 else 1
    places = np.arange(vis * row * col).reshape(vis // pairs, pairs, row, col)
    return places.transpose(0, 2, 1, 3).reshape(-1).tolist()


def share_kernel(cover_in, parts_in, first_all, out, cover, parts, first, sems):
    get_cover = pltpu.make_async_copy(cover_in, cover, sems.at[0])
    get_parts = pltpu.make_async_copy(parts_in, parts, sems.at[1])
    get_first = pltpu.make_async_copy(first_all.at[lax.axis_index("col")], first, sems.at[2])
    for copy in (get_cover, get_parts, get_first):
        copy.start()
    count_rows = parts.shape[2]
    get_cover.wait()
    get_parts.wait()
    components = []
    for component in range(2):
        strips = []
        for i in range(cover.shape[1]):
            cells = []
            for j in range(cover.shape[2]):
                block = parts[0, component, i * BLK : (i + 1) * BLK, j * BLK : (j + 1) * BLK]
                level = jnp.full(block.shape, cover[0, i, j].astype(jnp.float32)).astype(jnp.bfloat16)
                cells.append(block * level)
            strips.append(jnp.concatenate(cells, axis=1))
        components.append(jnp.concatenate(strips, axis=0))
    grid = jnp.concatenate(components, axis=0)
    upper = lax.broadcasted_iota(jnp.int32, (TILE, LANES), 0) < TILE // 2
    tall = first.shape[0] // 2
    get_first.wait()
    turned = lax.dot_general(first[...], grid, (((1,), (1,)), ((), ())), preferred_element_type=jnp.float32)
    mid_re = turned[:tall, :count_rows] - turned[tall:, count_rows:]
    mid_im = turned[tall:, :count_rows] + turned[:tall, count_rows:]
    for slot, device in enumerate(send_order()):
        here = slice(TILE * device, TILE * (device + 1))
        below = slice(TILE * (device + 1), TILE * (device + 2))
        middle = jnp.where(upper, mid_re[below], pltpu.roll(mid_im[below], TILE // 2, 0))
        out[slot] = jnp.concatenate([mid_re[here], middle, mid_im[here]], axis=0).astype(out.dtype)


def own_place():
    place, count = 0, 1
    for axis in ALL:
        place = place * lax.axis_size(axis) + lax.axis_index(axis)
        count = count * lax.axis_size(axis)
    return place, count - 1


def four_times(values):
    return jnp.concatenate([values] * 4, axis=1)


def weights_kernel(
    one_in, bias_in, two_in, bias_two_in, table_in, weights_one, weights_two, bias_rows, table, one, bias, two, bias_two, sems
):
    fetch = [
        pltpu.make_async_copy(one_in, one, sems.at[0]),
        pltpu.make_async_copy(bias_in, bias, sems.at[1]),
        pltpu.make_async_copy(two_in, two, sems.at[2]),
        pltpu.make_async_copy(bias_two_in, bias_two, sems.at[3]),
    ]
    get_table = pltpu.make_async_copy(table_in, table, sems.at[4])
    for copy in (*fetch, get_table):
        copy.start()
    for copy in fetch:
        copy.wait()
    channels = one.shape[2]
    rows = TILE + 2
    per_tile = LANES // channels
    lanes = -(-rows * channels // LANES) * LANES
    image_row = lax.broadcasted_iota(jnp.int32, (16, lanes), 0)
    hidden_row = lax.broadcasted_iota(jnp.int32, (16, lanes), 1) // channels
    place, last = own_place()
    held = (hidden_row >= jnp.where(place == 0, 1, 0)) & (hidden_row < jnp.where(place == last, rows - 1, rows))
    high, low = [], []
    for tap in range(3):
        band = jnp.zeros((16, lanes), jnp.float32)
        for shift in range(3):
            line = jnp.concatenate([four_times(one[shift, tap : tap + 1])] * (lanes // LANES), axis=1)
            band = jnp.where(held & (image_row - hidden_row == shift), line, band)
        high.append(band.astype(jnp.bfloat16).astype(jnp.float32))
        low.append(band - high[-1])
    line = jnp.concatenate([four_times(bias[...])] * (lanes // LANES), axis=1)
    with_bias = high[0]
    for piece in range(3):
        rounded = line.astype(jnp.bfloat16).astype(jnp.float32)
        with_bias = jnp.where(held & (image_row == 12 + piece), rounded, with_bias)
        line = line - rounded
    stacked = jnp.concatenate([with_bias, *high[1:], *high, *low], axis=0)
    weights_one[...] = stacked.T[: weights_one.shape[0]].astype(jnp.bfloat16)
    row = lax.broadcasted_iota(jnp.int32, bias_rows.shape, 0) // TILE
    lane = lax.broadcasted_iota(jnp.int32, bias_rows.shape, 1)
    line = jnp.where(row == lane, four_times(bias_two[...]), 0.0)
    bias_rows[...] = jnp.broadcast_to(jnp.sum(line, axis=1, keepdims=True), bias_rows.shape)
    lines = [[four_times(two[shift, tap].astype(jnp.float32)) for shift in range(3)] for tap in range(3)]
    row = lax.broadcasted_iota(jnp.int32, (TILE, LANES), 0)
    lane = lax.broadcasted_iota(jnp.int32, (TILE, LANES), 1) // channels
    zero = jnp.zeros((TILE, LANES), jnp.float32)
    for tile in range(-(-3 * rows // per_tile)):
        taps = sorted({(tile * per_tile + g) // rows for g in range(per_tile)} & {0, 1, 2})
        masks = []
        for tap in taps:
            hidden_row = tile * per_tile + lane - tap * rows
            inside = (hidden_row >= 0) & (hidden_row < rows)
            masks += [(tap, shift, inside & (hidden_row - row == shift)) for shift in range(3)]
        width = min(LANES, weights_two.shape[1] - tile * LANES)
        for channel in range(0, channels, 2):
            pair = []
            for k in (channel, channel + 1):
                values = zero
                for tap, shift, mask in masks:
                    values = jnp.where(mask, lines[tap][shift][k : k + 1], values)
                pair.append(values)
            block = jnp.concatenate(pair, axis=0).astype(jnp.bfloat16)
            weights_two[TILE * channel : TILE * (channel + 2), tile * LANES : tile * LANES + width] = block[:, :width]
    get_table.wait()


def shifted(values, width):
    lane = lax.broadcasted_iota(jnp.int32, values.shape, 1)
    zero = jnp.zeros_like(values)
    before = jnp.where(lane == 0, zero, pltpu.roll(values, 1, 1))
    after = jnp.where(lane == width - 1, zero, pltpu.roll(values, width - 1, 1))
    return before, values, after


def layers_kernel(shares, weights_one, weights_two, bias_rows, table, out, staged, sems):
    width = out.shape[2]
    row, col = lax.axis_size("row"), lax.axis_size("col")
    upper = lax.broadcasted_iota(jnp.int32, (TILE, 2 * LANES), 0) < TILE // 2
    depth = 2 * LANES
    image = jnp.zeros((4 * TILE, width), jnp.float32)
    for r in range(row):
        senders = [slot for slot, place in enumerate(send_order()) if place // col % row == r]
        total = shares[senders[0]].astype(jnp.float32)
        for sender in senders[1:]:
            total = total + shares[sender].astype(jnp.float32)
        middle = total[TILE : 2 * TILE]
        above = jnp.concatenate([total[:TILE], total[2 * TILE :]], axis=1)
        below = jnp.concatenate([middle, pltpu.roll(middle, TILE // 2, 0)], axis=1)
        turned = jnp.concatenate([above, jnp.where(upper, below, 0.0)], axis=0)
        high = turned.astype(jnp.bfloat16)
        low = (turned - high.astype(jnp.float32)).astype(jnp.bfloat16)
        block = table[r * depth : (r + 1) * depth]
        image = image + jnp.dot(jnp.concatenate([high, low], axis=0), block, preferred_element_type=jnp.float32)
    image = image[: 2 * TILE] + image[2 * TILE :]
    columns = jnp.concatenate(shifted(image, width), axis=0)
    high = columns.astype(jnp.bfloat16).astype(jnp.float32)
    low = columns - high
    row = lax.broadcasted_iota(jnp.int32, (48, width), 0)
    with_ones = jnp.where((row >= 12) & (row < 15), 1.0, high)
    stacked = jnp.concatenate([with_ones, low, high], axis=0).astype(jnp.bfloat16)
    hidden = jnp.dot(weights_one[...], stacked, preferred_element_type=jnp.float32)
    hidden = jnp.maximum(hidden, 0.0).astype(jnp.bfloat16)
    stacked = jnp.concatenate(shifted(hidden, width), axis=0)
    half = out.shape[0] // 2
    copies = []
    for part in range(2):
        rows = pl.ds(part * half * TILE, half * TILE)
        features = jnp.dot(weights_two[rows], stacked, preferred_element_type=jnp.float32)
        features = features + jnp.concatenate([bias_rows[rows]] * (width // LANES), axis=1)
        channels_of = pl.ds(part * half, half)
        staged[channels_of] = features.reshape(half, TILE, width).astype(out.dtype)
        copies.append(pltpu.make_async_copy(staged.at[channels_of], out.at[channels_of], sems.at[part]))
        copies[-1].start()
    for copy in copies:
        copy.wait()


def in_hbm(*arrays):
    return [pltpu.with_memory_space_constraint(array, pltpu.HBM) for array in arrays]


def direct(partials, coverage, conv_one, bias_one, conv_two, bias_two):
    count_row, count_col = lax.axis_size("row"), lax.axis_size("col")
    devices = lax.axis_size("vis") * count_row * count_col
    length = partials.shape[3] * count_col
    image_len = length // 2
    channels = conv_two.shape[2]
    first, second = grid_tables(length, count_row, count_col)
    vmem, hbm = pl.BlockSpec(memory_space=pltpu.VMEM), pl.BlockSpec(memory_space=pltpu.HBM)
    limit = pltpu.CompilerParams(vmem_limit_bytes=16 * 2**20)
    share = (devices, 2 * (TILE + 2 * HALO), LANES)
    shares = pl.pallas_call(
        share_kernel,
        out_shape=jax.ShapeDtypeStruct(share, jnp.bfloat16),
        in_specs=[hbm] * 3,
        out_specs=vmem,
        scratch_shapes=[
            pltpu.SMEM(coverage.shape, jnp.int32),
            pltpu.VMEM(partials.shape, jnp.bfloat16),
            pltpu.VMEM(first.shape[1:], jnp.bfloat16),
            pltpu.SemaphoreType.DMA((3,)),
        ],
        compiler_params=limit,
        name="shares",
    )(*in_hbm(coverage, partials, jnp.asarray(first)))
    arrived = lax.all_to_all(
        shares, ALL, split_axis=0, concat_axis=0, tiled=True, axis_index_groups=[send_order()]
    )
    rows = TILE + 2
    weights = pl.pallas_call(
        weights_kernel,
        out_shape=[
            jax.ShapeDtypeStruct((rows * channels, 3 * 48), jnp.bfloat16),
            jax.ShapeDtypeStruct((TILE * channels, 3 * rows * channels), jnp.bfloat16),
            jax.ShapeDtypeStruct((TILE * channels, LANES), jnp.float32),
            jax.ShapeDtypeStruct(second.shape, jnp.bfloat16),
        ],
        in_specs=[hbm] * 5,
        out_specs=[vmem] * 4,
        scratch_shapes=[
            pltpu.VMEM((3, 3, channels), jnp.float32),
            pltpu.VMEM((1, channels), jnp.float32),
            pltpu.VMEM(conv_two.shape, jnp.bfloat16),
            pltpu.VMEM((1, channels), jnp.float32),
            pltpu.SemaphoreType.DMA((5,)),
        ],
        compiler_params=limit,
        name="weights",
    )(*in_hbm(conv_one.transpose(1, 2, 0), bias_one[None], conv_two, bias_two[None], jnp.asarray(second)))
    return pl.pallas_call(
        layers_kernel,
        out_shape=jax.ShapeDtypeStruct((channels, TILE, image_len), jnp.bfloat16),
        in_specs=[vmem] * 5,
        out_specs=hbm,
        scratch_shapes=[
            pltpu.VMEM((channels, TILE, image_len), jnp.bfloat16),
            pltpu.SemaphoreType.DMA((2,)),
        ],
        compiler_params=limit,
        name="layers",
    )(arrived, *weights)


def local(partials, coverage, conv_one, bias_one, conv_two, bias_two):
    count_col = lax.axis_size("col")
    devices = lax.axis_size("vis") * lax.axis_size("row") * count_col
    image_len = partials.shape[3] * count_col // 2
    sent = devices * (TILE + 2 * HALO) * image_len * 2
    fits = partials.shape[2] == LANES and image_len == devices * TILE and conv_two.shape[2] * 4 == LANES and image_len == 2 * LANES and sent <= DIRECT_BYTES
    plan = direct if fits else staged
    return plan(partials, coverage, conv_one, bias_one, conv_two, bias_two)


def solution(mesh):
    placed = (P("vis", None, "row", "col"), P("vis", "row", "col"), P(), P(), P(), P())
    return jax.shard_map(
        local,
        mesh=mesh,
        in_specs=placed,
        out_specs=P(None, ALL, None),
        check_vma=False,
    )
```

```python
import math

import jax
import jax.numpy as jnp
import numpy as np
from jax import lax
from jax.experimental import pallas as pl
from jax.experimental.pallas import tpu as pltpu
from jax.sharding import PartitionSpec as P

BLK = 128
ALL = ("vis", "row", "col")
DIRECT_BYTES = 4 * 2**20
HALO = 2
TILE = 8
LANES = 128


def with_halo(cells, sides, width):
    for axis, dim in sides:
        count = lax.axis_size(axis)
        ends = count - 1
        head = lax.slice_in_dim(cells, 0, width, axis=dim)
        tail = lax.slice_in_dim(cells, cells.shape[dim] - width, cells.shape[dim], axis=dim)
        cells = jnp.concatenate(
            [
                lax.ppermute(tail, axis, [(i, (i + 1) % count) for i in range(ends)]),
                cells,
                lax.ppermute(head, axis, [((i + 1) % count, i) for i in range(ends)]),
            ],
            axis=dim,
        )
    return cells


def phase_table(numer, denom):
    angle = numer.astype(jnp.float32) * (2.0 * math.pi / denom)
    return (jnp.cos(angle), jnp.sin(angle))


def partial_transform(real_part, imag_part, block_of, keep_imag):
    batch = real_part.shape[0]
    count_blocks = real_part.shape[1]
    block_len = real_part.shape[2]
    length = count_blocks * block_len
    highest = lax.Precision.HIGHEST
    outer = jnp.arange(count_blocks, dtype=jnp.int32)
    inner = jnp.arange(block_len, dtype=jnp.int32)
    cos_one, sin_one = phase_table(block_of[:, None] * outer[None, :] % count_blocks, count_blocks)
    mid_re = jnp.einsum("lpt,px->lxt", real_part, cos_one, precision=highest) - jnp.einsum(
        "lpt,px->lxt", imag_part, sin_one, precision=highest
    )
    mid_im = jnp.einsum("lpt,px->lxt", real_part, sin_one, precision=highest) + jnp.einsum(
        "lpt,px->lxt", imag_part, cos_one, precision=highest
    )
    cos_two, sin_two = phase_table(outer[:, None] * inner[None, :] % length, length)
    parity = (1 - 2 * (outer % 2)).astype(jnp.float32)[:, None]
    cos_two = cos_two * parity
    sin_two = sin_two * parity
    turn_re = mid_re * cos_two - mid_im * sin_two
    turn_im = mid_re * sin_two + mid_im * cos_two
    kept = jnp.arange(block_len // 2, dtype=jnp.int32)
    picked = (kept + 3 * block_len // 4) % block_len
    cos_three, sin_three = phase_table(inner[:, None] * picked[None, :] % block_len, block_len)
    out_re = jnp.einsum("lxt,tj->ljx", turn_re, cos_three, precision=highest) - jnp.einsum(
        "lxt,tj->ljx", turn_im, sin_three, precision=highest
    )
    out_re = out_re.reshape(batch, length // 2)
    if keep_imag:
        out_im = jnp.einsum("lxt,tj->ljx", turn_re, sin_three, precision=highest) + jnp.einsum(
            "lxt,tj->ljx", turn_im, cos_three, precision=highest
        )
        return (out_re, out_im.reshape(batch, length // 2))
    return (out_re, out_re)


def first_layer(extended, conv_one, bias_one, count_rows):
    width = extended.shape[1]
    padded = jnp.pad(extended, ((0, 0), (1, 1)))
    summed = (
        jnp.zeros((conv_one.shape[0], count_rows, width), jnp.float32) + bias_one[:, None, None]
    )
    for shift_b in range(3):
        for shift_a in range(3):
            summed = (
                summed
                + conv_one[:, shift_b, shift_a][:, None, None]
                * padded[None, shift_b : shift_b + count_rows, shift_a : shift_a + width]
            )
    return jnp.maximum(summed, 0.0)


def second_layer(hidden_ext, conv_two, bias_two, count_rows):
    width = hidden_ext.shape[2]
    padded = jnp.pad(hidden_ext, ((0, 0), (0, 0), (1, 1)))
    summed = jnp.zeros((conv_two.shape[2], count_rows, width), jnp.float32)
    for shift_b in range(3):
        for shift_a in range(3):
            summed = summed + jnp.einsum(
                "kj,jba->kba",
                conv_two[shift_b, shift_a],
                padded[:, shift_b : shift_b + count_rows, shift_a : shift_a + width],
                preferred_element_type=jnp.float32,
            )
    return (summed + bias_two[:, None, None]).astype(jnp.bfloat16)


def staged(partials, coverage, conv_one, bias_one, conv_two, bias_two):
    count_vis = lax.axis_size("vis")
    count_row = lax.axis_size("row")
    count_col = lax.axis_size("col")
    grid_len = partials.shape[3] * count_col
    cover = coverage[0]
    block_rows = cover.shape[0]
    block_cols = cover.shape[1]
    spread = jnp.broadcast_to(cover[:, None, :, None], (block_rows, BLK, block_cols, BLK))
    spread = spread.reshape(block_rows * BLK, block_cols * BLK)
    count_blocks = count_vis * count_row
    row_block = grid_len // count_blocks
    row_share = row_block // count_col
    masked = partials[0] * spread.astype(jnp.bfloat16)[None]
    reduced = lax.psum_scatter(
        masked.astype(jnp.float32).astype(jnp.bfloat16), "vis", scatter_dimension=1, tiled=True
    ).astype(jnp.float32)
    grid_rows = lax.all_to_all(
        reduced.astype(jnp.bfloat16), "col", split_axis=1, concat_axis=2, tiled=True
    ).astype(reduced.dtype)
    natural = jnp.arange(count_blocks, dtype=jnp.int32)
    shaped = grid_rows.reshape(2, row_share, count_blocks, row_block)
    first_re, first_im = partial_transform(shaped[0], shaped[1], natural, True)
    stacked = jnp.stack([first_re, first_im])
    moved = lax.all_to_all(
        lax.all_to_all(
            stacked.astype(jnp.bfloat16), ("vis", "row"), split_axis=2, concat_axis=1, tiled=True
        ),
        "col",
        split_axis=2,
        concat_axis=1,
        tiled=True,
    ).astype(stacked.dtype)
    img_rows = moved.shape[2]
    arranged = moved.reshape(2, count_col, count_blocks, row_share, img_rows)
    arranged = arranged.transpose(0, 4, 2, 1, 3).reshape(2, img_rows, count_blocks, row_block)
    owners = natural % count_row * count_vis + natural // count_row
    image, unused = partial_transform(arranged[0], arranged[1], owners, False)
    image = image * (1.0 / grid_len)
    extended = with_halo(image.astype(jnp.bfloat16), ((("vis", "row", "col"), 0),), 1).astype(
        image.dtype
    )
    hidden = first_layer(extended, conv_one, bias_one, img_rows).astype(jnp.bfloat16)
    hidden_ext = with_halo(hidden, ((("vis", "row", "col"), 1),), 1)
    return second_layer(hidden_ext, conv_two, bias_two, img_rows)


def grid_tables(length, count_row, count_col):
    image_len = length // 2
    place = np.arange(length)[:, None] - length // 2
    pixel = np.arange(image_len)[None, :] - image_len // 2
    angle = (place * pixel % length) * (2.0 * math.pi / length)
    cos, sin = np.cos(angle), np.sin(angle)
    padded = np.pad(np.stack([cos.T, sin.T]), ((0, 0), (HALO, TILE - HALO), (0, 0)))
    first = padded.reshape(2 * (image_len + TILE), count_col, length // count_col).transpose(1, 0, 2)
    rows = length // count_row
    second = np.stack([cos.reshape(count_row, rows, image_len), -sin.reshape(count_row, rows, image_len)], axis=1)
    second = second.reshape(2 * length, image_len) / length
    return first.astype(jnp.bfloat16), second.astype(jnp.bfloat16)


def share_kernel(cover_in, parts_in, first_all, out, cover, parts, first, sems):
    get_cover = pltpu.make_async_copy(cover_in, cover, sems.at[0])
    get_parts = pltpu.make_async_copy(parts_in, parts, sems.at[1])
    get_first = pltpu.make_async_copy(first_all.at[lax.axis_index("col")], first, sems.at[2])
    for copy in (get_cover, get_parts, get_first):
        copy.start()
    count_rows = parts.shape[2]
    get_cover.wait()
    get_parts.wait()
    components = []
    for component in range(2):
        strips = []
        for i in range(cover.shape[1]):
            cells = []
            for j in range(cover.shape[2]):
                block = parts[0, component, i * BLK : (i + 1) * BLK, j * BLK : (j + 1) * BLK]
                level = jnp.full(block.shape, cover[0, i, j].astype(jnp.float32)).astype(jnp.bfloat16)
                cells.append(block * level)
            strips.append(jnp.concatenate(cells, axis=1))
        components.append(jnp.concatenate(strips, axis=0))
    grid = jnp.concatenate(components, axis=0)
    upper = lax.broadcasted_iota(jnp.int32, (TILE, LANES), 0) < TILE // 2
    devices = out.shape[0]
    tall = first.shape[0] // 2
    get_first.wait()
    turned = lax.dot_general(first[...], grid, (((1,), (1,)), ((), ())), preferred_element_type=jnp.float32)
    mid_re = turned[:tall, :count_rows] - turned[tall:, count_rows:]
    mid_im = turned[tall:, :count_rows] + turned[:tall, count_rows:]
    for device in range(devices):
        here = slice(TILE * device, TILE * (device + 1))
        below = slice(TILE * (device + 1), TILE * (device + 2))
        middle = jnp.where(upper, mid_re[below], pltpu.roll(mid_im[below], TILE // 2, 0))
        out[device] = jnp.concatenate([mid_re[here], middle, mid_im[here]], axis=0).astype(out.dtype)


def own_place():
    place, count = 0, 1
    for axis in ALL:
        place = place * lax.axis_size(axis) + lax.axis_index(axis)
        count = count * lax.axis_size(axis)
    return place, count - 1


def four_times(values):
    return jnp.concatenate([values] * 4, axis=1)


def weights_kernel(
    one_in, bias_in, two_in, bias_two_in, table_in, weights_one, weights_two, bias_rows, table, one, bias, two, bias_two, sems
):
    fetch = [
        pltpu.make_async_copy(one_in, one, sems.at[0]),
        pltpu.make_async_copy(bias_in, bias, sems.at[1]),
        pltpu.make_async_copy(two_in, two, sems.at[2]),
        pltpu.make_async_copy(bias_two_in, bias_two, sems.at[3]),
    ]
    get_table = pltpu.make_async_copy(table_in, table, sems.at[4])
    for copy in (*fetch, get_table):
        copy.start()
    for copy in fetch:
        copy.wait()
    channels = one.shape[2]
    rows = TILE + 2
    per_tile = LANES // channels
    lanes = -(-rows * channels // LANES) * LANES
    image_row = lax.broadcasted_iota(jnp.int32, (16, lanes), 0)
    hidden_row = lax.broadcasted_iota(jnp.int32, (16, lanes), 1) // channels
    place, last = own_place()
    held = (hidden_row >= jnp.where(place == 0, 1, 0)) & (hidden_row < jnp.where(place == last, rows - 1, rows))
    high, low = [], []
    for tap in range(3):
        band = jnp.zeros((16, lanes), jnp.float32)
        for shift in range(3):
            line = jnp.concatenate([four_times(one[shift, tap : tap + 1])] * (lanes // LANES), axis=1)
            band = jnp.where(held & (image_row - hidden_row == shift), line, band)
        high.append(band.astype(jnp.bfloat16).astype(jnp.float32))
        low.append(band - high[-1])
    line = jnp.concatenate([four_times(bias[...])] * (lanes // LANES), axis=1)
    with_bias = high[0]
    for piece in range(3):
        rounded = line.astype(jnp.bfloat16).astype(jnp.float32)
        with_bias = jnp.where(held & (image_row == 12 + piece), rounded, with_bias)
        line = line - rounded
    stacked = jnp.concatenate([with_bias, *high[1:], *high, *low], axis=0)
    weights_one[...] = stacked.T[: weights_one.shape[0]].astype(jnp.bfloat16)
    row = lax.broadcasted_iota(jnp.int32, bias_rows.shape, 0) // TILE
    lane = lax.broadcasted_iota(jnp.int32, bias_rows.shape, 1)
    line = jnp.where(row == lane, four_times(bias_two[...]), 0.0)
    bias_rows[...] = jnp.broadcast_to(jnp.sum(line, axis=1, keepdims=True), bias_rows.shape)
    lines = [[four_times(two[shift, tap].astype(jnp.float32)) for shift in range(3)] for tap in range(3)]
    row = lax.broadcasted_iota(jnp.int32, (TILE, LANES), 0)
    lane = lax.broadcasted_iota(jnp.int32, (TILE, LANES), 1) // channels
    zero = jnp.zeros((TILE, LANES), jnp.float32)
    for tile in range(-(-3 * rows // per_tile)):
        taps = sorted({(tile * per_tile + g) // rows for g in range(per_tile)} & {0, 1, 2})
        masks = []
        for tap in taps:
            hidden_row = tile * per_tile + lane - tap * rows
            inside = (hidden_row >= 0) & (hidden_row < rows)
            masks += [(tap, shift, inside & (hidden_row - row == shift)) for shift in range(3)]
        width = min(LANES, weights_two.shape[1] - tile * LANES)
        for channel in range(0, channels, 2):
            pair = []
            for k in (channel, channel + 1):
                values = zero
                for tap, shift, mask in masks:
                    values = jnp.where(mask, lines[tap][shift][k : k + 1], values)
                pair.append(values)
            block = jnp.concatenate(pair, axis=0).astype(jnp.bfloat16)
            weights_two[TILE * channel : TILE * (channel + 2), tile * LANES : tile * LANES + width] = block[:, :width]
    get_table.wait()


def shifted(values, width):
    lane = lax.broadcasted_iota(jnp.int32, values.shape, 1)
    zero = jnp.zeros_like(values)
    before = jnp.where(lane == 0, zero, pltpu.roll(values, 1, 1))
    after = jnp.where(lane == width - 1, zero, pltpu.roll(values, width - 1, 1))
    return before, values, after


def layers_kernel(shares, weights_one, weights_two, bias_rows, table, out, staged, sems):
    width = out.shape[2]
    vis, row, col = (lax.axis_size(axis) for axis in ALL)
    upper = lax.broadcasted_iota(jnp.int32, (TILE, 2 * LANES), 0) < TILE // 2
    depth = 2 * LANES
    image = jnp.zeros((4 * TILE, width), jnp.float32)
    for r in range(row):
        senders = [(v * row + r) * col + c for v in range(vis) for c in range(col)]
        total = shares[senders[0]].astype(jnp.float32)
        for sender in senders[1:]:
            total = total + shares[sender].astype(jnp.float32)
        middle = total[TILE : 2 * TILE]
        above = jnp.concatenate([total[:TILE], total[2 * TILE :]], axis=1)
        below = jnp.concatenate([middle, pltpu.roll(middle, TILE // 2, 0)], axis=1)
        turned = jnp.concatenate([above, jnp.where(upper, below, 0.0)], axis=0)
        high = turned.astype(jnp.bfloat16)
        low = (turned - high.astype(jnp.float32)).astype(jnp.bfloat16)
        block = table[r * depth : (r + 1) * depth]
        image = image + jnp.dot(jnp.concatenate([high, low], axis=0), block, preferred_element_type=jnp.float32)
    image = image[: 2 * TILE] + image[2 * TILE :]
    columns = jnp.concatenate(shifted(image, width), axis=0)
    high = columns.astype(jnp.bfloat16).astype(jnp.float32)
    low = columns - high
    row = lax.broadcasted_iota(jnp.int32, (48, width), 0)
    with_ones = jnp.where((row >= 12) & (row < 15), 1.0, high)
    stacked = jnp.concatenate([with_ones, low, high], axis=0).astype(jnp.bfloat16)
    hidden = jnp.dot(weights_one[...], stacked, preferred_element_type=jnp.float32)
    hidden = jnp.maximum(hidden, 0.0).astype(jnp.bfloat16)
    stacked = jnp.concatenate(shifted(hidden, width), axis=0)
    copies = []
    for part in range(staged.shape[0]):
        columns = slice(part * LANES, (part + 1) * LANES)
        features = jnp.dot(weights_two[...], stacked[:, columns], preferred_element_type=jnp.float32)
        staged[part] = (features + bias_rows[...]).reshape(staged.shape[1:]).astype(out.dtype)
        target = out.at[:, :, pl.ds(part * LANES, LANES)]
        copies.append(pltpu.make_async_copy(staged.at[part], target, sems.at[part]))
        copies[-1].start()
    for copy in copies:
        copy.wait()


def in_hbm(*arrays):
    return [pltpu.with_memory_space_constraint(array, pltpu.HBM) for array in arrays]


def direct(partials, coverage, conv_one, bias_one, conv_two, bias_two):
    count_row, count_col = lax.axis_size("row"), lax.axis_size("col")
    devices = lax.axis_size("vis") * count_row * count_col
    length = partials.shape[3] * count_col
    image_len = length // 2
    channels = conv_two.shape[2]
    first, second = grid_tables(length, count_row, count_col)
    vmem, hbm = pl.BlockSpec(memory_space=pltpu.VMEM), pl.BlockSpec(memory_space=pltpu.HBM)
    limit = pltpu.CompilerParams(vmem_limit_bytes=16 * 2**20)
    share = (devices, 2 * (TILE + 2 * HALO), LANES)
    shares = pl.pallas_call(
        share_kernel,
        out_shape=jax.ShapeDtypeStruct(share, jnp.bfloat16),
        in_specs=[hbm] * 3,
        out_specs=vmem,
        scratch_shapes=[
            pltpu.SMEM(coverage.shape, jnp.int32),
            pltpu.VMEM(partials.shape, jnp.bfloat16),
            pltpu.VMEM(first.shape[1:], jnp.bfloat16),
            pltpu.SemaphoreType.DMA((3,)),
        ],
        compiler_params=limit,
        name="shares",
    )(*in_hbm(coverage, partials, jnp.asarray(first)))
    arrived = lax.all_to_all(shares, ALL, split_axis=0, concat_axis=0, tiled=True)
    rows = TILE + 2
    weights = pl.pallas_call(
        weights_kernel,
        out_shape=[
            jax.ShapeDtypeStruct((rows * channels, 3 * 48), jnp.bfloat16),
            jax.ShapeDtypeStruct((TILE * channels, 3 * rows * channels), jnp.bfloat16),
            jax.ShapeDtypeStruct((TILE * channels, LANES), jnp.float32),
            jax.ShapeDtypeStruct(second.shape, jnp.bfloat16),
        ],
        in_specs=[hbm] * 5,
        out_specs=[vmem] * 4,
        scratch_shapes=[
            pltpu.VMEM((3, 3, channels), jnp.float32),
            pltpu.VMEM((1, channels), jnp.float32),
            pltpu.VMEM(conv_two.shape, jnp.bfloat16),
            pltpu.VMEM((1, channels), jnp.float32),
            pltpu.SemaphoreType.DMA((5,)),
        ],
        compiler_params=limit,
        name="weights",
    )(*in_hbm(conv_one.transpose(1, 2, 0), bias_one[None], conv_two, bias_two[None], jnp.asarray(second)))
    return pl.pallas_call(
        layers_kernel,
        out_shape=jax.ShapeDtypeStruct((channels, TILE, image_len), jnp.bfloat16),
        in_specs=[vmem] * 5,
        out_specs=hbm,
        scratch_shapes=[
            pltpu.VMEM((image_len // LANES, channels, TILE, LANES), jnp.bfloat16),
            pltpu.SemaphoreType.DMA((image_len // LANES,)),
        ],
        compiler_params=limit,
        name="layers",
    )(arrived, *weights)


def local(partials, coverage, conv_one, bias_one, conv_two, bias_two):
    count_col = lax.axis_size("col")
    devices = lax.axis_size("vis") * lax.axis_size("row") * count_col
    image_len = partials.shape[3] * count_col // 2
    sent = devices * (TILE + 2 * HALO) * image_len * 2
    fits = partials.shape[2] == LANES and image_len == devices * TILE and conv_two.shape[2] * 4 == LANES and image_len == 2 * LANES and sent <= DIRECT_BYTES
    plan = direct if fits else staged
    return plan(partials, coverage, conv_one, bias_one, conv_two, bias_two)


def solution(mesh):
    placed = (P("vis", None, "row", "col"), P("vis", "row", "col"), P(), P(), P(), P())
    return jax.shard_map(
        local,
        mesh=mesh,
        in_specs=placed,
        out_specs=P(None, ALL, None),
        check_vma=False,
    )
```

```python
import functools
import math

import jax
import jax.numpy as jnp
import numpy as np
from jax import lax
from jax.experimental import pallas as pl
from jax.experimental.pallas import tpu as pltpu
from jax.sharding import PartitionSpec as P

BLK = 128
ALL = ("vis", "row", "col")
DIRECT_BYTES = 4 * 2**20
HALO = 2
TILE = 8
LANES = 128


def with_halo(cells, sides, width):
    for axis, dim in sides:
        count = lax.axis_size(axis)
        ends = count - 1
        head = lax.slice_in_dim(cells, 0, width, axis=dim)
        tail = lax.slice_in_dim(cells, cells.shape[dim] - width, cells.shape[dim], axis=dim)
        cells = jnp.concatenate(
            [
                lax.ppermute(tail, axis, [(i, (i + 1) % count) for i in range(ends)]),
                cells,
                lax.ppermute(head, axis, [((i + 1) % count, i) for i in range(ends)]),
            ],
            axis=dim,
        )
    return cells


def phase_table(numer, denom):
    angle = numer.astype(jnp.float32) * (2.0 * math.pi / denom)
    return (jnp.cos(angle), jnp.sin(angle))


def partial_transform(real_part, imag_part, block_of, keep_imag):
    batch = real_part.shape[0]
    count_blocks = real_part.shape[1]
    block_len = real_part.shape[2]
    length = count_blocks * block_len
    highest = lax.Precision.HIGHEST
    outer = jnp.arange(count_blocks, dtype=jnp.int32)
    inner = jnp.arange(block_len, dtype=jnp.int32)
    cos_one, sin_one = phase_table(block_of[:, None] * outer[None, :] % count_blocks, count_blocks)
    mid_re = jnp.einsum("lpt,px->lxt", real_part, cos_one, precision=highest) - jnp.einsum(
        "lpt,px->lxt", imag_part, sin_one, precision=highest
    )
    mid_im = jnp.einsum("lpt,px->lxt", real_part, sin_one, precision=highest) + jnp.einsum(
        "lpt,px->lxt", imag_part, cos_one, precision=highest
    )
    cos_two, sin_two = phase_table(outer[:, None] * inner[None, :] % length, length)
    parity = (1 - 2 * (outer % 2)).astype(jnp.float32)[:, None]
    cos_two = cos_two * parity
    sin_two = sin_two * parity
    turn_re = mid_re * cos_two - mid_im * sin_two
    turn_im = mid_re * sin_two + mid_im * cos_two
    kept = jnp.arange(block_len // 2, dtype=jnp.int32)
    picked = (kept + 3 * block_len // 4) % block_len
    cos_three, sin_three = phase_table(inner[:, None] * picked[None, :] % block_len, block_len)
    out_re = jnp.einsum("lxt,tj->ljx", turn_re, cos_three, precision=highest) - jnp.einsum(
        "lxt,tj->ljx", turn_im, sin_three, precision=highest
    )
    out_re = out_re.reshape(batch, length // 2)
    if keep_imag:
        out_im = jnp.einsum("lxt,tj->ljx", turn_re, sin_three, precision=highest) + jnp.einsum(
            "lxt,tj->ljx", turn_im, cos_three, precision=highest
        )
        return (out_re, out_im.reshape(batch, length // 2))
    return (out_re, out_re)


def first_layer(extended, conv_one, bias_one, count_rows):
    width = extended.shape[1]
    padded = jnp.pad(extended, ((0, 0), (1, 1)))
    summed = (
        jnp.zeros((conv_one.shape[0], count_rows, width), jnp.float32) + bias_one[:, None, None]
    )
    for shift_b in range(3):
        for shift_a in range(3):
            summed = (
                summed
                + conv_one[:, shift_b, shift_a][:, None, None]
                * padded[None, shift_b : shift_b + count_rows, shift_a : shift_a + width]
            )
    return jnp.maximum(summed, 0.0)


def second_layer(hidden_ext, conv_two, bias_two, count_rows):
    width = hidden_ext.shape[2]
    padded = jnp.pad(hidden_ext, ((0, 0), (0, 0), (1, 1)))
    summed = jnp.zeros((conv_two.shape[2], count_rows, width), jnp.float32)
    for shift_b in range(3):
        for shift_a in range(3):
            summed = summed + jnp.einsum(
                "kj,jba->kba",
                conv_two[shift_b, shift_a],
                padded[:, shift_b : shift_b + count_rows, shift_a : shift_a + width],
                preferred_element_type=jnp.float32,
            )
    return (summed + bias_two[:, None, None]).astype(jnp.bfloat16)


def staged(partials, coverage, conv_one, bias_one, conv_two, bias_two):
    count_vis = lax.axis_size("vis")
    count_row = lax.axis_size("row")
    count_col = lax.axis_size("col")
    grid_len = partials.shape[3] * count_col
    cover = coverage[0]
    block_rows = cover.shape[0]
    block_cols = cover.shape[1]
    spread = jnp.broadcast_to(cover[:, None, :, None], (block_rows, BLK, block_cols, BLK))
    spread = spread.reshape(block_rows * BLK, block_cols * BLK)
    count_blocks = count_vis * count_row
    row_block = grid_len // count_blocks
    row_share = row_block // count_col
    masked = partials[0] * spread.astype(jnp.bfloat16)[None]
    reduced = lax.psum_scatter(
        masked.astype(jnp.float32).astype(jnp.bfloat16), "vis", scatter_dimension=1, tiled=True
    ).astype(jnp.float32)
    grid_rows = lax.all_to_all(
        reduced.astype(jnp.bfloat16), "col", split_axis=1, concat_axis=2, tiled=True
    ).astype(reduced.dtype)
    natural = jnp.arange(count_blocks, dtype=jnp.int32)
    shaped = grid_rows.reshape(2, row_share, count_blocks, row_block)
    first_re, first_im = partial_transform(shaped[0], shaped[1], natural, True)
    stacked = jnp.stack([first_re, first_im])
    moved = lax.all_to_all(
        lax.all_to_all(
            stacked.astype(jnp.bfloat16), ("vis", "row"), split_axis=2, concat_axis=1, tiled=True
        ),
        "col",
        split_axis=2,
        concat_axis=1,
        tiled=True,
    ).astype(stacked.dtype)
    img_rows = moved.shape[2]
    arranged = moved.reshape(2, count_col, count_blocks, row_share, img_rows)
    arranged = arranged.transpose(0, 4, 2, 1, 3).reshape(2, img_rows, count_blocks, row_block)
    owners = natural % count_row * count_vis + natural // count_row
    image, unused = partial_transform(arranged[0], arranged[1], owners, False)
    image = image * (1.0 / grid_len)
    extended = with_halo(image.astype(jnp.bfloat16), ((("vis", "row", "col"), 0),), 1).astype(
        image.dtype
    )
    hidden = first_layer(extended, conv_one, bias_one, img_rows).astype(jnp.bfloat16)
    hidden_ext = with_halo(hidden, ((("vis", "row", "col"), 1),), 1)
    return second_layer(hidden_ext, conv_two, bias_two, img_rows)


def grid_table(length):
    image_len = length // 2
    place = np.arange(length)[:, None] - length // 2
    pixel = np.arange(image_len)[None, :] - image_len // 2
    angle = (place * pixel % length) * (2.0 * math.pi / length)
    cos, sin = (wave.reshape(-1, LANES, image_len) for wave in (np.cos(angle), np.sin(angle)))
    return (np.stack([cos, -sin], axis=1).reshape(2 * length, image_len) / length).astype(jnp.bfloat16)


def phases(numer, length):
    turn = numer & (length - 1)
    turn = jnp.where(turn >= length // 2, turn - length, turn)
    angle = turn.astype(jnp.float32) * (2.0 * math.pi / length)
    return jnp.cos(angle), jnp.sin(angle)


def make_first(first, length):
    tall, cols = first.shape[0] // 2, first.shape[1]
    image_len = tall - TILE
    blocks = -(-tall // (TILE * TILE)) * TILE
    start = lax.axis_index("col") * cols - length // 2
    row = lax.broadcasted_iota(jnp.int32, (blocks, cols), 0) * TILE - HALO - image_len // 2
    cos_far, sin_far = phases(row * (start + lax.broadcasted_iota(jnp.int32, (blocks, cols), 1)), length)
    row = lax.broadcasted_iota(jnp.int32, (TILE, cols), 0)
    cos_near, sin_near = phases(row * (start + lax.broadcasted_iota(jnp.int32, (TILE, cols), 1)), length)
    cosines, sines = [], []
    for k in range(tall // TILE):
        cos_at, sin_at = cos_far[k : k + 1], sin_far[k : k + 1]
        cos = cos_at * cos_near - sin_at * sin_near
        sin = sin_at * cos_near + cos_at * sin_near
        pixel = row + (TILE * k - HALO)
        if k == 0 or k == tall // TILE - 1:
            inside = (pixel >= 0) & (pixel < image_len)
            cos, sin = jnp.where(inside, cos, 0.0), jnp.where(inside, sin, 0.0)
        cosines.append(cos)
        sines.append(sin)
    first[...] = jnp.concatenate(cosines + sines, axis=0).astype(first.dtype)


def share_kernel(length, cover_in, parts_in, out, cover, parts, first, sems):
    get_cover = pltpu.make_async_copy(cover_in, cover, sems.at[0])
    get_parts = pltpu.make_async_copy(parts_in, parts, sems.at[1])
    for copy in (get_parts, get_cover):
        copy.start()
    make_first(first, length)
    count_rows = parts.shape[2]
    get_cover.wait()
    get_parts.wait()
    components = []
    for component in range(2):
        strips = []
        for i in range(cover.shape[1]):
            cells = []
            for j in range(cover.shape[2]):
                block = parts[0, component, i * BLK : (i + 1) * BLK, j * BLK : (j + 1) * BLK]
                level = jnp.full(block.shape, cover[0, i, j].astype(jnp.float32)).astype(jnp.bfloat16)
                cells.append(block * level)
            strips.append(jnp.concatenate(cells, axis=1))
        components.append(jnp.concatenate(strips, axis=0))
    grid = jnp.concatenate(components, axis=0)
    upper = lax.broadcasted_iota(jnp.int32, (TILE, LANES), 0) < TILE // 2
    devices = out.shape[0]
    tall = first.shape[0] // 2
    turned = lax.dot_general(first[...], grid, (((1,), (1,)), ((), ())), preferred_element_type=jnp.float32)
    mid_re = turned[:tall, :count_rows] - turned[tall:, count_rows:]
    mid_im = turned[tall:, :count_rows] + turned[:tall, count_rows:]
    for device in range(devices):
        here = slice(TILE * device, TILE * (device + 1))
        below = slice(TILE * (device + 1), TILE * (device + 2))
        middle = jnp.where(upper, mid_re[below], pltpu.roll(mid_im[below], TILE // 2, 0))
        out[device] = jnp.concatenate([mid_re[here], middle, mid_im[here]], axis=0).astype(out.dtype)


def own_place():
    place, count = 0, 1
    for axis in ALL:
        place = place * lax.axis_size(axis) + lax.axis_index(axis)
        count = count * lax.axis_size(axis)
    return place, count - 1


def four_times(values):
    return jnp.concatenate([values] * 4, axis=1)


def weights_kernel(
    one_in, bias_in, two_in, bias_two_in, table_in, weights_one, weights_two, bias_rows, table, one, bias, two, bias_two, sems
):
    fetch = [
        pltpu.make_async_copy(one_in, one, sems.at[0]),
        pltpu.make_async_copy(bias_in, bias, sems.at[1]),
        pltpu.make_async_copy(two_in, two, sems.at[2]),
        pltpu.make_async_copy(bias_two_in, bias_two, sems.at[3]),
    ]
    get_table = pltpu.make_async_copy(table_in, table, sems.at[4])
    for copy in (*fetch, get_table):
        copy.start()
    for copy in fetch:
        copy.wait()
    channels = one.shape[2]
    rows = TILE + 2
    per_tile = LANES // channels
    lanes = -(-rows * channels // LANES) * LANES
    image_row = lax.broadcasted_iota(jnp.int32, (16, lanes), 0)
    hidden_row = lax.broadcasted_iota(jnp.int32, (16, lanes), 1) // channels
    place, last = own_place()
    held = (hidden_row >= jnp.where(place == 0, 1, 0)) & (hidden_row < jnp.where(place == last, rows - 1, rows))
    high, low = [], []
    for tap in range(3):
        band = jnp.zeros((16, lanes), jnp.float32)
        for shift in range(3):
            line = jnp.concatenate([four_times(one[shift, tap : tap + 1])] * (lanes // LANES), axis=1)
            band = jnp.where(held & (image_row - hidden_row == shift), line, band)
        high.append(band.astype(jnp.bfloat16).astype(jnp.float32))
        low.append(band - high[-1])
    line = jnp.concatenate([four_times(bias[...])] * (lanes // LANES), axis=1)
    with_bias = high[0]
    for piece in range(3):
        rounded = line.astype(jnp.bfloat16).astype(jnp.float32)
        with_bias = jnp.where(held & (image_row == 12 + piece), rounded, with_bias)
        line = line - rounded
    stacked = jnp.concatenate([with_bias, *high[1:], *high, *low], axis=0)
    weights_one[...] = stacked.T[: weights_one.shape[0]].astype(jnp.bfloat16)
    row = lax.broadcasted_iota(jnp.int32, bias_rows.shape, 0) // TILE
    lane = lax.broadcasted_iota(jnp.int32, bias_rows.shape, 1)
    line = jnp.where(row == lane, four_times(bias_two[...]), 0.0)
    bias_rows[...] = jnp.broadcast_to(jnp.sum(line, axis=1, keepdims=True), bias_rows.shape)
    lines = [[four_times(two[shift, tap].astype(jnp.float32)) for shift in range(3)] for tap in range(3)]
    row = lax.broadcasted_iota(jnp.int32, (TILE, LANES), 0)
    lane = lax.broadcasted_iota(jnp.int32, (TILE, LANES), 1) // channels
    zero = jnp.zeros((TILE, LANES), jnp.float32)
    for tile in range(-(-3 * rows // per_tile)):
        taps = sorted({(tile * per_tile + g) // rows for g in range(per_tile)} & {0, 1, 2})
        masks = []
        for tap in taps:
            hidden_row = tile * per_tile + lane - tap * rows
            inside = (hidden_row >= 0) & (hidden_row < rows)
            masks += [(tap, shift, inside & (hidden_row - row == shift)) for shift in range(3)]
        width = min(LANES, weights_two.shape[1] - tile * LANES)
        for channel in range(0, channels, 2):
            pair = []
            for k in (channel, channel + 1):
                values = zero
                for tap, shift, mask in masks:
                    values = jnp.where(mask, lines[tap][shift][k : k + 1], values)
                pair.append(values)
            block = jnp.concatenate(pair, axis=0).astype(jnp.bfloat16)
            weights_two[TILE * channel : TILE * (channel + 2), tile * LANES : tile * LANES + width] = block[:, :width]
    get_table.wait()


def shifted(values, width):
    lane = lax.broadcasted_iota(jnp.int32, values.shape, 1)
    zero = jnp.zeros_like(values)
    before = jnp.where(lane == 0, zero, pltpu.roll(values, 1, 1))
    after = jnp.where(lane == width - 1, zero, pltpu.roll(values, width - 1, 1))
    return before, values, after


def layers_kernel(shares, weights_one, weights_two, bias_rows, table, out, staged, sems):
    width = out.shape[2]
    vis, row, col = (lax.axis_size(axis) for axis in ALL)
    upper = lax.broadcasted_iota(jnp.int32, (TILE, LANES), 0) < TILE // 2
    above, below = [], []
    for r in range(row):
        senders = [(v * row + r) * col + c for v in range(vis) for c in range(col)]
        total = shares[senders[0]].astype(jnp.float32)
        for sender in senders[1:]:
            total = total + shares[sender].astype(jnp.float32)
        middle = total[TILE : 2 * TILE]
        above += [total[:TILE], total[2 * TILE :]]
        below += [jnp.where(upper, middle, 0.0), jnp.where(upper, pltpu.roll(middle, TILE // 2, 0), 0.0)]
    turned = jnp.concatenate([jnp.concatenate(above, axis=1), jnp.concatenate(below, axis=1)], axis=0)
    high = turned.astype(jnp.bfloat16)
    low = (turned - high.astype(jnp.float32)).astype(jnp.bfloat16)
    image = jnp.dot(jnp.concatenate([high, low], axis=0), table[...], preferred_element_type=jnp.float32)
    image = image[: 2 * TILE] + image[2 * TILE :]
    columns = jnp.concatenate(shifted(image, width), axis=0)
    high = columns.astype(jnp.bfloat16).astype(jnp.float32)
    low = columns - high
    row = lax.broadcasted_iota(jnp.int32, (48, width), 0)
    with_ones = jnp.where((row >= 12) & (row < 15), 1.0, high)
    stacked = jnp.concatenate([with_ones, low, high], axis=0).astype(jnp.bfloat16)
    hidden = jnp.dot(weights_one[...], stacked, preferred_element_type=jnp.float32)
    hidden = jnp.maximum(hidden, 0.0).astype(jnp.bfloat16)
    stacked = jnp.concatenate(shifted(hidden, width), axis=0)
    half = out.shape[0] // 2
    copies = []
    for part in range(2):
        rows = pl.ds(part * half * TILE, half * TILE)
        features = jnp.dot(weights_two[rows], stacked, preferred_element_type=jnp.float32)
        features = features + jnp.concatenate([bias_rows[rows]] * (width // LANES), axis=1)
        channels_of = pl.ds(part * half, half)
        staged[channels_of] = features.reshape(half, TILE, width).astype(out.dtype)
        copies.append(pltpu.make_async_copy(staged.at[channels_of], out.at[channels_of], sems.at[part]))
        copies[-1].start()
    for copy in copies:
        copy.wait()


def in_hbm(*arrays):
    return [pltpu.with_memory_space_constraint(array, pltpu.HBM) for array in arrays]


def direct(partials, coverage, conv_one, bias_one, conv_two, bias_two):
    count_row, count_col = lax.axis_size("row"), lax.axis_size("col")
    devices = lax.axis_size("vis") * count_row * count_col
    length = partials.shape[3] * count_col
    image_len = length // 2
    channels = conv_two.shape[2]
    second = grid_table(length)
    vmem, hbm = pl.BlockSpec(memory_space=pltpu.VMEM), pl.BlockSpec(memory_space=pltpu.HBM)
    limit = pltpu.CompilerParams(vmem_limit_bytes=16 * 2**20)
    share = (devices, 2 * (TILE + 2 * HALO), LANES)
    shares = pl.pallas_call(
        functools.partial(share_kernel, length),
        out_shape=jax.ShapeDtypeStruct(share, jnp.bfloat16),
        in_specs=[hbm] * 2,
        out_specs=vmem,
        scratch_shapes=[
            pltpu.SMEM(coverage.shape, jnp.int32),
            pltpu.VMEM(partials.shape, jnp.bfloat16),
            pltpu.VMEM((2 * (image_len + TILE), partials.shape[3]), jnp.bfloat16),
            pltpu.SemaphoreType.DMA((2,)),
        ],
        compiler_params=limit,
        name="shares",
    )(*in_hbm(coverage, partials))
    arrived = lax.all_to_all(shares, ALL, split_axis=0, concat_axis=0, tiled=True)
    rows = TILE + 2
    weights = pl.pallas_call(
        weights_kernel,
        out_shape=[
            jax.ShapeDtypeStruct((rows * channels, 3 * 48), jnp.bfloat16),
            jax.ShapeDtypeStruct((TILE * channels, 3 * rows * channels), jnp.bfloat16),
            jax.ShapeDtypeStruct((TILE * channels, LANES), jnp.float32),
            jax.ShapeDtypeStruct(second.shape, jnp.bfloat16),
        ],
        in_specs=[hbm] * 5,
        out_specs=[vmem] * 4,
        scratch_shapes=[
            pltpu.VMEM((3, 3, channels), jnp.float32),
            pltpu.VMEM((1, channels), jnp.float32),
            pltpu.VMEM(conv_two.shape, jnp.bfloat16),
            pltpu.VMEM((1, channels), jnp.float32),
            pltpu.SemaphoreType.DMA((5,)),
        ],
        compiler_params=limit,
        name="weights",
    )(*in_hbm(conv_one.transpose(1, 2, 0), bias_one[None], conv_two, bias_two[None], jnp.asarray(second)))
    return pl.pallas_call(
        layers_kernel,
        out_shape=jax.ShapeDtypeStruct((channels, TILE, image_len), jnp.bfloat16),
        in_specs=[vmem] * 5,
        out_specs=hbm,
        scratch_shapes=[
            pltpu.VMEM((channels, TILE, image_len), jnp.bfloat16),
            pltpu.SemaphoreType.DMA((2,)),
        ],
        compiler_params=limit,
        name="layers",
    )(arrived, *weights)


def local(partials, coverage, conv_one, bias_one, conv_two, bias_two):
    count_col = lax.axis_size("col")
    devices = lax.axis_size("vis") * lax.axis_size("row") * count_col
    image_len = partials.shape[3] * count_col // 2
    sent = devices * (TILE + 2 * HALO) * image_len * 2
    fits = partials.shape[2] == LANES and image_len == devices * TILE and conv_two.shape[2] * 4 == LANES and image_len == 2 * LANES and sent <= DIRECT_BYTES
    plan = direct if fits else staged
    return plan(partials, coverage, conv_one, bias_one, conv_two, bias_two)


def solution(mesh):
    placed = (P("vis", None, "row", "col"), P("vis", "row", "col"), P(), P(), P(), P())
    return jax.shard_map(
        local,
        mesh=mesh,
        in_specs=placed,
        out_specs=P(None, ALL, None),
        check_vma=False,
    )
```

```python
import functools
import math

import jax
import jax.numpy as jnp
import numpy as np
from jax import lax
from jax.experimental import pallas as pl
from jax.experimental.pallas import tpu as pltpu
from jax.sharding import PartitionSpec as P

BLK = 128
ALL = ("vis", "row", "col")
DIRECT_BYTES = 4 * 2**20
HALO = 2
TILE = 8
LANES = 128


def with_halo(cells, sides, width):
    for axis, dim in sides:
        count = lax.axis_size(axis)
        ends = count - 1
        head = lax.slice_in_dim(cells, 0, width, axis=dim)
        tail = lax.slice_in_dim(cells, cells.shape[dim] - width, cells.shape[dim], axis=dim)
        cells = jnp.concatenate(
            [
                lax.ppermute(tail, axis, [(i, (i + 1) % count) for i in range(ends)]),
                cells,
                lax.ppermute(head, axis, [((i + 1) % count, i) for i in range(ends)]),
            ],
            axis=dim,
        )
    return cells


def phase_table(numer, denom):
    angle = numer.astype(jnp.float32) * (2.0 * math.pi / denom)
    return (jnp.cos(angle), jnp.sin(angle))


def partial_transform(real_part, imag_part, block_of, keep_imag):
    batch = real_part.shape[0]
    count_blocks = real_part.shape[1]
    block_len = real_part.shape[2]
    length = count_blocks * block_len
    highest = lax.Precision.HIGHEST
    outer = jnp.arange(count_blocks, dtype=jnp.int32)
    inner = jnp.arange(block_len, dtype=jnp.int32)
    cos_one, sin_one = phase_table(block_of[:, None] * outer[None, :] % count_blocks, count_blocks)
    mid_re = jnp.einsum("lpt,px->lxt", real_part, cos_one, precision=highest) - jnp.einsum(
        "lpt,px->lxt", imag_part, sin_one, precision=highest
    )
    mid_im = jnp.einsum("lpt,px->lxt", real_part, sin_one, precision=highest) + jnp.einsum(
        "lpt,px->lxt", imag_part, cos_one, precision=highest
    )
    cos_two, sin_two = phase_table(outer[:, None] * inner[None, :] % length, length)
    parity = (1 - 2 * (outer % 2)).astype(jnp.float32)[:, None]
    cos_two = cos_two * parity
    sin_two = sin_two * parity
    turn_re = mid_re * cos_two - mid_im * sin_two
    turn_im = mid_re * sin_two + mid_im * cos_two
    kept = jnp.arange(block_len // 2, dtype=jnp.int32)
    picked = (kept + 3 * block_len // 4) % block_len
    cos_three, sin_three = phase_table(inner[:, None] * picked[None, :] % block_len, block_len)
    out_re = jnp.einsum("lxt,tj->ljx", turn_re, cos_three, precision=highest) - jnp.einsum(
        "lxt,tj->ljx", turn_im, sin_three, precision=highest
    )
    out_re = out_re.reshape(batch, length // 2)
    if keep_imag:
        out_im = jnp.einsum("lxt,tj->ljx", turn_re, sin_three, precision=highest) + jnp.einsum(
            "lxt,tj->ljx", turn_im, cos_three, precision=highest
        )
        return (out_re, out_im.reshape(batch, length // 2))
    return (out_re, out_re)


def first_layer(extended, conv_one, bias_one, count_rows):
    width = extended.shape[1]
    padded = jnp.pad(extended, ((0, 0), (1, 1)))
    summed = (
        jnp.zeros((conv_one.shape[0], count_rows, width), jnp.float32) + bias_one[:, None, None]
    )
    for shift_b in range(3):
        for shift_a in range(3):
            summed = (
                summed
                + conv_one[:, shift_b, shift_a][:, None, None]
                * padded[None, shift_b : shift_b + count_rows, shift_a : shift_a + width]
            )
    return jnp.maximum(summed, 0.0)


def second_layer(hidden_ext, conv_two, bias_two, count_rows):
    width = hidden_ext.shape[2]
    padded = jnp.pad(hidden_ext, ((0, 0), (0, 0), (1, 1)))
    summed = jnp.zeros((conv_two.shape[2], count_rows, width), jnp.float32)
    for shift_b in range(3):
        for shift_a in range(3):
            summed = summed + jnp.einsum(
                "kj,jba->kba",
                conv_two[shift_b, shift_a],
                padded[:, shift_b : shift_b + count_rows, shift_a : shift_a + width],
                preferred_element_type=jnp.float32,
            )
    return (summed + bias_two[:, None, None]).astype(jnp.bfloat16)


def staged(partials, coverage, conv_one, bias_one, conv_two, bias_two):
    count_vis = lax.axis_size("vis")
    count_row = lax.axis_size("row")
    count_col = lax.axis_size("col")
    grid_len = partials.shape[3] * count_col
    cover = coverage[0]
    block_rows = cover.shape[0]
    block_cols = cover.shape[1]
    spread = jnp.broadcast_to(cover[:, None, :, None], (block_rows, BLK, block_cols, BLK))
    spread = spread.reshape(block_rows * BLK, block_cols * BLK)
    count_blocks = count_vis * count_row
    row_block = grid_len // count_blocks
    row_share = row_block // count_col
    masked = partials[0] * spread.astype(jnp.bfloat16)[None]
    reduced = lax.psum_scatter(
        masked.astype(jnp.float32).astype(jnp.bfloat16), "vis", scatter_dimension=1, tiled=True
    ).astype(jnp.float32)
    grid_rows = lax.all_to_all(
        reduced.astype(jnp.bfloat16), "col", split_axis=1, concat_axis=2, tiled=True
    ).astype(reduced.dtype)
    natural = jnp.arange(count_blocks, dtype=jnp.int32)
    shaped = grid_rows.reshape(2, row_share, count_blocks, row_block)
    first_re, first_im = partial_transform(shaped[0], shaped[1], natural, True)
    stacked = jnp.stack([first_re, first_im])
    moved = lax.all_to_all(
        lax.all_to_all(
            stacked.astype(jnp.bfloat16), ("vis", "row"), split_axis=2, concat_axis=1, tiled=True
        ),
        "col",
        split_axis=2,
        concat_axis=1,
        tiled=True,
    ).astype(stacked.dtype)
    img_rows = moved.shape[2]
    arranged = moved.reshape(2, count_col, count_blocks, row_share, img_rows)
    arranged = arranged.transpose(0, 4, 2, 1, 3).reshape(2, img_rows, count_blocks, row_block)
    owners = natural % count_row * count_vis + natural // count_row
    image, unused = partial_transform(arranged[0], arranged[1], owners, False)
    image = image * (1.0 / grid_len)
    extended = with_halo(image.astype(jnp.bfloat16), ((("vis", "row", "col"), 0),), 1).astype(
        image.dtype
    )
    hidden = first_layer(extended, conv_one, bias_one, img_rows).astype(jnp.bfloat16)
    hidden_ext = with_halo(hidden, ((("vis", "row", "col"), 1),), 1)
    return second_layer(hidden_ext, conv_two, bias_two, img_rows)


def grid_table(length):
    image_len = length // 2
    place = np.arange(length)[:, None] - length // 2
    pixel = np.arange(image_len)[None, :] - image_len // 2
    angle = (place * pixel % length) * (2.0 * math.pi / length)
    cos, sin = (wave.reshape(-1, LANES, image_len) for wave in (np.cos(angle), np.sin(angle)))
    return (np.stack([cos, -sin], axis=1).reshape(2 * length, image_len) / length).astype(jnp.bfloat16)


def phases(numer, length):
    turn = numer & (length - 1)
    turn = jnp.where(turn >= length // 2, turn - length, turn)
    angle = turn.astype(jnp.float32) * (2.0 * math.pi / length)
    return jnp.cos(angle), jnp.sin(angle)


def make_first(first, length):
    tall, cols = first.shape[0] // 2, first.shape[1]
    image_len = tall - TILE
    start = lax.axis_index("col") * cols - length // 2
    place = start + lax.broadcasted_iota(jnp.int32, (TILE, cols), 1)
    row = lax.broadcasted_iota(jnp.int32, (TILE, cols), 0)
    cos_far, sin_far = phases((row * TILE * TILE - HALO - image_len // 2) * place, length)
    cos_mid, sin_mid = phases(row * TILE * place, length)
    cos_near, sin_near = phases(row * place, length)
    cosines, sines = [], []
    for k in range(tall // TILE):
        n, m = divmod(k, TILE)
        if m == 0:
            cos_at, sin_at = cos_far[n : n + 1], sin_far[n : n + 1]
            cos_tile = cos_at * cos_mid - sin_at * sin_mid
            sin_tile = sin_at * cos_mid + cos_at * sin_mid
        cos_at, sin_at = cos_tile[m : m + 1], sin_tile[m : m + 1]
        cos = cos_at * cos_near - sin_at * sin_near
        sin = sin_at * cos_near + cos_at * sin_near
        pixel = row + (TILE * k - HALO)
        if k == 0 or k == tall // TILE - 1:
            inside = (pixel >= 0) & (pixel < image_len)
            cos, sin = jnp.where(inside, cos, 0.0), jnp.where(inside, sin, 0.0)
        cosines.append(cos)
        sines.append(sin)
    first[...] = jnp.concatenate(cosines + sines, axis=0).astype(first.dtype)


def share_kernel(length, cover_in, parts_in, out, cover, parts, first, sems):
    get_cover = pltpu.make_async_copy(cover_in, cover, sems.at[0])
    get_parts = pltpu.make_async_copy(parts_in, parts, sems.at[1])
    for copy in (get_parts, get_cover):
        copy.start()
    make_first(first, length)
    count_rows = parts.shape[2]
    get_cover.wait()
    get_parts.wait()
    components = []
    for component in range(2):
        strips = []
        for i in range(cover.shape[1]):
            cells = []
            for j in range(cover.shape[2]):
                block = parts[0, component, i * BLK : (i + 1) * BLK, j * BLK : (j + 1) * BLK]
                level = jnp.full(block.shape, cover[0, i, j].astype(jnp.float32)).astype(jnp.bfloat16)
                cells.append(block * level)
            strips.append(jnp.concatenate(cells, axis=1))
        components.append(jnp.concatenate(strips, axis=0))
    grid = jnp.concatenate(components, axis=0)
    upper = lax.broadcasted_iota(jnp.int32, (TILE, LANES), 0) < TILE // 2
    devices = out.shape[0]
    tall = first.shape[0] // 2
    turned = lax.dot_general(first[...], grid, (((1,), (1,)), ((), ())), preferred_element_type=jnp.float32)
    mid_re = turned[:tall, :count_rows] - turned[tall:, count_rows:]
    mid_im = turned[tall:, :count_rows] + turned[:tall, count_rows:]
    for device in range(devices):
        here = slice(TILE * device, TILE * (device + 1))
        below = slice(TILE * (device + 1), TILE * (device + 2))
        middle = jnp.where(upper, mid_re[below], pltpu.roll(mid_im[below], TILE // 2, 0))
        out[device] = jnp.concatenate([mid_re[here], middle, mid_im[here]], axis=0).astype(out.dtype)


def own_place():
    place, count = 0, 1
    for axis in ALL:
        place = place * lax.axis_size(axis) + lax.axis_index(axis)
        count = count * lax.axis_size(axis)
    return place, count - 1


def four_times(values):
    return jnp.concatenate([values] * 4, axis=1)


def weights_kernel(
    one_in, bias_in, two_in, bias_two_in, table_in, weights_one, weights_two, bias_rows, table, one, bias, two, bias_two, sems
):
    fetch = [
        pltpu.make_async_copy(one_in, one, sems.at[0]),
        pltpu.make_async_copy(bias_in, bias, sems.at[1]),
        pltpu.make_async_copy(two_in, two, sems.at[2]),
        pltpu.make_async_copy(bias_two_in, bias_two, sems.at[3]),
    ]
    get_table = pltpu.make_async_copy(table_in, table, sems.at[4])
    for copy in (*fetch, get_table):
        copy.start()
    for copy in fetch:
        copy.wait()
    channels = one.shape[2]
    rows = TILE + 2
    per_tile = LANES // channels
    lanes = -(-rows * channels // LANES) * LANES
    image_row = lax.broadcasted_iota(jnp.int32, (16, lanes), 0)
    hidden_row = lax.broadcasted_iota(jnp.int32, (16, lanes), 1) // channels
    place, last = own_place()
    held = (hidden_row >= jnp.where(place == 0, 1, 0)) & (hidden_row < jnp.where(place == last, rows - 1, rows))
    high, low = [], []
    for tap in range(3):
        band = jnp.zeros((16, lanes), jnp.float32)
        for shift in range(3):
            line = jnp.concatenate([four_times(one[shift, tap : tap + 1])] * (lanes // LANES), axis=1)
            band = jnp.where(held & (image_row - hidden_row == shift), line, band)
        high.append(band.astype(jnp.bfloat16).astype(jnp.float32))
        low.append(band - high[-1])
    line = jnp.concatenate([four_times(bias[...])] * (lanes // LANES), axis=1)
    with_bias = high[0]
    for piece in range(3):
        rounded = line.astype(jnp.bfloat16).astype(jnp.float32)
        with_bias = jnp.where(held & (image_row == 12 + piece), rounded, with_bias)
        line = line - rounded
    stacked = jnp.concatenate([with_bias, *high[1:], *high, *low], axis=0)
    weights_one[...] = stacked.T[: weights_one.shape[0]].astype(jnp.bfloat16)
    row = lax.broadcasted_iota(jnp.int32, bias_rows.shape, 0) // TILE
    lane = lax.broadcasted_iota(jnp.int32, bias_rows.shape, 1)
    line = jnp.where(row == lane, four_times(bias_two[...]), 0.0)
    bias_rows[...] = jnp.broadcast_to(jnp.sum(line, axis=1, keepdims=True), bias_rows.shape)
    lines = [[four_times(two[shift, tap].astype(jnp.float32)) for shift in range(3)] for tap in range(3)]
    row = lax.broadcasted_iota(jnp.int32, (TILE, LANES), 0)
    lane = lax.broadcasted_iota(jnp.int32, (TILE, LANES), 1) // channels
    zero = jnp.zeros((TILE, LANES), jnp.float32)
    for tile in range(-(-3 * rows // per_tile)):
        taps = sorted({(tile * per_tile + g) // rows for g in range(per_tile)} & {0, 1, 2})
        masks = []
        for tap in taps:
            hidden_row = tile * per_tile + lane - tap * rows
            inside = (hidden_row >= 0) & (hidden_row < rows)
            masks += [(tap, shift, inside & (hidden_row - row == shift)) for shift in range(3)]
        width = min(LANES, weights_two.shape[1] - tile * LANES)
        for channel in range(0, channels, 2):
            pair = []
            for k in (channel, channel + 1):
                values = zero
                for tap, shift, mask in masks:
                    values = jnp.where(mask, lines[tap][shift][k : k + 1], values)
                pair.append(values)
            block = jnp.concatenate(pair, axis=0).astype(jnp.bfloat16)
            weights_two[TILE * channel : TILE * (channel + 2), tile * LANES : tile * LANES + width] = block[:, :width]
    get_table.wait()


def shifted(values, width):
    lane = lax.broadcasted_iota(jnp.int32, values.shape, 1)
    zero = jnp.zeros_like(values)
    before = jnp.where(lane == 0, zero, pltpu.roll(values, 1, 1))
    after = jnp.where(lane == width - 1, zero, pltpu.roll(values, width - 1, 1))
    return before, values, after


def layers_kernel(shares, weights_one, weights_two, bias_rows, table, out, staged, sems):
    width = out.shape[2]
    vis, row, col = (lax.axis_size(axis) for axis in ALL)
    upper = lax.broadcasted_iota(jnp.int32, (TILE, LANES), 0) < TILE // 2
    above, below = [], []
    for r in range(row):
        senders = [(v * row + r) * col + c for v in range(vis) for c in range(col)]
        total = shares[senders[0]].astype(jnp.float32)
        for sender in senders[1:]:
            total = total + shares[sender].astype(jnp.float32)
        middle = total[TILE : 2 * TILE]
        above += [total[:TILE], total[2 * TILE :]]
        below += [jnp.where(upper, middle, 0.0), jnp.where(upper, pltpu.roll(middle, TILE // 2, 0), 0.0)]
    turned = jnp.concatenate([jnp.concatenate(above, axis=1), jnp.concatenate(below, axis=1)], axis=0)
    high = turned.astype(jnp.bfloat16)
    low = (turned - high.astype(jnp.float32)).astype(jnp.bfloat16)
    image = jnp.dot(jnp.concatenate([high, low], axis=0), table[...], preferred_element_type=jnp.float32)
    image = image[: 2 * TILE] + image[2 * TILE :]
    columns = jnp.concatenate(shifted(image, width), axis=0)
    high = columns.astype(jnp.bfloat16).astype(jnp.float32)
    low = columns - high
    row = lax.broadcasted_iota(jnp.int32, (48, width), 0)
    with_ones = jnp.where((row >= 12) & (row < 15), 1.0, high)
    stacked = jnp.concatenate([with_ones, low, high], axis=0).astype(jnp.bfloat16)
    hidden = jnp.dot(weights_one[...], stacked, preferred_element_type=jnp.float32)
    hidden = jnp.maximum(hidden, 0.0).astype(jnp.bfloat16)
    stacked = jnp.concatenate(shifted(hidden, width), axis=0)
    half = out.shape[0] // 2
    copies = []
    for part in range(2):
        rows = pl.ds(part * half * TILE, half * TILE)
        features = jnp.dot(weights_two[rows], stacked, preferred_element_type=jnp.float32)
        features = features + jnp.concatenate([bias_rows[rows]] * (width // LANES), axis=1)
        channels_of = pl.ds(part * half, half)
        staged[channels_of] = features.reshape(half, TILE, width).astype(out.dtype)
        copies.append(pltpu.make_async_copy(staged.at[channels_of], out.at[channels_of], sems.at[part]))
        copies[-1].start()
    for copy in copies:
        copy.wait()


def in_hbm(*arrays):
    return [pltpu.with_memory_space_constraint(array, pltpu.HBM) for array in arrays]


def direct(partials, coverage, conv_one, bias_one, conv_two, bias_two):
    count_row, count_col = lax.axis_size("row"), lax.axis_size("col")
    devices = lax.axis_size("vis") * count_row * count_col
    length = partials.shape[3] * count_col
    image_len = length // 2
    channels = conv_two.shape[2]
    second = grid_table(length)
    vmem, hbm = pl.BlockSpec(memory_space=pltpu.VMEM), pl.BlockSpec(memory_space=pltpu.HBM)
    limit = pltpu.CompilerParams(vmem_limit_bytes=16 * 2**20)
    share = (devices, 2 * (TILE + 2 * HALO), LANES)
    shares = pl.pallas_call(
        functools.partial(share_kernel, length),
        out_shape=jax.ShapeDtypeStruct(share, jnp.bfloat16),
        in_specs=[hbm] * 2,
        out_specs=vmem,
        scratch_shapes=[
            pltpu.SMEM(coverage.shape, jnp.int32),
            pltpu.VMEM(partials.shape, jnp.bfloat16),
            pltpu.VMEM((2 * (image_len + TILE), partials.shape[3]), jnp.bfloat16),
            pltpu.SemaphoreType.DMA((2,)),
        ],
        compiler_params=limit,
        name="shares",
    )(*in_hbm(coverage, partials))
    arrived = lax.all_to_all(shares, ALL, split_axis=0, concat_axis=0, tiled=True)
    rows = TILE + 2
    weights = pl.pallas_call(
        weights_kernel,
        out_shape=[
            jax.ShapeDtypeStruct((rows * channels, 3 * 48), jnp.bfloat16),
            jax.ShapeDtypeStruct((TILE * channels, 3 * rows * channels), jnp.bfloat16),
            jax.ShapeDtypeStruct((TILE * channels, LANES), jnp.float32),
            jax.ShapeDtypeStruct(second.shape, jnp.bfloat16),
        ],
        in_specs=[hbm] * 5,
        out_specs=[vmem] * 4,
        scratch_shapes=[
            pltpu.VMEM((3, 3, channels), jnp.float32),
            pltpu.VMEM((1, channels), jnp.float32),
            pltpu.VMEM(conv_two.shape, jnp.bfloat16),
            pltpu.VMEM((1, channels), jnp.float32),
            pltpu.SemaphoreType.DMA((5,)),
        ],
        compiler_params=limit,
        name="weights",
    )(*in_hbm(conv_one.transpose(1, 2, 0), bias_one[None], conv_two, bias_two[None], jnp.asarray(second)))
    return pl.pallas_call(
        layers_kernel,
        out_shape=jax.ShapeDtypeStruct((channels, TILE, image_len), jnp.bfloat16),
        in_specs=[vmem] * 5,
        out_specs=hbm,
        scratch_shapes=[
            pltpu.VMEM((channels, TILE, image_len), jnp.bfloat16),
            pltpu.SemaphoreType.DMA((2,)),
        ],
        compiler_params=limit,
        name="layers",
    )(arrived, *weights)


def local(partials, coverage, conv_one, bias_one, conv_two, bias_two):
    count_col = lax.axis_size("col")
    devices = lax.axis_size("vis") * lax.axis_size("row") * count_col
    image_len = partials.shape[3] * count_col // 2
    sent = devices * (TILE + 2 * HALO) * image_len * 2
    fits = partials.shape[2] == LANES and image_len == devices * TILE and conv_two.shape[2] * 4 == LANES and image_len == 2 * LANES and sent <= DIRECT_BYTES
    plan = direct if fits else staged
    return plan(partials, coverage, conv_one, bias_one, conv_two, bias_two)


def solution(mesh):
    placed = (P("vis", None, "row", "col"), P("vis", "row", "col"), P(), P(), P(), P())
    return jax.shard_map(
        local,
        mesh=mesh,
        in_specs=placed,
        out_specs=P(None, ALL, None),
        check_vma=False,
    )
```

```python
import functools
import math

import jax
import jax.numpy as jnp
import numpy as np
from jax import lax
from jax.experimental import pallas as pl
from jax.experimental.pallas import tpu as pltpu
from jax.sharding import PartitionSpec as P

BLK = 128
ALL = ("vis", "row", "col")
DIRECT_BYTES = 4 * 2**20
HALO = 2
TILE = 8
LANES = 128


def with_halo(cells, sides, width):
    for axis, dim in sides:
        count = lax.axis_size(axis)
        ends = count - 1
        head = lax.slice_in_dim(cells, 0, width, axis=dim)
        tail = lax.slice_in_dim(cells, cells.shape[dim] - width, cells.shape[dim], axis=dim)
        cells = jnp.concatenate(
            [
                lax.ppermute(tail, axis, [(i, (i + 1) % count) for i in range(ends)]),
                cells,
                lax.ppermute(head, axis, [((i + 1) % count, i) for i in range(ends)]),
            ],
            axis=dim,
        )
    return cells


def phase_table(numer, denom):
    angle = numer.astype(jnp.float32) * (2.0 * math.pi / denom)
    return (jnp.cos(angle), jnp.sin(angle))


def partial_transform(real_part, imag_part, block_of, keep_imag):
    batch = real_part.shape[0]
    count_blocks = real_part.shape[1]
    block_len = real_part.shape[2]
    length = count_blocks * block_len
    highest = lax.Precision.HIGHEST
    outer = jnp.arange(count_blocks, dtype=jnp.int32)
    inner = jnp.arange(block_len, dtype=jnp.int32)
    cos_one, sin_one = phase_table(block_of[:, None] * outer[None, :] % count_blocks, count_blocks)
    mid_re = jnp.einsum("lpt,px->lxt", real_part, cos_one, precision=highest) - jnp.einsum(
        "lpt,px->lxt", imag_part, sin_one, precision=highest
    )
    mid_im = jnp.einsum("lpt,px->lxt", real_part, sin_one, precision=highest) + jnp.einsum(
        "lpt,px->lxt", imag_part, cos_one, precision=highest
    )
    cos_two, sin_two = phase_table(outer[:, None] * inner[None, :] % length, length)
    parity = (1 - 2 * (outer % 2)).astype(jnp.float32)[:, None]
    cos_two = cos_two * parity
    sin_two = sin_two * parity
    turn_re = mid_re * cos_two - mid_im * sin_two
    turn_im = mid_re * sin_two + mid_im * cos_two
    kept = jnp.arange(block_len // 2, dtype=jnp.int32)
    picked = (kept + 3 * block_len // 4) % block_len
    cos_three, sin_three = phase_table(inner[:, None] * picked[None, :] % block_len, block_len)
    out_re = jnp.einsum("lxt,tj->ljx", turn_re, cos_three, precision=highest) - jnp.einsum(
        "lxt,tj->ljx", turn_im, sin_three, precision=highest
    )
    out_re = out_re.reshape(batch, length // 2)
    if keep_imag:
        out_im = jnp.einsum("lxt,tj->ljx", turn_re, sin_three, precision=highest) + jnp.einsum(
            "lxt,tj->ljx", turn_im, cos_three, precision=highest
        )
        return (out_re, out_im.reshape(batch, length // 2))
    return (out_re, out_re)


def first_layer(extended, conv_one, bias_one, count_rows):
    width = extended.shape[1]
    padded = jnp.pad(extended, ((0, 0), (1, 1)))
    summed = (
        jnp.zeros((conv_one.shape[0], count_rows, width), jnp.float32) + bias_one[:, None, None]
    )
    for shift_b in range(3):
        for shift_a in range(3):
            summed = (
                summed
                + conv_one[:, shift_b, shift_a][:, None, None]
                * padded[None, shift_b : shift_b + count_rows, shift_a : shift_a + width]
            )
    return jnp.maximum(summed, 0.0)


def second_layer(hidden_ext, conv_two, bias_two, count_rows):
    width = hidden_ext.shape[2]
    padded = jnp.pad(hidden_ext, ((0, 0), (0, 0), (1, 1)))
    summed = jnp.zeros((conv_two.shape[2], count_rows, width), jnp.float32)
    for shift_b in range(3):
        for shift_a in range(3):
            summed = summed + jnp.einsum(
                "kj,jba->kba",
                conv_two[shift_b, shift_a],
                padded[:, shift_b : shift_b + count_rows, shift_a : shift_a + width],
                preferred_element_type=jnp.float32,
            )
    return (summed + bias_two[:, None, None]).astype(jnp.bfloat16)


def staged(partials, coverage, conv_one, bias_one, conv_two, bias_two):
    count_vis = lax.axis_size("vis")
    count_row = lax.axis_size("row")
    count_col = lax.axis_size("col")
    grid_len = partials.shape[3] * count_col
    cover = coverage[0]
    block_rows = cover.shape[0]
    block_cols = cover.shape[1]
    spread = jnp.broadcast_to(cover[:, None, :, None], (block_rows, BLK, block_cols, BLK))
    spread = spread.reshape(block_rows * BLK, block_cols * BLK)
    count_blocks = count_vis * count_row
    row_block = grid_len // count_blocks
    row_share = row_block // count_col
    masked = partials[0] * spread.astype(jnp.bfloat16)[None]
    reduced = lax.psum_scatter(
        masked.astype(jnp.float32).astype(jnp.bfloat16), "vis", scatter_dimension=1, tiled=True
    ).astype(jnp.float32)
    grid_rows = lax.all_to_all(
        reduced.astype(jnp.bfloat16), "col", split_axis=1, concat_axis=2, tiled=True
    ).astype(reduced.dtype)
    natural = jnp.arange(count_blocks, dtype=jnp.int32)
    shaped = grid_rows.reshape(2, row_share, count_blocks, row_block)
    first_re, first_im = partial_transform(shaped[0], shaped[1], natural, True)
    stacked = jnp.stack([first_re, first_im])
    moved = lax.all_to_all(
        lax.all_to_all(
            stacked.astype(jnp.bfloat16), ("vis", "row"), split_axis=2, concat_axis=1, tiled=True
        ),
        "col",
        split_axis=2,
        concat_axis=1,
        tiled=True,
    ).astype(stacked.dtype)
    img_rows = moved.shape[2]
    arranged = moved.reshape(2, count_col, count_blocks, row_share, img_rows)
    arranged = arranged.transpose(0, 4, 2, 1, 3).reshape(2, img_rows, count_blocks, row_block)
    owners = natural % count_row * count_vis + natural // count_row
    image, unused = partial_transform(arranged[0], arranged[1], owners, False)
    image = image * (1.0 / grid_len)
    extended = with_halo(image.astype(jnp.bfloat16), ((("vis", "row", "col"), 0),), 1).astype(
        image.dtype
    )
    hidden = first_layer(extended, conv_one, bias_one, img_rows).astype(jnp.bfloat16)
    hidden_ext = with_halo(hidden, ((("vis", "row", "col"), 1),), 1)
    return second_layer(hidden_ext, conv_two, bias_two, img_rows)


def grid_table(length):
    image_len = length // 2
    place = np.arange(length)[:, None] - length // 2
    pixel = np.arange(image_len)[None, :] - image_len // 2
    angle = (place * pixel % length) * (2.0 * math.pi / length)
    cos, sin = (wave.reshape(-1, LANES, image_len) for wave in (np.cos(angle), np.sin(angle)))
    return (np.stack([cos, -sin], axis=1).reshape(2 * length, image_len) / length).astype(jnp.bfloat16)


def phases(numer, length):
    turn = numer & (length - 1)
    turn = jnp.where(turn >= length // 2, turn - length, turn)
    angle = turn.astype(jnp.float32) * (2.0 * math.pi / length)
    return jnp.cos(angle), jnp.sin(angle)


def make_first(first, length):
    tall, cols = first.shape[0] // 2, first.shape[1]
    image_len = tall - TILE
    start = lax.axis_index("col") * cols - length // 2
    place = start + lax.broadcasted_iota(jnp.int32, (TILE, cols), 1)
    row = lax.broadcasted_iota(jnp.int32, (TILE, cols), 0)
    cos_far, sin_far = phases((row * TILE * TILE - HALO - image_len // 2) * place, length)
    cos_mid, sin_mid = phases(row * TILE * place, length)
    cos_near, sin_near = phases(row * place, length)
    cosines, sines = [], []
    for k in range(tall // TILE):
        n, m = divmod(k, TILE)
        if m == 0:
            cos_at, sin_at = cos_far[n : n + 1], sin_far[n : n + 1]
            cos_tile = cos_at * cos_mid - sin_at * sin_mid
            sin_tile = sin_at * cos_mid + cos_at * sin_mid
        cos_at, sin_at = cos_tile[m : m + 1], sin_tile[m : m + 1]
        cos = cos_at * cos_near - sin_at * sin_near
        sin = sin_at * cos_near + cos_at * sin_near
        pixel = row + (TILE * k - HALO)
        if k == 0 or k == tall // TILE - 1:
            inside = (pixel >= 0) & (pixel < image_len)
            cos, sin = jnp.where(inside, cos, 0.0), jnp.where(inside, sin, 0.0)
        cosines.append(cos)
        sines.append(sin)
    first[...] = jnp.concatenate(cosines + sines, axis=0).astype(first.dtype)


def share_kernel(length, cover_in, parts_in, out, cover, parts, first, sems):
    get_cover = pltpu.make_async_copy(cover_in, cover, sems.at[0])
    get_parts = pltpu.make_async_copy(parts_in, parts, sems.at[1])
    for copy in (get_cover, get_parts):
        copy.start()
    make_first(first, length)
    count_rows = parts.shape[2]
    get_cover.wait()
    get_parts.wait()
    components = []
    for component in range(2):
        strips = []
        for i in range(cover.shape[1]):
            cells = []
            for j in range(cover.shape[2]):
                block = parts[0, component, i * BLK : (i + 1) * BLK, j * BLK : (j + 1) * BLK]
                level = jnp.full(block.shape, cover[0, i, j].astype(jnp.float32)).astype(jnp.bfloat16)
                cells.append(block * level)
            strips.append(jnp.concatenate(cells, axis=1))
        components.append(jnp.concatenate(strips, axis=0))
    grid = jnp.concatenate(components, axis=0)
    upper = lax.broadcasted_iota(jnp.int32, (TILE, LANES), 0) < TILE // 2
    devices = out.shape[0]
    tall = first.shape[0] // 2
    turned = lax.dot_general(first[...], grid, (((1,), (1,)), ((), ())), preferred_element_type=jnp.float32)
    mid_re = turned[:tall, :count_rows] - turned[tall:, count_rows:]
    mid_im = turned[tall:, :count_rows] + turned[:tall, count_rows:]
    for device in range(devices):
        here = slice(TILE * device, TILE * (device + 1))
        below = slice(TILE * (device + 1), TILE * (device + 2))
        middle = jnp.where(upper, mid_re[below], pltpu.roll(mid_im[below], TILE // 2, 0))
        out[device] = jnp.concatenate([mid_re[here], middle, mid_im[here]], axis=0).astype(out.dtype)


def own_place():
    place, count = 0, 1
    for axis in ALL:
        place = place * lax.axis_size(axis) + lax.axis_index(axis)
        count = count * lax.axis_size(axis)
    return place, count - 1


def four_times(values):
    return jnp.concatenate([values] * 4, axis=1)


def weights_kernel(
    one_in, bias_in, two_in, bias_two_in, table_in, weights_one, weights_two, bias_rows, table, one, bias, two, bias_two, sems
):
    fetch = [
        pltpu.make_async_copy(one_in, one, sems.at[0]),
        pltpu.make_async_copy(bias_in, bias, sems.at[1]),
        pltpu.make_async_copy(two_in, two, sems.at[2]),
        pltpu.make_async_copy(bias_two_in, bias_two, sems.at[3]),
    ]
    get_table = pltpu.make_async_copy(table_in, table, sems.at[4])
    for copy in (*fetch, get_table):
        copy.start()
    for copy in fetch:
        copy.wait()
    channels = one.shape[2]
    rows = TILE + 2
    per_tile = LANES // channels
    lanes = -(-rows * channels // LANES) * LANES
    image_row = lax.broadcasted_iota(jnp.int32, (16, lanes), 0)
    hidden_row = lax.broadcasted_iota(jnp.int32, (16, lanes), 1) // channels
    place, last = own_place()
    held = (hidden_row >= jnp.where(place == 0, 1, 0)) & (hidden_row < jnp.where(place == last, rows - 1, rows))
    high, low = [], []
    for tap in range(3):
        band = jnp.zeros((16, lanes), jnp.float32)
        for shift in range(3):
            line = jnp.concatenate([four_times(one[shift, tap : tap + 1])] * (lanes // LANES), axis=1)
            band = jnp.where(held & (image_row - hidden_row == shift), line, band)
        high.append(band.astype(jnp.bfloat16).astype(jnp.float32))
        low.append(band - high[-1])
    line = jnp.concatenate([four_times(bias[...])] * (lanes // LANES), axis=1)
    with_bias = high[0]
    for piece in range(3):
        rounded = line.astype(jnp.bfloat16).astype(jnp.float32)
        with_bias = jnp.where(held & (image_row == 12 + piece), rounded, with_bias)
        line = line - rounded
    stacked = jnp.concatenate([with_bias, *high[1:], *high, *low], axis=0)
    weights_one[...] = stacked.T[: weights_one.shape[0]].astype(jnp.bfloat16)
    row = lax.broadcasted_iota(jnp.int32, bias_rows.shape, 0) // TILE
    lane = lax.broadcasted_iota(jnp.int32, bias_rows.shape, 1)
    line = jnp.where(row == lane, four_times(bias_two[...]), 0.0)
    bias_rows[...] = jnp.broadcast_to(jnp.sum(line, axis=1, keepdims=True), bias_rows.shape)
    lines = [[four_times(two[shift, tap].astype(jnp.float32)) for shift in range(3)] for tap in range(3)]
    row = lax.broadcasted_iota(jnp.int32, (TILE, LANES), 0)
    lane = lax.broadcasted_iota(jnp.int32, (TILE, LANES), 1) // channels
    zero = jnp.zeros((TILE, LANES), jnp.float32)
    for tile in range(-(-3 * rows // per_tile)):
        taps = sorted({(tile * per_tile + g) // rows for g in range(per_tile)} & {0, 1, 2})
        masks = []
        for tap in taps:
            hidden_row = tile * per_tile + lane - tap * rows
            inside = (hidden_row >= 0) & (hidden_row < rows)
            masks += [(tap, shift, inside & (hidden_row - row == shift)) for shift in range(3)]
        width = min(LANES, weights_two.shape[1] - tile * LANES)
        for channel in range(0, channels, 2):
            pair = []
            for k in (channel, channel + 1):
                values = zero
                for tap, shift, mask in masks:
                    values = jnp.where(mask, lines[tap][shift][k : k + 1], values)
                pair.append(values)
            block = jnp.concatenate(pair, axis=0).astype(jnp.bfloat16)
            weights_two[TILE * channel : TILE * (channel + 2), tile * LANES : tile * LANES + width] = block[:, :width]
    get_table.wait()


def shifted(values, width):
    lane = lax.broadcasted_iota(jnp.int32, values.shape, 1)
    zero = jnp.zeros_like(values)
    before = jnp.where(lane == 0, zero, pltpu.roll(values, 1, 1))
    after = jnp.where(lane == width - 1, zero, pltpu.roll(values, width - 1, 1))
    return before, values, after


def layers_kernel(shares, weights_one, weights_two, bias_rows, table, out, staged, sems):
    width = out.shape[2]
    vis, row, col = (lax.axis_size(axis) for axis in ALL)
    upper = lax.broadcasted_iota(jnp.int32, (TILE, LANES), 0) < TILE // 2
    above, below = [], []
    for r in range(row):
        senders = [(v * row + r) * col + c for v in range(vis) for c in range(col)]
        total = shares[senders[0]].astype(jnp.float32)
        for sender in senders[1:]:
            total = total + shares[sender].astype(jnp.float32)
        middle = total[TILE : 2 * TILE]
        above += [total[:TILE], total[2 * TILE :]]
        below += [jnp.where(upper, middle, 0.0), jnp.where(upper, pltpu.roll(middle, TILE // 2, 0), 0.0)]
    turned = jnp.concatenate([jnp.concatenate(above, axis=1), jnp.concatenate(below, axis=1)], axis=0)
    high = turned.astype(jnp.bfloat16)
    low = (turned - high.astype(jnp.float32)).astype(jnp.bfloat16)
    image = jnp.dot(jnp.concatenate([high, low], axis=0), table[...], preferred_element_type=jnp.float32)
    image = image[: 2 * TILE] + image[2 * TILE :]
    columns = jnp.concatenate(shifted(image, width), axis=0)
    high = columns.astype(jnp.bfloat16).astype(jnp.float32)
    low = columns - high
    row = lax.broadcasted_iota(jnp.int32, (48, width), 0)
    with_ones = jnp.where((row >= 12) & (row < 15), 1.0, high)
    stacked = jnp.concatenate([with_ones, low, high], axis=0).astype(jnp.bfloat16)
    hidden = jnp.dot(weights_one[...], stacked, preferred_element_type=jnp.float32)
    hidden = jnp.maximum(hidden, 0.0).astype(jnp.bfloat16)
    stacked = jnp.concatenate(shifted(hidden, width), axis=0)
    cut = out.shape[0] * 5 // 8
    copies = []
    for part, (start, count) in enumerate(((0, cut), (cut, out.shape[0] - cut))):
        rows = pl.ds(start * TILE, count * TILE)
        features = jnp.dot(weights_two[rows], stacked, preferred_element_type=jnp.float32)
        features = features + jnp.concatenate([bias_rows[rows]] * (width // LANES), axis=1)
        channels_of = pl.ds(start, count)
        staged[channels_of] = features.reshape(count, TILE, width).astype(out.dtype)
        copies.append(pltpu.make_async_copy(staged.at[channels_of], out.at[channels_of], sems.at[part]))
        copies[-1].start()
    for copy in copies:
        copy.wait()


def in_hbm(*arrays):
    return [pltpu.with_memory_space_constraint(array, pltpu.HBM) for array in arrays]


def direct(partials, coverage, conv_one, bias_one, conv_two, bias_two):
    count_row, count_col = lax.axis_size("row"), lax.axis_size("col")
    devices = lax.axis_size("vis") * count_row * count_col
    length = partials.shape[3] * count_col
    image_len = length // 2
    channels = conv_two.shape[2]
    second = grid_table(length)
    vmem, hbm = pl.BlockSpec(memory_space=pltpu.VMEM), pl.BlockSpec(memory_space=pltpu.HBM)
    limit = pltpu.CompilerParams(vmem_limit_bytes=16 * 2**20)
    share = (devices, 2 * (TILE + 2 * HALO), LANES)
    shares = pl.pallas_call(
        functools.partial(share_kernel, length),
        out_shape=jax.ShapeDtypeStruct(share, jnp.bfloat16),
        in_specs=[hbm] * 2,
        out_specs=vmem,
        scratch_shapes=[
            pltpu.SMEM(coverage.shape, jnp.int32),
            pltpu.VMEM(partials.shape, jnp.bfloat16),
            pltpu.VMEM((2 * (image_len + TILE), partials.shape[3]), jnp.bfloat16),
            pltpu.SemaphoreType.DMA((2,)),
        ],
        compiler_params=limit,
        name="shares",
    )(*in_hbm(coverage, partials))
    arrived = lax.all_to_all(shares, ALL, split_axis=0, concat_axis=0, tiled=True)
    rows = TILE + 2
    weights = pl.pallas_call(
        weights_kernel,
        out_shape=[
            jax.ShapeDtypeStruct((rows * channels, 3 * 48), jnp.bfloat16),
            jax.ShapeDtypeStruct((TILE * channels, 3 * rows * channels), jnp.bfloat16),
            jax.ShapeDtypeStruct((TILE * channels, LANES), jnp.float32),
            jax.ShapeDtypeStruct(second.shape, jnp.bfloat16),
        ],
        in_specs=[hbm] * 5,
        out_specs=[vmem] * 4,
        scratch_shapes=[
            pltpu.VMEM((3, 3, channels), jnp.float32),
            pltpu.VMEM((1, channels), jnp.float32),
            pltpu.VMEM(conv_two.shape, jnp.bfloat16),
            pltpu.VMEM((1, channels), jnp.float32),
            pltpu.SemaphoreType.DMA((5,)),
        ],
        compiler_params=limit,
        name="weights",
    )(*in_hbm(conv_one.transpose(1, 2, 0), bias_one[None], conv_two, bias_two[None], jnp.asarray(second)))
    return pl.pallas_call(
        layers_kernel,
        out_shape=jax.ShapeDtypeStruct((channels, TILE, image_len), jnp.bfloat16),
        in_specs=[vmem] * 5,
        out_specs=hbm,
        scratch_shapes=[
            pltpu.VMEM((channels, TILE, image_len), jnp.bfloat16),
            pltpu.SemaphoreType.DMA((2,)),
        ],
        compiler_params=limit,
        name="layers",
    )(arrived, *weights)


def local(partials, coverage, conv_one, bias_one, conv_two, bias_two):
    count_col = lax.axis_size("col")
    devices = lax.axis_size("vis") * lax.axis_size("row") * count_col
    image_len = partials.shape[3] * count_col // 2
    sent = devices * (TILE + 2 * HALO) * image_len * 2
    fits = partials.shape[2] == LANES and image_len == devices * TILE and conv_two.shape[2] * 4 == LANES and image_len == 2 * LANES and sent <= DIRECT_BYTES
    plan = direct if fits else staged
    return plan(partials, coverage, conv_one, bias_one, conv_two, bias_two)


def solution(mesh):
    placed = (P("vis", None, "row", "col"), P("vis", "row", "col"), P(), P(), P(), P())
    return jax.shard_map(
        local,
        mesh=mesh,
        in_specs=placed,
        out_specs=P(None, ALL, None),
        check_vma=False,
    )
```
